32 devices in a mesh: expert: 8 (over y, x, core), fsdp: 4 (over z).
Axes of the slice: x: 2, y: 2, z: 4, core: 2. Of those that a mesh axis runs over, the one named last changes fastest.
Arguments:
- tokens: bfloat16 [8192, 2048], P(('expert', 'fsdp')), may hold values from -6 to 6
- cotangent: bfloat16 [8192, 2048], P(('expert', 'fsdp')), may hold values from -6 to 6
- lengths: int32 [64], replicated, may hold values from 1 to 224, as said below
- owners: int32 [64], replicated, may hold values from 0 to 31, as said below
- routes: int32 [8192, 8], P(('expert', 'fsdp')), may hold values from 0 to 31, all different within a row; in each aligned block of 256 rows (0 to 255, 256 to 511, ...) at most 80 rows name the same one
- w_query: bfloat16 [2048, 4096], P(('expert', 'fsdp')), may hold values from -0.125 to 0.125
- key_weight: bfloat16 [2048, 512], P(('expert', 'fsdp')), may hold values from -0.125 to 0.125
- value_weight: bfloat16 [2048, 512], P(('expert', 'fsdp')), may hold values from -0.125 to 0.125
- w_out: bfloat16 [4096, 2048], P(('expert', 'fsdp')), may hold values from -0.375 to 0.375
- w_router: bfloat16 [2048, 32], P(('expert', 'fsdp')), may hold values from -0.0625 to 0.0625
- norm_gains: bfloat16 [4352], P(('expert', 'fsdp')), may hold values from 0.099609375 to 1.8984375
- w_gate: bfloat16 [32, 2048, 768], P(('expert', 'fsdp')), may hold values from -0.125 to 0.125
- w_up: bfloat16 [32, 2048, 768], P(('expert', 'fsdp')), may hold values from -0.125 to 0.125
- w_down: bfloat16 [32, 768, 2048], P(('expert', 'fsdp')), may hold values from -0.875 to 0.875
Outputs:
- block_out: bfloat16 [8192, 2048], P(('expert', 'fsdp'))
- grad_tokens: float32 [8192, 2048], P(('expert', 'fsdp'))
- grad_query: float32 [2048, 4096], P(('expert', 'fsdp'))
- grad_key: float32 [2048, 512], P(('expert', 'fsdp'))
- grad_value: float32 [2048, 512], P(('expert', 'fsdp'))
- grad_out: float32 [4096, 2048], P(('expert', 'fsdp'))
- grad_router: float32 [2048, 32], P(('expert', 'fsdp'))
- grad_gains: float32 [4352], P(('expert', 'fsdp'))
- grad_gate: float32 [32, 2048, 768], P(('expert', 'fsdp'))
- grad_up: float32 [32, 2048, 768], P(('expert', 'fsdp'))
- grad_down: float32 [32, 768, 2048], P(('expert', 'fsdp'))
The draws below stay inside these ranges and needn't reach their ends.
Inputs may be any that keep to these rules, and one draw needn't show every extreme that they name: `lengths`: sequences 2 i and 2 i + 1 have the same owner, every device owns exactly two sequences, and the two sequences of a device have at most 256 tokens together; the longest sequence has 224 tokens. `owners`: every device owns exactly two sequences. `routes`: the 8 experts of a slot differ; within the slots of one device (aligned blocks of 256 rows) no expert is named by more than 80 rows, padding slots included.
All inputs are finite; a program needn't handle non-finite values.
Results may differ from the reference program's by a relative error of at most 0.018.
Values may be sent and summed in bfloat16 or wider, within the bound.
A program may use at most 384 MiB of HBM per device.

```python
import math
import jax
import jax.numpy as jnp
import numpy as np
from jax import lax

MODEL_DIM = 2048
QUERY_HEADS = 32
KEY_VALUE_HEADS = 4
HEAD_DIM = 128
FF = 768
TOP = 8
TOKENS_PER_CHIP = 256
EXPERTS = 32
CAP = 80
TOKENS = 8192
N_EXPERT = 8
N_FSDP = 4


def sequence_plan(key):
    pair_count = N_EXPERT * N_FSDP
    placed = jax.random.permutation(jax.random.fold_in(key, 11), pair_count).astype(jnp.int32)
    first_len = jax.random.randint(jax.random.fold_in(key, 12), (pair_count,), TOKENS_PER_CHIP // 8, TOKENS_PER_CHIP * 7 // 8 + 1)
    chosen = jax.random.randint(jax.random.fold_in(key, 13), (), 0, pair_count)
    first_len = jnp.where(jnp.arange(pair_count) == chosen, TOKENS_PER_CHIP * 7 // 8, first_len)
    second_len = jax.random.randint(jax.random.fold_in(key, 14), (pair_count,), 1, TOKENS_PER_CHIP - first_len + 1)
    lengths = jnp.stack([first_len, second_len], axis=1).reshape(-1).astype(jnp.int32)
    owners = jnp.repeat(placed, 2).astype(jnp.int32)
    return (lengths, owners)


def draw_lengths(key, part):
    return sequence_plan(key)[0]


def draw_owners(key, part):
    return sequence_plan(key)[1]


def level_of(own_key, dims, pieces, low, top_value):
    def one(axis_at, blocks):
        draws = jax.random.uniform(jax.random.fold_in(jax.random.fold_in(own_key, 6), axis_at), (blocks,), jnp.float32, low / len(pieces), top_value / len(pieces))
        return jnp.repeat(jnp.exp(draws), dims[axis_at] // blocks).reshape((-1,) + (1,) * (len(dims) - axis_at - 1))

    level = one(*pieces[0])
    for cut in pieces[1:]:
        level = level * one(*cut)
    return level


def deal_out(own_key, own, number, rows, amount, top, most, slope):
    sequence = jax.random.permutation(own_key, amount)
    heavy_load, ordinary = load_shares(amount, rows * top, most, slope, True), load_shares(amount, rows * top, most, slope, False)
    places = jnp.arange(amount)

    def named(sizes, rotation):
        used = int((sizes > 0).sum())
        fixed = max(1, used // 4)
        shifted = fixed + (places - fixed + rotation * (used - fixed)) % max(1, amount - fixed)
        return jnp.zeros((amount,), jnp.int32).at[sequence[jnp.where(places < fixed, places, shifted)]].set(jnp.asarray(sizes, jnp.int32))

    sizes = jnp.where(number % 4 == 0, named(heavy_load, number // 4), named(ordinary, number - number // 4 - 1))
    mixed = jax.random.permutation(jax.random.fold_in(own, 3), amount)
    source_of, receiver = mixed[0:amount // 2 * 2:2], mixed[1:amount // 2 * 2:2]
    room = jnp.minimum(sizes[source_of] - 1, most - sizes[receiver]) // 2
    room = jnp.where((source_of == sequence[0]) | (receiver == sequence[0]) | (sizes[receiver] == 0), 0, jnp.maximum(room, 0))
    shifted = jax.random.randint(jax.random.fold_in(own, 4), (amount // 2,), 0, 1 << 20) % (room + 1)
    sizes = sizes.at[source_of].add(-shifted).at[receiver].add(shifted)
    labels = jnp.searchsorted(jnp.cumsum(sizes), jnp.arange(rows * top), side="right").astype(jnp.int32)
    table = labels.reshape(top, rows).T
    table = table[jax.random.permutation(jax.random.fold_in(own, 1), rows)]
    rotation = jax.random.randint(jax.random.fold_in(own, 2), (rows, 1), 0, top)
    return jnp.take_along_axis(table, (jnp.arange(top)[None, :] + rotation) % top, axis=1)


def load_shares(number_of, total, reach, slope, full):
    weights = [(1 << 20) // math.isqrt(rank ** slope) + 1 for rank in range(1, number_of + 1)]
    largest = reach if full else min(reach, max(-(-total // number_of), total * weights[0] // sum(weights)))
    least = 1 if total - largest >= number_of - 1 else 0
    given, rest = [largest] + [least] * (number_of - 1), total - largest - least * (number_of - 1)
    while rest > 0:
        movable = [i for i in range(1, number_of) if given[i] < largest] or [i for i in range(1, number_of) if given[i] < reach]
        pool, left = sum([weights[i] for i in movable]), rest
        for i in movable:
            extra = min(reach - given[i], max(1, left * weights[i] // pool), rest)
            given[i] = given[i] + extra
            rest = rest - extra
    return np.array(given)


def centred(key, extent, deviation, bound, shards=(), kind=jnp.bfloat16):
    values = deviation * jax.random.normal(key, extent, jnp.float32)
    if shards:
        values = values * level_of(key, extent, shards, -0.22, 0.18)
    return jnp.clip(values, -bound, bound).astype(kind)


def setup_inputs(seed: int = 0) -> dict:
    arg_keys = jax.random.split(jax.random.key(seed), 15)
    tokens = centred(arg_keys[0], (TOKENS, MODEL_DIM), 1.0, 6.0, ((0, 32),))
    cotangent = centred(arg_keys[1], (TOKENS, MODEL_DIM), 1.0, 6.0, ((0, 32),))
    lengths = draw_lengths(jax.random.fold_in(arg_keys[14], 71), 0)
    owners = draw_owners(jax.random.fold_in(arg_keys[14], 71), 0)
    routes_keys = jax.random.split(jax.random.fold_in(arg_keys[4], 1), TOKENS // TOKENS_PER_CHIP)
    routes_turns = jax.random.permutation(jax.random.fold_in(arg_keys[4], 3), TOKENS // TOKENS_PER_CHIP)
    routes = jax.vmap(lambda own, number: deal_out(jax.random.fold_in(arg_keys[4], 2), own, number, TOKENS_PER_CHIP, EXPERTS, TOP, CAP, 1))(routes_keys, routes_turns).reshape((TOKENS, TOP))
    w_query = centred(arg_keys[5], (MODEL_DIM, QUERY_HEADS * HEAD_DIM), MODEL_DIM ** -0.5, 0.125, ((0, 32),))
    key_weight = centred(arg_keys[6], (MODEL_DIM, KEY_VALUE_HEADS * HEAD_DIM), MODEL_DIM ** -0.5, 0.125, ((0, 32),))
    value_weight = centred(arg_keys[7], (MODEL_DIM, KEY_VALUE_HEADS * HEAD_DIM), MODEL_DIM ** -0.5, 0.125, ((0, 32),))
    w_out = centred(arg_keys[8], (QUERY_HEADS * HEAD_DIM, MODEL_DIM), (QUERY_HEADS * HEAD_DIM // 16) ** -0.5, 0.375, ((0, 32),))
    w_router = centred(arg_keys[9], (MODEL_DIM, EXPERTS), (4 * MODEL_DIM) ** -0.5, 0.0625, ((0, 32),))
    norm_gains = jnp.clip(1.0 + 0.18 * jax.random.normal(arg_keys[10], (2 * MODEL_DIM + 2 * HEAD_DIM,), jnp.float32), 0.099609375, 1.8984375).astype(jnp.bfloat16)
    w_gate = centred(arg_keys[11], (EXPERTS, MODEL_DIM, FF), MODEL_DIM ** -0.5, 0.125, ((0, 32),))
    w_up = centred(arg_keys[12], (EXPERTS, MODEL_DIM, FF), MODEL_DIM ** -0.5, 0.125, ((0, 32),))
    w_down = centred(arg_keys[13], (EXPERTS, FF, MODEL_DIM), (FF // 16) ** -0.5, 0.875, ((0, 32),))
    return {"tokens": tokens, "cotangent": cotangent, "lengths": lengths, "owners": owners, "routes": routes, "w_query": w_query, "key_weight": key_weight, "value_weight": value_weight, "w_out": w_out, "w_router": w_router, "norm_gains": norm_gains, "w_gate": w_gate, "w_up": w_up, "w_down": w_down}


HIGH_PRECISION = lax.Precision.HIGHEST
EPSILON = 1e-06

@jax.custom_vjp
def lower_precision(v):
    return lax.optimization_barrier(v.astype(jnp.bfloat16)).astype(jnp.float32)

@jax.custom_vjp
def lower_precision_back(v):
    return v

def low_keep(v):
    return (lower_precision(v), None)

def low_pass(kept, grad):
    return (grad,)

def back_keep(v):
    return (v, None)

def back_low(kept, grad):
    return (lower_precision(grad),)
lower_precision.defvjp(low_keep, low_pass)
lower_precision_back.defvjp(back_keep, back_low)

def rms_norm(values, gain_row):
    return values * lax.rsqrt(lax.optimization_barrier(jnp.mean(values * values, axis=-1, keepdims=True)) + EPSILON) * gain_row

def rotate(values, token_position):
    half_size = values.shape[-1] // 2
    frequency = jnp.power(1000000.0, -2.0 * jnp.arange(half_size, dtype=jnp.float32) / values.shape[-1])
    angles = token_position.astype(jnp.float32)[:, None] * frequency[None, :]
    cosine = jnp.cos(angles)[:, None, :]
    sine_val = jnp.sin(angles)[:, None, :]
    first_half = values[..., :half_size]
    second_half = values[..., half_size:]
    return jnp.concatenate([first_half * cosine - second_half * sine_val, second_half * cosine + first_half * sine_val], axis=-1)

def prepare_attention(token_position, head_count, raw_rows, gain_row):
    shaped = raw_rows.reshape(raw_rows.shape[0], head_count, -1)
    return rotate(rms_norm(shaped, gain_row), token_position)

def layout(lengths, owners, device, row_count):
    seq_order = jnp.arange(lengths.shape[0], dtype=jnp.int32)
    owned = (owners == device).astype(jnp.int32)
    earlier = (seq_order[None, :] < seq_order[:, None]).astype(jnp.int32)
    starts = lax.optimization_barrier(jnp.sum(earlier * (owned * lengths)[None, :], axis=1))
    row_index = jnp.arange(row_count, dtype=jnp.int32)
    inside = owned[None, :] * (row_index[:, None] >= starts[None, :]).astype(jnp.int32) * (row_index[:, None] < (starts + lengths)[None, :]).astype(jnp.int32)
    live_rows = lax.optimization_barrier(jnp.sum(inside, axis=1))
    segment = lax.optimization_barrier(jnp.sum(inside * (seq_order[None, :] + 1), axis=1)) - 1
    token_position = lax.optimization_barrier(jnp.sum(inside * (row_index[:, None] - starts[None, :]), axis=1))
    return (live_rows, segment, token_position)

def allowed_mask(segment):
    row_index = jnp.arange(segment.shape[0], dtype=jnp.int32)
    same_seq = (segment[:, None] == segment[None, :]) & (segment[:, None] >= 0) & (row_index[None, :] <= row_index[:, None])
    return same_seq | (row_index[:, None] == row_index[None, :])

def slot_table(routes, live_rows, experts):
    flat_routes = routes.reshape(-1)
    route_live = jnp.repeat(live_rows, routes.shape[1])
    onehot = (flat_routes[:, None] == jnp.arange(experts, dtype=jnp.int32)[None, :]).astype(jnp.int32) * route_live[:, None]
    before = jnp.cumsum(onehot, axis=0) - onehot
    slot_of = lax.optimization_barrier(jnp.sum(before * onehot, axis=1))
    return (slot_of.reshape(routes.shape).astype(jnp.int32), route_live.reshape(routes.shape))

def gate_values(routes, logits):
    probs_all = jax.nn.softmax(logits, axis=-1)
    picked = jnp.take_along_axis(probs_all, routes, axis=1)
    return picked / lax.optimization_barrier(jnp.sum(picked, axis=1, keepdims=True))

def device_layer(weights, block, lengths, owners):
    w_query, key_weight, value_weight, w_out, w_router, norm_gains, w_gate, w_up, w_down = weights
    tokens, routes, device = block
    live_rows, segment, token_position = layout(lengths, owners, device, TOKENS_PER_CHIP)
    live_col = live_rows.astype(jnp.float32)[:, None]
    gain_one = norm_gains[:MODEL_DIM]
    gain_two = norm_gains[MODEL_DIM:2 * MODEL_DIM]
    query_norm_gain = norm_gains[2 * MODEL_DIM:2 * MODEL_DIM + HEAD_DIM]
    key_norm_gain = norm_gains[2 * MODEL_DIM + HEAD_DIM:]
    normed_inputs = lower_precision(rms_norm(tokens, gain_one))
    query_projected = lower_precision_back(jnp.dot(normed_inputs, w_query, precision=HIGH_PRECISION))
    key_projected = lower_precision_back(jnp.dot(normed_inputs, key_weight, precision=HIGH_PRECISION))
    value_projected_rows = lower_precision(lower_precision_back(jnp.dot(normed_inputs, value_weight, precision=HIGH_PRECISION))).reshape(TOKENS_PER_CHIP, KEY_VALUE_HEADS, HEAD_DIM)
    query_normalized = lower_precision(prepare_attention(token_position, QUERY_HEADS, query_projected, query_norm_gain)).reshape(TOKENS_PER_CHIP, KEY_VALUE_HEADS, QUERY_HEADS // KEY_VALUE_HEADS, HEAD_DIM)
    key_normalized = lower_precision(prepare_attention(token_position, KEY_VALUE_HEADS, key_projected, key_norm_gain))
    scores = lower_precision_back(jnp.einsum('tkgd,skd->kgts', query_normalized, key_normalized, precision=HIGH_PRECISION) * HEAD_DIM ** (-0.5))
    scores = jnp.where(allowed_mask(segment)[None, None], scores, -1e+30)
    row_peak = lax.optimization_barrier(jnp.max(scores, axis=-1, keepdims=True))
    exponent = jnp.exp(scores - row_peak)
    attend = lower_precision(exponent / lax.optimization_barrier(jnp.sum(exponent, axis=-1, keepdims=True)))
    mixed = jnp.einsum('kgts,skd->tkgd', attend, value_projected_rows, precision=HIGH_PRECISION).reshape(TOKENS_PER_CHIP, QUERY_HEADS * HEAD_DIM)
    mixed = lower_precision(lower_precision_back(mixed))
    hidden = tokens + live_col * lower_precision_back(jnp.dot(mixed, w_out, precision=HIGH_PRECISION))
    normed_two = lower_precision(rms_norm(hidden, gain_two))
    logits = lower_precision_back(jnp.dot(normed_two, w_router, precision=HIGH_PRECISION))
    gate_weights = gate_values(routes, logits)
    slot_of, route_live = slot_table(routes, live_rows, EXPERTS)
    live_f = route_live.astype(jnp.float32)
    copies = lower_precision_back(jnp.broadcast_to(normed_two[:, None, :], (TOKENS_PER_CHIP, TOP, MODEL_DIM))) * live_f[:, :, None]
    buffer = jnp.zeros((EXPERTS, CAP, MODEL_DIM), jnp.float32).at[routes, slot_of].add(copies)
    gate_part = lower_precision_back(jnp.einsum('ecd,edf->ecf', buffer, w_gate, precision=HIGH_PRECISION))
    up_part = lower_precision_back(jnp.einsum('ecd,edf->ecf', buffer, w_up, precision=HIGH_PRECISION))
    inner = lower_precision(jax.nn.silu(gate_part) * up_part)
    result = lower_precision(lower_precision_back(jnp.einsum('ecf,efd->ecd', inner, w_down, precision=HIGH_PRECISION)))
    picked = result[routes, slot_of]
    return hidden + lax.optimization_barrier(jnp.sum((gate_weights * live_f)[:, :, None] * picked, axis=1))

def reference(tokens, cotangent, lengths, owners, routes, w_query, key_weight, value_weight, w_out, w_router, norm_gains, w_gate, w_up, w_down):
    device_count = N_EXPERT * N_FSDP
    params = tuple((item.astype(jnp.float32) for item in (w_query, key_weight, value_weight, w_out, w_router, norm_gains, w_gate, w_up, w_down)))
    token_blocks = tokens.astype(jnp.float32).reshape(device_count, TOKENS_PER_CHIP, MODEL_DIM)
    route_blocks = routes.reshape(device_count, TOKENS_PER_CHIP, TOP)
    device_ids = jnp.arange(device_count, dtype=jnp.int32)

    def forward(token_all, *weights):

        def one_device(block):
            return device_layer(weights, block, lengths, owners)
        return lax.map(jax.checkpoint(one_device), (token_all, route_blocks, device_ids))
    output, pullback = jax.vjp(forward, token_blocks, *params)
    grads = pullback(cotangent.astype(jnp.float32).reshape(device_count, TOKENS_PER_CHIP, MODEL_DIM))
    return (output.reshape(TOKENS, MODEL_DIM).astype(jnp.bfloat16), grads[0].reshape(TOKENS, MODEL_DIM), grads[1], grads[2], grads[3], grads[4], grads[5], grads[6], grads[7], grads[8], grads[9])
```

```python
from functools import partial

import jax
import jax.numpy as jnp
from jax import lax
from jax.experimental import pallas as pl
from jax.experimental.pallas import tpu as pltpu
from jax.sharding import PartitionSpec as P

EPSILON = 1e-06
MESH = pl.DeviceIdType.MESH
BF = jnp.bfloat16
F32 = jnp.float32
HEAD = 128
ANY = pl.BlockSpec(memory_space=pl.ANY)
VM = pl.BlockSpec(memory_space=pltpu.VMEM)
DMA = pltpu.SemaphoreType.DMA
BIG = 60 * 1024 * 1024


def dot(a, b):
    return lax.dot_general(a, b, (((1,), (0,)), ((), ())), preferred_element_type=F32)


def dot_last(a, b):
    return lax.dot_general(a, b, (((1,), (1,)), ((), ())), preferred_element_type=F32)


def dot_first(a, b):
    return lax.dot_general(a, b, (((0,), (0,)), ((), ())), preferred_element_type=F32)


def place():
    return lax.axis_index("expert"), lax.axis_index("fsdp")


def remote(src, dst, send, recv, where):
    return pltpu.make_async_remote_copy(
        src_ref=src,
        dst_ref=dst,
        send_sem=send,
        recv_sem=recv,
        device_id=where,
        device_id_type=MESH,
    )


def near(z, k, n_z):
    sign = 1 - 2 * (z // (n_z // 2))
    return lax.rem(z + sign * k + n_z, n_z)


def greet_all(n_e, n_z):
    e, z = place()
    me, n = e * n_z + z, n_e * n_z
    barrier = pltpu.get_barrier_semaphore()

    @pl.loop(1, n)
    def _(k):
        other = lax.rem(me + k, n)
        pl.semaphore_signal(
            barrier,
            inc=1,
            device_id=(other // n_z, lax.rem(other, n_z)),
            device_id_type=MESH,
        )

    pl.semaphore_wait(barrier, n - 1)


def greet(n_e, n_z, along_z):
    e, z = place()
    barrier = pltpu.get_barrier_semaphore()
    for k in range(1, n_e):
        pl.semaphore_signal(
            barrier, inc=1, device_id=(lax.rem(e + k, n_e), z), device_id_type=MESH
        )
    count = n_e - 1
    if along_z:
        for k in range(1, n_z):
            pl.semaphore_signal(
                barrier, inc=1, device_id=(e, lax.rem(z + k, n_z)), device_id_type=MESH
            )
        count += n_z - 1
    pl.semaphore_wait(barrier, count)


def ranked(z, k, n_z):
    half = n_z // 2
    top = z // half
    low = z + top * (n_z - 1 - 2 * z)
    at = k - low * jnp.where(k == 1, 1, 0)
    return at + top * (n_z - 1 - 2 * at)


def partner_chip(chip, k):
    low = lax.rem(lax.rem(chip, 2) + lax.rem(k, 2), 2)
    high = lax.rem(chip // 2 + k // 2, 2)
    return 2 * high + low


def chain_start(n_z, src, dst_at, send, recv):
    e, z = place()

    @pl.when(z + 1 < n_z)
    def _():
        remote(src, dst_at(z), send.at[0], recv.at[z], (e, z + 1)).start()

    @pl.when(z > 0)
    def _():
        remote(src, dst_at(z), send.at[1], recv.at[z], (e, z - 1)).start()


def chain_take(n_z, k, dst_at, send, recv):
    e, z = place()
    sz = ranked(z, k, n_z)
    block = dst_at(sz)
    step = jnp.where(sz < z, 1, -1)
    remote(block, block, send.at[1 + k], recv.at[sz], (e, sz)).wait_recv()

    @pl.when((z + step >= 0) & (z + step < n_z))
    def _():
        remote(block, block, send.at[1 + k], recv.at[sz], (e, z + step)).start()

    return sz


def chain_end(n_z, src, dst_at, send, recv):
    e, z = place()

    @pl.when(z + 1 < n_z)
    def _():
        remote(src, dst_at(z), send.at[0], recv.at[z], (e, z + 1)).wait_send()

    @pl.when(z > 0)
    def _():
        remote(src, dst_at(z), send.at[1], recv.at[z], (e, z - 1)).wait_send()

    for k in range(1, n_z):
        sz = ranked(z, k, n_z)
        step = jnp.where(sz < z, 1, -1)

        @pl.when((z + step >= 0) & (z + step < n_z))
        def _(k=k, sz=sz, step=step):
            block = dst_at(sz)
            remote(block, block, send.at[1 + k], recv.at[sz], (e, z + step)).wait_send()


def plane_gather_start(n_e, x_ref, out_ref, own, send, recv, sib_send, sib_recv):
    e, z = place()
    nc, chip, core = n_e // 2, e // 2, lax.rem(e, 2)
    pltpu.make_async_copy(x_ref, out_ref.at[e], own).start()
    for k in range(1, nc):
        j = lax.rem(chip + k, nc)
        remote(
            x_ref, out_ref.at[e], send.at[k], recv.at[chip], (2 * j + core, z)
        ).start()
    remote(
        x_ref, out_ref.at[e], sib_send.at[0], sib_recv.at[chip], (2 * chip + 1 - core, z)
    ).start()


def plane_gather_end(n_e, x_ref, out_ref, own, send, recv, sib_send, sib_recv):
    e, z = place()
    nc, chip, core = n_e // 2, e // 2, lax.rem(e, 2)
    sib = (2 * chip + 1 - core, z)
    for k in range(1, nc):
        j = lax.rem(chip + nc - k, nc)
        block = out_ref.at[2 * j + core]
        remote(x_ref, block, send.at[k], recv.at[j], (2 * j + core, z)).wait()
        remote(block, block, sib_send.at[k], sib_recv.at[j], sib).start()
    for k in range(nc):
        j = lax.rem(chip + nc - k, nc)
        block = out_ref.at[2 * j + 1 - core]
        remote(x_ref, block, sib_send.at[k], sib_recv.at[j], sib).wait()
    pltpu.make_async_copy(x_ref, out_ref.at[e], own).wait()


def share_kernel(
    n_e,
    n_z,
    x_ref,
    ct_ref,
    rt_ref,
    wq_ref,
    wo_ref,
    mi_ref,
    xs_ref,
    cts_ref,
    rts_ref,
    wqs_ref,
    wos_ref,
    mis_ref,
    own,
    x_send,
    x_recv,
    sib_send,
    sib_recv,
    z_send,
    z_recv,
    a_send,
    a_recv,
):
    e, z = place()
    n, me = n_e * n_z, e * n_z + z
    greet_all(n_e, n_z)
    gather = (n_e, x_ref, xs_ref, own.at[0], x_send, x_recv, sib_send, sib_recv)
    plane_gather_start(*gather)

    def other_of(k):
        other = lax.rem(me + k, n)
        return other, other // n_z, lax.rem(other, n_z)

    @pl.loop(1, n)
    def _(k):
        other, oe, oz = other_of(k)
        remote(
            wq_ref.at[oe], wqs_ref.at[me], a_send.at[0, k], a_recv.at[0, me], (oe, oz)
        ).start()
        remote(
            mi_ref, mis_ref.at[me], a_send.at[1, k], a_recv.at[1, me], (oe, oz)
        ).start()

    along = ((rt_ref, rts_ref), (wo_ref, wos_ref), (ct_ref, cts_ref))
    for i, (src, dst) in enumerate(along):
        for k in range(1, n_z):
            oz = near(z, k, n_z)
            remote(src, dst.at[z], z_send.at[i, k], z_recv.at[i, z], (e, oz)).start()
        pltpu.make_async_copy(src, dst.at[z], own.at[1 + i]).start()
    pltpu.make_async_copy(wq_ref.at[e], wqs_ref.at[me], own.at[4]).start()
    pltpu.make_async_copy(mi_ref, mis_ref.at[me], own.at[5]).start()

    plane_gather_end(*gather)

    @pl.loop(1, n)
    def _(k):
        other, oe, oz = other_of(k)
        remote(
            wq_ref.at[oe],
            wqs_ref.at[other],
            a_send.at[0, k],
            a_recv.at[0, other],
            (oe, oz),
        ).wait()
        remote(
            mi_ref, mis_ref.at[other], a_send.at[1, k], a_recv.at[1, other], (oe, oz)
        ).wait()

    for i, (src, dst) in enumerate(along):
        for k in range(1, n_z):
            oz = near(z, k, n_z)
            remote(src, dst.at[oz], z_send.at[i, k], z_recv.at[i, oz], (e, oz)).wait()
        pltpu.make_async_copy(src, dst.at[z], own.at[1 + i]).wait()
    pltpu.make_async_copy(wq_ref.at[e], wqs_ref.at[me], own.at[4]).wait()
    pltpu.make_async_copy(mi_ref, mis_ref.at[me], own.at[5]).wait()


def share(n_e, n_z, tokens, cotangent, routes, wq, wo, misc):
    n, nc = n_e * n_z, n_e // 2

    def like(lead, a):
        return jax.ShapeDtypeStruct((lead,) + a.shape, a.dtype)

    return pl.pallas_call(
        partial(share_kernel, n_e, n_z),
        out_shape=(
            like(n_e, tokens),
            like(n_z, cotangent),
            like(n_z, routes),
            like(n, wq[0]),
            like(n_z, wo),
            like(n, misc),
        ),
        in_specs=[ANY] * 6,
        out_specs=(ANY,) * 6,
        scratch_shapes=[
            DMA((6,)),
            DMA((nc,)),
            DMA((nc,)),
            DMA((nc,)),
            DMA((nc,)),
            DMA((3, n_z)),
            DMA((3, n_z)),
            DMA((2, n)),
            DMA((2, n)),
        ],
        compiler_params=pltpu.CompilerParams(collective_id=1, has_side_effects=True),
        name="share",
    )(tokens, cotangent, routes, wq, wo, misc)


def plane_sum_body(
    n_e, part_ref, total_ref, mine, sib, far, own, send, recv, sib_send, sib_recv
):
    e, z = place()
    nc, chip, core = n_e // 2, e // 2, lax.rem(e, 2)
    rows = total_ref.shape[0]
    step = 32
    other = (2 * chip + 1 - core, z)
    for k in range(nc):
        j = lax.rem(chip + 1 + k, nc)
        remote(
            part_ref.at[2 * j + 1 - core],
            sib.at[j],
            sib_send.at[j],
            sib_recv.at[j],
            other,
        ).start()
        pltpu.make_async_copy(part_ref.at[2 * j + core], mine.at[j], own.at[j]).start()
    for k in range(nc):
        j = lax.rem(chip + 1 + k, nc)
        remote(
            part_ref.at[2 * j + 1 - core],
            sib.at[j],
            sib_send.at[j],
            sib_recv.at[j],
            other,
        ).wait()
        pltpu.make_async_copy(part_ref.at[2 * j + core], mine.at[j], own.at[j]).wait()
        if k < nc - 1:

            @pl.loop(0, rows, step=step)
            def _(r, j=j):
                at = pl.ds(pl.multiple_of(r, step), step)
                mine[j, at, :] = (
                    mine[j, at, :].astype(F32) + sib[j, at, :].astype(F32)
                ).astype(BF)

            remote(
                mine.at[j], far.at[chip], send.at[j], recv.at[chip], (2 * j + core, z)
            ).start()
        else:

            @pl.loop(0, rows, step=step)
            def _(r, j=j):
                at = pl.ds(pl.multiple_of(r, step), step)
                total_ref[at, :] = mine[j, at, :].astype(F32) + sib[j, at, :].astype(F32)

    for k in range(1, nc):
        j = lax.rem(chip + nc - k, nc)
        remote(
            mine.at[j], far.at[j], send.at[j], recv.at[j], (2 * j + core, z)
        ).wait()

        @pl.loop(0, rows, step=step)
        def _(r, j=j):
            at = pl.ds(pl.multiple_of(r, step), step)
            total_ref[at, :] += far[j, at, :].astype(F32)


def plane_sum_scratch(n_e, part):
    nc = n_e // 2
    block = (nc,) + part.shape[1:]
    return [pltpu.VMEM(block, BF)] * 3 + [DMA((nc,))] * 5


def plane_sum_kernel(n_e, n_z, part_ref, total_ref, *scratch):
    greet(n_e, n_z, False)
    plane_sum_body(n_e, part_ref, total_ref, *scratch)


def plane_sum(n_e, n_z, part):
    return pl.pallas_call(
        partial(plane_sum_kernel, n_e, n_z),
        out_shape=jax.ShapeDtypeStruct(part.shape[1:], F32),
        in_specs=[ANY],
        out_specs=VM,
        scratch_shapes=plane_sum_scratch(n_e, part),
        compiler_params=pltpu.CompilerParams(
            collective_id=2, has_side_effects=True, vmem_limit_bytes=BIG
        ),
        name="plane_sum",
    )(part)


def plane_gather_kernel(n_e, n_z, x_ref, out_ref, *sems):
    greet(n_e, n_z, False)
    plane_gather_start(n_e, x_ref, out_ref, *sems)
    plane_gather_end(n_e, x_ref, out_ref, *sems)


def plane_gather(n_e, n_z, x):
    nc = n_e // 2
    return pl.pallas_call(
        partial(plane_gather_kernel, n_e, n_z),
        out_shape=jax.ShapeDtypeStruct((n_e,) + x.shape, x.dtype),
        in_specs=[ANY],
        out_specs=ANY,
        scratch_shapes=[DMA] + [DMA((nc,))] * 4,
        compiler_params=pltpu.CompilerParams(collective_id=3, has_side_effects=True),
        name="plane_gather",
    )(x)


def pieces(columns, wide=512):
    cuts = list(range(0, columns - columns % wide, wide)) + [columns - columns % wide]
    spans = [(a, b - a) for a, b in zip(cuts, cuts[1:])]
    if columns % wide:
        spans.append((cuts[-1], columns % wide))
    return spans


def rows_out(n_e, cap, k, sz, src, d_ref, rows, out_ref, own, send, recv):
    e, z = place()
    pick = d_ref[sz]
    for start, size in pieces(src.shape[-1]):
        rows[k, :, start : start + size] = dot(pick, src[:, start : start + size]).astype(BF)
    for i in range(1, n_e + 1):
        oe = lax.rem(e + i, n_e)
        block = rows.at[k, pl.ds(pl.multiple_of(oe * cap, 16), cap), :]
        if i < n_e:
            remote(block, out_ref.at[sz, e], send.at[k, i], recv.at[sz, e], (oe, z)).start()
        else:
            pltpu.make_async_copy(block, out_ref.at[sz, e], own.at[k]).start()


def rows_out_wait(n_e, cap, k, sz, rows, out_ref, own, send, recv):
    e, z = place()
    for i in range(1, n_e + 1):
        oe = lax.rem(e + i, n_e)
        at = pl.ds(pl.multiple_of(oe * cap, 16), cap)
        block = rows.at[k, at, :]
        if i < n_e:
            remote(
                block, out_ref.at[sz, oe], send.at[k, i], recv.at[sz, oe], (oe, z)
            ).wait()
        else:
            pltpu.make_async_copy(block, out_ref.at[sz, e], own.at[k]).wait()


def open_kernel(
    n_e,
    n_z,
    cap,
    x_ref,
    ct_ref,
    rt_ref,
    wq_ref,
    wo_ref,
    mi_ref,
    pick_ref,
    xs_ref,
    rts_ref,
    wqs_ref,
    wos_ref,
    mis_ref,
    dy_ref,
    rows,
    own,
    x_send,
    x_recv,
    sib_send,
    sib_recv,
    w_send,
    w_recv,
    zw_send,
    zw_recv,
    zo_send,
    zo_recv,
    zr_send,
    zr_recv,
    m_send,
    m_recv,
    r_send,
    r_recv,
):
    e, z = place()
    n, me = n_e * n_z, e * n_z + z
    greet_all(n_e, n_z)

    def plane_peer(i):
        return lax.rem(e + i, n_e)

    for i in range(1, n_e):
        oe = plane_peer(i)
        remote(
            wq_ref.at[oe], wqs_ref.at[e, z], w_send.at[i], w_recv.at[e], (oe, z)
        ).start()
    kept = (
        (wq_ref.at[e], wqs_ref.at[e, z]),
        (wo_ref, wos_ref.at[z]),
        (rt_ref, rts_ref.at[z]),
        (mi_ref, mis_ref.at[me]),
    )
    for i, (src, dst) in enumerate(kept):
        pltpu.make_async_copy(src, dst, own.at[i]).start()
    out_chain = (lambda s: wos_ref.at[s], zo_send, zo_recv)
    chain_start(n_z, wo_ref, *out_chain)
    for k in range(1, n_z):
        oz = near(z, k, n_z)
        remote(rt_ref, rts_ref.at[z], zr_send.at[k], zr_recv.at[z], (e, oz)).start()

    def other_of(k):
        other = lax.rem(me + k, n)
        return other, (other // n_z, lax.rem(other, n_z))

    @pl.loop(1, n)
    def _(k):
        other, where = other_of(k)
        remote(mi_ref, mis_ref.at[me], m_send.at[k], m_recv.at[me], where).start()

    gather = (n_e, x_ref, xs_ref, own.at[4], x_send, x_recv, sib_send, sib_recv)
    plane_gather_start(*gather)
    pick = pick_ref[...]
    for start, size in pieces(ct_ref.shape[-1]):
        rows[:, start : start + size] = dot(pick, ct_ref[:, start : start + size]).astype(BF)
    for i in range(1, n_e + 1):
        oe = plane_peer(i)
        block = rows.at[pl.ds(pl.multiple_of(oe * cap, 16), cap), :]
        if i < n_e:
            remote(block, dy_ref.at[e], r_send.at[i], r_recv.at[e], (oe, z)).start()
        else:
            pltpu.make_async_copy(block, dy_ref.at[e], own.at[5]).start()

    for i in range(1, n_e):
        oe = plane_peer(i)
        remote(
            wq_ref.at[oe], wqs_ref.at[oe, z], w_send.at[i], w_recv.at[oe], (oe, z)
        ).wait()
    pltpu.make_async_copy(*kept[0], own.at[0]).wait()
    in_chain = (lambda s: wqs_ref.at[:, s], zw_send, zw_recv)
    chain_start(n_z, wqs_ref.at[:, z], *in_chain)
    for k in range(1, n_z):
        chain_take(n_z, k, *out_chain)
        chain_take(n_z, k, *in_chain)
        if k == n_z - 2:
            plane_gather_end(*gather)
    chain_end(n_z, wo_ref, *out_chain)
    chain_end(n_z, wqs_ref.at[:, z], *in_chain)
    for k in range(1, n_z):
        oz = near(z, k, n_z)
        remote(rt_ref, rts_ref.at[oz], zr_send.at[k], zr_recv.at[oz], (e, oz)).wait()

    @pl.loop(1, n)
    def _(k):
        other, where = other_of(k)
        remote(mi_ref, mis_ref.at[other], m_send.at[k], m_recv.at[other], where).wait()

    for i in range(1, n_e + 1):
        oe = plane_peer(i)
        block = rows.at[pl.ds(pl.multiple_of(oe * cap, 16), cap), :]
        if i < n_e:
            remote(block, dy_ref.at[oe], r_send.at[i], r_recv.at[oe], (oe, z)).wait()
        else:
            pltpu.make_async_copy(block, dy_ref.at[e], own.at[5]).wait()
    for i, (src, dst) in enumerate(kept):
        if i:
            pltpu.make_async_copy(src, dst, own.at[i]).wait()


def open_layer(n_e, n_z, cap, tokens, cotangent, routes, wq, wo, misc, pick):
    n, nc = n_e * n_z, n_e // 2
    _, shard, columns = wq.shape
    width = tokens.shape[1]

    def like(lead, a):
        return jax.ShapeDtypeStruct((lead,) + a.shape, a.dtype)

    return pl.pallas_call(
        partial(open_kernel, n_e, n_z, cap),
        out_shape=(
            like(n_e, tokens),
            like(n_z, routes),
            jax.ShapeDtypeStruct((n_e, n_z, shard, columns), BF),
            like(n_z, wo),
            like(n, misc),
            jax.ShapeDtypeStruct((n_e, cap, width), BF),
        ),
        in_specs=[ANY, VM] + [ANY] * 4 + [VM],
        out_specs=(ANY,) * 6,
        scratch_shapes=[
            pltpu.VMEM((n_e * cap, width), BF),
            DMA((6,)),
            DMA((nc,)),
            DMA((nc,)),
            DMA((nc,)),
            DMA((nc,)),
            DMA((n_e,)),
            DMA((n_e,)),
            DMA((n_z + 1,)),
            DMA((n_z,)),
            DMA((n_z + 1,)),
            DMA((n_z,)),
            DMA((n_z,)),
            DMA((n_z,)),
            DMA((n,)),
            DMA((n,)),
            DMA((n_e,)),
            DMA((n_e,)),
        ],
        compiler_params=pltpu.CompilerParams(
            collective_id=11, has_side_effects=True, vmem_limit_bytes=BIG
        ),
        name="open_layer",
    )(tokens, cotangent, routes, wq, wo, misc, pick)


def dispatch_kernel(
    n_e,
    n_z,
    cap,
    tok_ref,
    d_ref,
    out_ref,
    zbuf,
    rows,
    own,
    z_send,
    z_recv,
    send,
    recv,
):
    e, z = place()
    greet(n_e, n_z, True)
    chain = (lambda s: zbuf.at[s], z_send, z_recv)
    chain_start(n_z, tok_ref, *chain)
    for k in range(n_z):
        sz = chain_take(n_z, k, *chain) if k else z
        src = zbuf.at[sz] if k else tok_ref
        rows_out(n_e, cap, k, sz, src, d_ref, rows, out_ref, own, send, recv)
    for k in range(n_z):
        sz = ranked(z, k, n_z) if k else z
        rows_out_wait(n_e, cap, k, sz, rows, out_ref, own, send, recv)
    chain_end(n_z, tok_ref, *chain)


def dispatch(n_e, n_z, cap, tok, picks):
    count, columns = tok.shape
    return pl.pallas_call(
        partial(dispatch_kernel, n_e, n_z, cap),
        out_shape=jax.ShapeDtypeStruct((n_z, n_e, cap, columns), BF),
        in_specs=[VM, VM],
        out_specs=ANY,
        scratch_shapes=[
            pltpu.VMEM((n_z, count, columns), BF),
            pltpu.VMEM((n_z, n_e * cap, columns), BF),
            DMA((n_z,)),
            DMA((n_z + 1,)),
            DMA((n_z,)),
            DMA((n_z, n_e)),
            DMA((n_z, n_e)),
        ],
        compiler_params=pltpu.CompilerParams(
            collective_id=4, has_side_effects=True, vmem_limit_bytes=BIG
        ),
        name="dispatch",
    )(tok, picks)


def send_kernel(n_e, n_z, cap, src_ref, d_ref, out_ref, rows, own, send, recv):
    e, z = place()
    greet(n_e, n_z, False)
    for k in range(n_z):
        sz = near(z, k, n_z)
        rows_out(n_e, cap, k, sz, src_ref.at[sz], d_ref, rows, out_ref, own, send, recv)
    for k in range(n_z):
        rows_out_wait(n_e, cap, k, near(z, k, n_z), rows, out_ref, own, send, recv)


def send_rows(n_e, n_z, cap, src, picks):
    columns = src.shape[-1]
    return pl.pallas_call(
        partial(send_kernel, n_e, n_z, cap),
        out_shape=jax.ShapeDtypeStruct((n_z, n_e, cap, columns), BF),
        in_specs=[VM, VM],
        out_specs=ANY,
        scratch_shapes=[
            pltpu.VMEM((n_z, n_e * cap, columns), BF),
            DMA((n_z,)),
            DMA((n_z, n_e)),
            DMA((n_z, n_e)),
        ],
        compiler_params=pltpu.CompilerParams(
            collective_id=5, has_side_effects=True, vmem_limit_bytes=BIG
        ),
        name="send_rows",
    )(src, picks)


def give_back_kernel(
    n_e,
    n_z,
    cap,
    y_ref,
    d_ref,
    out_ref,
    rbuf,
    pbuf,
    own,
    send,
    recv,
    z_own,
    z_send,
    z_recv,
):
    e, z = place()
    greet(n_e, n_z, True)
    order = list(range(n_z - 1, -1, -1))
    for k in order:
        sz = near(z, k, n_z)
        for i in range(1, n_e + 1):
            oe = lax.rem(e + i, n_e)
            if i < n_e:
                remote(
                    y_ref.at[sz, oe],
                    rbuf.at[sz, e],
                    send.at[k, i],
                    recv.at[sz, e],
                    (oe, z),
                ).start()
            else:
                pltpu.make_async_copy(y_ref.at[sz, e], rbuf.at[sz, e], own.at[k]).start()
    for k in order:
        sz = near(z, k, n_z)
        for i in range(1, n_e + 1):
            oe = lax.rem(e + i, n_e)
            if i < n_e:
                remote(
                    y_ref.at[sz, oe],
                    rbuf.at[sz, oe],
                    send.at[k, i],
                    recv.at[sz, oe],
                    (oe, z),
                ).wait()
            else:
                pltpu.make_async_copy(y_ref.at[sz, e], rbuf.at[sz, e], own.at[k]).wait()
        pick = d_ref[sz]
        for start, size in pieces(pbuf.shape[-1]):
            block = rbuf[sz, :, :, start : start + size].reshape(n_e * cap, size)
            pbuf[k, :, start : start + size] = dot(pick, block).astype(BF)
        if k:
            remote(
                pbuf.at[k], out_ref.at[z], z_send.at[k], z_recv.at[z], (e, sz)
            ).start()
        else:
            pltpu.make_async_copy(pbuf.at[k], out_ref.at[z], z_own).start()
    for k in order:
        sz = near(z, k, n_z)
        if k:
            remote(
                pbuf.at[k], out_ref.at[sz], z_send.at[k], z_recv.at[sz], (e, sz)
            ).wait()
        else:
            pltpu.make_async_copy(pbuf.at[k], out_ref.at[z], z_own).wait()


def give_back(n_e, n_z, cap, y, picks, number):
    columns = y.shape[-1]
    count = picks.shape[1]
    return pl.pallas_call(
        partial(give_back_kernel, n_e, n_z, cap),
        out_shape=jax.ShapeDtypeStruct((n_z, count, columns), BF),
        in_specs=[ANY, VM],
        out_specs=ANY,
        scratch_shapes=[
            pltpu.VMEM((n_z, n_e, cap, columns), BF),
            pltpu.VMEM((n_z, count, columns), BF),
            DMA((n_z,)),
            DMA((n_z, n_e)),
            DMA((n_z, n_e)),
            DMA,
            DMA((n_z,)),
            DMA((n_z,)),
        ],
        compiler_params=pltpu.CompilerParams(
            collective_id=number, has_side_effects=True, vmem_limit_bytes=BIG
        ),
        name="give_back",
    )(y, picks)


def finish_kernel(
    n_e,
    n_z,
    part_ref,
    gw_ref,
    go_ref,
    gm_ref,
    total_ref,
    gws_ref,
    gos_ref,
    gms_ref,
    own_g,
    a_send,
    a_recv,
    z_send,
    z_recv,
    *scratch,
):
    e, z = place()
    n, me = n_e * n_z, e * n_z + z
    greet_all(n_e, n_z)

    def other_of(k):
        other = lax.rem(me + k, n)
        return other, (other // n_z, lax.rem(other, n_z))

    @pl.loop(1, n)
    def _(k):
        other, where = other_of(k)
        remote(
            gw_ref.at[other], gws_ref.at[me], a_send.at[0, k], a_recv.at[0, me], where
        ).start()
        remote(
            gm_ref.at[other], gms_ref.at[me], a_send.at[1, k], a_recv.at[1, me], where
        ).start()

    for k in range(1, n_z):
        oz = near(z, k, n_z)
        remote(
            go_ref.at[oz], gos_ref.at[z], z_send.at[k], z_recv.at[z], (e, oz)
        ).start()
    mine = (
        (gw_ref.at[me], gws_ref.at[me]),
        (gm_ref.at[me], gms_ref.at[me]),
        (go_ref.at[z], gos_ref.at[z]),
    )
    for i, (src, dst) in enumerate(mine):
        pltpu.make_async_copy(src, dst, own_g.at[i]).start()

    plane_sum_body(n_e, part_ref, total_ref, *scratch)

    @pl.loop(1, n)
    def _(k):
        other, where = other_of(k)
        remote(
            gw_ref.at[other],
            gws_ref.at[other],
            a_send.at[0, k],
            a_recv.at[0, other],
            where,
        ).wait()
        remote(
            gm_ref.at[other],
            gms_ref.at[other],
            a_send.at[1, k],
            a_recv.at[1, other],
            where,
        ).wait()

    for k in range(1, n_z):
        oz = near(z, k, n_z)
        remote(
            go_ref.at[oz], gos_ref.at[oz], z_send.at[k], z_recv.at[oz], (e, oz)
        ).wait()
    for i, (src, dst) in enumerate(mine):
        pltpu.make_async_copy(src, dst, own_g.at[i]).wait()


def finish(n_e, n_z, part, gw, go, gm):
    n = n_e * n_z
    return pl.pallas_call(
        partial(finish_kernel, n_e, n_z),
        out_shape=(
            jax.ShapeDtypeStruct(part.shape[1:], F32),
            jax.ShapeDtypeStruct(gw.shape, gw.dtype),
            jax.ShapeDtypeStruct(go.shape, go.dtype),
            jax.ShapeDtypeStruct(gm.shape, gm.dtype),
        ),
        in_specs=[ANY] * 4,
        out_specs=(VM, ANY, ANY, ANY),
        scratch_shapes=[
            DMA((3,)),
            DMA((2, n)),
            DMA((2, n)),
            DMA((n_z,)),
            DMA((n_z,)),
        ]
        + plane_sum_scratch(n_e, part),
        compiler_params=pltpu.CompilerParams(
            collective_id=8, has_side_effects=True, vmem_limit_bytes=BIG
        ),
        name="finish",
    )(part, gw, go, gm)


def head_norm(u, gain):
    r = lax.rsqrt(jnp.mean(u * u, axis=-1, keepdims=True) + EPSILON)
    return u * r * gain


def turn(u, cos, sin):
    return u * cos + pltpu.roll(u, HEAD // 2, 1) * sin


def turn_back(u, cos, sin):
    return u * cos - pltpu.roll(u, HEAD // 2, 1) * sin


def turns(table):
    other = pltpu.roll(table, HEAD // 2, 1)
    first = lax.broadcasted_iota(jnp.int32, table.shape, 1) < HEAD // 2
    return jnp.where(first, table, other), jnp.where(first, -other, table)


def may_see(seg_row):
    count = seg_row.shape[1]
    i = lax.broadcasted_iota(jnp.int32, (count, count), 0)
    j = lax.broadcasted_iota(jnp.int32, (count, count), 1)
    seg_col = jnp.sum(jnp.where(i == j, seg_row, 0.0), axis=1, keepdims=True)
    return ((seg_col == seg_row) & (seg_col >= 0) & (j <= i)) | (i == j)


def probabilities(q, k, allowed):
    scores = jnp.where(allowed, dot_last(q, k) * (HEAD**-0.5), -1e30)
    peak = jnp.max(scores, axis=-1, keepdims=True)
    weight = jnp.exp(scores - peak)
    return weight / jnp.sum(weight, axis=-1, keepdims=True)


def attend_block(
    heads, x, cos, sin, allowed, w_ref, wo_ref, g1_ref, gh_ref, n1_ref, raw_ref, v_ref, mix_ref
):
    x = x.astype(F32)
    r = lax.rsqrt(jnp.mean(x * x, axis=-1, keepdims=True) + EPSILON)
    n1 = (x * r * g1_ref[...]).astype(BF)
    n1_ref[...] = n1
    raw = dot(n1, w_ref[...])
    qk = (heads + 1) * HEAD
    raw_ref[...] = raw[:, :qk]
    value = raw[:, qk:].astype(BF)
    v_ref[...] = value
    gq, gk = gh_ref[0:1, :], gh_ref[1:2, :]
    key = turn(head_norm(raw[:, heads * HEAD : qk], gk), cos, sin).astype(BF)
    for h in range(heads):
        at = slice(h * HEAD, (h + 1) * HEAD)
        query = turn(head_norm(raw[:, at], gq), cos, sin).astype(BF)
        weight = probabilities(query, key, allowed).astype(BF)
        mix_ref[:, at] = dot(weight, value).astype(BF)
    return dot(mix_ref[...], wo_ref[...]).astype(BF)


def attend_kernel(
    heads,
    x_ref,
    turn_ref,
    seg_ref,
    w_ref,
    wo_ref,
    g1_ref,
    gh_ref,
    n1_ref,
    raw_ref,
    v_ref,
    mix_ref,
    part_ref,
):
    part_ref[0] = attend_block(
        heads,
        x_ref[0],
        *turns(turn_ref[0]),
        may_see(seg_ref[0]),
        w_ref,
        wo_ref,
        g1_ref,
        gh_ref,
        n1_ref.at[0],
        raw_ref.at[0],
        v_ref.at[0],
        mix_ref.at[0],
    )


def attend(n_e, heads, xs, turn_table, seg, w, wo, g1, gh):
    _, count, width = xs.shape

    def block(*shape):
        return pl.BlockSpec((1,) + shape, lambda b: (b, 0, 0))

    def whole(*shape):
        return pl.BlockSpec(shape, lambda b: (0, 0))

    outs = ((width, BF), ((heads + 1) * HEAD, F32), (HEAD, BF), (heads * HEAD, BF), (width, BF))
    return pl.pallas_call(
        partial(attend_kernel, heads),
        grid=(n_e,),
        out_shape=tuple(jax.ShapeDtypeStruct((n_e, count, c), t) for c, t in outs),
        in_specs=[
            block(count, width),
            block(count, HEAD),
            block(1, count),
            whole(*w.shape),
            whole(*wo.shape),
            whole(*g1.shape),
            whole(*gh.shape),
        ],
        out_specs=tuple(block(count, c) for c, _ in outs),
        compiler_params=pltpu.CompilerParams(vmem_limit_bytes=BIG),
        name="attend",
    )(xs, turn_table, seg, w, wo, g1, gh)


def front_kernel(
    n_e,
    n_z,
    cap,
    heads,
    xs_ref,
    ct_ref,
    pick_ref,
    turn_ref,
    seg_ref,
    w_ref,
    wo_ref,
    g1_ref,
    gh_ref,
    n1_ref,
    raw_ref,
    v_ref,
    mix_ref,
    total_ref,
    dy_ref,
    xbuf,
    n1buf,
    rawbuf,
    vbuf,
    mixbuf,
    away,
    mine,
    sib,
    far,
    zbuf,
    rows,
    x_sem,
    o_sem,
    sib_send,
    sib_recv,
    send,
    recv,
    z_send,
    z_recv,
    r_send,
    r_recv,
    r_own,
):
    e, z = place()
    nc, chip, core = n_e // 2, e // 2, lax.rem(e, 2)
    sibling = (2 * chip + 1 - core, z)
    count = total_ref.shape[0]
    step = 32
    greet(n_e, n_z, True)
    chain = (lambda s: zbuf.at[s], z_send, z_recv)
    chain_start(n_z, ct_ref, *chain)

    def blocks(k):
        j = partner_chip(chip, nc - 1 - k)
        return j, (2 * j + 1 - core, 2 * j + core)

    def load(b, slot):
        return pltpu.make_async_copy(xs_ref.at[b], xbuf.at[slot], x_sem.at[slot])

    def stores(b, slot):
        pairs = ((n1buf, n1_ref), (rawbuf, raw_ref), (vbuf, v_ref), (mixbuf, mix_ref))
        return [
            pltpu.make_async_copy(src.at[slot], dst.at[b], o_sem.at[i, slot])
            for i, (src, dst) in enumerate(pairs)
        ]

    for slot in range(2):
        load(blocks(0)[1][slot], slot).start()

    @pl.loop(0, nc)
    def _(k):
        j, pair = blocks(k)
        for slot, b in enumerate(pair):
            load(b, slot).wait()

            @pl.when(k > 0)
            def _(b=b, slot=slot):
                for copy in stores(b, slot):
                    copy.wait()

            part = attend_block(
                heads,
                xbuf[slot],
                *turns(turn_ref[b]),
                may_see(seg_ref[b]),
                w_ref,
                wo_ref,
                g1_ref,
                gh_ref,
                n1buf.at[slot],
                rawbuf.at[slot],
                vbuf.at[slot],
                mixbuf.at[slot],
            )
            for copy in stores(b, slot):
                copy.start()

            @pl.when(k < nc - 1)
            def _(slot=slot):
                load(blocks(k + 1)[1][slot], slot).start()

            if slot == 0:
                away[j] = part
                remote(
                    away.at[j], sib.at[j], sib_send.at[j], sib_recv.at[j], sibling
                ).start()
            else:
                mine[j] = part
        remote(away.at[j], sib.at[j], sib_send.at[j], sib_recv.at[j], sibling).wait()

        @pl.when(k < nc - 1)
        def _():
            @pl.loop(0, count, step=step)
            def _(r):
                at = pl.ds(pl.multiple_of(r, step), step)
                mine[j, at, :] = (
                    mine[j, at, :].astype(F32) + sib[j, at, :].astype(F32)
                ).astype(BF)

            remote(
                mine.at[j], far.at[chip], send.at[j], recv.at[chip], (2 * j + core, z)
            ).start()

        @pl.when((k > 0) & (k < n_z))
        def _():
            sz = chain_take(n_z, k, *chain)
            rows_out(
                n_e,
                cap,
                k - 1,
                sz,
                zbuf.at[sz],
                pick_ref,
                rows,
                dy_ref,
                r_own,
                r_send,
                r_recv,
            )

    @pl.loop(0, count, step=step)
    def _(r):
        at = pl.ds(pl.multiple_of(r, step), step)
        total_ref[at, :] = mine[chip, at, :].astype(F32) + sib[chip, at, :].astype(F32)

    for k in range(nc - 1, 0, -1):
        j = partner_chip(chip, k)
        remote(
            mine.at[j], far.at[j], send.at[j], recv.at[j], (2 * j + core, z)
        ).wait()

        @pl.loop(0, count, step=step)
        def _(r, j=j):
            at = pl.ds(pl.multiple_of(r, step), step)
            total_ref[at, :] += far[j, at, :].astype(F32)

    for slot, b in enumerate(blocks(nc - 1)[1]):
        for copy in stores(b, slot):
            copy.wait()
    for k in range(1, n_z):
        rows_out_wait(
            n_e, cap, k - 1, ranked(z, k, n_z), rows, dy_ref, r_own, r_send, r_recv
        )
    chain_end(n_z, ct_ref, *chain)


def front(n_e, n_z, cap, heads, xs, ct, picks, turn_table, seg, w, wo, g1, gh):
    _, count, width = xs.shape
    nc = n_e // 2
    outs = ((width, BF), ((heads + 1) * HEAD, F32), (HEAD, BF), (heads * HEAD, BF))
    bufs = [pltpu.VMEM((2, count, width), BF)]
    bufs += [pltpu.VMEM((2, count, c), t) for c, t in outs]
    bufs += [pltpu.VMEM((nc, count, width), BF)] * 4
    bufs += [
        pltpu.VMEM((n_z, count, width), BF),
        pltpu.VMEM((n_z - 1, n_e * cap, width), BF),
    ]
    return pl.pallas_call(
        partial(front_kernel, n_e, n_z, cap, heads),
        out_shape=tuple(jax.ShapeDtypeStruct((n_e, count, c), t) for c, t in outs)
        + (
            jax.ShapeDtypeStruct((count, width), F32),
            jax.ShapeDtypeStruct((n_z, n_e, cap, width), BF),
        ),
        in_specs=[ANY] + [VM] * 8,
        out_specs=(ANY,) * 4 + (VM, ANY),
        scratch_shapes=bufs
        + [
            DMA((2,)),
            DMA((4, 2)),
            DMA((nc,)),
            DMA((nc,)),
            DMA((nc,)),
            DMA((nc,)),
            DMA((n_z + 1,)),
            DMA((n_z,)),
            DMA((n_z, n_e)),
            DMA((n_z, n_e)),
            DMA((n_z,)),
        ],
        compiler_params=pltpu.CompilerParams(
            collective_id=12, has_side_effects=True, vmem_limit_bytes=BIG
        ),
        name="front",
    )(xs, ct, picks, turn_table, seg, w, wo, g1, gh)


def norm_back(u, gain, dv):
    r = lax.rsqrt(jnp.mean(u * u, axis=-1, keepdims=True) + EPSILON)
    nu = u * r
    dgain = jnp.sum(dv * nu, axis=0, keepdims=True)
    scaled = dv * gain
    du = r * (scaled - nu * jnp.mean(scaled * nu, axis=-1, keepdims=True))
    return du, dgain


def attend_back_block(
    heads,
    da,
    n1,
    raw_ref,
    value,
    cos,
    sin,
    allowed,
    w_ref,
    wo_ref,
    gh_ref,
    dmix,
    dcat,
    g1_ref,
    ghg_ref,
):
    dmix[...] = dot_last(da, wo_ref[...]).astype(BF)
    gq, gk = gh_ref[0:1, :], gh_ref[1:2, :]
    qk = (heads + 1) * HEAD
    key_raw = raw_ref[:, heads * HEAD : qk]
    key = turn(head_norm(key_raw, gk), cos, sin).astype(BF)
    count = key.shape[0]
    dkey = jnp.zeros((count, HEAD), F32)
    dvalue = jnp.zeros((count, HEAD), F32)
    dgq = jnp.zeros((1, HEAD), F32)
    scale = HEAD**-0.5
    for h in range(heads):
        at = slice(h * HEAD, (h + 1) * HEAD)
        query_raw = raw_ref[:, at]
        query = turn(head_norm(query_raw, gq), cos, sin).astype(BF)
        weight = probabilities(query, key, allowed)
        dm = dmix[:, at]
        dweight = dot_last(dm, value)
        delta = jnp.sum(weight * dweight, axis=-1, keepdims=True)
        dscore = (weight * (dweight - delta)).astype(BF)
        dquery = dot(dscore, key) * scale
        dkey += dot_first(dscore, query) * scale
        dvalue += dot_first(weight.astype(BF), dm)
        du, dg = norm_back(query_raw, gq, turn_back(dquery, cos, sin))
        dcat[:, at] = du.astype(BF)
        dgq += dg
    du, dgk = norm_back(key_raw, gk, turn_back(dkey, cos, sin))
    dcat[:, heads * HEAD : qk] = du.astype(BF)
    dcat[:, qk:] = dvalue.astype(BF)
    ghg_ref[0:1, :] += dgq
    ghg_ref[1:2, :] += dgk
    dn = dot_last(dcat[...], w_ref[...])
    g1_ref[...] += jnp.sum(dn * n1.astype(F32), axis=0, keepdims=True)
    return dn.astype(BF)


def attend_back_kernel(
    heads,
    steps,
    da_ref,
    n1_ref,
    raw_ref,
    v_ref,
    mix_ref,
    turn_ref,
    seg_ref,
    w_ref,
    wo_ref,
    gh_ref,
    dn_ref,
    gw_ref,
    go_ref,
    g1_ref,
    ghg_ref,
    acc_w,
    acc_o,
    dcat,
    dmix,
):
    step = pl.program_id(0)

    @pl.when(step == 0)
    def _():
        acc_w[...] = jnp.zeros_like(acc_w)
        acc_o[...] = jnp.zeros_like(acc_o)
        g1_ref[...] = jnp.zeros_like(g1_ref)
        ghg_ref[...] = jnp.zeros_like(ghg_ref)

    da, n1 = da_ref[0], n1_ref[0]
    dn_ref[0] = attend_back_block(
        heads,
        da,
        n1,
        raw_ref.at[0],
        v_ref[0],
        *turns(turn_ref[0]),
        may_see(seg_ref[0]),
        w_ref,
        wo_ref,
        gh_ref,
        dmix,
        dcat,
        g1_ref,
        ghg_ref,
    )
    acc_w[...] += dot_first(n1, dcat[...])
    acc_o[...] += dot_first(mix_ref[0], da)

    @pl.when(step == steps - 1)
    def _():
        gw_ref[...] = acc_w[...].astype(BF)
        go_ref[...] = acc_o[...].astype(BF)


def attend_back(n_e, heads, da, n1, raw, v, mix, turn_table, seg, w, wo, gh):
    _, count, width = da.shape

    def block(*shape):
        return pl.BlockSpec((1,) + shape, lambda b: (b, 0, 0))

    def whole(*shape):
        return pl.BlockSpec(shape, lambda b: (0, 0))

    return pl.pallas_call(
        partial(attend_back_kernel, heads, n_e),
        grid=(n_e,),
        out_shape=(
            jax.ShapeDtypeStruct((n_e, count, width), BF),
            jax.ShapeDtypeStruct(w.shape, BF),
            jax.ShapeDtypeStruct(wo.shape, BF),
            jax.ShapeDtypeStruct((1, width), F32),
            jax.ShapeDtypeStruct((8, HEAD), F32),
        ),
        in_specs=[
            block(count, width),
            block(count, width),
            block(*raw.shape[1:]),
            block(count, HEAD),
            block(*mix.shape[1:]),
            block(count, HEAD),
            block(1, count),
            whole(*w.shape),
            whole(*wo.shape),
            whole(*gh.shape),
        ],
        out_specs=(
            block(count, width),
            whole(*w.shape),
            whole(*wo.shape),
            whole(1, width),
            whole(8, HEAD),
        ),
        scratch_shapes=[
            pltpu.VMEM(w.shape, F32),
            pltpu.VMEM(wo.shape, F32),
            pltpu.VMEM((count, (heads + 2) * HEAD), BF),
            pltpu.VMEM((count, heads * HEAD), BF),
        ],
        compiler_params=pltpu.CompilerParams(vmem_limit_bytes=BIG),
        name="attend_back",
    )(da, n1, raw, v, mix, turn_table, seg, w, wo, gh)


def back_kernel(
    n_e,
    n_z,
    cap,
    heads,
    da_ref,
    r_ref,
    rfar_ref,
    gr_ref,
    n1_ref,
    raw_ref,
    v_ref,
    mix_ref,
    unpick_ref,
    g2_ref,
    turn_ref,
    seg_ref,
    w_ref,
    wo_ref,
    g1_ref,
    gh_ref,
    total_ref,
    part_ref,
    gws_ref,
    goo_ref,
    gor_ref,
    gol_ref,
    grs_ref,
    gvs_ref,
    ret_ref,
    gwr_ref,
    gwl_ref,
    rsum,
    gplane,
    das,
    n1s,
    raws,
    vs,
    mixs,
    dcats,
    dmix,
    gsum,
    ghsum,
    gvec,
    gtotal,
    away,
    mine,
    sib,
    far,
    rbuf,
    gob,
    own,
    in_sem,
    raw_sem,
    d_send,
    d_recv,
    ds_send,
    ds_recv,
    a_send,
    a_recv,
    b_send,
    b_recv,
    b_own,
    p_send,
    p_recv,
    o_send,
    or_recv,
    ol_recv,
    w_send,
    wr_recv,
    wl_recv,
    s_send,
    s_recv,
    t_sem,
    v_send,
    v_recv,
    vz_send,
    vz_recv,
    sib_send,
    sib_recv,
    send,
    recv,
):
    e, z = place()
    n, me = n_e * n_z, e * n_z + z
    nc, chip, core = n_e // 2, e // 2, lax.rem(e, 2)
    sibling = (2 * chip + 1 - core, z)
    count, width = total_ref.shape
    shard = width // n
    head_rows = mixs.shape[-1] // n_z
    step = 32
    greet_all(n_e, n_z)

    def other_of(k):
        other = lax.rem(me + k, n)
        return other, (other // n_z, lax.rem(other, n_z))

    def far_chip(k):
        return (2 * partner_chip(chip, k) + core, z)

    def give_da(k):
        return remote(
            da_ref, das.at[e], d_send.at[k], d_recv.at[chip], far_chip(k)
        )

    remote(da_ref, das.at[e], ds_send.at[0], ds_recv.at[chip], sibling).start()
    for k in range(1, nc - 1):
        give_da(k).start()
    own_da = pltpu.make_async_copy(da_ref, das.at[e], own.at[0])
    own_da.start()

    @pl.loop(1, n)
    def _(k):
        other, where = other_of(k)
        remote(
            gr_ref.at[other], grs_ref.at[me], a_send.at[k], a_recv.at[me], where
        ).start()

    own_gr = pltpu.make_async_copy(gr_ref.at[me], grs_ref.at[me], own.at[1])
    own_gr.start()
    for i, (src, dst) in enumerate(((n1_ref, n1s), (v_ref, vs), (mix_ref, mixs))):
        pltpu.make_async_copy(src, dst, in_sem.at[i]).start()

    def load_raw(b, slot):
        return pltpu.make_async_copy(raw_ref.at[b], raws.at[slot], raw_sem.at[slot])

    def blocks(k):
        j = partner_chip(chip, k)
        return j, (2 * j + core, 2 * j + 1 - core)

    def source(k):
        return jnp.where(k == 0, z, ranked(z, k, n_z))

    def give_rows(k):
        sz = source(k)
        for i in range(1, n_e):
            oe = lax.rem(e + i, n_e)
            remote(
                r_ref.at[sz, oe],
                ret_ref.at[sz, e],
                b_send.at[k, i],
                b_recv.at[sz, e],
                (oe, z),
            ).start()
        pltpu.make_async_copy(r_ref.at[sz, e], ret_ref.at[sz, e], b_own.at[k]).start()

    for slot in range(2):
        load_raw(blocks(0)[1][slot], slot).start()
    gsum[...] = jnp.zeros_like(gsum)
    ghsum[...] = jnp.zeros_like(ghsum)
    for i, (src, dst) in enumerate(((n1_ref, n1s), (v_ref, vs), (mix_ref, mixs))):
        pltpu.make_async_copy(src, dst, in_sem.at[i]).wait()

    tokens = n_e * count

    def out_weights():
        da_all = das[...].reshape(tokens, width)
        for oz in range(n_z):
            at = slice(oz * head_rows, (oz + 1) * head_rows)
            gob[oz] = dot_first(mixs[:, :, at].reshape(tokens, head_rows), da_all).astype(BF)
        pass_all(out_pass, 0)

    def pass_sum(d, step, stage, block, inbox, recv, send, add):
        distance = z if step > 0 else n_z - 1 - z
        going = (d > z) if step > 0 else (d < z)

        @pl.when(going & (distance == stage))
        def _():
            if stage:
                remote(block, inbox.at[d], send.at[d], recv.at[d], (e, z - step)).wait_recv()
                add(d, inbox)
            remote(block, inbox.at[d], send.at[d], recv.at[d], (e, z + step)).start()

    def pass_all(one_pass, stage):
        for d in range(n_z - 1):
            one_pass(n_z - 1 - d, 1, stage)
            one_pass(d, -1, stage)

    def out_add(d, inbox):
        fetch = pltpu.make_async_copy(inbox.at[d], away.at[0:head_rows], t_sem.at[0])
        fetch.start()
        fetch.wait()

        @pl.loop(0, head_rows, step=step)
        def _(r):
            at = pl.ds(pl.multiple_of(r, step), step)
            gob[d, at, :] = (gob[d, at, :].astype(F32) + away[at, :].astype(F32)).astype(BF)

    def out_pass(d, step, stage):
        inbox, recv = (gor_ref, or_recv) if step > 0 else (gol_ref, ol_recv)
        pass_sum(d, step, stage, gob.at[d], inbox, recv, o_send, out_add)

    parts = dcats.shape[-1] // (n_z * shard)

    def shard_at(d):
        return pl.ds(pl.multiple_of(d * shard, shard), shard)

    def weight_add(d, inbox):
        for p in range(parts):
            there = away.at[p * shard : (p + 1) * shard]
            pltpu.make_async_copy(inbox.at[d, p], there, t_sem.at[p]).start()
        for p in range(parts):
            there = away.at[p * shard : (p + 1) * shard]
            pltpu.make_async_copy(inbox.at[d, p], there, t_sem.at[p]).wait()

            @pl.loop(0, shard, step=step)
            def _(r, p=p):
                at = pl.ds(pl.multiple_of(d * shard + r, step), step)
                came = away[pl.ds(pl.multiple_of(p * shard + r, step), step), :]
                n1s[p, at, :] = (n1s[p, at, :].astype(F32) + came.astype(F32)).astype(BF)

    def weight_pass(d, step, stage):
        inbox, recv = (gwr_ref, wr_recv) if step > 0 else (gwl_ref, wl_recv)
        block = n1s.at[0:parts, shard_at(d), :]
        pass_sum(d, step, stage, block, inbox, recv, w_send, weight_add)

    def sum_rows(src, dst, k):
        sz = source(k)
        unpick = unpick_ref[sz]
        cuts = pieces(width, 256)

        def fetch(p):
            start, size = cuts[p]
            return pltpu.make_async_copy(
                src.at[:, :, start : start + size], rbuf.at[p % 2], in_sem.at[p % 2]
            )

        fetch(0).start()
        for p, (start, size) in enumerate(cuts):
            if p + 1 < len(cuts):
                fetch(p + 1).start()
            fetch(p).wait()
            block = rbuf[p % 2].reshape(n_e * cap, size)
            dst[:, start : start + size] = dot(unpick, block).astype(BF)

    def sum_of(k):
        return rsum if k == n_z - 1 else das.at[k]

    def send_sum(k):
        sz = source(k)
        return remote(sum_of(k), part_ref.at[z], p_send.at[k], p_recv.at[z], (e, sz))

    def take_rows(k):
        sz = source(k)
        for i in range(1, n_e):
            oe = lax.rem(e + i, n_e)
            remote(
                r_ref.at[sz, oe],
                ret_ref.at[sz, oe],
                b_send.at[k, i],
                b_recv.at[sz, oe],
                (oe, z),
            ).wait()
        pltpu.make_async_copy(r_ref.at[sz, e], ret_ref.at[sz, e], b_own.at[k]).wait()
        sum_rows(ret_ref.at[sz], sum_of(k), k)

    sum_rows(rfar_ref, rsum, n_z - 1)
    send_sum(n_z - 1).start()

    @pl.loop(0, nc)
    def _(k):
        j, pair = blocks(k)

        @pl.when(k == 0)
        def _():
            pltpu.make_async_copy(da_ref, das.at[e], own.at[0]).wait()

        @pl.when(k > 0)
        def _():
            block = das.at[2 * j + core]
            remote(da_ref, block, d_send.at[k], d_recv.at[j], far_chip(k)).wait_recv()
            remote(block, block, ds_send.at[k], ds_recv.at[j], sibling).start()

        def sibling_da():
            remote(
                da_ref, das.at[pair[1]], ds_send.at[k], ds_recv.at[j], sibling
            ).wait_recv()

        @pl.when(k == nc - 1)
        def _():
            sibling_da()
            out_weights()

        for slot, b in enumerate(pair):
            if slot == 1:
                pl.when(k < nc - 1)(sibling_da)
            load_raw(b, slot).wait()
            part = attend_back_block(
                heads,
                das[b],
                n1s[b],
                raws.at[slot],
                vs[b],
                *turns(turn_ref[b]),
                may_see(seg_ref[b]),
                w_ref,
                wo_ref,
                gh_ref,
                dmix,
                dcats.at[b],
                gsum,
                ghsum,
            )

            @pl.when(k < nc - 1)
            def _(slot=slot):
                load_raw(blocks(k + 1)[1][slot], slot).start()

            if slot == 0:
                mine[j] = part
            else:
                away[...] = part
        to_sibling = remote(
            away, sib.at[lax.rem(k, 2)], sib_send, sib_recv.at[lax.rem(k, 2)], sibling
        )
        to_sibling.start()

        @pl.when(k == 0)
        def _():
            give_da(nc - 1).start()

        @pl.when((k > 0) & (k < n_z - 1))
        def _():
            give_rows(n_z - 1 - k)

        to_sibling.wait()

        @pl.when(k > 0)
        def _():
            @pl.loop(0, count, step=step)
            def _(r):
                at = pl.ds(pl.multiple_of(r, step), step)
                mine[j, at, :] = (
                    mine[j, at, :].astype(F32) + sib[lax.rem(k, 2), at, :].astype(F32)
                ).astype(BF)

            remote(
                mine.at[j], far.at[k - 1], send.at[k - 1], recv.at[k - 1], far_chip(k)
            ).start()

        @pl.when(k == 0)
        def _():
            @pl.loop(0, count, step=step)
            def _(r):
                at = pl.ds(pl.multiple_of(r, step), step)
                total_ref[at, :] = mine[j, at, :].astype(F32) + sib[0, at, :].astype(F32)

    remote(da_ref, das.at[e], ds_send.at[0], ds_recv.at[chip], sibling).wait_send()
    for k in range(1, nc):
        give_da(k).wait_send()
        block = das.at[2 * partner_chip(chip, k) + core]
        remote(block, block, ds_send.at[k], ds_recv.at[chip], sibling).wait_send()

    give_rows(0)
    pltpu.make_async_copy(gob.at[z], goo_ref, own.at[3]).start()
    pass_all(out_pass, 1)
    take_rows(n_z - 2)
    send_sum(n_z - 2).start()

    dcat = dcats[...].reshape(tokens, -1)

    @pl.loop(0, n_e)
    def _(t):
        at = pl.ds(pl.multiple_of(t * n_z * shard, n_z * shard), n_z * shard)
        rows = dot_first(n1s[:, :, at].reshape(tokens, n_z * shard), dcat).astype(BF)
        for p in range(parts):
            n1s[p, :, at] = rows[:, p * n_z * shard : (p + 1) * n_z * shard]

    pass_all(weight_pass, 0)

    lanes = 128
    g1 = gsum[...] / g1_ref[...]
    per = width // lanes
    for i in range(per):
        gvec[i : i + 1, :] = g1[:, i * lanes : (i + 1) * lanes]
        gvec[per + i : per + i + 1, :] = g2_ref[:, i * lanes : (i + 1) * lanes]
    gvec[2 * per : 2 * per + 8, :] = ghsum[...]

    for i in range(1, n_e):
        oe = lax.rem(e + i, n_e)
        remote(gvec, gplane.at[e], v_send.at[i], v_recv.at[e], (oe, z)).start()
    gplane[e] = gvec[...]
    for k in range(1, nc):
        j = partner_chip(chip, k)
        remote(
            mine.at[j], far.at[k - 1], send.at[k - 1], recv.at[k - 1], far_chip(k)
        ).wait()

        @pl.loop(0, count, step=step)
        def _(r, k=k):
            at = pl.ds(pl.multiple_of(r, step), step)
            total_ref[at, :] += far[k - 1, at, :].astype(F32)

    pass_all(out_pass, 2)
    for k in range(n_z - 3, 0, -1):
        take_rows(k)
        send_sum(k).start()
    pass_all(weight_pass, 1)
    take_rows(0)
    pltpu.make_async_copy(das.at[0], part_ref.at[z], own.at[6]).start()
    pass_all(weight_pass, 2)

    for came, inbox, recv_w, there in (
        (z > 0, gwr_ref, wr_recv, z - 1),
        (z < n_z - 1, gwl_ref, wl_recv, z + 1),
    ):

        @pl.when(came)
        def _(inbox=inbox, recv_w=recv_w, there=there):
            block = n1s.at[0:parts, shard_at(z), :]
            remote(block, inbox.at[z], w_send.at[z], recv_w.at[z], (e, there)).wait_recv()
            weight_add(z, inbox)

    def weight_block(t):
        at = pl.ds(pl.multiple_of(t * n_z * shard, n_z * shard), n_z * shard)
        return n1s.at[0:parts, shard_at(z), at]

    for i in range(1, n_e):
        oe = lax.rem(e + i, n_e)
        remote(weight_block(oe), gws_ref.at[e], s_send.at[i], s_recv.at[e], (oe, z)).start()
    pltpu.make_async_copy(weight_block(e), gws_ref.at[e], own.at[2]).start()
    for i in range(1, n_e):
        oe = lax.rem(e + i, n_e)
        remote(gvec, gplane.at[oe], v_send.at[i], v_recv.at[oe], (oe, z)).wait()
    gtotal[...] = jnp.sum(gplane[...], axis=0)
    for k in range(1, n_z):
        oz = near(z, k, n_z)
        remote(gtotal, gvs_ref.at[z], vz_send.at[k], vz_recv.at[z], (e, oz)).start()
    own_gv = pltpu.make_async_copy(gtotal, gvs_ref.at[z], own.at[4])
    own_gv.start()

    @pl.loop(1, n)
    def _(k):
        other, where = other_of(k)
        remote(
            gr_ref.at[other],
            grs_ref.at[other],
            a_send.at[k],
            a_recv.at[other],
            where,
        ).wait()

    for i in range(1, n_e):
        oe = lax.rem(e + i, n_e)
        remote(weight_block(oe), gws_ref.at[oe], s_send.at[i], s_recv.at[oe], (oe, z)).wait()
    for d in range(n_z):

        @pl.when(d != z)
        def _(d=d):
            remote(gob.at[d], gor_ref.at[d], o_send.at[d], or_recv.at[d], (e, d)).wait_send()
            block = n1s.at[0:parts, shard_at(d), :]
            remote(block, gwr_ref.at[d], w_send.at[d], wr_recv.at[d], (e, d)).wait_send()

    for came, inbox, recv_o, there in (
        (z > 0, gor_ref, or_recv, z - 1),
        (z < n_z - 1, gol_ref, ol_recv, z + 1),
    ):

        @pl.when(came)
        def _(inbox=inbox, recv_o=recv_o, there=there):
            remote(
                gob.at[z], inbox.at[z], o_send.at[z], recv_o.at[z], (e, there)
            ).wait_recv()

    for k in range(1, n_z):
        oz = near(z, k, n_z)
        remote(
            gtotal, gvs_ref.at[oz], vz_send.at[k], vz_recv.at[oz], (e, oz)
        ).wait()
        sz = ranked(z, k, n_z)
        remote(
            sum_of(k), part_ref.at[sz], p_send.at[k], p_recv.at[sz], (e, sz)
        ).wait()
    own_gr.wait()
    pltpu.make_async_copy(weight_block(e), gws_ref.at[e], own.at[2]).wait()
    pltpu.make_async_copy(gob.at[z], goo_ref, own.at[3]).wait()
    own_gv.wait()
    pltpu.make_async_copy(das.at[0], part_ref.at[z], own.at[6]).wait()


def back(
    n_e, n_z, cap, heads, da, r_rows, r_far, gr, n1, raw, v, mix, unpicks, g2, turn_table, seg, w, wo, g1, gh
):
    n, nc = n_e * n_z, n_e // 2
    count, width = da.shape
    shard = width // n
    columns = w.shape[1]
    parts = columns // (n_z * shard)
    out_block = (wo.shape[0] // n_z, width)
    vec_rows = 2 * width // 128 + 8
    block = (count, width)

    def sems(*shape):
        return DMA(shape)

    return pl.pallas_call(
        partial(back_kernel, n_e, n_z, cap, heads),
        out_shape=(
            jax.ShapeDtypeStruct(block, F32),
            jax.ShapeDtypeStruct((n_z,) + block, BF),
            jax.ShapeDtypeStruct((n_e, parts, shard, n_z * shard), BF),
            jax.ShapeDtypeStruct(out_block, BF),
            jax.ShapeDtypeStruct((n_z,) + out_block, BF),
            jax.ShapeDtypeStruct((n_z,) + out_block, BF),
            jax.ShapeDtypeStruct(gr.shape, F32),
            jax.ShapeDtypeStruct((n_z, vec_rows, 128), F32),
            jax.ShapeDtypeStruct(r_rows.shape, BF),
            jax.ShapeDtypeStruct((n_z, parts, shard, width), BF),
            jax.ShapeDtypeStruct((n_z, parts, shard, width), BF),
        ),
        in_specs=[ANY] * 8 + [VM] * 8,
        out_specs=(VM,) + (ANY,) * 10,
        scratch_shapes=[
            pltpu.VMEM(block, BF),
            pltpu.VMEM((n_e, vec_rows, 128), F32),
            pltpu.VMEM((n_e,) + block, BF),
            pltpu.VMEM(n1.shape, BF),
            pltpu.VMEM((2,) + raw.shape[1:], F32),
            pltpu.VMEM(v.shape, BF),
            pltpu.VMEM(mix.shape, BF),
            pltpu.VMEM((n_e, count, columns), BF),
            pltpu.VMEM((count, heads * HEAD), BF),
            pltpu.VMEM((1, width), F32),
            pltpu.VMEM((8, HEAD), F32),
            pltpu.VMEM((vec_rows, 128), F32),
            pltpu.VMEM((vec_rows, 128), F32),
            pltpu.VMEM(block, BF),
            pltpu.VMEM((nc,) + block, BF),
            pltpu.VMEM((2,) + block, BF),
            pltpu.VMEM((nc - 1,) + block, BF),
            pltpu.VMEM((2, n_e, cap, 256), BF),
            pltpu.VMEM((n_z, wo.shape[0] // n_z, width), BF),
            sems(7),
            sems(3),
            sems(2),
            sems(nc),
            sems(nc),
            sems(nc),
            sems(nc),
            sems(n),
            sems(n),
            sems(n_z, n_e),
            sems(n_z, n_e),
            sems(n_z),
            sems(n_z),
            sems(n_z),
            sems(n_z),
            sems(n_z),
            sems(n_z),
            sems(n_z),
            sems(n_z),
            sems(n_z),
            sems(n_e),
            sems(n_e),
            sems(parts),
            sems(n_e),
            sems(n_e),
            sems(n_z),
            sems(n_z),
            DMA,
            sems(2),
            sems(nc),
            sems(nc),
        ],
        compiler_params=pltpu.CompilerParams(
            collective_id=14, has_side_effects=True, vmem_limit_bytes=63 * 1024 * 1024
        ),
        name="back",
    )(da, r_rows, r_far, gr, n1, raw, v, mix, unpicks, g2, turn_table, seg, w, wo, g1, gh)


def expert_kernel(
    n_z,
    experts,
    width,
    x_ref,
    dy_ref,
    wg_ref,
    wu_ref,
    wd_ref,
    r_ref,
    dx_ref,
    gg_ref,
    gu_ref,
    gd_ref,
):
    step = pl.program_id(0)

    @pl.when(step == 0)
    def _():
        gg_ref[...] = jnp.zeros_like(gg_ref)
        gu_ref[...] = jnp.zeros_like(gu_ref)
        gd_ref[...] = jnp.zeros_like(gd_ref)

    e, z = place()
    me = e * n_z + z
    x = x_ref[:, :width]
    extra = x_ref[:, width:].astype(F32)
    lane = lax.broadcasted_iota(jnp.int32, extra.shape, 1)
    gate = jnp.sum(
        jnp.where((lane == me) | (lane == experts + me), extra, 0.0), axis=1, keepdims=True
    )
    gate_part = dot(x, wg_ref[...])
    up_part = dot(x, wu_ref[...])
    sig = 1.0 / (1.0 + jnp.exp(-gate_part))
    act = gate_part * sig
    inner = (act * up_part).astype(BF)
    r_ref[...] = (dot(inner, wd_ref[...]) * gate).astype(BF)
    dy = dy_ref[...]
    dinner = dot_last(dy, wd_ref[...])
    inner_f = inner.astype(F32)
    dgate = jnp.sum(dinner * inner_f, axis=1, keepdims=True)
    gd_ref[...] += dot_first((inner_f * gate).astype(BF), dy)
    dinner = dinner * gate
    dgp = (dinner * up_part * sig * (1.0 + gate_part * (1.0 - sig))).astype(BF)
    dup = (dinner * act).astype(BF)
    dx_ref[:, :width] = (dot_last(dgp, wg_ref[...]) + dot_last(dup, wu_ref[...])).astype(BF)
    high = dgate.astype(BF).astype(F32)
    dx_ref[:, width:] = jnp.where(
        lane == me, high, jnp.where(lane == experts + me, dgate - high, 0.0)
    ).astype(BF)
    gg_ref[...] += dot_first(x, dgp)
    gu_ref[...] += dot_first(x, dup)


def expert_run(n_z, experts, x, dy, wg, wu, wd):
    rows, columns = x.shape
    width, hidden = wg.shape
    tile = 512

    def block(c):
        return pl.BlockSpec((tile, c), lambda b: (b, 0))

    def whole(shape):
        return pl.BlockSpec(shape, lambda b: (0, 0), pipeline_mode=pl.Buffered(1))

    return pl.pallas_call(
        partial(expert_kernel, n_z, experts, width),
        grid=(rows // tile,),
        out_shape=(
            jax.ShapeDtypeStruct((rows, width), BF),
            jax.ShapeDtypeStruct((rows, columns), BF),
            jax.ShapeDtypeStruct((width, hidden), F32),
            jax.ShapeDtypeStruct((width, hidden), F32),
            jax.ShapeDtypeStruct((hidden, width), F32),
        ),
        in_specs=[
            block(columns),
            block(width),
            whole(wg.shape),
            whole(wu.shape),
            whole(wd.shape),
        ],
        out_specs=(
            block(width),
            block(columns),
            whole(wg.shape),
            whole(wu.shape),
            whole(wd.shape),
        ),
        compiler_params=pltpu.CompilerParams(vmem_limit_bytes=BIG),
        name="experts",
    )(x, dy, wg, wu, wd)


def expert_tile(width, experts, me, x_ext, dy, wg_ref, wu_ref, wd_ref):
    x = x_ext[:, :width]
    extra = x_ext[:, width:].astype(F32)
    lane = lax.broadcasted_iota(jnp.int32, extra.shape, 1)
    gate = jnp.sum(
        jnp.where((lane == me) | (lane == experts + me), extra, 0.0), axis=1, keepdims=True
    )
    gate_part = dot(x, wg_ref[...])
    up_part = dot(x, wu_ref[...])
    sig = 1.0 / (1.0 + jnp.exp(-gate_part))
    act = gate_part * sig
    inner = (act * up_part).astype(BF)
    result = (dot(inner, wd_ref[...]) * gate).astype(BF)
    dinner = dot_last(dy, wd_ref[...])
    inner_f = inner.astype(F32)
    dgate = jnp.sum(dinner * inner_f, axis=1, keepdims=True)
    gated = (inner_f * gate).astype(BF)
    dinner = dinner * gate
    dgp = (dinner * up_part * sig * (1.0 + gate_part * (1.0 - sig))).astype(BF)
    dup = (dinner * act).astype(BF)
    dx = (dot_last(dgp, wg_ref[...]) + dot_last(dup, wu_ref[...])).astype(BF)
    high = dgate.astype(BF).astype(F32)
    back = jnp.where(
        lane == me, high, jnp.where(lane == experts + me, dgate - high, 0.0)
    ).astype(BF)
    return result, dx, back, gated, dgp, dup


def moe_kernel(
    n_e,
    n_z,
    cap,
    tok_ref,
    pick_ref,
    unpick_ref,
    near_ref,
    far_ref,
    wg_ref,
    wu_ref,
    wd_ref,
    xs_ref,
    r_ref,
    dx_ref,
    ret_ref,
    part_ref,
    gi_ref,
    dg_ref,
    du_ref,
    gg_ref,
    gu_ref,
    gd_ref,
    rret_ref,
    zbuf,
    z_send,
    z_recv,
    r_send,
    r_recv,
    r_own,
    in_sem,
    out_sem,
    b_send,
    b_recv,
    b_own,
    p_send,
    p_recv,
    p_own,
    e_send,
    e_recv,
    g_sem,
    t_sem,
    w_sem,
):
    e, z = place()
    me = e * n_z + z
    width = far_ref.shape[-1]
    hidden = wd_ref.shape[0]
    experts = n_e * n_z
    columns = tok_ref.shape[-1]
    last = n_z - 1
    inner = (z > 0) & (z < last)
    greet(n_e, n_z, True)
    chain = (lambda s: zbuf.at[s], z_send, z_recv)
    chain_start(n_z, tok_ref, *chain)

    def source(k):
        return jnp.where(k == 0, z, ranked(z, k, n_z))

    def give_one(k, i):
        sz, oe = source(k), lax.rem(e + i, n_e)
        return remote(
            dx_ref.at[sz, oe],
            ret_ref.at[sz, e],
            b_send.at[k, i],
            b_recv.at[sz, e],
            (oe, z),
        )

    def give_own(k):
        sz = source(k)
        return pltpu.make_async_copy(dx_ref.at[sz, e], ret_ref.at[sz, e], b_own.at[k])

    def give(k):
        for i in range(1, n_e):
            give_one(k, i).start()
        give_own(k).start()

    def store(k, tiles, i):
        src, dst = tiles[i]
        return pltpu.make_async_copy(src, dst.at[source(k)], out_sem.at[i])

    def first_phase(rows, xt, yt, rt, dxt, git, dgt, dut):
        out_args = (xs_ref, r_own, r_send, r_recv)
        rows_out(n_e, cap, 0, z, tok_ref, pick_ref, rows, *out_args)
        tiles = ((dxt, dx_ref), (rt, r_ref), (git, gi_ref), (dgt, dg_ref), (dut, du_ref))

        def load_y(src):
            return pltpu.make_async_copy(src, yt, in_sem.at[1])

        @pl.loop(0, n_z)
        def _(k):
            sz = source(k)

            @pl.when(k == 0)
            def _():
                load_y(near_ref).start()

            @pl.when(k > 0)
            def _():
                load_y(far_ref.at[sz]).start()

            @pl.when(jnp.where(inner, k == 0, k < last))
            def _():
                chain_take(n_z, k + 1, *chain)

            @pl.when(inner & (k + 2 < n_z))
            def _():
                chain_take(n_z, k + 2, *chain)

            @pl.when(k < last)
            def _():
                nz = source(k + 1)
                rows_out(n_e, cap, k + 1, nz, zbuf.at[nz], pick_ref, rows, *out_args)

            rows_out_wait(n_e, cap, k, sz, rows, *out_args)
            fetch = pltpu.make_async_copy(xs_ref.at[sz], xt, in_sem.at[0])
            fetch.start()
            fetch.wait()
            load_y(far_ref.at[sz]).wait()

            @pl.when((k > 0) & (k < last))
            def _():
                store(k, tiles, 0).wait()

            @pl.when(k > 0)
            def _():
                for i in range(1, 5):
                    store(k, tiles, i).wait()

            result, dx, back, gated, dgp, dup = expert_tile(
                width,
                experts,
                me,
                xt[...].reshape(n_e * cap, -1),
                yt[...].reshape(n_e * cap, -1),
                wg_ref,
                wu_ref,
                wd_ref,
            )
            rt[...] = result.reshape(n_e, cap, -1)
            dxt[:, :, :width] = dx.reshape(n_e, cap, -1)
            dxt[:, :, width:] = back.reshape(n_e, cap, -1)
            git[...] = gated.reshape(n_e, cap, -1)
            dgt[...] = dgp.reshape(n_e, cap, -1)
            dut[...] = dup.reshape(n_e, cap, -1)
            for i in range(5):
                store(k, tiles, i).start()

            @pl.when(k >= last - 1)
            def _():
                store(k, tiles, 0).wait()
                give(k)

        for i in range(1, 5):
            store(last, tiles, i).wait()

    def row_buffer(c):
        return pltpu.VMEM((n_e, cap, c), BF)

    pl.run_scoped(
        first_phase,
        pltpu.VMEM((n_z, n_e * cap, columns), BF),
        row_buffer(columns),
        row_buffer(width),
        row_buffer(width),
        row_buffer(columns),
        row_buffer(hidden),
        row_buffer(hidden),
        row_buffer(hidden),
    )
    chain_end(n_z, tok_ref, *chain)

    give(1)
    far_z = source(last)

    def give_result(i):
        oe = lax.rem(e + i, n_e)
        return remote(
            r_ref.at[far_z, oe], rret_ref.at[e], e_send.at[i], e_recv.at[e], (oe, z)
        )

    for i in range(1, n_e):
        give_result(i).start()
    own_result = pltpu.make_async_copy(r_ref.at[far_z, e], rret_ref.at[e], in_sem.at[0])
    own_result.start()
    give(0)
    size = 256
    count = width // size

    def second_phase(gis, dgs, dus, xc, yc, ggt, gut, gdt, rbuf):
        whole = ((gi_ref, gis), (dg_ref, dgs), (du_ref, dus))
        for i, (src, dst) in enumerate(whole):
            pltpu.make_async_copy(src, dst, g_sem.at[i]).start()

        def pairs(t):
            at = pl.ds(pl.multiple_of(t * size, size), size)
            slot = lax.rem(t, 2)
            copies = [
                pltpu.make_async_copy(xs_ref.at[:, :, :, at], xc.at[slot], t_sem.at[0, slot])
            ]
            for k in range(n_z):
                src = far_ref.at[source(k), :, :, at] if k else near_ref.at[:, :, at]
                copies.append(
                    pltpu.make_async_copy(
                        src, yc.at[slot, source(k)], t_sem.at[1 + k, slot]
                    )
                )
            return copies

        def results(t):
            at = pl.ds(pl.multiple_of(t * size, size), size)
            slot = lax.rem(t, 2)
            return [
                pltpu.make_async_copy(ggt.at[slot], gg_ref.at[at], w_sem.at[0, slot]),
                pltpu.make_async_copy(gut.at[slot], gu_ref.at[at], w_sem.at[1, slot]),
                pltpu.make_async_copy(gdt.at[slot], gd_ref.at[:, at], w_sem.at[2, slot]),
            ]

        def weight_tile(t):
            slot = lax.rem(t, 2)

            @pl.when(t + 1 < count)
            def _():
                for copy in pairs(t + 1):
                    copy.start()

            for copy in pairs(t):
                copy.wait()

            @pl.when(t >= 2)
            def _():
                for copy in results(t):
                    copy.wait()

            total = n_z * n_e * cap
            x = xc[slot].reshape(total, size)
            ggt[slot] = dot_first(x, dgs[...].reshape(total, hidden)).astype(BF)
            gut[slot] = dot_first(x, dus[...].reshape(total, hidden)).astype(BF)
            gdt[slot] = dot_first(
                gis[...].reshape(total, hidden), yc[slot].reshape(total, size)
            ).astype(BF)
            for copy in results(t):
                copy.start()

        def combine(k):
            sz = source(k)
            for i in range(1, n_e):
                oe = lax.rem(e + i, n_e)
                remote(
                    dx_ref.at[sz, oe],
                    ret_ref.at[sz, oe],
                    b_send.at[k, i],
                    b_recv.at[sz, oe],
                    (oe, z),
                ).wait()
            give_own(k).wait()
            unpick = unpick_ref[sz]
            cuts = pieces(columns)

            def fetch(p):
                start, wide = cuts[p]
                return pltpu.make_async_copy(
                    ret_ref.at[sz, :, :, start : start + wide],
                    rbuf.at[p % 2, :, :, 0:wide],
                    in_sem.at[1 + p % 2],
                )

            fetch(0).start()
            for p, (start, wide) in enumerate(cuts):
                if p + 1 < len(cuts):
                    fetch(p + 1).start()
                fetch(p).wait()
                block = rbuf[p % 2, :, :, 0:wide].reshape(n_e * cap, wide)
                zbuf[k, :, start : start + wide] = dot(unpick, block).astype(BF)

            @pl.when(k > 0)
            def _():
                remote(
                    zbuf.at[k], part_ref.at[z], p_send.at[k], p_recv.at[z], (e, sz)
                ).start()

            @pl.when(k == 0)
            def _():
                pltpu.make_async_copy(zbuf.at[k], part_ref.at[z], p_own).start()

        for copy in pairs(0):
            copy.start()
        for i, (src, dst) in enumerate(whole):
            pltpu.make_async_copy(src, dst, g_sem.at[i]).wait()
        share_of = count // n_z

        @pl.loop(0, n_z)
        def _(i):
            @pl.loop(0, share_of)
            def _(t):
                weight_tile(i * share_of + t)

            k = jnp.where(i == 0, last - 1, jnp.where(i == 1, last, last - i))
            combine(k)

        for t in (count - 2, count - 1):
            for copy in results(t):
                copy.wait()

    total_shape = (n_z, n_e, cap)
    pl.run_scoped(
        second_phase,
        pltpu.VMEM(total_shape + (hidden,), BF),
        pltpu.VMEM(total_shape + (hidden,), BF),
        pltpu.VMEM(total_shape + (hidden,), BF),
        pltpu.VMEM((2,) + total_shape + (size,), BF),
        pltpu.VMEM((2,) + total_shape + (size,), BF),
        pltpu.VMEM((2, size, hidden), BF),
        pltpu.VMEM((2, size, hidden), BF),
        pltpu.VMEM((2, hidden, size), BF),
        pltpu.VMEM((2, n_e, cap, pieces(columns)[0][1]), BF),
    )
    for i in range(1, n_e):
        oe = lax.rem(e + i, n_e)
        remote(
            r_ref.at[far_z, oe], rret_ref.at[oe], e_send.at[i], e_recv.at[oe], (oe, z)
        ).wait()
    own_result.wait()
    pltpu.make_async_copy(zbuf.at[0], part_ref.at[z], p_own).wait()
    for k in range(1, n_z):
        sz = ranked(z, k, n_z)
        remote(
            zbuf.at[k], part_ref.at[sz], p_send.at[k], p_recv.at[sz], (e, sz)
        ).wait()


def moe(n_e, n_z, cap, tok, picks, unpicks, dy_near, dy_far, wg, wu, wd):
    count, columns = tok.shape
    width, hidden = wg.shape

    def rows_of(c):
        return jax.ShapeDtypeStruct((n_z, n_e, cap, c), BF)

    return pl.pallas_call(
        partial(moe_kernel, n_e, n_z, cap),
        out_shape=(
            rows_of(columns),
            rows_of(width),
            rows_of(columns),
            rows_of(columns),
            jax.ShapeDtypeStruct((n_z, count, columns), BF),
            rows_of(hidden),
            rows_of(hidden),
            rows_of(hidden),
            jax.ShapeDtypeStruct((width, hidden), BF),
            jax.ShapeDtypeStruct((width, hidden), BF),
            jax.ShapeDtypeStruct((hidden, width), BF),
            jax.ShapeDtypeStruct((n_e, cap, width), BF),
        ),
        in_specs=[VM, VM, VM, ANY, ANY, VM, VM, VM],
        out_specs=(ANY,) * 12,
        scratch_shapes=[
            pltpu.VMEM((n_z, count, columns), BF),
            DMA((n_z + 1,)),
            DMA((n_z,)),
            DMA((n_z, n_e)),
            DMA((n_z, n_e)),
            DMA((n_z,)),
            DMA((3,)),
            DMA((5,)),
            DMA((n_z, n_e)),
            DMA((n_z, n_e)),
            DMA((n_z,)),
            DMA((n_z,)),
            DMA((n_z,)),
            DMA,
            DMA((n_e,)),
            DMA((n_e,)),
            DMA((3,)),
            DMA((1 + n_z, 2)),
            DMA((3, 2)),
        ],
        compiler_params=pltpu.CompilerParams(
            collective_id=13, has_side_effects=True, vmem_limit_bytes=63 * 1024 * 1024
        ),
        name="moe",
    )(tok, picks, unpicks, dy_near, dy_far, wg, wu, wd)


def layout(lengths, owners, device, row_count):
    seq_order = jnp.arange(lengths.shape[0], dtype=jnp.int32)
    owned = (owners == device).astype(jnp.int32)
    earlier = (seq_order[None, :] < seq_order[:, None]).astype(jnp.int32)
    starts = jnp.sum(earlier * (owned * lengths)[None, :], axis=1)
    row_index = jnp.arange(row_count, dtype=jnp.int32)
    inside = (
        owned[None, :]
        * (row_index[:, None] >= starts[None, :]).astype(jnp.int32)
        * (row_index[:, None] < (starts + lengths)[None, :]).astype(jnp.int32)
    )
    live_rows = jnp.sum(inside, axis=1)
    segment = jnp.sum(inside * (seq_order[None, :] + 1), axis=1) - 1
    token_position = jnp.sum(inside * (row_index[:, None] - starts[None, :]), axis=1)
    return (live_rows, segment, token_position)


def named_experts(routes, experts):
    return jnp.any(routes[..., None] == jnp.arange(experts, dtype=jnp.int32), axis=-2)


def slot_picks(n_e, n_z, z, cap, named, live):
    sources, count, experts = named.shape
    used = named & (live[:, :, None] > 0)
    order = jnp.arange(count)
    lower = (order[None, :] < order[:, None]).astype(BF)
    slots = jnp.einsum("ts,zse->zte", lower, used.astype(BF), preferred_element_type=F32)
    slots = jnp.where(used, slots, -1.0)
    column = jnp.arange(n_e * cap, dtype=jnp.int32)
    spread = (
        jnp.arange(experts, dtype=jnp.int32)[:, None] == (column // cap * n_z + z)[None, :]
    ).astype(BF)
    slots = slots.astype(BF)
    slot_ids = lax.rem(column, cap).astype(F32)
    picks = jnp.einsum("ec,ste->sct", spread, slots, preferred_element_type=F32)
    unpicks = jnp.einsum("ste,ec->stc", slots, spread, preferred_element_type=F32)
    return (
        (picks == slot_ids[None, :, None]).astype(BF),
        (unpicks == slot_ids).astype(BF),
    )


def split_float(values):
    high = values.astype(BF)
    return high, (values - high.astype(F32)).astype(BF)


def pad_lanes(values, lanes):
    return jnp.pad(values, ((0, 0), (0, lanes - values.shape[1])))


def local(
    n_e,
    n_z,
    tokens,
    cotangent,
    lengths,
    owners,
    routes,
    w_query,
    key_weight,
    value_weight,
    w_out,
    w_router,
    norm_gains,
    w_gate,
    w_up,
    w_down,
):
    n = n_e * n_z
    count, width = tokens.shape
    shard = w_query.shape[0]
    experts, top = w_router.shape[1], routes.shape[1]
    q_heads, kv_heads = w_query.shape[1] // HEAD, key_weight.shape[1] // HEAD
    heads = q_heads // n_e
    cap = count * top * 5 // (4 * experts)
    cap = -(-cap // 16) * 16
    e, z = place()

    wq_blocks = w_query.reshape(shard, n_e, heads * HEAD)
    sharing = n_e // kv_heads
    wk_blocks = jnp.repeat(key_weight.reshape(shard, kv_heads, HEAD), sharing, axis=1)
    wv_blocks = jnp.repeat(value_weight.reshape(shard, kv_heads, HEAD), sharing, axis=1)
    w_blocks = jnp.concatenate([wq_blocks, wk_blocks, wv_blocks], axis=2).transpose(1, 0, 2)
    router_rows = shard * experts // 128
    gain_rows = -(-norm_gains.shape[0] // 128)
    misc_rows = -(-(router_rows + gain_rows) // 16) * 16
    misc = jnp.concatenate(
        [
            w_router.reshape(-1),
            norm_gains,
            jnp.zeros((misc_rows - router_rows) * 128 - norm_gains.shape[0], BF),
        ]
    ).reshape(misc_rows, 128)
    routes_flat = routes.reshape(-1, 128)

    device = e * n_z + z
    plane_ids = jnp.arange(n_e, dtype=jnp.int32) * n_z + z
    column_ids = e * n_z + jnp.arange(n_z, dtype=jnp.int32)
    live_both, segment, position = jax.vmap(lambda d: layout(lengths, owners, d, count))(
        jnp.concatenate([plane_ids, column_ids])
    )
    live_all = live_both[n_e:]
    live_own = lax.dynamic_index_in_dim(live_all, z, keepdims=False)
    named_own = named_experts(routes, experts)
    small = n_e == 8 and n_z == 4
    if small:
        pick_own = slot_picks(n_e, n_z, z, cap, named_own[None], live_own[None])[0][0]
        xs, rts, w_all, wo_all, misc_all, dy_near = open_layer(
            n_e, n_z, cap, tokens, cotangent, routes_flat, w_blocks, w_out, misc, pick_own
        )
    else:
        xs, cts, rts, w_all, wo_all, misc_all = share(
            n_e, n_z, tokens, cotangent, routes_flat, w_blocks, w_out, misc
        )
    w_all = w_all.reshape(n * shard, -1)
    wo_all = wo_all.reshape(-1, width)
    router_w = misc_all[:, :router_rows].reshape(n * shard, experts)
    gains = (
        misc_all[:, router_rows:]
        .reshape(n, -1)[:, : norm_gains.shape[0]]
        .reshape(-1)
        .astype(F32)
    )
    gain_one = gains[None, :width]
    gain_two = gains[None, width : 2 * width]
    gain_heads = jnp.pad(gains[2 * width :].reshape(2, HEAD), ((0, 6), (0, 0)))

    half = HEAD // 2
    frequency = jnp.power(1000000.0, -2.0 * jnp.arange(half, dtype=F32) / HEAD)
    angles = position[:n_e].astype(F32)[:, :, None] * frequency
    turn_table = jnp.concatenate([jnp.cos(angles), jnp.sin(angles)], axis=-1)
    seg = segment[:n_e].astype(F32)[:, None, :]

    named_all = named_experts(rts.reshape(n_z, count, top), experts)
    picks, unpicks = slot_picks(n_e, n_z, z, cap, named_all, live_all)
    live = live_own.astype(F32)[:, None]
    named = named_own.astype(F32)

    shape = (turn_table, seg, w_all, wo_all, gain_one, gain_heads)
    if small:
        n1, raw, value, mix, attn_rows, dy_far = front(
            n_e, n_z, cap, heads, xs, cotangent, picks, *shape
        )
    else:
        dy_rows = send_rows(n_e, n_z, cap, cts, picks)
        n1, raw, value, mix, part = attend(n_e, heads, xs, *shape)
        attn_rows = plane_sum(n_e, n_z, part)

    inputs = tokens.astype(F32)
    hidden = inputs + live * attn_rows
    r_two = lax.rsqrt(jnp.mean(hidden * hidden, axis=-1, keepdims=True) + EPSILON)
    nu_two = hidden * r_two
    n2 = (nu_two * gain_two).astype(BF)
    logits = dot(n2, router_w)
    probs = jax.nn.softmax(logits, axis=-1)
    chosen = probs * named
    chosen_sum = jnp.sum(chosen, axis=1, keepdims=True)
    gates = chosen / chosen_sum
    lanes = -(-2 * experts // 128) * 128
    extra = pad_lanes(jnp.concatenate(split_float(gates), axis=1), lanes)
    tok = jnp.concatenate([n2, extra], axis=1)
    experts_w = (w_gate[0], w_up[0], w_down[0])
    if small:
        moved = moe(n_e, n_z, cap, tok, picks, unpicks, dy_near, dy_far, *experts_w)
        r_rows, dx_back = moved[1], moved[4]
        grad_gate, grad_up, grad_down = (a.astype(F32) for a in moved[8:11])
        r_far = moved[11]
    else:
        x_rows = dispatch(n_e, n_z, cap, tok, picks)
        r_rows, dx_rows, grad_gate, grad_up, grad_down = expert_run(
            n_z,
            experts,
            x_rows.reshape(-1, width + lanes),
            dy_rows.reshape(-1, width),
            *experts_w,
        )
        r_rows = r_rows.reshape(dy_rows.shape)
        dx_back = give_back(n_e, n_z, cap, dx_rows.reshape(x_rows.shape), unpicks, 6)

    dx_sum = jnp.sum(dx_back.astype(F32), axis=0)
    dgates = dx_sum[:, width : width + experts] + dx_sum[:, width + experts : width + 2 * experts]
    dchosen = (
        named * (dgates - jnp.sum(dgates * gates, axis=1, keepdims=True)) / chosen_sum
    )
    dlogits = (probs * (dchosen - jnp.sum(probs * dchosen, axis=1, keepdims=True))).astype(BF)
    grad_router = dot_first(n2, dlogits)
    dn2 = dx_sum[:, :width] + dot_last(dlogits, router_w)
    upstream = cotangent.astype(F32)
    grad_gain_two = jnp.sum(dn2 * nu_two, axis=0)
    scaled = dn2 * gain_two
    dhidden = upstream + r_two * (
        scaled - nu_two * jnp.mean(scaled * nu_two, axis=-1, keepdims=True)
    )
    da = (live * dhidden).astype(BF)
    gain_size = norm_gains.shape[0]
    grad_router = grad_router.reshape(n, router_rows, 128)
    if small:
        dn1, r_back, gws, goo, gor, gol, grs, gvs, *_ = back(
            n_e,
            n_z,
            cap,
            heads,
            da,
            r_rows,
            r_far,
            grad_router,
            n1,
            raw,
            value,
            mix,
            unpicks,
            grad_gain_two[None],
            *shape,
        )
        gw_sum = gws.astype(F32).transpose(0, 2, 1, 3).reshape(n_e, shard, -1)
        lower_sum, upper_sum = (
            jnp.where(came, lax.dynamic_index_in_dim(inbox, z, keepdims=False).astype(F32), 0.0)
            for came, inbox in ((z > 0, gor), (z < n_z - 1, gol))
        )
        grad_out = goo.astype(F32) + lower_sum + upper_sum
        grad_router = jnp.sum(grs, axis=0)
        grad_gains = lax.dynamic_slice_in_dim(
            jnp.sum(gvs, axis=0).reshape(-1), device * gain_size, gain_size
        )
    else:
        r_back = give_back(n_e, n_z, cap, r_rows, unpicks, 7)
        da_all = plane_gather(n_e, n_z, da)
        dn_part, gw, go, g1_part, gh_part = attend_back(
            n_e,
            heads,
            da_all,
            n1,
            raw,
            value,
            mix,
            turn_table,
            seg,
            w_all,
            wo_all,
            gain_heads,
        )
        gain_all = jnp.concatenate(
            [(g1_part / gain_one)[0], grad_gain_two, gh_part[0], gh_part[1]]
        ).reshape(n, -1)
        grad_rows = -(-(router_rows + gain_rows) // 8) * 8
        gain_all = pad_lanes(gain_all, (grad_rows - router_rows) * 128)
        gm = jnp.concatenate([grad_router, gain_all.reshape(n, -1, 128)], axis=1)
        dn1, gws, gos, gms = finish(
            n_e,
            n_z,
            dn_part,
            gw.reshape(n, shard, -1),
            go.reshape(n_z, -1, width),
            gm,
        )
        gw_sum = jnp.sum(gws.reshape(n_e, n_z, shard, -1).astype(F32), axis=1)
        grad_out = jnp.sum(gos.astype(F32), axis=0)
        gm_sum = jnp.sum(gms, axis=0)
        grad_router = gm_sum[:router_rows]
        grad_gains = gm_sum[router_rows:].reshape(-1)[:gain_size]
    block_out = (hidden + jnp.sum(r_back.astype(F32), axis=0)).astype(BF)
    r_one = lax.rsqrt(jnp.mean(inputs * inputs, axis=-1, keepdims=True) + EPSILON)
    nu_one = inputs * r_one
    scaled = dn1 * gain_one
    grad_tokens = dhidden + r_one * (
        scaled - nu_one * jnp.mean(scaled * nu_one, axis=-1, keepdims=True)
    )
    q_size = heads * HEAD
    grad_query = gw_sum[:, :, :q_size].transpose(1, 0, 2).reshape(shard, -1)
    kv_sum = gw_sum[:, :, q_size:].reshape(kv_heads, -1, shard, 2 * HEAD).sum(axis=1)
    grad_key = kv_sum[:, :, :HEAD].transpose(1, 0, 2).reshape(shard, -1)
    grad_value = kv_sum[:, :, HEAD:].transpose(1, 0, 2).reshape(shard, -1)
    return (
        block_out,
        grad_tokens,
        grad_query,
        grad_key,
        grad_value,
        grad_out,
        grad_router.reshape(shard, experts),
        grad_gains,
        grad_gate[None],
        grad_up[None],
        grad_down[None],
    )


def solution(mesh):
    both = ("expert", "fsdp")
    two, three = P(both, None), P(both, None, None)
    return jax.shard_map(
        partial(local, mesh.shape["expert"], mesh.shape["fsdp"]),
        mesh=mesh,
        in_specs=(two, two, P(), P(), two) + (two,) * 5 + (P(both),) + (three,) * 3,
        out_specs=(two,) * 7 + (P(both),) + (three,) * 3,
        check_vma=False,
    )
```

```python
from functools import partial

import jax
import jax.numpy as jnp
from jax import lax
from jax.experimental import pallas as pl
from jax.experimental.pallas import tpu as pltpu
from jax.sharding import PartitionSpec as P

EPSILON = 1e-06
MESH = pl.DeviceIdType.MESH
BF = jnp.bfloat16
F32 = jnp.float32
HEAD = 128
ANY = pl.BlockSpec(memory_space=pl.ANY)
VM = pl.BlockSpec(memory_space=pltpu.VMEM)
DMA = pltpu.SemaphoreType.DMA
BIG = 60 * 1024 * 1024


def dot(a, b):
    return lax.dot_general(a, b, (((1,), (0,)), ((), ())), preferred_element_type=F32)


def dot_last(a, b):
    return lax.dot_general(a, b, (((1,), (1,)), ((), ())), preferred_element_type=F32)


def dot_first(a, b):
    return lax.dot_general(a, b, (((0,), (0,)), ((), ())), preferred_element_type=F32)


def place():
    return lax.axis_index("expert"), lax.axis_index("fsdp")


def remote(src, dst, send, recv, where):
    return pltpu.make_async_remote_copy(
        src_ref=src,
        dst_ref=dst,
        send_sem=send,
        recv_sem=recv,
        device_id=where,
        device_id_type=MESH,
    )


def near(z, k, n_z):
    sign = 1 - 2 * (z // (n_z // 2))
    return lax.rem(z + sign * k + n_z, n_z)


def greet_all(n_e, n_z):
    e, z = place()
    me, n = e * n_z + z, n_e * n_z
    barrier = pltpu.get_barrier_semaphore()

    @pl.loop(1, n)
    def _(k):
        other = lax.rem(me + k, n)
        pl.semaphore_signal(
            barrier,
            inc=1,
            device_id=(other // n_z, lax.rem(other, n_z)),
            device_id_type=MESH,
        )

    pl.semaphore_wait(barrier, n - 1)


def greet(n_e, n_z, along_z):
    e, z = place()
    barrier = pltpu.get_barrier_semaphore()
    for k in range(1, n_e):
        pl.semaphore_signal(
            barrier, inc=1, device_id=(lax.rem(e + k, n_e), z), device_id_type=MESH
        )
    count = n_e - 1
    if along_z:
        for k in range(1, n_z):
            pl.semaphore_signal(
                barrier, inc=1, device_id=(e, lax.rem(z + k, n_z)), device_id_type=MESH
            )
        count += n_z - 1
    pl.semaphore_wait(barrier, count)


def ranked(z, k, n_z):
    half = n_z // 2
    top = z // half
    low = z + top * (n_z - 1 - 2 * z)
    at = k - low * jnp.where(k == 1, 1, 0)
    return at + top * (n_z - 1 - 2 * at)


def partner_chip(chip, k):
    low = lax.rem(lax.rem(chip, 2) + lax.rem(k, 2), 2)
    high = lax.rem(chip // 2 + k // 2, 2)
    return 2 * high + low


def chain_start(n_z, src, dst_at, send, recv):
    e, z = place()

    @pl.when(z + 1 < n_z)
    def _():
        remote(src, dst_at(z), send.at[0], recv.at[z], (e, z + 1)).start()

    @pl.when(z > 0)
    def _():
        remote(src, dst_at(z), send.at[1], recv.at[z], (e, z - 1)).start()


def chain_take(n_z, k, dst_at, send, recv):
    e, z = place()
    sz = ranked(z, k, n_z)
    block = dst_at(sz)
    step = jnp.where(sz < z, 1, -1)
    remote(block, block, send.at[1 + k], recv.at[sz], (e, sz)).wait_recv()

    @pl.when((z + step >= 0) & (z + step < n_z))
    def _():
        remote(block, block, send.at[1 + k], recv.at[sz], (e, z + step)).start()

    return sz


def chain_end(n_z, src, dst_at, send, recv):
    e, z = place()

    @pl.when(z + 1 < n_z)
    def _():
        remote(src, dst_at(z), send.at[0], recv.at[z], (e, z + 1)).wait_send()

    @pl.when(z > 0)
    def _():
        remote(src, dst_at(z), send.at[1], recv.at[z], (e, z - 1)).wait_send()

    for k in range(1, n_z):
        sz = ranked(z, k, n_z)
        step = jnp.where(sz < z, 1, -1)

        @pl.when((z + step >= 0) & (z + step < n_z))
        def _(k=k, sz=sz, step=step):
            block = dst_at(sz)
            remote(block, block, send.at[1 + k], recv.at[sz], (e, z + step)).wait_send()


def plane_gather_start(n_e, x_ref, out_ref, own, send, recv, sib_send, sib_recv):
    e, z = place()
    nc, chip, core = n_e // 2, e // 2, lax.rem(e, 2)
    pltpu.make_async_copy(x_ref, out_ref.at[e], own).start()
    for k in range(1, nc):
        j = lax.rem(chip + k, nc)
        remote(
            x_ref, out_ref.at[e], send.at[k], recv.at[chip], (2 * j + core, z)
        ).start()
    remote(
        x_ref, out_ref.at[e], sib_send.at[0], sib_recv.at[chip], (2 * chip + 1 - core, z)
    ).start()


def plane_gather_end(n_e, x_ref, out_ref, own, send, recv, sib_send, sib_recv):
    e, z = place()
    nc, chip, core = n_e // 2, e // 2, lax.rem(e, 2)
    sib = (2 * chip + 1 - core, z)
    for k in range(1, nc):
        j = lax.rem(chip + nc - k, nc)
        block = out_ref.at[2 * j + core]
        remote(x_ref, block, send.at[k], recv.at[j], (2 * j + core, z)).wait()
        remote(block, block, sib_send.at[k], sib_recv.at[j], sib).start()
    for k in range(nc):
        j = lax.rem(chip + nc - k, nc)
        block = out_ref.at[2 * j + 1 - core]
        remote(x_ref, block, sib_send.at[k], sib_recv.at[j], sib).wait()
    pltpu.make_async_copy(x_ref, out_ref.at[e], own).wait()


def share_kernel(
    n_e,
    n_z,
    x_ref,
    ct_ref,
    rt_ref,
    wq_ref,
    wo_ref,
    mi_ref,
    xs_ref,
    cts_ref,
    rts_ref,
    wqs_ref,
    wos_ref,
    mis_ref,
    own,
    x_send,
    x_recv,
    sib_send,
    sib_recv,
    z_send,
    z_recv,
    a_send,
    a_recv,
):
    e, z = place()
    n, me = n_e * n_z, e * n_z + z
    greet_all(n_e, n_z)
    gather = (n_e, x_ref, xs_ref, own.at[0], x_send, x_recv, sib_send, sib_recv)
    plane_gather_start(*gather)

    def other_of(k):
        other = lax.rem(me + k, n)
        return other, other // n_z, lax.rem(other, n_z)

    @pl.loop(1, n)
    def _(k):
        other, oe, oz = other_of(k)
        remote(
            wq_ref.at[oe], wqs_ref.at[me], a_send.at[0, k], a_recv.at[0, me], (oe, oz)
        ).start()
        remote(
            mi_ref, mis_ref.at[me], a_send.at[1, k], a_recv.at[1, me], (oe, oz)
        ).start()

    along = ((rt_ref, rts_ref), (wo_ref, wos_ref), (ct_ref, cts_ref))
    for i, (src, dst) in enumerate(along):
        for k in range(1, n_z):
            oz = near(z, k, n_z)
            remote(src, dst.at[z], z_send.at[i, k], z_recv.at[i, z], (e, oz)).start()
        pltpu.make_async_copy(src, dst.at[z], own.at[1 + i]).start()
    pltpu.make_async_copy(wq_ref.at[e], wqs_ref.at[me], own.at[4]).start()
    pltpu.make_async_copy(mi_ref, mis_ref.at[me], own.at[5]).start()

    plane_gather_end(*gather)

    @pl.loop(1, n)
    def _(k):
        other, oe, oz = other_of(k)
        remote(
            wq_ref.at[oe],
            wqs_ref.at[other],
            a_send.at[0, k],
            a_recv.at[0, other],
            (oe, oz),
        ).wait()
        remote(
            mi_ref, mis_ref.at[other], a_send.at[1, k], a_recv.at[1, other], (oe, oz)
        ).wait()

    for i, (src, dst) in enumerate(along):
        for k in range(1, n_z):
            oz = near(z, k, n_z)
            remote(src, dst.at[oz], z_send.at[i, k], z_recv.at[i, oz], (e, oz)).wait()
        pltpu.make_async_copy(src, dst.at[z], own.at[1 + i]).wait()
    pltpu.make_async_copy(wq_ref.at[e], wqs_ref.at[me], own.at[4]).wait()
    pltpu.make_async_copy(mi_ref, mis_ref.at[me], own.at[5]).wait()


def share(n_e, n_z, tokens, cotangent, routes, wq, wo, misc):
    n, nc = n_e * n_z, n_e // 2

    def like(lead, a):
        return jax.ShapeDtypeStruct((lead,) + a.shape, a.dtype)

    return pl.pallas_call(
        partial(share_kernel, n_e, n_z),
        out_shape=(
            like(n_e, tokens),
            like(n_z, cotangent),
            like(n_z, routes),
            like(n, wq[0]),
            like(n_z, wo),
            like(n, misc),
        ),
        in_specs=[ANY] * 6,
        out_specs=(ANY,) * 6,
        scratch_shapes=[
            DMA((6,)),
            DMA((nc,)),
            DMA((nc,)),
            DMA((nc,)),
            DMA((nc,)),
            DMA((3, n_z)),
            DMA((3, n_z)),
            DMA((2, n)),
            DMA((2, n)),
        ],
        compiler_params=pltpu.CompilerParams(collective_id=1, has_side_effects=True),
        name="share",
    )(tokens, cotangent, routes, wq, wo, misc)


def plane_sum_body(
    n_e, part_ref, total_ref, mine, sib, far, own, send, recv, sib_send, sib_recv
):
    e, z = place()
    nc, chip, core = n_e // 2, e // 2, lax.rem(e, 2)
    rows = total_ref.shape[0]
    step = 32
    other = (2 * chip + 1 - core, z)
    for k in range(nc):
        j = lax.rem(chip + 1 + k, nc)
        remote(
            part_ref.at[2 * j + 1 - core],
            sib.at[j],
            sib_send.at[j],
            sib_recv.at[j],
            other,
        ).start()
        pltpu.make_async_copy(part_ref.at[2 * j + core], mine.at[j], own.at[j]).start()
    for k in range(nc):
        j = lax.rem(chip + 1 + k, nc)
        remote(
            part_ref.at[2 * j + 1 - core],
            sib.at[j],
            sib_send.at[j],
            sib_recv.at[j],
            other,
        ).wait()
        pltpu.make_async_copy(part_ref.at[2 * j + core], mine.at[j], own.at[j]).wait()
        if k < nc - 1:

            @pl.loop(0, rows, step=step)
            def _(r, j=j):
                at = pl.ds(pl.multiple_of(r, step), step)
                mine[j, at, :] = (
                    mine[j, at, :].astype(F32) + sib[j, at, :].astype(F32)
                ).astype(BF)

            remote(
                mine.at[j], far.at[chip], send.at[j], recv.at[chip], (2 * j + core, z)
            ).start()
        else:

            @pl.loop(0, rows, step=step)
            def _(r, j=j):
                at = pl.ds(pl.multiple_of(r, step), step)
                total_ref[at, :] = mine[j, at, :].astype(F32) + sib[j, at, :].astype(F32)

    for k in range(1, nc):
        j = lax.rem(chip + nc - k, nc)
        remote(
            mine.at[j], far.at[j], send.at[j], recv.at[j], (2 * j + core, z)
        ).wait()

        @pl.loop(0, rows, step=step)
        def _(r, j=j):
            at = pl.ds(pl.multiple_of(r, step), step)
            total_ref[at, :] += far[j, at, :].astype(F32)


def plane_sum_scratch(n_e, part):
    nc = n_e // 2
    block = (nc,) + part.shape[1:]
    return [pltpu.VMEM(block, BF)] * 3 + [DMA((nc,))] * 5


def plane_sum_kernel(n_e, n_z, part_ref, total_ref, *scratch):
    greet(n_e, n_z, False)
    plane_sum_body(n_e, part_ref, total_ref, *scratch)


def plane_sum(n_e, n_z, part):
    return pl.pallas_call(
        partial(plane_sum_kernel, n_e, n_z),
        out_shape=jax.ShapeDtypeStruct(part.shape[1:], F32),
        in_specs=[ANY],
        out_specs=VM,
        scratch_shapes=plane_sum_scratch(n_e, part),
        compiler_params=pltpu.CompilerParams(
            collective_id=2, has_side_effects=True, vmem_limit_bytes=BIG
        ),
        name="plane_sum",
    )(part)


def plane_gather_kernel(n_e, n_z, x_ref, out_ref, *sems):
    greet(n_e, n_z, False)
    plane_gather_start(n_e, x_ref, out_ref, *sems)
    plane_gather_end(n_e, x_ref, out_ref, *sems)


def plane_gather(n_e, n_z, x):
    nc = n_e // 2
    return pl.pallas_call(
        partial(plane_gather_kernel, n_e, n_z),
        out_shape=jax.ShapeDtypeStruct((n_e,) + x.shape, x.dtype),
        in_specs=[ANY],
        out_specs=ANY,
        scratch_shapes=[DMA] + [DMA((nc,))] * 4,
        compiler_params=pltpu.CompilerParams(collective_id=3, has_side_effects=True),
        name="plane_gather",
    )(x)


def pieces(columns, wide=512):
    cuts = list(range(0, columns - columns % wide, wide)) + [columns - columns % wide]
    spans = [(a, b - a) for a, b in zip(cuts, cuts[1:])]
    if columns % wide:
        spans.append((cuts[-1], columns % wide))
    return spans


def rows_out(n_e, cap, k, sz, src, d_ref, rows, out_ref, own, send, recv):
    e, z = place()
    pick = d_ref[sz]
    for start, size in pieces(src.shape[-1]):
        rows[k, :, start : start + size] = dot(pick, src[:, start : start + size]).astype(BF)
    for i in range(1, n_e + 1):
        oe = lax.rem(e + i, n_e)
        block = rows.at[k, pl.ds(pl.multiple_of(oe * cap, 16), cap), :]
        if i < n_e:
            remote(block, out_ref.at[sz, e], send.at[k, i], recv.at[sz, e], (oe, z)).start()
        else:
            pltpu.make_async_copy(block, out_ref.at[sz, e], own.at[k]).start()


def rows_out_wait(n_e, cap, k, sz, rows, out_ref, own, send, recv):
    e, z = place()
    for i in range(1, n_e + 1):
        oe = lax.rem(e + i, n_e)
        at = pl.ds(pl.multiple_of(oe * cap, 16), cap)
        block = rows.at[k, at, :]
        if i < n_e:
            remote(
                block, out_ref.at[sz, oe], send.at[k, i], recv.at[sz, oe], (oe, z)
            ).wait()
        else:
            pltpu.make_async_copy(block, out_ref.at[sz, e], own.at[k]).wait()


def open_kernel(
    n_e,
    n_z,
    cap,
    x_ref,
    ct_ref,
    rt_ref,
    wq_ref,
    wo_ref,
    mi_ref,
    pick_ref,
    xs_ref,
    rts_ref,
    wqs_ref,
    wos_ref,
    mis_ref,
    dy_ref,
    rows,
    own,
    x_send,
    x_recv,
    sib_send,
    sib_recv,
    w_send,
    w_recv,
    zw_send,
    zw_recv,
    zo_send,
    zo_recv,
    zr_send,
    zr_recv,
    m_send,
    m_recv,
    r_send,
    r_recv,
):
    e, z = place()
    n, me = n_e * n_z, e * n_z + z
    greet_all(n_e, n_z)

    def plane_peer(i):
        return lax.rem(e + i, n_e)

    for i in range(1, n_e):
        oe = plane_peer(i)
        remote(
            wq_ref.at[oe], wqs_ref.at[e, z], w_send.at[i], w_recv.at[e], (oe, z)
        ).start()
    kept = (
        (wq_ref.at[e], wqs_ref.at[e, z]),
        (wo_ref, wos_ref.at[z]),
        (rt_ref, rts_ref.at[z]),
        (mi_ref, mis_ref.at[me]),
    )
    for i, (src, dst) in enumerate(kept):
        pltpu.make_async_copy(src, dst, own.at[i]).start()
    out_chain = (lambda s: wos_ref.at[s], zo_send, zo_recv)
    chain_start(n_z, wo_ref, *out_chain)
    for k in range(1, n_z):
        oz = near(z, k, n_z)
        remote(rt_ref, rts_ref.at[z], zr_send.at[k], zr_recv.at[z], (e, oz)).start()

    def other_of(k):
        other = lax.rem(me + k, n)
        return other, (other // n_z, lax.rem(other, n_z))

    @pl.loop(1, n)
    def _(k):
        other, where = other_of(k)
        remote(mi_ref, mis_ref.at[me], m_send.at[k], m_recv.at[me], where).start()

    gather = (n_e, x_ref, xs_ref, own.at[4], x_send, x_recv, sib_send, sib_recv)
    plane_gather_start(*gather)
    pick = pick_ref[...]
    for start, size in pieces(ct_ref.shape[-1]):
        rows[:, start : start + size] = dot(pick, ct_ref[:, start : start + size]).astype(BF)
    for i in range(1, n_e + 1):
        oe = plane_peer(i)
        block = rows.at[pl.ds(pl.multiple_of(oe * cap, 16), cap), :]
        if i < n_e:
            remote(block, dy_ref.at[e], r_send.at[i], r_recv.at[e], (oe, z)).start()
        else:
            pltpu.make_async_copy(block, dy_ref.at[e], own.at[5]).start()

    for i in range(1, n_e):
        oe = plane_peer(i)
        remote(
            wq_ref.at[oe], wqs_ref.at[oe, z], w_send.at[i], w_recv.at[oe], (oe, z)
        ).wait()
    pltpu.make_async_copy(*kept[0], own.at[0]).wait()
    in_chain = (lambda s: wqs_ref.at[:, s], zw_send, zw_recv)
    chain_start(n_z, wqs_ref.at[:, z], *in_chain)
    for k in range(1, n_z):
        chain_take(n_z, k, *out_chain)
        chain_take(n_z, k, *in_chain)
        if k == n_z - 2:
            plane_gather_end(*gather)
    chain_end(n_z, wo_ref, *out_chain)
    chain_end(n_z, wqs_ref.at[:, z], *in_chain)
    for k in range(1, n_z):
        oz = near(z, k, n_z)
        remote(rt_ref, rts_ref.at[oz], zr_send.at[k], zr_recv.at[oz], (e, oz)).wait()

    @pl.loop(1, n)
    def _(k):
        other, where = other_of(k)
        remote(mi_ref, mis_ref.at[other], m_send.at[k], m_recv.at[other], where).wait()

    for i in range(1, n_e + 1):
        oe = plane_peer(i)
        block = rows.at[pl.ds(pl.multiple_of(oe * cap, 16), cap), :]
        if i < n_e:
            remote(block, dy_ref.at[oe], r_send.at[i], r_recv.at[oe], (oe, z)).wait()
        else:
            pltpu.make_async_copy(block, dy_ref.at[e], own.at[5]).wait()
    for i, (src, dst) in enumerate(kept):
        if i:
            pltpu.make_async_copy(src, dst, own.at[i]).wait()


def open_layer(n_e, n_z, cap, tokens, cotangent, routes, wq, wo, misc, pick):
    n, nc = n_e * n_z, n_e // 2
    _, shard, columns = wq.shape
    width = tokens.shape[1]

    def like(lead, a):
        return jax.ShapeDtypeStruct((lead,) + a.shape, a.dtype)

    return pl.pallas_call(
        partial(open_kernel, n_e, n_z, cap),
        out_shape=(
            like(n_e, tokens),
            like(n_z, routes),
            jax.ShapeDtypeStruct((n_e, n_z, shard, columns), BF),
            like(n_z, wo),
            like(n, misc),
            jax.ShapeDtypeStruct((n_e, cap, width), BF),
        ),
        in_specs=[ANY, VM] + [ANY] * 4 + [VM],
        out_specs=(ANY,) * 6,
        scratch_shapes=[
            pltpu.VMEM((n_e * cap, width), BF),
            DMA((6,)),
            DMA((nc,)),
            DMA((nc,)),
            DMA((nc,)),
            DMA((nc,)),
            DMA((n_e,)),
            DMA((n_e,)),
            DMA((n_z + 1,)),
            DMA((n_z,)),
            DMA((n_z + 1,)),
            DMA((n_z,)),
            DMA((n_z,)),
            DMA((n_z,)),
            DMA((n,)),
            DMA((n,)),
            DMA((n_e,)),
            DMA((n_e,)),
        ],
        compiler_params=pltpu.CompilerParams(
            collective_id=11, has_side_effects=True, vmem_limit_bytes=BIG
        ),
        name="open_layer",
    )(tokens, cotangent, routes, wq, wo, misc, pick)


def dispatch_kernel(
    n_e,
    n_z,
    cap,
    tok_ref,
    d_ref,
    out_ref,
    zbuf,
    rows,
    own,
    z_send,
    z_recv,
    send,
    recv,
):
    e, z = place()
    greet(n_e, n_z, True)
    chain = (lambda s: zbuf.at[s], z_send, z_recv)
    chain_start(n_z, tok_ref, *chain)
    for k in range(n_z):
        sz = chain_take(n_z, k, *chain) if k else z
        src = zbuf.at[sz] if k else tok_ref
        rows_out(n_e, cap, k, sz, src, d_ref, rows, out_ref, own, send, recv)
    for k in range(n_z):
        sz = ranked(z, k, n_z) if k else z
        rows_out_wait(n_e, cap, k, sz, rows, out_ref, own, send, recv)
    chain_end(n_z, tok_ref, *chain)


def dispatch(n_e, n_z, cap, tok, picks):
    count, columns = tok.shape
    return pl.pallas_call(
        partial(dispatch_kernel, n_e, n_z, cap),
        out_shape=jax.ShapeDtypeStruct((n_z, n_e, cap, columns), BF),
        in_specs=[VM, VM],
        out_specs=ANY,
        scratch_shapes=[
            pltpu.VMEM((n_z, count, columns), BF),
            pltpu.VMEM((n_z, n_e * cap, columns), BF),
            DMA((n_z,)),
            DMA((n_z + 1,)),
            DMA((n_z,)),
            DMA((n_z, n_e)),
            DMA((n_z, n_e)),
        ],
        compiler_params=pltpu.CompilerParams(
            collective_id=4, has_side_effects=True, vmem_limit_bytes=BIG
        ),
        name="dispatch",
    )(tok, picks)


def send_kernel(n_e, n_z, cap, src_ref, d_ref, out_ref, rows, own, send, recv):
    e, z = place()
    greet(n_e, n_z, False)
    for k in range(n_z):
        sz = near(z, k, n_z)
        rows_out(n_e, cap, k, sz, src_ref.at[sz], d_ref, rows, out_ref, own, send, recv)
    for k in range(n_z):
        rows_out_wait(n_e, cap, k, near(z, k, n_z), rows, out_ref, own, send, recv)


def send_rows(n_e, n_z, cap, src, picks):
    columns = src.shape[-1]
    return pl.pallas_call(
        partial(send_kernel, n_e, n_z, cap),
        out_shape=jax.ShapeDtypeStruct((n_z, n_e, cap, columns), BF),
        in_specs=[VM, VM],
        out_specs=ANY,
        scratch_shapes=[
            pltpu.VMEM((n_z, n_e * cap, columns), BF),
            DMA((n_z,)),
            DMA((n_z, n_e)),
            DMA((n_z, n_e)),
        ],
        compiler_params=pltpu.CompilerParams(
            collective_id=5, has_side_effects=True, vmem_limit_bytes=BIG
        ),
        name="send_rows",
    )(src, picks)


def give_back_kernel(
    n_e,
    n_z,
    cap,
    y_ref,
    d_ref,
    out_ref,
    rbuf,
    pbuf,
    own,
    send,
    recv,
    z_own,
    z_send,
    z_recv,
):
    e, z = place()
    greet(n_e, n_z, True)
    order = list(range(n_z - 1, -1, -1))
    for k in order:
        sz = near(z, k, n_z)
        for i in range(1, n_e + 1):
            oe = lax.rem(e + i, n_e)
            if i < n_e:
                remote(
                    y_ref.at[sz, oe],
                    rbuf.at[sz, e],
                    send.at[k, i],
                    recv.at[sz, e],
                    (oe, z),
                ).start()
            else:
                pltpu.make_async_copy(y_ref.at[sz, e], rbuf.at[sz, e], own.at[k]).start()
    for k in order:
        sz = near(z, k, n_z)
        for i in range(1, n_e + 1):
            oe = lax.rem(e + i, n_e)
            if i < n_e:
                remote(
                    y_ref.at[sz, oe],
                    rbuf.at[sz, oe],
                    send.at[k, i],
                    recv.at[sz, oe],
                    (oe, z),
                ).wait()
            else:
                pltpu.make_async_copy(y_ref.at[sz, e], rbuf.at[sz, e], own.at[k]).wait()
        pick = d_ref[sz]
        for start, size in pieces(pbuf.shape[-1]):
            block = rbuf[sz, :, :, start : start + size].reshape(n_e * cap, size)
            pbuf[k, :, start : start + size] = dot(pick, block).astype(BF)
        if k:
            remote(
                pbuf.at[k], out_ref.at[z], z_send.at[k], z_recv.at[z], (e, sz)
            ).start()
        else:
            pltpu.make_async_copy(pbuf.at[k], out_ref.at[z], z_own).start()
    for k in order:
        sz = near(z, k, n_z)
        if k:
            remote(
                pbuf.at[k], out_ref.at[sz], z_send.at[k], z_recv.at[sz], (e, sz)
            ).wait()
        else:
            pltpu.make_async_copy(pbuf.at[k], out_ref.at[z], z_own).wait()


def give_back(n_e, n_z, cap, y, picks, number):
    columns = y.shape[-1]
    count = picks.shape[1]
    return pl.pallas_call(
        partial(give_back_kernel, n_e, n_z, cap),
        out_shape=jax.ShapeDtypeStruct((n_z, count, columns), BF),
        in_specs=[ANY, VM],
        out_specs=ANY,
        scratch_shapes=[
            pltpu.VMEM((n_z, n_e, cap, columns), BF),
            pltpu.VMEM((n_z, count, columns), BF),
            DMA((n_z,)),
            DMA((n_z, n_e)),
            DMA((n_z, n_e)),
            DMA,
            DMA((n_z,)),
            DMA((n_z,)),
        ],
        compiler_params=pltpu.CompilerParams(
            collective_id=number, has_side_effects=True, vmem_limit_bytes=BIG
        ),
        name="give_back",
    )(y, picks)


def finish_kernel(
    n_e,
    n_z,
    part_ref,
    gw_ref,
    go_ref,
    gm_ref,
    total_ref,
    gws_ref,
    gos_ref,
    gms_ref,
    own_g,
    a_send,
    a_recv,
    z_send,
    z_recv,
    *scratch,
):
    e, z = place()
    n, me = n_e * n_z, e * n_z + z
    greet_all(n_e, n_z)

    def other_of(k):
        other = lax.rem(me + k, n)
        return other, (other // n_z, lax.rem(other, n_z))

    @pl.loop(1, n)
    def _(k):
        other, where = other_of(k)
        remote(
            gw_ref.at[other], gws_ref.at[me], a_send.at[0, k], a_recv.at[0, me], where
        ).start()
        remote(
            gm_ref.at[other], gms_ref.at[me], a_send.at[1, k], a_recv.at[1, me], where
        ).start()

    for k in range(1, n_z):
        oz = near(z, k, n_z)
        remote(
            go_ref.at[oz], gos_ref.at[z], z_send.at[k], z_recv.at[z], (e, oz)
        ).start()
    mine = (
        (gw_ref.at[me], gws_ref.at[me]),
        (gm_ref.at[me], gms_ref.at[me]),
        (go_ref.at[z], gos_ref.at[z]),
    )
    for i, (src, dst) in enumerate(mine):
        pltpu.make_async_copy(src, dst, own_g.at[i]).start()

    plane_sum_body(n_e, part_ref, total_ref, *scratch)

    @pl.loop(1, n)
    def _(k):
        other, where = other_of(k)
        remote(
            gw_ref.at[other],
            gws_ref.at[other],
            a_send.at[0, k],
            a_recv.at[0, other],
            where,
        ).wait()
        remote(
            gm_ref.at[other],
            gms_ref.at[other],
            a_send.at[1, k],
            a_recv.at[1, other],
            where,
        ).wait()

    for k in range(1, n_z):
        oz = near(z, k, n_z)
        remote(
            go_ref.at[oz], gos_ref.at[oz], z_send.at[k], z_recv.at[oz], (e, oz)
        ).wait()
    for i, (src, dst) in enumerate(mine):
        pltpu.make_async_copy(src, dst, own_g.at[i]).wait()


def finish(n_e, n_z, part, gw, go, gm):
    n = n_e * n_z
    return pl.pallas_call(
        partial(finish_kernel, n_e, n_z),
        out_shape=(
            jax.ShapeDtypeStruct(part.shape[1:], F32),
            jax.ShapeDtypeStruct(gw.shape, gw.dtype),
            jax.ShapeDtypeStruct(go.shape, go.dtype),
            jax.ShapeDtypeStruct(gm.shape, gm.dtype),
        ),
        in_specs=[ANY] * 4,
        out_specs=(VM, ANY, ANY, ANY),
        scratch_shapes=[
            DMA((3,)),
            DMA((2, n)),
            DMA((2, n)),
            DMA((n_z,)),
            DMA((n_z,)),
        ]
        + plane_sum_scratch(n_e, part),
        compiler_params=pltpu.CompilerParams(
            collective_id=8, has_side_effects=True, vmem_limit_bytes=BIG
        ),
        name="finish",
    )(part, gw, go, gm)


def head_norm(u, gain):
    r = lax.rsqrt(jnp.mean(u * u, axis=-1, keepdims=True) + EPSILON)
    return u * r * gain


def turn(u, cos, sin):
    return u * cos + pltpu.roll(u, HEAD // 2, 1) * sin


def turn_back(u, cos, sin):
    return u * cos - pltpu.roll(u, HEAD // 2, 1) * sin


def turns(table):
    other = pltpu.roll(table, HEAD // 2, 1)
    first = lax.broadcasted_iota(jnp.int32, table.shape, 1) < HEAD // 2
    return jnp.where(first, table, other), jnp.where(first, -other, table)


def may_see(seg_row):
    count = seg_row.shape[1]
    i = lax.broadcasted_iota(jnp.int32, (count, count), 0)
    j = lax.broadcasted_iota(jnp.int32, (count, count), 1)
    seg_col = jnp.sum(jnp.where(i == j, seg_row, 0.0), axis=1, keepdims=True)
    return ((seg_col == seg_row) & (seg_col >= 0) & (j <= i)) | (i == j)


def probabilities(q, k, allowed):
    scores = jnp.where(allowed, dot_last(q, k) * (HEAD**-0.5), -1e30)
    peak = jnp.max(scores, axis=-1, keepdims=True)
    weight = jnp.exp(scores - peak)
    return weight / jnp.sum(weight, axis=-1, keepdims=True)


def attend_block(
    heads, x, cos, sin, allowed, w_ref, wo_ref, g1_ref, gh_ref, n1_ref, raw_ref, v_ref, mix_ref
):
    x = x.astype(F32)
    r = lax.rsqrt(jnp.mean(x * x, axis=-1, keepdims=True) + EPSILON)
    n1 = (x * r * g1_ref[...]).astype(BF)
    n1_ref[...] = n1
    raw = dot(n1, w_ref[...])
    qk = (heads + 1) * HEAD
    raw_ref[...] = raw[:, :qk]
    value = raw[:, qk:].astype(BF)
    v_ref[...] = value
    gq, gk = gh_ref[0:1, :], gh_ref[1:2, :]
    key = turn(head_norm(raw[:, heads * HEAD : qk], gk), cos, sin).astype(BF)
    for h in range(heads):
        at = slice(h * HEAD, (h + 1) * HEAD)
        query = turn(head_norm(raw[:, at], gq), cos, sin).astype(BF)
        weight = probabilities(query, key, allowed).astype(BF)
        mix_ref[:, at] = dot(weight, value).astype(BF)
    return dot(mix_ref[...], wo_ref[...]).astype(BF)


def attend_kernel(
    heads,
    x_ref,
    turn_ref,
    seg_ref,
    w_ref,
    wo_ref,
    g1_ref,
    gh_ref,
    n1_ref,
    raw_ref,
    v_ref,
    mix_ref,
    part_ref,
):
    part_ref[0] = attend_block(
        heads,
        x_ref[0],
        *turns(turn_ref[0]),
        may_see(seg_ref[0]),
        w_ref,
        wo_ref,
        g1_ref,
        gh_ref,
        n1_ref.at[0],
        raw_ref.at[0],
        v_ref.at[0],
        mix_ref.at[0],
    )


def attend(n_e, heads, xs, turn_table, seg, w, wo, g1, gh):
    _, count, width = xs.shape

    def block(*shape):
        return pl.BlockSpec((1,) + shape, lambda b: (b, 0, 0))

    def whole(*shape):
        return pl.BlockSpec(shape, lambda b: (0, 0))

    outs = ((width, BF), ((heads + 1) * HEAD, F32), (HEAD, BF), (heads * HEAD, BF), (width, BF))
    return pl.pallas_call(
        partial(attend_kernel, heads),
        grid=(n_e,),
        out_shape=tuple(jax.ShapeDtypeStruct((n_e, count, c), t) for c, t in outs),
        in_specs=[
            block(count, width),
            block(count, HEAD),
            block(1, count),
            whole(*w.shape),
            whole(*wo.shape),
            whole(*g1.shape),
            whole(*gh.shape),
        ],
        out_specs=tuple(block(count, c) for c, _ in outs),
        compiler_params=pltpu.CompilerParams(vmem_limit_bytes=BIG),
        name="attend",
    )(xs, turn_table, seg, w, wo, g1, gh)


def front_kernel(
    n_e,
    n_z,
    cap,
    heads,
    xs_ref,
    ct_ref,
    pick_ref,
    turn_ref,
    seg_ref,
    w_ref,
    wo_ref,
    g1_ref,
    gh_ref,
    n1_ref,
    raw_ref,
    v_ref,
    mix_ref,
    total_ref,
    dy_ref,
    xbuf,
    n1buf,
    rawbuf,
    vbuf,
    mixbuf,
    away,
    mine,
    sib,
    far,
    via,
    zbuf,
    rows,
    x_sem,
    o_sem,
    sib_send,
    sib_recv,
    send,
    recv,
    via_send,
    via_recv,
    z_send,
    z_recv,
    r_send,
    r_recv,
    r_own,
):
    e, z = place()
    nc, chip, core = n_e // 2, e // 2, lax.rem(e, 2)
    sibling = (2 * chip + 1 - core, z)
    count = total_ref.shape[0]
    step = 32
    greet(n_e, n_z, True)
    chain = (lambda s: zbuf.at[s], z_send, z_recv)
    chain_start(n_z, ct_ref, *chain)

    def blocks(k):
        j = partner_chip(chip, nc - 1 - k)
        return j, (2 * j + 1 - core, 2 * j + core)

    half = count // 2

    def via_copy(p):
        rows = pl.ds(pl.multiple_of(p * half, half), half)
        there = (2 * partner_chip(chip, p + 1) + core, z)
        return remote(
            mine.at[partner_chip(chip, nc - 1), rows, :],
            via.at[p],
            via_send.at[p],
            via_recv.at[p],
            there,
        )

    def far_copy(p):
        j = partner_chip(chip, 2 - p)
        return remote(mine.at[j], far.at[p], send.at[p], recv.at[p], (2 * j + core, z))

    def load(b, slot):
        return pltpu.make_async_copy(xs_ref.at[b], xbuf.at[slot], x_sem.at[slot])

    def stores(b, slot):
        pairs = ((n1buf, n1_ref), (rawbuf, raw_ref), (vbuf, v_ref), (mixbuf, mix_ref))
        return [
            pltpu.make_async_copy(src.at[slot], dst.at[b], o_sem.at[i, slot])
            for i, (src, dst) in enumerate(pairs)
        ]

    for slot in range(2):
        load(blocks(0)[1][slot], slot).start()

    @pl.loop(0, nc)
    def _(k):
        j, pair = blocks(k)
        for slot, b in enumerate(pair):
            load(b, slot).wait()

            @pl.when(k > 0)
            def _(b=b, slot=slot):
                for copy in stores(b, slot):
                    copy.wait()

            part = attend_block(
                heads,
                xbuf[slot],
                *turns(turn_ref[b]),
                may_see(seg_ref[b]),
                w_ref,
                wo_ref,
                g1_ref,
                gh_ref,
                n1buf.at[slot],
                rawbuf.at[slot],
                vbuf.at[slot],
                mixbuf.at[slot],
            )
            for copy in stores(b, slot):
                copy.start()

            @pl.when(k < nc - 1)
            def _(slot=slot):
                load(blocks(k + 1)[1][slot], slot).start()

            if slot == 0:
                away[j] = part
                remote(
                    away.at[j], sib.at[j], sib_send.at[j], sib_recv.at[j], sibling
                ).start()
            else:
                mine[j] = part
        remote(away.at[j], sib.at[j], sib_send.at[j], sib_recv.at[j], sibling).wait()

        @pl.when(k < nc - 1)
        def _():
            @pl.loop(0, count, step=step)
            def _(r):
                at = pl.ds(pl.multiple_of(r, step), step)
                mine[j, at, :] = (
                    mine[j, at, :].astype(F32) + sib[j, at, :].astype(F32)
                ).astype(BF)

        @pl.when(k == 0)
        def _():
            for p in range(2):
                via_copy(p).start()

        @pl.when((k > 0) & (k < nc - 1))
        def _():
            via_copy(k - 1).wait_recv()

            @pl.loop(0, half, step=step)
            def _(r):
                at = pl.ds(pl.multiple_of((k - 1) * half + r, step), step)
                came = via[k - 1, pl.ds(pl.multiple_of(r, step), step), :]
                mine[j, at, :] = (mine[j, at, :].astype(F32) + came.astype(F32)).astype(BF)

            far_copy(k - 1).start()

        @pl.when((k > 0) & (k < n_z))
        def _():
            sz = chain_take(n_z, k, *chain)
            rows_out(
                n_e,
                cap,
                k - 1,
                sz,
                zbuf.at[sz],
                pick_ref,
                rows,
                dy_ref,
                r_own,
                r_send,
                r_recv,
            )

    @pl.loop(0, count, step=step)
    def _(r):
        at = pl.ds(pl.multiple_of(r, step), step)
        total_ref[at, :] = mine[chip, at, :].astype(F32) + sib[chip, at, :].astype(F32)

    for p in range(2):
        far_copy(p).wait()

        @pl.loop(0, count, step=step)
        def _(r, p=p):
            at = pl.ds(pl.multiple_of(r, step), step)
            total_ref[at, :] += far[p, at, :].astype(F32)

        via_copy(p).wait_send()

    for slot, b in enumerate(blocks(nc - 1)[1]):
        for copy in stores(b, slot):
            copy.wait()
    for k in range(1, n_z):
        rows_out_wait(
            n_e, cap, k - 1, ranked(z, k, n_z), rows, dy_ref, r_own, r_send, r_recv
        )
    chain_end(n_z, ct_ref, *chain)


def front(n_e, n_z, cap, heads, xs, ct, picks, turn_table, seg, w, wo, g1, gh):
    _, count, width = xs.shape
    nc = n_e // 2
    outs = ((width, BF), ((heads + 1) * HEAD, F32), (HEAD, BF), (heads * HEAD, BF))
    bufs = [pltpu.VMEM((2, count, width), BF)]
    bufs += [pltpu.VMEM((2, count, c), t) for c, t in outs]
    bufs += [pltpu.VMEM((nc, count, width), BF)] * 3
    bufs += [pltpu.VMEM((2, count, width), BF), pltpu.VMEM((2, count // 2, width), BF)]
    bufs += [
        pltpu.VMEM((n_z, count, width), BF),
        pltpu.VMEM((n_z - 1, n_e * cap, width), BF),
    ]
    return pl.pallas_call(
        partial(front_kernel, n_e, n_z, cap, heads),
        out_shape=tuple(jax.ShapeDtypeStruct((n_e, count, c), t) for c, t in outs)
        + (
            jax.ShapeDtypeStruct((count, width), F32),
            jax.ShapeDtypeStruct((n_z, n_e, cap, width), BF),
        ),
        in_specs=[ANY] + [VM] * 8,
        out_specs=(ANY,) * 4 + (VM, ANY),
        scratch_shapes=bufs
        + [
            DMA((2,)),
            DMA((4, 2)),
            DMA((nc,)),
            DMA((nc,)),
            DMA((2,)),
            DMA((2,)),
            DMA((2,)),
            DMA((2,)),
            DMA((n_z + 1,)),
            DMA((n_z,)),
            DMA((n_z, n_e)),
            DMA((n_z, n_e)),
            DMA((n_z,)),
        ],
        compiler_params=pltpu.CompilerParams(
            collective_id=12, has_side_effects=True, vmem_limit_bytes=BIG
        ),
        name="front",
    )(xs, ct, picks, turn_table, seg, w, wo, g1, gh)


def norm_back(u, gain, dv):
    r = lax.rsqrt(jnp.mean(u * u, axis=-1, keepdims=True) + EPSILON)
    nu = u * r
    dgain = jnp.sum(dv * nu, axis=0, keepdims=True)
    scaled = dv * gain
    du = r * (scaled - nu * jnp.mean(scaled * nu, axis=-1, keepdims=True))
    return du, dgain


def attend_back_block(
    heads,
    da,
    n1,
    raw_ref,
    value,
    cos,
    sin,
    allowed,
    w_ref,
    wo_ref,
    gh_ref,
    dmix,
    dcat,
    g1_ref,
    ghg_ref,
):
    dmix[...] = dot_last(da, wo_ref[...]).astype(BF)
    gq, gk = gh_ref[0:1, :], gh_ref[1:2, :]
    qk = (heads + 1) * HEAD
    key_raw = raw_ref[:, heads * HEAD : qk]
    key = turn(head_norm(key_raw, gk), cos, sin).astype(BF)
    count = key.shape[0]
    dkey = jnp.zeros((count, HEAD), F32)
    dvalue = jnp.zeros((count, HEAD), F32)
    dgq = jnp.zeros((1, HEAD), F32)
    scale = HEAD**-0.5
    for h in range(heads):
        at = slice(h * HEAD, (h + 1) * HEAD)
        query_raw = raw_ref[:, at]
        query = turn(head_norm(query_raw, gq), cos, sin).astype(BF)
        weight = probabilities(query, key, allowed)
        dm = dmix[:, at]
        dweight = dot_last(dm, value)
        delta = jnp.sum(weight * dweight, axis=-1, keepdims=True)
        dscore = (weight * (dweight - delta)).astype(BF)
        dquery = dot(dscore, key) * scale
        dkey += dot_first(dscore, query) * scale
        dvalue += dot_first(weight.astype(BF), dm)
        du, dg = norm_back(query_raw, gq, turn_back(dquery, cos, sin))
        dcat[:, at] = du.astype(BF)
        dgq += dg
    du, dgk = norm_back(key_raw, gk, turn_back(dkey, cos, sin))
    dcat[:, heads * HEAD : qk] = du.astype(BF)
    dcat[:, qk:] = dvalue.astype(BF)
    ghg_ref[0:1, :] += dgq
    ghg_ref[1:2, :] += dgk
    dn = dot_last(dcat[...], w_ref[...])
    g1_ref[...] += jnp.sum(dn * n1.astype(F32), axis=0, keepdims=True)
    return dn.astype(BF)


def attend_back_kernel(
    heads,
    steps,
    da_ref,
    n1_ref,
    raw_ref,
    v_ref,
    mix_ref,
    turn_ref,
    seg_ref,
    w_ref,
    wo_ref,
    gh_ref,
    dn_ref,
    gw_ref,
    go_ref,
    g1_ref,
    ghg_ref,
    acc_w,
    acc_o,
    dcat,
    dmix,
):
    step = pl.program_id(0)

    @pl.when(step == 0)
    def _():
        acc_w[...] = jnp.zeros_like(acc_w)
        acc_o[...] = jnp.zeros_like(acc_o)
        g1_ref[...] = jnp.zeros_like(g1_ref)
        ghg_ref[...] = jnp.zeros_like(ghg_ref)

    da, n1 = da_ref[0], n1_ref[0]
    dn_ref[0] = attend_back_block(
        heads,
        da,
        n1,
        raw_ref.at[0],
        v_ref[0],
        *turns(turn_ref[0]),
        may_see(seg_ref[0]),
        w_ref,
        wo_ref,
        gh_ref,
        dmix,
        dcat,
        g1_ref,
        ghg_ref,
    )
    acc_w[...] += dot_first(n1, dcat[...])
    acc_o[...] += dot_first(mix_ref[0], da)

    @pl.when(step == steps - 1)
    def _():
        gw_ref[...] = acc_w[...].astype(BF)
        go_ref[...] = acc_o[...].astype(BF)


def attend_back(n_e, heads, da, n1, raw, v, mix, turn_table, seg, w, wo, gh):
    _, count, width = da.shape

    def block(*shape):
        return pl.BlockSpec((1,) + shape, lambda b: (b, 0, 0))

    def whole(*shape):
        return pl.BlockSpec(shape, lambda b: (0, 0))

    return pl.pallas_call(
        partial(attend_back_kernel, heads, n_e),
        grid=(n_e,),
        out_shape=(
            jax.ShapeDtypeStruct((n_e, count, width), BF),
            jax.ShapeDtypeStruct(w.shape, BF),
            jax.ShapeDtypeStruct(wo.shape, BF),
            jax.ShapeDtypeStruct((1, width), F32),
            jax.ShapeDtypeStruct((8, HEAD), F32),
        ),
        in_specs=[
            block(count, width),
            block(count, width),
            block(*raw.shape[1:]),
            block(count, HEAD),
            block(*mix.shape[1:]),
            block(count, HEAD),
            block(1, count),
            whole(*w.shape),
            whole(*wo.shape),
            whole(*gh.shape),
        ],
        out_specs=(
            block(count, width),
            whole(*w.shape),
            whole(*wo.shape),
            whole(1, width),
            whole(8, HEAD),
        ),
        scratch_shapes=[
            pltpu.VMEM(w.shape, F32),
            pltpu.VMEM(wo.shape, F32),
            pltpu.VMEM((count, (heads + 2) * HEAD), BF),
            pltpu.VMEM((count, heads * HEAD), BF),
        ],
        compiler_params=pltpu.CompilerParams(vmem_limit_bytes=BIG),
        name="attend_back",
    )(da, n1, raw, v, mix, turn_table, seg, w, wo, gh)


def back_kernel(
    n_e,
    n_z,
    cap,
    heads,
    da_ref,
    r_ref,
    rfar_ref,
    gr_ref,
    n1_ref,
    raw_ref,
    v_ref,
    mix_ref,
    unpick_ref,
    g2_ref,
    turn_ref,
    seg_ref,
    w_ref,
    wo_ref,
    g1_ref,
    gh_ref,
    total_ref,
    part_ref,
    gws_ref,
    goo_ref,
    gor_ref,
    gol_ref,
    grs_ref,
    gvs_ref,
    ret_ref,
    gwr_ref,
    gwl_ref,
    rsum,
    gplane,
    das,
    n1s,
    raws,
    vs,
    mixs,
    dcats,
    dmix,
    gsum,
    ghsum,
    gvec,
    gtotal,
    away,
    mine,
    sib,
    far,
    rbuf,
    gob,
    own,
    in_sem,
    raw_sem,
    d_send,
    d_recv,
    ds_send,
    ds_recv,
    a_send,
    a_recv,
    b_send,
    b_recv,
    b_own,
    p_send,
    p_recv,
    o_send,
    or_recv,
    ol_recv,
    w_send,
    wr_recv,
    wl_recv,
    s_send,
    s_recv,
    t_sem,
    v_send,
    v_recv,
    vz_send,
    vz_recv,
    sib_send,
    sib_recv,
    send,
    recv,
):
    e, z = place()
    n, me = n_e * n_z, e * n_z + z
    nc, chip, core = n_e // 2, e // 2, lax.rem(e, 2)
    sibling = (2 * chip + 1 - core, z)
    count, width = total_ref.shape
    shard = width // n
    head_rows = mixs.shape[-1] // n_z
    step = 32
    greet_all(n_e, n_z)

    def other_of(k):
        other = lax.rem(me + k, n)
        return other, (other // n_z, lax.rem(other, n_z))

    def far_chip(k):
        return (2 * partner_chip(chip, k) + core, z)

    def give_da(k):
        return remote(
            da_ref, das.at[e], d_send.at[k], d_recv.at[chip], far_chip(k)
        )

    remote(da_ref, das.at[e], ds_send.at[0], ds_recv.at[chip], sibling).start()
    for k in range(1, nc - 1):
        give_da(k).start()
    own_da = pltpu.make_async_copy(da_ref, das.at[e], own.at[0])
    own_da.start()

    @pl.loop(1, n)
    def _(k):
        other, where = other_of(k)
        remote(
            gr_ref.at[other], grs_ref.at[me], a_send.at[k], a_recv.at[me], where
        ).start()

    own_gr = pltpu.make_async_copy(gr_ref.at[me], grs_ref.at[me], own.at[1])
    own_gr.start()
    for i, (src, dst) in enumerate(((n1_ref, n1s), (v_ref, vs), (mix_ref, mixs))):
        pltpu.make_async_copy(src, dst, in_sem.at[i]).start()

    def load_raw(b, slot):
        return pltpu.make_async_copy(raw_ref.at[b], raws.at[slot], raw_sem.at[slot])

    def blocks(k):
        j = partner_chip(chip, k)
        return j, (2 * j + core, 2 * j + 1 - core)

    def source(k):
        return jnp.where(k == 0, z, ranked(z, k, n_z))

    def give_rows(k):
        sz = source(k)
        for i in range(1, n_e):
            oe = lax.rem(e + i, n_e)
            remote(
                r_ref.at[sz, oe],
                ret_ref.at[sz, e],
                b_send.at[k, i],
                b_recv.at[sz, e],
                (oe, z),
            ).start()
        pltpu.make_async_copy(r_ref.at[sz, e], ret_ref.at[sz, e], b_own.at[k]).start()

    for slot in range(2):
        load_raw(blocks(0)[1][slot], slot).start()
    gsum[...] = jnp.zeros_like(gsum)
    ghsum[...] = jnp.zeros_like(ghsum)
    for i, (src, dst) in enumerate(((n1_ref, n1s), (v_ref, vs), (mix_ref, mixs))):
        pltpu.make_async_copy(src, dst, in_sem.at[i]).wait()

    tokens = n_e * count

    def out_weights():
        da_all = das[...].reshape(tokens, width)
        for oz in range(n_z):
            at = slice(oz * head_rows, (oz + 1) * head_rows)
            gob[oz] = dot_first(mixs[:, :, at].reshape(tokens, head_rows), da_all).astype(BF)
        pass_all(out_pass, 0)

    def pass_sum(d, step, stage, block, inbox, recv, send, add):
        distance = z if step > 0 else n_z - 1 - z
        going = (d > z) if step > 0 else (d < z)

        @pl.when(going & (distance == stage))
        def _():
            if stage:
                remote(block, inbox.at[d], send.at[d], recv.at[d], (e, z - step)).wait_recv()
                add(d, inbox)
            remote(block, inbox.at[d], send.at[d], recv.at[d], (e, z + step)).start()

    def pass_all(one_pass, stage, steps=range(n_z - 1)):
        for d in steps:
            one_pass(n_z - 1 - d, 1, stage)
            one_pass(d, -1, stage)

    def out_add(d, inbox):
        fetch = pltpu.make_async_copy(inbox.at[d], away.at[0:head_rows], t_sem.at[0])
        fetch.start()
        fetch.wait()

        @pl.loop(0, head_rows, step=step)
        def _(r):
            at = pl.ds(pl.multiple_of(r, step), step)
            gob[d, at, :] = (gob[d, at, :].astype(F32) + away[at, :].astype(F32)).astype(BF)

    def out_pass(d, step, stage):
        inbox, recv = (gor_ref, or_recv) if step > 0 else (gol_ref, ol_recv)
        pass_sum(d, step, stage, gob.at[d], inbox, recv, o_send, out_add)

    parts = dcats.shape[-1] // (n_z * shard)

    def shard_at(d):
        return pl.ds(pl.multiple_of(d * shard, shard), shard)

    def weight_add(d, inbox):
        for p in range(parts):
            there = away.at[p * shard : (p + 1) * shard]
            pltpu.make_async_copy(inbox.at[d, p], there, t_sem.at[p]).start()
        for p in range(parts):
            there = away.at[p * shard : (p + 1) * shard]
            pltpu.make_async_copy(inbox.at[d, p], there, t_sem.at[p]).wait()

            @pl.loop(0, shard, step=step)
            def _(r, p=p):
                at = pl.ds(pl.multiple_of(d * shard + r, step), step)
                came = away[pl.ds(pl.multiple_of(p * shard + r, step), step), :]
                n1s[p, at, :] = (n1s[p, at, :].astype(F32) + came.astype(F32)).astype(BF)

    def weight_pass(d, step, stage):
        inbox, recv = (gwr_ref, wr_recv) if step > 0 else (gwl_ref, wl_recv)
        block = n1s.at[0:parts, shard_at(d), :]
        pass_sum(d, step, stage, block, inbox, recv, w_send, weight_add)

    def sum_rows(src, dst, k):
        sz = source(k)
        unpick = unpick_ref[sz]
        cuts = pieces(width)

        def fetch(p):
            start, size = cuts[p]
            return pltpu.make_async_copy(
                src.at[:, :, start : start + size], rbuf.at[p % 2], in_sem.at[p % 2]
            )

        fetch(0).start()
        for p, (start, size) in enumerate(cuts):
            if p + 1 < len(cuts):
                fetch(p + 1).start()
            fetch(p).wait()
            block = rbuf[p % 2].reshape(n_e * cap, size)
            dst[:, start : start + size] = dot(unpick, block).astype(BF)

    def sum_of(k):
        return rsum if k == n_z - 1 else das.at[k]

    def send_sum(k):
        sz = source(k)
        return remote(sum_of(k), part_ref.at[z], p_send.at[k], p_recv.at[z], (e, sz))

    def take_rows(k):
        sz = source(k)
        for i in range(1, n_e):
            oe = lax.rem(e + i, n_e)
            remote(
                r_ref.at[sz, oe],
                ret_ref.at[sz, oe],
                b_send.at[k, i],
                b_recv.at[sz, oe],
                (oe, z),
            ).wait()
        pltpu.make_async_copy(r_ref.at[sz, e], ret_ref.at[sz, e], b_own.at[k]).wait()
        sum_rows(ret_ref.at[sz], sum_of(k), k)

    sum_rows(rfar_ref, rsum, n_z - 1)
    send_sum(n_z - 1).start()

    @pl.loop(0, nc)
    def _(k):
        j, pair = blocks(k)

        @pl.when(k == 0)
        def _():
            pltpu.make_async_copy(da_ref, das.at[e], own.at[0]).wait()

        @pl.when(k > 0)
        def _():
            block = das.at[2 * j + core]
            remote(da_ref, block, d_send.at[k], d_recv.at[j], far_chip(k)).wait_recv()
            remote(block, block, ds_send.at[k], ds_recv.at[j], sibling).start()

        def sibling_da():
            remote(
                da_ref, das.at[pair[1]], ds_send.at[k], ds_recv.at[j], sibling
            ).wait_recv()

        for slot, b in enumerate(pair):
            if slot == 1:
                sibling_da()
            load_raw(b, slot).wait()
            part = attend_back_block(
                heads,
                das[b],
                n1s[b],
                raws.at[slot],
                vs[b],
                *turns(turn_ref[b]),
                may_see(seg_ref[b]),
                w_ref,
                wo_ref,
                gh_ref,
                dmix,
                dcats.at[b],
                gsum,
                ghsum,
            )

            @pl.when(k < nc - 1)
            def _(slot=slot):
                load_raw(blocks(k + 1)[1][slot], slot).start()

            if slot == 0:
                mine[j] = part
            else:
                away[...] = part
        to_sibling = remote(
            away, sib.at[lax.rem(k, 2)], sib_send, sib_recv.at[lax.rem(k, 2)], sibling
        )
        to_sibling.start()

        @pl.when(k == 0)
        def _():
            give_da(nc - 1).start()

        @pl.when((k > 0) & (k < n_z - 1))
        def _():
            give_rows(n_z - 1 - k)

        to_sibling.wait()

        @pl.when(k > 0)
        def _():
            @pl.loop(0, count, step=step)
            def _(r):
                at = pl.ds(pl.multiple_of(r, step), step)
                mine[j, at, :] = (
                    mine[j, at, :].astype(F32) + sib[lax.rem(k, 2), at, :].astype(F32)
                ).astype(BF)

            remote(
                mine.at[j], far.at[k - 1], send.at[k - 1], recv.at[k - 1], far_chip(k)
            ).start()

        @pl.when(k == 0)
        def _():
            @pl.loop(0, count, step=step)
            def _(r):
                at = pl.ds(pl.multiple_of(r, step), step)
                total_ref[at, :] = mine[j, at, :].astype(F32) + sib[0, at, :].astype(F32)

    remote(da_ref, das.at[e], ds_send.at[0], ds_recv.at[chip], sibling).wait_send()
    for k in range(1, nc):
        give_da(k).wait_send()
        block = das.at[2 * partner_chip(chip, k) + core]
        remote(block, block, ds_send.at[k], ds_recv.at[chip], sibling).wait_send()

    give_rows(0)

    dcat = dcats[...].reshape(tokens, -1)

    @pl.loop(0, n_e)
    def _(t):
        at = pl.ds(pl.multiple_of(t * n_z * shard, n_z * shard), n_z * shard)
        rows = dot_first(n1s[:, :, at].reshape(tokens, n_z * shard), dcat).astype(BF)
        for p in range(parts):
            n1s[p, :, at] = rows[:, p * n_z * shard : (p + 1) * n_z * shard]

    pass_all(weight_pass, 0)
    out_weights()
    pltpu.make_async_copy(gob.at[z], goo_ref, own.at[3]).start()
    lanes = 128
    g1 = gsum[...] / g1_ref[...]
    per = width // lanes
    for i in range(per):
        gvec[i : i + 1, :] = g1[:, i * lanes : (i + 1) * lanes]
        gvec[per + i : per + i + 1, :] = g2_ref[:, i * lanes : (i + 1) * lanes]
    gvec[2 * per : 2 * per + 8, :] = ghsum[...]

    for i in range(1, n_e):
        oe = lax.rem(e + i, n_e)
        remote(gvec, gplane.at[e], v_send.at[i], v_recv.at[e], (oe, z)).start()
    gplane[e] = gvec[...]
    pass_all(weight_pass, 1, range(1))
    take_rows(n_z - 2)
    send_sum(n_z - 2).start()
    pass_all(weight_pass, 1, range(1, n_z - 1))
    pass_all(weight_pass, 2)
    for k in range(n_z - 3, 0, -1):
        take_rows(k)
        send_sum(k).start()
    pass_all(out_pass, 1)

    for came, inbox, recv_w, there in (
        (z > 0, gwr_ref, wr_recv, z - 1),
        (z < n_z - 1, gwl_ref, wl_recv, z + 1),
    ):

        @pl.when(came)
        def _(inbox=inbox, recv_w=recv_w, there=there):
            block = n1s.at[0:parts, shard_at(z), :]
            remote(block, inbox.at[z], w_send.at[z], recv_w.at[z], (e, there)).wait_recv()
            weight_add(z, inbox)

    def weight_block(t):
        at = pl.ds(pl.multiple_of(t * n_z * shard, n_z * shard), n_z * shard)
        return n1s.at[0:parts, shard_at(z), at]

    for i in range(1, n_e):
        oe = lax.rem(e + i, n_e)
        remote(weight_block(oe), gws_ref.at[e], s_send.at[i], s_recv.at[e], (oe, z)).start()
    pltpu.make_async_copy(weight_block(e), gws_ref.at[e], own.at[2]).start()
    for k in range(1, nc):
        j = partner_chip(chip, k)
        remote(
            mine.at[j], far.at[k - 1], send.at[k - 1], recv.at[k - 1], far_chip(k)
        ).wait()

        @pl.loop(0, count, step=step)
        def _(r, k=k):
            at = pl.ds(pl.multiple_of(r, step), step)
            total_ref[at, :] += far[k - 1, at, :].astype(F32)

    pass_all(out_pass, 2)
    for i in range(1, n_e):
        oe = lax.rem(e + i, n_e)
        remote(gvec, gplane.at[oe], v_send.at[i], v_recv.at[oe], (oe, z)).wait()
    gtotal[...] = jnp.sum(gplane[...], axis=0)
    for k in range(1, n_z):
        oz = near(z, k, n_z)
        remote(gtotal, gvs_ref.at[z], vz_send.at[k], vz_recv.at[z], (e, oz)).start()
    own_gv = pltpu.make_async_copy(gtotal, gvs_ref.at[z], own.at[4])
    own_gv.start()
    take_rows(0)
    pltpu.make_async_copy(das.at[0], part_ref.at[z], own.at[6]).start()

    @pl.loop(1, n)
    def _(k):
        other, where = other_of(k)
        remote(
            gr_ref.at[other],
            grs_ref.at[other],
            a_send.at[k],
            a_recv.at[other],
            where,
        ).wait()

    for i in range(1, n_e):
        oe = lax.rem(e + i, n_e)
        remote(weight_block(oe), gws_ref.at[oe], s_send.at[i], s_recv.at[oe], (oe, z)).wait()
    for d in range(n_z):

        @pl.when(d != z)
        def _(d=d):
            remote(gob.at[d], gor_ref.at[d], o_send.at[d], or_recv.at[d], (e, d)).wait_send()
            block = n1s.at[0:parts, shard_at(d), :]
            remote(block, gwr_ref.at[d], w_send.at[d], wr_recv.at[d], (e, d)).wait_send()

    for came, inbox, recv_o, there in (
        (z > 0, gor_ref, or_recv, z - 1),
        (z < n_z - 1, gol_ref, ol_recv, z + 1),
    ):

        @pl.when(came)
        def _(inbox=inbox, recv_o=recv_o, there=there):
            remote(
                gob.at[z], inbox.at[z], o_send.at[z], recv_o.at[z], (e, there)
            ).wait_recv()

    for k in range(1, n_z):
        oz = near(z, k, n_z)
        remote(
            gtotal, gvs_ref.at[oz], vz_send.at[k], vz_recv.at[oz], (e, oz)
        ).wait()
        sz = ranked(z, k, n_z)
        remote(
            sum_of(k), part_ref.at[sz], p_send.at[k], p_recv.at[sz], (e, sz)
        ).wait()
    own_gr.wait()
    pltpu.make_async_copy(weight_block(e), gws_ref.at[e], own.at[2]).wait()
    pltpu.make_async_copy(gob.at[z], goo_ref, own.at[3]).wait()
    own_gv.wait()
    pltpu.make_async_copy(das.at[0], part_ref.at[z], own.at[6]).wait()


def back(
    n_e, n_z, cap, heads, da, r_rows, r_far, gr, n1, raw, v, mix, unpicks, g2, turn_table, seg, w, wo, g1, gh
):
    n, nc = n_e * n_z, n_e // 2
    count, width = da.shape
    shard = width // n
    columns = w.shape[1]
    parts = columns // (n_z * shard)
    out_block = (wo.shape[0] // n_z, width)
    vec_rows = 2 * width // 128 + 8
    block = (count, width)

    def sems(*shape):
        return DMA(shape)

    return pl.pallas_call(
        partial(back_kernel, n_e, n_z, cap, heads),
        out_shape=(
            jax.ShapeDtypeStruct(block, F32),
            jax.ShapeDtypeStruct((n_z,) + block, BF),
            jax.ShapeDtypeStruct((n_e, parts, shard, n_z * shard), BF),
            jax.ShapeDtypeStruct(out_block, BF),
            jax.ShapeDtypeStruct((n_z,) + out_block, BF),
            jax.ShapeDtypeStruct((n_z,) + out_block, BF),
            jax.ShapeDtypeStruct(gr.shape, F32),
            jax.ShapeDtypeStruct((n_z, vec_rows, 128), F32),
            jax.ShapeDtypeStruct(r_rows.shape, BF),
            jax.ShapeDtypeStruct((n_z, parts, shard, width), BF),
            jax.ShapeDtypeStruct((n_z, parts, shard, width), BF),
        ),
        in_specs=[ANY] * 8 + [VM] * 8,
        out_specs=(VM,) + (ANY,) * 10,
        scratch_shapes=[
            pltpu.VMEM(block, BF),
            pltpu.VMEM((n_e, vec_rows, 128), F32),
            pltpu.VMEM((n_e,) + block, BF),
            pltpu.VMEM(n1.shape, BF),
            pltpu.VMEM((2,) + raw.shape[1:], F32),
            pltpu.VMEM(v.shape, BF),
            pltpu.VMEM(mix.shape, BF),
            pltpu.VMEM((n_e, count, columns), BF),
            pltpu.VMEM((count, heads * HEAD), BF),
            pltpu.VMEM((1, width), F32),
            pltpu.VMEM((8, HEAD), F32),
            pltpu.VMEM((vec_rows, 128), F32),
            pltpu.VMEM((vec_rows, 128), F32),
            pltpu.VMEM(block, BF),
            pltpu.VMEM((nc,) + block, BF),
            pltpu.VMEM((2,) + block, BF),
            pltpu.VMEM((nc - 1,) + block, BF),
            pltpu.VMEM((2, n_e, cap, pieces(width)[0][1]), BF),
            pltpu.VMEM((n_z, wo.shape[0] // n_z, width), BF),
            sems(7),
            sems(3),
            sems(2),
            sems(nc),
            sems(nc),
            sems(nc),
            sems(nc),
            sems(n),
            sems(n),
            sems(n_z, n_e),
            sems(n_z, n_e),
            sems(n_z),
            sems(n_z),
            sems(n_z),
            sems(n_z),
            sems(n_z),
            sems(n_z),
            sems(n_z),
            sems(n_z),
            sems(n_z),
            sems(n_e),
            sems(n_e),
            sems(parts),
            sems(n_e),
            sems(n_e),
            sems(n_z),
            sems(n_z),
            DMA,
            sems(2),
            sems(nc),
            sems(nc),
        ],
        compiler_params=pltpu.CompilerParams(
            collective_id=14, has_side_effects=True, vmem_limit_bytes=63 * 1024 * 1024
        ),
        name="back",
    )(da, r_rows, r_far, gr, n1, raw, v, mix, unpicks, g2, turn_table, seg, w, wo, g1, gh)


def expert_kernel(
    n_z,
    experts,
    width,
    x_ref,
    dy_ref,
    wg_ref,
    wu_ref,
    wd_ref,
    r_ref,
    dx_ref,
    gg_ref,
    gu_ref,
    gd_ref,
):
    step = pl.program_id(0)

    @pl.when(step == 0)
    def _():
        gg_ref[...] = jnp.zeros_like(gg_ref)
        gu_ref[...] = jnp.zeros_like(gu_ref)
        gd_ref[...] = jnp.zeros_like(gd_ref)

    e, z = place()
    me = e * n_z + z
    x = x_ref[:, :width]
    extra = x_ref[:, width:].astype(F32)
    lane = lax.broadcasted_iota(jnp.int32, extra.shape, 1)
    gate = jnp.sum(
        jnp.where((lane == me) | (lane == experts + me), extra, 0.0), axis=1, keepdims=True
    )
    gate_part = dot(x, wg_ref[...])
    up_part = dot(x, wu_ref[...])
    sig = 1.0 / (1.0 + jnp.exp(-gate_part))
    act = gate_part * sig
    inner = (act * up_part).astype(BF)
    r_ref[...] = (dot(inner, wd_ref[...]) * gate).astype(BF)
    dy = dy_ref[...]
    dinner = dot_last(dy, wd_ref[...])
    inner_f = inner.astype(F32)
    dgate = jnp.sum(dinner * inner_f, axis=1, keepdims=True)
    gd_ref[...] += dot_first((inner_f * gate).astype(BF), dy)
    dinner = dinner * gate
    dgp = (dinner * up_part * sig * (1.0 + gate_part * (1.0 - sig))).astype(BF)
    dup = (dinner * act).astype(BF)
    dx_ref[:, :width] = (dot_last(dgp, wg_ref[...]) + dot_last(dup, wu_ref[...])).astype(BF)
    high = dgate.astype(BF).astype(F32)
    dx_ref[:, width:] = jnp.where(
        lane == me, high, jnp.where(lane == experts + me, dgate - high, 0.0)
    ).astype(BF)
    gg_ref[...] += dot_first(x, dgp)
    gu_ref[...] += dot_first(x, dup)


def expert_run(n_z, experts, x, dy, wg, wu, wd):
    rows, columns = x.shape
    width, hidden = wg.shape
    tile = 512

    def block(c):
        return pl.BlockSpec((tile, c), lambda b: (b, 0))

    def whole(shape):
        return pl.BlockSpec(shape, lambda b: (0, 0), pipeline_mode=pl.Buffered(1))

    return pl.pallas_call(
        partial(expert_kernel, n_z, experts, width),
        grid=(rows // tile,),
        out_shape=(
            jax.ShapeDtypeStruct((rows, width), BF),
            jax.ShapeDtypeStruct((rows, columns), BF),
            jax.ShapeDtypeStruct((width, hidden), F32),
            jax.ShapeDtypeStruct((width, hidden), F32),
            jax.ShapeDtypeStruct((hidden, width), F32),
        ),
        in_specs=[
            block(columns),
            block(width),
            whole(wg.shape),
            whole(wu.shape),
            whole(wd.shape),
        ],
        out_specs=(
            block(width),
            block(columns),
            whole(wg.shape),
            whole(wu.shape),
            whole(wd.shape),
        ),
        compiler_params=pltpu.CompilerParams(vmem_limit_bytes=BIG),
        name="experts",
    )(x, dy, wg, wu, wd)


def expert_tile(width, experts, me, x_ext, dy, wg_ref, wu_ref, wd_ref):
    x = x_ext[:, :width]
    extra = x_ext[:, width:].astype(F32)
    lane = lax.broadcasted_iota(jnp.int32, extra.shape, 1)
    gate = jnp.sum(
        jnp.where((lane == me) | (lane == experts + me), extra, 0.0), axis=1, keepdims=True
    )
    gate_part = dot(x, wg_ref[...])
    up_part = dot(x, wu_ref[...])
    sig = 1.0 / (1.0 + jnp.exp(-gate_part))
    act = gate_part * sig
    inner = (act * up_part).astype(BF)
    result = (dot(inner, wd_ref[...]) * gate).astype(BF)
    dinner = dot_last(dy, wd_ref[...])
    inner_f = inner.astype(F32)
    dgate = jnp.sum(dinner * inner_f, axis=1, keepdims=True)
    gated = (inner_f * gate).astype(BF)
    dinner = dinner * gate
    dgp = (dinner * up_part * sig * (1.0 + gate_part * (1.0 - sig))).astype(BF)
    dup = (dinner * act).astype(BF)
    dx = (dot_last(dgp, wg_ref[...]) + dot_last(dup, wu_ref[...])).astype(BF)
    high = dgate.astype(BF).astype(F32)
    back = jnp.where(
        lane == me, high, jnp.where(lane == experts + me, dgate - high, 0.0)
    ).astype(BF)
    return result, dx, back, gated, dgp, dup


def moe_kernel(
    n_e,
    n_z,
    cap,
    tok_ref,
    pick_ref,
    unpick_ref,
    near_ref,
    far_ref,
    wg_ref,
    wu_ref,
    wd_ref,
    xs_ref,
    r_ref,
    dx_ref,
    ret_ref,
    part_ref,
    gi_ref,
    dg_ref,
    du_ref,
    gg_ref,
    gu_ref,
    gd_ref,
    rret_ref,
    zbuf,
    z_send,
    z_recv,
    r_send,
    r_recv,
    r_own,
    in_sem,
    out_sem,
    b_send,
    b_recv,
    b_own,
    p_send,
    p_recv,
    p_own,
    e_send,
    e_recv,
    g_sem,
    t_sem,
    w_sem,
):
    e, z = place()
    me = e * n_z + z
    width = far_ref.shape[-1]
    hidden = wd_ref.shape[0]
    experts = n_e * n_z
    columns = tok_ref.shape[-1]
    last = n_z - 1
    inner = (z > 0) & (z < last)
    greet(n_e, n_z, True)
    chain = (lambda s: zbuf.at[s], z_send, z_recv)
    chain_start(n_z, tok_ref, *chain)

    def source(k):
        return jnp.where(k == 0, z, ranked(z, k, n_z))

    def give_one(k, i):
        sz, oe = source(k), lax.rem(e + i, n_e)
        return remote(
            dx_ref.at[sz, oe],
            ret_ref.at[sz, e],
            b_send.at[k, i],
            b_recv.at[sz, e],
            (oe, z),
        )

    def give_own(k):
        sz = source(k)
        return pltpu.make_async_copy(dx_ref.at[sz, e], ret_ref.at[sz, e], b_own.at[k])

    def give(k):
        for i in range(1, n_e):
            give_one(k, i).start()
        give_own(k).start()

    def store(k, tiles, i):
        src, dst = tiles[i]
        return pltpu.make_async_copy(src, dst.at[source(k)], out_sem.at[i])

    def first_phase(rows, xt, yt, rt, dxt, git, dgt, dut):
        out_args = (xs_ref, r_own, r_send, r_recv)
        rows_out(n_e, cap, 0, z, tok_ref, pick_ref, rows, *out_args)
        tiles = ((dxt, dx_ref), (rt, r_ref), (git, gi_ref), (dgt, dg_ref), (dut, du_ref))

        def load_y(src):
            return pltpu.make_async_copy(src, yt, in_sem.at[1])

        @pl.loop(0, n_z)
        def _(k):
            sz = source(k)

            @pl.when(k == 0)
            def _():
                load_y(near_ref).start()

            @pl.when(k > 0)
            def _():
                load_y(far_ref.at[sz]).start()

            @pl.when(jnp.where(inner, k == 0, k < last))
            def _():
                chain_take(n_z, k + 1, *chain)

            @pl.when(inner & (k + 2 < n_z))
            def _():
                chain_take(n_z, k + 2, *chain)

            @pl.when(k < last)
            def _():
                nz = source(k + 1)
                rows_out(n_e, cap, k + 1, nz, zbuf.at[nz], pick_ref, rows, *out_args)

            rows_out_wait(n_e, cap, k, sz, rows, *out_args)
            fetch = pltpu.make_async_copy(xs_ref.at[sz], xt, in_sem.at[0])
            fetch.start()
            fetch.wait()
            load_y(far_ref.at[sz]).wait()

            @pl.when((k > 0) & (k < last))
            def _():
                store(k, tiles, 0).wait()

            @pl.when(k > 0)
            def _():
                for i in range(1, 5):
                    store(k, tiles, i).wait()

            result, dx, back, gated, dgp, dup = expert_tile(
                width,
                experts,
                me,
                xt[...].reshape(n_e * cap, -1),
                yt[...].reshape(n_e * cap, -1),
                wg_ref,
                wu_ref,
                wd_ref,
            )
            rt[...] = result.reshape(n_e, cap, -1)
            dxt[:, :, :width] = dx.reshape(n_e, cap, -1)
            dxt[:, :, width:] = back.reshape(n_e, cap, -1)
            git[...] = gated.reshape(n_e, cap, -1)
            dgt[...] = dgp.reshape(n_e, cap, -1)
            dut[...] = dup.reshape(n_e, cap, -1)
            for i in range(5):
                store(k, tiles, i).start()

            @pl.when(k >= last - 1)
            def _():
                store(k, tiles, 0).wait()
                give(k)

        for i in range(1, 5):
            store(last, tiles, i).wait()

    def row_buffer(c):
        return pltpu.VMEM((n_e, cap, c), BF)

    pl.run_scoped(
        first_phase,
        pltpu.VMEM((n_z, n_e * cap, columns), BF),
        row_buffer(columns),
        row_buffer(width),
        row_buffer(width),
        row_buffer(columns),
        row_buffer(hidden),
        row_buffer(hidden),
        row_buffer(hidden),
    )
    chain_end(n_z, tok_ref, *chain)

    give(1)
    far_z = source(last)

    def give_result(i):
        oe = lax.rem(e + i, n_e)
        return remote(
            r_ref.at[far_z, oe], rret_ref.at[e], e_send.at[i], e_recv.at[e], (oe, z)
        )

    for i in range(1, n_e):
        give_result(i).start()
    own_result = pltpu.make_async_copy(r_ref.at[far_z, e], rret_ref.at[e], in_sem.at[0])
    own_result.start()
    give(0)
    size = 256
    count = width // size

    def second_phase(gis, dgs, dus, xc, yc, ggt, gut, gdt, rbuf):
        whole = ((gi_ref, gis), (dg_ref, dgs), (du_ref, dus))
        for i, (src, dst) in enumerate(whole):
            pltpu.make_async_copy(src, dst, g_sem.at[i]).start()

        def pairs(t):
            at = pl.ds(pl.multiple_of(t * size, size), size)
            slot = lax.rem(t, 2)
            copies = [
                pltpu.make_async_copy(xs_ref.at[:, :, :, at], xc.at[slot], t_sem.at[0, slot])
            ]
            for k in range(n_z):
                src = far_ref.at[source(k), :, :, at] if k else near_ref.at[:, :, at]
                copies.append(
                    pltpu.make_async_copy(
                        src, yc.at[slot, source(k)], t_sem.at[1 + k, slot]
                    )
                )
            return copies

        def results(t):
            at = pl.ds(pl.multiple_of(t * size, size), size)
            slot = lax.rem(t, 2)
            return [
                pltpu.make_async_copy(ggt.at[slot], gg_ref.at[at], w_sem.at[0, slot]),
                pltpu.make_async_copy(gut.at[slot], gu_ref.at[at], w_sem.at[1, slot]),
                pltpu.make_async_copy(gdt.at[slot], gd_ref.at[:, at], w_sem.at[2, slot]),
            ]

        def weight_tile(t):
            slot = lax.rem(t, 2)

            @pl.when(t + 1 < count)
            def _():
                for copy in pairs(t + 1):
                    copy.start()

            for copy in pairs(t):
                copy.wait()

            @pl.when(t >= 2)
            def _():
                for copy in results(t):
                    copy.wait()

            total = n_z * n_e * cap
            x = xc[slot].reshape(total, size)
            ggt[slot] = dot_first(x, dgs[...].reshape(total, hidden)).astype(BF)
            gut[slot] = dot_first(x, dus[...].reshape(total, hidden)).astype(BF)
            gdt[slot] = dot_first(
                gis[...].reshape(total, hidden), yc[slot].reshape(total, size)
            ).astype(BF)
            for copy in results(t):
                copy.start()

        def combine(k):
            sz = source(k)
            for i in range(1, n_e):
                oe = lax.rem(e + i, n_e)
                remote(
                    dx_ref.at[sz, oe],
                    ret_ref.at[sz, oe],
                    b_send.at[k, i],
                    b_recv.at[sz, oe],
                    (oe, z),
                ).wait()
            give_own(k).wait()
            unpick = unpick_ref[sz]
            cuts = pieces(columns)

            def fetch(p):
                start, wide = cuts[p]
                return pltpu.make_async_copy(
                    ret_ref.at[sz, :, :, start : start + wide],
                    rbuf.at[p % 2, :, :, 0:wide],
                    in_sem.at[1 + p % 2],
                )

            fetch(0).start()
            for p, (start, wide) in enumerate(cuts):
                if p + 1 < len(cuts):
                    fetch(p + 1).start()
                fetch(p).wait()
                block = rbuf[p % 2, :, :, 0:wide].reshape(n_e * cap, wide)
                zbuf[k, :, start : start + wide] = dot(unpick, block).astype(BF)

            @pl.when(k > 0)
            def _():
                remote(
                    zbuf.at[k], part_ref.at[z], p_send.at[k], p_recv.at[z], (e, sz)
                ).start()

            @pl.when(k == 0)
            def _():
                pltpu.make_async_copy(zbuf.at[k], part_ref.at[z], p_own).start()

        for copy in pairs(0):
            copy.start()
        for i, (src, dst) in enumerate(whole):
            pltpu.make_async_copy(src, dst, g_sem.at[i]).wait()
        share_of = count // n_z

        @pl.loop(0, n_z)
        def _(i):
            @pl.loop(0, share_of)
            def _(t):
                weight_tile(i * share_of + t)

            k = jnp.where(i == 0, last - 1, jnp.where(i == 1, last, last - i))
            combine(k)

        for t in (count - 2, count - 1):
            for copy in results(t):
                copy.wait()

    total_shape = (n_z, n_e, cap)
    pl.run_scoped(
        second_phase,
        pltpu.VMEM(total_shape + (hidden,), BF),
        pltpu.VMEM(total_shape + (hidden,), BF),
        pltpu.VMEM(total_shape + (hidden,), BF),
        pltpu.VMEM((2,) + total_shape + (size,), BF),
        pltpu.VMEM((2,) + total_shape + (size,), BF),
        pltpu.VMEM((2, size, hidden), BF),
        pltpu.VMEM((2, size, hidden), BF),
        pltpu.VMEM((2, hidden, size), BF),
        pltpu.VMEM((2, n_e, cap, pieces(columns)[0][1]), BF),
    )
    for i in range(1, n_e):
        oe = lax.rem(e + i, n_e)
        remote(
            r_ref.at[far_z, oe], rret_ref.at[oe], e_send.at[i], e_recv.at[oe], (oe, z)
        ).wait()
    own_result.wait()
    pltpu.make_async_copy(zbuf.at[0], part_ref.at[z], p_own).wait()
    for k in range(1, n_z):
        sz = ranked(z, k, n_z)
        remote(
            zbuf.at[k], part_ref.at[sz], p_send.at[k], p_recv.at[sz], (e, sz)
        ).wait()


def moe(n_e, n_z, cap, tok, picks, unpicks, dy_near, dy_far, wg, wu, wd):
    count, columns = tok.shape
    width, hidden = wg.shape

    def rows_of(c):
        return jax.ShapeDtypeStruct((n_z, n_e, cap, c), BF)

    return pl.pallas_call(
        partial(moe_kernel, n_e, n_z, cap),
        out_shape=(
            rows_of(columns),
            rows_of(width),
            rows_of(columns),
            rows_of(columns),
            jax.ShapeDtypeStruct((n_z, count, columns), BF),
            rows_of(hidden),
            rows_of(hidden),
            rows_of(hidden),
            jax.ShapeDtypeStruct((width, hidden), BF),
            jax.ShapeDtypeStruct((width, hidden), BF),
            jax.ShapeDtypeStruct((hidden, width), BF),
            jax.ShapeDtypeStruct((n_e, cap, width), BF),
        ),
        in_specs=[VM, VM, VM, ANY, ANY, VM, VM, VM],
        out_specs=(ANY,) * 12,
        scratch_shapes=[
            pltpu.VMEM((n_z, count, columns), BF),
            DMA((n_z + 1,)),
            DMA((n_z,)),
            DMA((n_z, n_e)),
            DMA((n_z, n_e)),
            DMA((n_z,)),
            DMA((3,)),
            DMA((5,)),
            DMA((n_z, n_e)),
            DMA((n_z, n_e)),
            DMA((n_z,)),
            DMA((n_z,)),
            DMA((n_z,)),
            DMA,
            DMA((n_e,)),
            DMA((n_e,)),
            DMA((3,)),
            DMA((1 + n_z, 2)),
            DMA((3, 2)),
        ],
        compiler_params=pltpu.CompilerParams(
            collective_id=13, has_side_effects=True, vmem_limit_bytes=63 * 1024 * 1024
        ),
        name="moe",
    )(tok, picks, unpicks, dy_near, dy_far, wg, wu, wd)


def layout(lengths, owners, device, row_count):
    seq_order = jnp.arange(lengths.shape[0], dtype=jnp.int32)
    owned = (owners == device).astype(jnp.int32)
    earlier = (seq_order[None, :] < seq_order[:, None]).astype(jnp.int32)
    starts = jnp.sum(earlier * (owned * lengths)[None, :], axis=1)
    row_index = jnp.arange(row_count, dtype=jnp.int32)
    inside = (
        owned[None, :]
        * (row_index[:, None] >= starts[None, :]).astype(jnp.int32)
        * (row_index[:, None] < (starts + lengths)[None, :]).astype(jnp.int32)
    )
    live_rows = jnp.sum(inside, axis=1)
    segment = jnp.sum(inside * (seq_order[None, :] + 1), axis=1) - 1
    token_position = jnp.sum(inside * (row_index[:, None] - starts[None, :]), axis=1)
    return (live_rows, segment, token_position)


def named_experts(routes, experts):
    return jnp.any(routes[..., None] == jnp.arange(experts, dtype=jnp.int32), axis=-2)


def slot_picks(n_e, n_z, z, cap, named, live):
    sources, count, experts = named.shape
    used = named & (live[:, :, None] > 0)
    order = jnp.arange(count)
    lower = (order[None, :] < order[:, None]).astype(BF)
    slots = jnp.einsum("ts,zse->zte", lower, used.astype(BF), preferred_element_type=F32)
    slots = jnp.where(used, slots, -1.0)
    column = jnp.arange(n_e * cap, dtype=jnp.int32)
    spread = (
        jnp.arange(experts, dtype=jnp.int32)[:, None] == (column // cap * n_z + z)[None, :]
    ).astype(BF)
    slots = slots.astype(BF)
    slot_ids = lax.rem(column, cap).astype(F32)
    picks = jnp.einsum("ec,ste->sct", spread, slots, preferred_element_type=F32)
    unpicks = jnp.einsum("ste,ec->stc", slots, spread, preferred_element_type=F32)
    return (
        (picks == slot_ids[None, :, None]).astype(BF),
        (unpicks == slot_ids).astype(BF),
    )


def split_float(values):
    high = values.astype(BF)
    return high, (values - high.astype(F32)).astype(BF)


def pad_lanes(values, lanes):
    return jnp.pad(values, ((0, 0), (0, lanes - values.shape[1])))


def local(
    n_e,
    n_z,
    tokens,
    cotangent,
    lengths,
    owners,
    routes,
    w_query,
    key_weight,
    value_weight,
    w_out,
    w_router,
    norm_gains,
    w_gate,
    w_up,
    w_down,
):
    n = n_e * n_z
    count, width = tokens.shape
    shard = w_query.shape[0]
    experts, top = w_router.shape[1], routes.shape[1]
    q_heads, kv_heads = w_query.shape[1] // HEAD, key_weight.shape[1] // HEAD
    heads = q_heads // n_e
    cap = count * top * 5 // (4 * experts)
    cap = -(-cap // 16) * 16
    e, z = place()

    wq_blocks = w_query.reshape(shard, n_e, heads * HEAD)
    sharing = n_e // kv_heads
    wk_blocks = jnp.repeat(key_weight.reshape(shard, kv_heads, HEAD), sharing, axis=1)
    wv_blocks = jnp.repeat(value_weight.reshape(shard, kv_heads, HEAD), sharing, axis=1)
    w_blocks = jnp.concatenate([wq_blocks, wk_blocks, wv_blocks], axis=2).transpose(1, 0, 2)
    router_rows = shard * experts // 128
    gain_rows = -(-norm_gains.shape[0] // 128)
    misc_rows = -(-(router_rows + gain_rows) // 16) * 16
    misc = jnp.concatenate(
        [
            w_router.reshape(-1),
            norm_gains,
            jnp.zeros((misc_rows - router_rows) * 128 - norm_gains.shape[0], BF),
        ]
    ).reshape(misc_rows, 128)
    routes_flat = routes.reshape(-1, 128)

    device = e * n_z + z
    plane_ids = jnp.arange(n_e, dtype=jnp.int32) * n_z + z
    column_ids = e * n_z + jnp.arange(n_z, dtype=jnp.int32)
    live_both, segment, position = jax.vmap(lambda d: layout(lengths, owners, d, count))(
        jnp.concatenate([plane_ids, column_ids])
    )
    live_all = live_both[n_e:]
    live_own = lax.dynamic_index_in_dim(live_all, z, keepdims=False)
    named_own = named_experts(routes, experts)
    small = n_e == 8 and n_z == 4
    if small:
        pick_own = slot_picks(n_e, n_z, z, cap, named_own[None], live_own[None])[0][0]
        xs, rts, w_all, wo_all, misc_all, dy_near = open_layer(
            n_e, n_z, cap, tokens, cotangent, routes_flat, w_blocks, w_out, misc, pick_own
        )
    else:
        xs, cts, rts, w_all, wo_all, misc_all = share(
            n_e, n_z, tokens, cotangent, routes_flat, w_blocks, w_out, misc
        )
    w_all = w_all.reshape(n * shard, -1)
    wo_all = wo_all.reshape(-1, width)
    router_w = misc_all[:, :router_rows].reshape(n * shard, experts)
    gains = (
        misc_all[:, router_rows:]
        .reshape(n, -1)[:, : norm_gains.shape[0]]
        .reshape(-1)
        .astype(F32)
    )
    gain_one = gains[None, :width]
    gain_two = gains[None, width : 2 * width]
    gain_heads = jnp.pad(gains[2 * width :].reshape(2, HEAD), ((0, 6), (0, 0)))

    half = HEAD // 2
    frequency = jnp.power(1000000.0, -2.0 * jnp.arange(half, dtype=F32) / HEAD)
    angles = position[:n_e].astype(F32)[:, :, None] * frequency
    turn_table = jnp.concatenate([jnp.cos(angles), jnp.sin(angles)], axis=-1)
    seg = segment[:n_e].astype(F32)[:, None, :]

    named_all = named_experts(rts.reshape(n_z, count, top), experts)
    picks, unpicks = slot_picks(n_e, n_z, z, cap, named_all, live_all)
    live = live_own.astype(F32)[:, None]
    named = named_own.astype(F32)

    shape = (turn_table, seg, w_all, wo_all, gain_one, gain_heads)
    if small:
        n1, raw, value, mix, attn_rows, dy_far = front(
            n_e, n_z, cap, heads, xs, cotangent, picks, *shape
        )
    else:
        dy_rows = send_rows(n_e, n_z, cap, cts, picks)
        n1, raw, value, mix, part = attend(n_e, heads, xs, *shape)
        attn_rows = plane_sum(n_e, n_z, part)

    inputs = tokens.astype(F32)
    hidden = inputs + live * attn_rows
    r_two = lax.rsqrt(jnp.mean(hidden * hidden, axis=-1, keepdims=True) + EPSILON)
    nu_two = hidden * r_two
    n2 = (nu_two * gain_two).astype(BF)
    logits = dot(n2, router_w)
    probs = jax.nn.softmax(logits, axis=-1)
    chosen = probs * named
    chosen_sum = jnp.sum(chosen, axis=1, keepdims=True)
    gates = chosen / chosen_sum
    lanes = -(-2 * experts // 128) * 128
    extra = pad_lanes(jnp.concatenate(split_float(gates), axis=1), lanes)
    tok = jnp.concatenate([n2, extra], axis=1)
    experts_w = (w_gate[0], w_up[0], w_down[0])
    if small:
        moved = moe(n_e, n_z, cap, tok, picks, unpicks, dy_near, dy_far, *experts_w)
        r_rows, dx_back = moved[1], moved[4]
        grad_gate, grad_up, grad_down = (a.astype(F32) for a in moved[8:11])
        r_far = moved[11]
    else:
        x_rows = dispatch(n_e, n_z, cap, tok, picks)
        r_rows, dx_rows, grad_gate, grad_up, grad_down = expert_run(
            n_z,
            experts,
            x_rows.reshape(-1, width + lanes),
            dy_rows.reshape(-1, width),
            *experts_w,
        )
        r_rows = r_rows.reshape(dy_rows.shape)
        dx_back = give_back(n_e, n_z, cap, dx_rows.reshape(x_rows.shape), unpicks, 6)

    dx_sum = jnp.sum(dx_back.astype(F32), axis=0)
    dgates = dx_sum[:, width : width + experts] + dx_sum[:, width + experts : width + 2 * experts]
    dchosen = (
        named * (dgates - jnp.sum(dgates * gates, axis=1, keepdims=True)) / chosen_sum
    )
    dlogits = (probs * (dchosen - jnp.sum(probs * dchosen, axis=1, keepdims=True))).astype(BF)
    grad_router = dot_first(n2, dlogits)
    dn2 = dx_sum[:, :width] + dot_last(dlogits, router_w)
    upstream = cotangent.astype(F32)
    grad_gain_two = jnp.sum(dn2 * nu_two, axis=0)
    scaled = dn2 * gain_two
    dhidden = upstream + r_two * (
        scaled - nu_two * jnp.mean(scaled * nu_two, axis=-1, keepdims=True)
    )
    da = (live * dhidden).astype(BF)
    gain_size = norm_gains.shape[0]
    grad_router = grad_router.reshape(n, router_rows, 128)
    if small:
        dn1, r_back, gws, goo, gor, gol, grs, gvs, *_ = back(
            n_e,
            n_z,
            cap,
            heads,
            da,
            r_rows,
            r_far,
            grad_router,
            n1,
            raw,
            value,
            mix,
            unpicks,
            grad_gain_two[None],
            *shape,
        )
        gw_sum = gws.astype(F32).transpose(0, 2, 1, 3).reshape(n_e, shard, -1)
        lower_sum, upper_sum = (
            jnp.where(came, lax.dynamic_index_in_dim(inbox, z, keepdims=False).astype(F32), 0.0)
            for came, inbox in ((z > 0, gor), (z < n_z - 1, gol))
        )
        grad_out = goo.astype(F32) + lower_sum + upper_sum
        grad_router = jnp.sum(grs, axis=0)
        grad_gains = lax.dynamic_slice_in_dim(
            jnp.sum(gvs, axis=0).reshape(-1), device * gain_size, gain_size
        )
    else:
        r_back = give_back(n_e, n_z, cap, r_rows, unpicks, 7)
        da_all = plane_gather(n_e, n_z, da)
        dn_part, gw, go, g1_part, gh_part = attend_back(
            n_e,
            heads,
            da_all,
            n1,
            raw,
            value,
            mix,
            turn_table,
            seg,
            w_all,
            wo_all,
            gain_heads,
        )
        gain_all = jnp.concatenate(
            [(g1_part / gain_one)[0], grad_gain_two, gh_part[0], gh_part[1]]
        ).reshape(n, -1)
        grad_rows = -(-(router_rows + gain_rows) // 8) * 8
        gain_all = pad_lanes(gain_all, (grad_rows - router_rows) * 128)
        gm = jnp.concatenate([grad_router, gain_all.reshape(n, -1, 128)], axis=1)
        dn1, gws, gos, gms = finish(
            n_e,
            n_z,
            dn_part,
            gw.reshape(n, shard, -1),
            go.reshape(n_z, -1, width),
            gm,
        )
        gw_sum = jnp.sum(gws.reshape(n_e, n_z, shard, -1).astype(F32), axis=1)
        grad_out = jnp.sum(gos.astype(F32), axis=0)
        gm_sum = jnp.sum(gms, axis=0)
        grad_router = gm_sum[:router_rows]
        grad_gains = gm_sum[router_rows:].reshape(-1)[:gain_size]
    block_out = (hidden + jnp.sum(r_back.astype(F32), axis=0)).astype(BF)
    r_one = lax.rsqrt(jnp.mean(inputs * inputs, axis=-1, keepdims=True) + EPSILON)
    nu_one = inputs * r_one
    scaled = dn1 * gain_one
    grad_tokens = dhidden + r_one * (
        scaled - nu_one * jnp.mean(scaled * nu_one, axis=-1, keepdims=True)
    )
    q_size = heads * HEAD
    grad_query = gw_sum[:, :, :q_size].transpose(1, 0, 2).reshape(shard, -1)
    kv_sum = gw_sum[:, :, q_size:].reshape(kv_heads, -1, shard, 2 * HEAD).sum(axis=1)
    grad_key = kv_sum[:, :, :HEAD].transpose(1, 0, 2).reshape(shard, -1)
    grad_value = kv_sum[:, :, HEAD:].transpose(1, 0, 2).reshape(shard, -1)
    return (
        block_out,
        grad_tokens,
        grad_query,
        grad_key,
        grad_value,
        grad_out,
        grad_router.reshape(shard, experts),
        grad_gains,
        grad_gate[None],
        grad_up[None],
        grad_down[None],
    )


def solution(mesh):
    both = ("expert", "fsdp")
    two, three = P(both, None), P(both, None, None)
    return jax.shard_map(
        partial(local, mesh.shape["expert"], mesh.shape["fsdp"]),
        mesh=mesh,
        in_specs=(two, two, P(), P(), two) + (two,) * 5 + (P(both),) + (three,) * 3,
        out_specs=(two,) * 7 + (P(both),) + (three,) * 3,
        check_vma=False,
    )
```

```python
from functools import partial

import jax
import jax.numpy as jnp
from jax import lax
from jax.experimental import pallas as pl
from jax.experimental.pallas import tpu as pltpu
from jax.sharding import PartitionSpec as P

EPSILON = 1e-06
MESH = pl.DeviceIdType.MESH
BF = jnp.bfloat16
F32 = jnp.float32
HEAD = 128
ANY = pl.BlockSpec(memory_space=pl.ANY)
VM = pl.BlockSpec(memory_space=pltpu.VMEM)
DMA = pltpu.SemaphoreType.DMA
BIG = 60 * 1024 * 1024


def dot(a, b):
    return lax.dot_general(a, b, (((1,), (0,)), ((), ())), preferred_element_type=F32)


def dot_last(a, b):
    return lax.dot_general(a, b, (((1,), (1,)), ((), ())), preferred_element_type=F32)


def dot_first(a, b):
    return lax.dot_general(a, b, (((0,), (0,)), ((), ())), preferred_element_type=F32)


def place():
    return lax.axis_index("expert"), lax.axis_index("fsdp")


def remote(src, dst, send, recv, where):
    return pltpu.make_async_remote_copy(
        src_ref=src,
        dst_ref=dst,
        send_sem=send,
        recv_sem=recv,
        device_id=where,
        device_id_type=MESH,
    )


def near(z, k, n_z):
    sign = 1 - 2 * (z // (n_z // 2))
    return lax.rem(z + sign * k + n_z, n_z)


def greet_all(n_e, n_z):
    e, z = place()
    me, n = e * n_z + z, n_e * n_z
    barrier = pltpu.get_barrier_semaphore()

    @pl.loop(1, n)
    def _(k):
        other = lax.rem(me + k, n)
        pl.semaphore_signal(
            barrier,
            inc=1,
            device_id=(other // n_z, lax.rem(other, n_z)),
            device_id_type=MESH,
        )

    pl.semaphore_wait(barrier, n - 1)


def greet(n_e, n_z, along_z):
    e, z = place()
    barrier = pltpu.get_barrier_semaphore()
    for k in range(1, n_e):
        pl.semaphore_signal(
            barrier, inc=1, device_id=(lax.rem(e + k, n_e), z), device_id_type=MESH
        )
    count = n_e - 1
    if along_z:
        for k in range(1, n_z):
            pl.semaphore_signal(
                barrier, inc=1, device_id=(e, lax.rem(z + k, n_z)), device_id_type=MESH
            )
        count += n_z - 1
    pl.semaphore_wait(barrier, count)


def ranked(z, k, n_z):
    half = n_z // 2
    top = z // half
    low = z + top * (n_z - 1 - 2 * z)
    at = k - low * jnp.where(k == 1, 1, 0)
    return at + top * (n_z - 1 - 2 * at)


def partner_chip(chip, k):
    low = lax.rem(lax.rem(chip, 2) + lax.rem(k, 2), 2)
    high = lax.rem(chip // 2 + k // 2, 2)
    return 2 * high + low


def chain_start(n_z, src, dst_at, send, recv):
    e, z = place()

    @pl.when(z + 1 < n_z)
    def _():
        remote(src, dst_at(z), send.at[0], recv.at[z], (e, z + 1)).start()

    @pl.when(z > 0)
    def _():
        remote(src, dst_at(z), send.at[1], recv.at[z], (e, z - 1)).start()


def chain_take(n_z, k, dst_at, send, recv):
    e, z = place()
    sz = ranked(z, k, n_z)
    block = dst_at(sz)
    step = jnp.where(sz < z, 1, -1)
    remote(block, block, send.at[1 + k], recv.at[sz], (e, sz)).wait_recv()

    @pl.when((z + step >= 0) & (z + step < n_z))
    def _():
        remote(block, block, send.at[1 + k], recv.at[sz], (e, z + step)).start()

    return sz


def chain_end(n_z, src, dst_at, send, recv):
    e, z = place()

    @pl.when(z + 1 < n_z)
    def _():
        remote(src, dst_at(z), send.at[0], recv.at[z], (e, z + 1)).wait_send()

    @pl.when(z > 0)
    def _():
        remote(src, dst_at(z), send.at[1], recv.at[z], (e, z - 1)).wait_send()

    for k in range(1, n_z):
        sz = ranked(z, k, n_z)
        step = jnp.where(sz < z, 1, -1)

        @pl.when((z + step >= 0) & (z + step < n_z))
        def _(k=k, sz=sz, step=step):
            block = dst_at(sz)
            remote(block, block, send.at[1 + k], recv.at[sz], (e, z + step)).wait_send()


def plane_gather_start(n_e, x_ref, out_ref, own, send, recv, sib_send, sib_recv):
    e, z = place()
    nc, chip, core = n_e // 2, e // 2, lax.rem(e, 2)
    pltpu.make_async_copy(x_ref, out_ref.at[e], own).start()
    for k in range(1, nc):
        j = lax.rem(chip + k, nc)
        remote(
            x_ref, out_ref.at[e], send.at[k], recv.at[chip], (2 * j + core, z)
        ).start()
    remote(
        x_ref, out_ref.at[e], sib_send.at[0], sib_recv.at[chip], (2 * chip + 1 - core, z)
    ).start()


def plane_gather_end(n_e, x_ref, out_ref, own, send, recv, sib_send, sib_recv):
    e, z = place()
    nc, chip, core = n_e // 2, e // 2, lax.rem(e, 2)
    sib = (2 * chip + 1 - core, z)
    for k in range(1, nc):
        j = lax.rem(chip + nc - k, nc)
        block = out_ref.at[2 * j + core]
        remote(x_ref, block, send.at[k], recv.at[j], (2 * j + core, z)).wait()
        remote(block, block, sib_send.at[k], sib_recv.at[j], sib).start()
    for k in range(nc):
        j = lax.rem(chip + nc - k, nc)
        block = out_ref.at[2 * j + 1 - core]
        remote(x_ref, block, sib_send.at[k], sib_recv.at[j], sib).wait()
    pltpu.make_async_copy(x_ref, out_ref.at[e], own).wait()


def share_kernel(
    n_e,
    n_z,
    x_ref,
    ct_ref,
    rt_ref,
    wq_ref,
    wo_ref,
    mi_ref,
    xs_ref,
    cts_ref,
    rts_ref,
    wqs_ref,
    wos_ref,
    mis_ref,
    own,
    x_send,
    x_recv,
    sib_send,
    sib_recv,
    z_send,
    z_recv,
    a_send,
    a_recv,
):
    e, z = place()
    n, me = n_e * n_z, e * n_z + z
    greet_all(n_e, n_z)
    gather = (n_e, x_ref, xs_ref, own.at[0], x_send, x_recv, sib_send, sib_recv)
    plane_gather_start(*gather)

    def other_of(k):
        other = lax.rem(me + k, n)
        return other, other // n_z, lax.rem(other, n_z)

    @pl.loop(1, n)
    def _(k):
        other, oe, oz = other_of(k)
        remote(
            wq_ref.at[oe], wqs_ref.at[me], a_send.at[0, k], a_recv.at[0, me], (oe, oz)
        ).start()
        remote(
            mi_ref, mis_ref.at[me], a_send.at[1, k], a_recv.at[1, me], (oe, oz)
        ).start()

    along = ((rt_ref, rts_ref), (wo_ref, wos_ref), (ct_ref, cts_ref))
    for i, (src, dst) in enumerate(along):
        for k in range(1, n_z):
            oz = near(z, k, n_z)
            remote(src, dst.at[z], z_send.at[i, k], z_recv.at[i, z], (e, oz)).start()
        pltpu.make_async_copy(src, dst.at[z], own.at[1 + i]).start()
    pltpu.make_async_copy(wq_ref.at[e], wqs_ref.at[me], own.at[4]).start()
    pltpu.make_async_copy(mi_ref, mis_ref.at[me], own.at[5]).start()

    plane_gather_end(*gather)

    @pl.loop(1, n)
    def _(k):
        other, oe, oz = other_of(k)
        remote(
            wq_ref.at[oe],
            wqs_ref.at[other],
            a_send.at[0, k],
            a_recv.at[0, other],
            (oe, oz),
        ).wait()
        remote(
            mi_ref, mis_ref.at[other], a_send.at[1, k], a_recv.at[1, other], (oe, oz)
        ).wait()

    for i, (src, dst) in enumerate(along):
        for k in range(1, n_z):
            oz = near(z, k, n_z)
            remote(src, dst.at[oz], z_send.at[i, k], z_recv.at[i, oz], (e, oz)).wait()
        pltpu.make_async_copy(src, dst.at[z], own.at[1 + i]).wait()
    pltpu.make_async_copy(wq_ref.at[e], wqs_ref.at[me], own.at[4]).wait()
    pltpu.make_async_copy(mi_ref, mis_ref.at[me], own.at[5]).wait()


def share(n_e, n_z, tokens, cotangent, routes, wq, wo, misc):
    n, nc = n_e * n_z, n_e // 2

    def like(lead, a):
        return jax.ShapeDtypeStruct((lead,) + a.shape, a.dtype)

    return pl.pallas_call(
        partial(share_kernel, n_e, n_z),
        out_shape=(
            like(n_e, tokens),
            like(n_z, cotangent),
            like(n_z, routes),
            like(n, wq[0]),
            like(n_z, wo),
            like(n, misc),
        ),
        in_specs=[ANY] * 6,
        out_specs=(ANY,) * 6,
        scratch_shapes=[
            DMA((6,)),
            DMA((nc,)),
            DMA((nc,)),
            DMA((nc,)),
            DMA((nc,)),
            DMA((3, n_z)),
            DMA((3, n_z)),
            DMA((2, n)),
            DMA((2, n)),
        ],
        compiler_params=pltpu.CompilerParams(collective_id=1, has_side_effects=True),
        name="share",
    )(tokens, cotangent, routes, wq, wo, misc)


def plane_sum_body(
    n_e, part_ref, total_ref, mine, sib, far, own, send, recv, sib_send, sib_recv
):
    e, z = place()
    nc, chip, core = n_e // 2, e // 2, lax.rem(e, 2)
    rows = total_ref.shape[0]
    step = 32
    other = (2 * chip + 1 - core, z)
    for k in range(nc):
        j = lax.rem(chip + 1 + k, nc)
        remote(
            part_ref.at[2 * j + 1 - core],
            sib.at[j],
            sib_send.at[j],
            sib_recv.at[j],
            other,
        ).start()
        pltpu.make_async_copy(part_ref.at[2 * j + core], mine.at[j], own.at[j]).start()
    for k in range(nc):
        j = lax.rem(chip + 1 + k, nc)
        remote(
            part_ref.at[2 * j + 1 - core],
            sib.at[j],
            sib_send.at[j],
            sib_recv.at[j],
            other,
        ).wait()
        pltpu.make_async_copy(part_ref.at[2 * j + core], mine.at[j], own.at[j]).wait()
        if k < nc - 1:

            @pl.loop(0, rows, step=step)
            def _(r, j=j):
                at = pl.ds(pl.multiple_of(r, step), step)
                mine[j, at, :] = (
                    mine[j, at, :].astype(F32) + sib[j, at, :].astype(F32)
                ).astype(BF)

            remote(
                mine.at[j], far.at[chip], send.at[j], recv.at[chip], (2 * j + core, z)
            ).start()
        else:

            @pl.loop(0, rows, step=step)
            def _(r, j=j):
                at = pl.ds(pl.multiple_of(r, step), step)
                total_ref[at, :] = mine[j, at, :].astype(F32) + sib[j, at, :].astype(F32)

    for k in range(1, nc):
        j = lax.rem(chip + nc - k, nc)
        remote(
            mine.at[j], far.at[j], send.at[j], recv.at[j], (2 * j + core, z)
        ).wait()

        @pl.loop(0, rows, step=step)
        def _(r, j=j):
            at = pl.ds(pl.multiple_of(r, step), step)
            total_ref[at, :] += far[j, at, :].astype(F32)


def plane_sum_scratch(n_e, part):
    nc = n_e // 2
    block = (nc,) + part.shape[1:]
    return [pltpu.VMEM(block, BF)] * 3 + [DMA((nc,))] * 5


def plane_sum_kernel(n_e, n_z, part_ref, total_ref, *scratch):
    greet(n_e, n_z, False)
    plane_sum_body(n_e, part_ref, total_ref, *scratch)


def plane_sum(n_e, n_z, part):
    return pl.pallas_call(
        partial(plane_sum_kernel, n_e, n_z),
        out_shape=jax.ShapeDtypeStruct(part.shape[1:], F32),
        in_specs=[ANY],
        out_specs=VM,
        scratch_shapes=plane_sum_scratch(n_e, part),
        compiler_params=pltpu.CompilerParams(
            collective_id=2, has_side_effects=True, vmem_limit_bytes=BIG
        ),
        name="plane_sum",
    )(part)


def plane_gather_kernel(n_e, n_z, x_ref, out_ref, *sems):
    greet(n_e, n_z, False)
    plane_gather_start(n_e, x_ref, out_ref, *sems)
    plane_gather_end(n_e, x_ref, out_ref, *sems)


def plane_gather(n_e, n_z, x):
    nc = n_e // 2
    return pl.pallas_call(
        partial(plane_gather_kernel, n_e, n_z),
        out_shape=jax.ShapeDtypeStruct((n_e,) + x.shape, x.dtype),
        in_specs=[ANY],
        out_specs=ANY,
        scratch_shapes=[DMA] + [DMA((nc,))] * 4,
        compiler_params=pltpu.CompilerParams(collective_id=3, has_side_effects=True),
        name="plane_gather",
    )(x)


def pieces(columns, wide=512):
    cuts = list(range(0, columns - columns % wide, wide)) + [columns - columns % wide]
    spans = [(a, b - a) for a, b in zip(cuts, cuts[1:])]
    if columns % wide:
        spans.append((cuts[-1], columns % wide))
    return spans


def rows_out(n_e, cap, k, sz, src, d_ref, rows, out_ref, own, send, recv):
    e, z = place()
    pick = d_ref[sz]
    for start, size in pieces(src.shape[-1]):
        rows[k, :, start : start + size] = dot(pick, src[:, start : start + size]).astype(BF)
    for i in range(1, n_e + 1):
        oe = lax.rem(e + i, n_e)
        block = rows.at[k, pl.ds(pl.multiple_of(oe * cap, 16), cap), :]
        if i < n_e:
            remote(block, out_ref.at[sz, e], send.at[k, i], recv.at[sz, e], (oe, z)).start()
        else:
            pltpu.make_async_copy(block, out_ref.at[sz, e], own.at[k]).start()


def rows_out_wait(n_e, cap, k, sz, rows, out_ref, own, send, recv):
    e, z = place()
    for i in range(1, n_e + 1):
        oe = lax.rem(e + i, n_e)
        at = pl.ds(pl.multiple_of(oe * cap, 16), cap)
        block = rows.at[k, at, :]
        if i < n_e:
            remote(
                block, out_ref.at[sz, oe], send.at[k, i], recv.at[sz, oe], (oe, z)
            ).wait()
        else:
            pltpu.make_async_copy(block, out_ref.at[sz, e], own.at[k]).wait()


def open_kernel(
    n_e,
    n_z,
    cap,
    x_ref,
    ct_ref,
    rt_ref,
    wq_ref,
    wo_ref,
    mi_ref,
    pick_ref,
    xs_ref,
    rts_ref,
    wqs_ref,
    wos_ref,
    mis_ref,
    dy_ref,
    rows,
    own,
    x_send,
    x_recv,
    sib_send,
    sib_recv,
    w_send,
    w_recv,
    zw_send,
    zw_recv,
    zo_send,
    zo_recv,
    zr_send,
    zr_recv,
    m_send,
    m_recv,
    r_send,
    r_recv,
):
    e, z = place()
    n, me = n_e * n_z, e * n_z + z
    greet_all(n_e, n_z)

    def plane_peer(i):
        return lax.rem(e + i, n_e)

    for i in range(1, n_e):
        oe = plane_peer(i)
        remote(
            wq_ref.at[oe], wqs_ref.at[e, z], w_send.at[i], w_recv.at[e], (oe, z)
        ).start()
    kept = (
        (wq_ref.at[e], wqs_ref.at[e, z]),
        (wo_ref, wos_ref.at[z]),
        (rt_ref, rts_ref.at[z]),
        (mi_ref, mis_ref.at[me]),
    )
    for i, (src, dst) in enumerate(kept):
        pltpu.make_async_copy(src, dst, own.at[i]).start()
    out_chain = (lambda s: wos_ref.at[s], zo_send, zo_recv)
    chain_start(n_z, wo_ref, *out_chain)
    for k in range(1, n_z):
        oz = near(z, k, n_z)
        remote(rt_ref, rts_ref.at[z], zr_send.at[k], zr_recv.at[z], (e, oz)).start()

    def other_of(k):
        other = lax.rem(me + k, n)
        return other, (other // n_z, lax.rem(other, n_z))

    @pl.loop(1, n)
    def _(k):
        other, where = other_of(k)
        remote(mi_ref, mis_ref.at[me], m_send.at[k], m_recv.at[me], where).start()

    gather = (n_e, x_ref, xs_ref, own.at[4], x_send, x_recv, sib_send, sib_recv)
    plane_gather_start(*gather)
    pick = pick_ref[...]
    for start, size in pieces(ct_ref.shape[-1]):
        rows[:, start : start + size] = dot(pick, ct_ref[:, start : start + size]).astype(BF)
    for i in range(1, n_e + 1):
        oe = plane_peer(i)
        block = rows.at[pl.ds(pl.multiple_of(oe * cap, 16), cap), :]
        if i < n_e:
            remote(block, dy_ref.at[e], r_send.at[i], r_recv.at[e], (oe, z)).start()
        else:
            pltpu.make_async_copy(block, dy_ref.at[e], own.at[5]).start()

    for i in range(1, n_e):
        oe = plane_peer(i)
        remote(
            wq_ref.at[oe], wqs_ref.at[oe, z], w_send.at[i], w_recv.at[oe], (oe, z)
        ).wait()
    pltpu.make_async_copy(*kept[0], own.at[0]).wait()
    in_chain = (lambda s: wqs_ref.at[:, s], zw_send, zw_recv)
    chain_start(n_z, wqs_ref.at[:, z], *in_chain)
    for k in range(1, n_z):
        chain_take(n_z, k, *out_chain)
        chain_take(n_z, k, *in_chain)
        if k == n_z - 2:
            plane_gather_end(*gather)
    chain_end(n_z, wo_ref, *out_chain)
    chain_end(n_z, wqs_ref.at[:, z], *in_chain)
    for k in range(1, n_z):
        oz = near(z, k, n_z)
        remote(rt_ref, rts_ref.at[oz], zr_send.at[k], zr_recv.at[oz], (e, oz)).wait()

    @pl.loop(1, n)
    def _(k):
        other, where = other_of(k)
        remote(mi_ref, mis_ref.at[other], m_send.at[k], m_recv.at[other], where).wait()

    for i in range(1, n_e + 1):
        oe = plane_peer(i)
        block = rows.at[pl.ds(pl.multiple_of(oe * cap, 16), cap), :]
        if i < n_e:
            remote(block, dy_ref.at[oe], r_send.at[i], r_recv.at[oe], (oe, z)).wait()
        else:
            pltpu.make_async_copy(block, dy_ref.at[e], own.at[5]).wait()
    for i, (src, dst) in enumerate(kept):
        if i:
            pltpu.make_async_copy(src, dst, own.at[i]).wait()


def open_layer(n_e, n_z, cap, tokens, cotangent, routes, wq, wo, misc, pick):
    n, nc = n_e * n_z, n_e // 2
    _, shard, columns = wq.shape
    width = tokens.shape[1]

    def like(lead, a):
        return jax.ShapeDtypeStruct((lead,) + a.shape, a.dtype)

    return pl.pallas_call(
        partial(open_kernel, n_e, n_z, cap),
        out_shape=(
            like(n_e, tokens),
            like(n_z, routes),
            jax.ShapeDtypeStruct((n_e, n_z, shard, columns), BF),
            like(n_z, wo),
            like(n, misc),
            jax.ShapeDtypeStruct((n_e, cap, width), BF),
        ),
        in_specs=[ANY, VM] + [ANY] * 4 + [VM],
        out_specs=(ANY,) * 6,
        scratch_shapes=[
            pltpu.VMEM((n_e * cap, width), BF),
            DMA((6,)),
            DMA((nc,)),
            DMA((nc,)),
            DMA((nc,)),
            DMA((nc,)),
            DMA((n_e,)),
            DMA((n_e,)),
            DMA((n_z + 1,)),
            DMA((n_z,)),
            DMA((n_z + 1,)),
            DMA((n_z,)),
            DMA((n_z,)),
            DMA((n_z,)),
            DMA((n,)),
            DMA((n,)),
            DMA((n_e,)),
            DMA((n_e,)),
        ],
        compiler_params=pltpu.CompilerParams(
            collective_id=11, has_side_effects=True, vmem_limit_bytes=BIG
        ),
        name="open_layer",
    )(tokens, cotangent, routes, wq, wo, misc, pick)


def dispatch_kernel(
    n_e,
    n_z,
    cap,
    tok_ref,
    d_ref,
    out_ref,
    zbuf,
    rows,
    own,
    z_send,
    z_recv,
    send,
    recv,
):
    e, z = place()
    greet(n_e, n_z, True)
    chain = (lambda s: zbuf.at[s], z_send, z_recv)
    chain_start(n_z, tok_ref, *chain)
    for k in range(n_z):
        sz = chain_take(n_z, k, *chain) if k else z
        src = zbuf.at[sz] if k else tok_ref
        rows_out(n_e, cap, k, sz, src, d_ref, rows, out_ref, own, send, recv)
    for k in range(n_z):
        sz = ranked(z, k, n_z) if k else z
        rows_out_wait(n_e, cap, k, sz, rows, out_ref, own, send, recv)
    chain_end(n_z, tok_ref, *chain)


def dispatch(n_e, n_z, cap, tok, picks):
    count, columns = tok.shape
    return pl.pallas_call(
        partial(dispatch_kernel, n_e, n_z, cap),
        out_shape=jax.ShapeDtypeStruct((n_z, n_e, cap, columns), BF),
        in_specs=[VM, VM],
        out_specs=ANY,
        scratch_shapes=[
            pltpu.VMEM((n_z, count, columns), BF),
            pltpu.VMEM((n_z, n_e * cap, columns), BF),
            DMA((n_z,)),
            DMA((n_z + 1,)),
            DMA((n_z,)),
            DMA((n_z, n_e)),
            DMA((n_z, n_e)),
        ],
        compiler_params=pltpu.CompilerParams(
            collective_id=4, has_side_effects=True, vmem_limit_bytes=BIG
        ),
        name="dispatch",
    )(tok, picks)


def send_kernel(n_e, n_z, cap, src_ref, d_ref, out_ref, rows, own, send, recv):
    e, z = place()
    greet(n_e, n_z, False)
    for k in range(n_z):
        sz = near(z, k, n_z)
        rows_out(n_e, cap, k, sz, src_ref.at[sz], d_ref, rows, out_ref, own, send, recv)
    for k in range(n_z):
        rows_out_wait(n_e, cap, k, near(z, k, n_z), rows, out_ref, own, send, recv)


def send_rows(n_e, n_z, cap, src, picks):
    columns = src.shape[-1]
    return pl.pallas_call(
        partial(send_kernel, n_e, n_z, cap),
        out_shape=jax.ShapeDtypeStruct((n_z, n_e, cap, columns), BF),
        in_specs=[VM, VM],
        out_specs=ANY,
        scratch_shapes=[
            pltpu.VMEM((n_z, n_e * cap, columns), BF),
            DMA((n_z,)),
            DMA((n_z, n_e)),
            DMA((n_z, n_e)),
        ],
        compiler_params=pltpu.CompilerParams(
            collective_id=5, has_side_effects=True, vmem_limit_bytes=BIG
        ),
        name="send_rows",
    )(src, picks)


def give_back_kernel(
    n_e,
    n_z,
    cap,
    y_ref,
    d_ref,
    out_ref,
    rbuf,
    pbuf,
    own,
    send,
    recv,
    z_own,
    z_send,
    z_recv,
):
    e, z = place()
    greet(n_e, n_z, True)
    order = list(range(n_z - 1, -1, -1))
    for k in order:
        sz = near(z, k, n_z)
        for i in range(1, n_e + 1):
            oe = lax.rem(e + i, n_e)
            if i < n_e:
                remote(
                    y_ref.at[sz, oe],
                    rbuf.at[sz, e],
                    send.at[k, i],
                    recv.at[sz, e],
                    (oe, z),
                ).start()
            else:
                pltpu.make_async_copy(y_ref.at[sz, e], rbuf.at[sz, e], own.at[k]).start()
    for k in order:
        sz = near(z, k, n_z)
        for i in range(1, n_e + 1):
            oe = lax.rem(e + i, n_e)
            if i < n_e:
                remote(
                    y_ref.at[sz, oe],
                    rbuf.at[sz, oe],
                    send.at[k, i],
                    recv.at[sz, oe],
                    (oe, z),
                ).wait()
            else:
                pltpu.make_async_copy(y_ref.at[sz, e], rbuf.at[sz, e], own.at[k]).wait()
        pick = d_ref[sz]
        for start, size in pieces(pbuf.shape[-1]):
            block = rbuf[sz, :, :, start : start + size].reshape(n_e * cap, size)
            pbuf[k, :, start : start + size] = dot(pick, block).astype(BF)
        if k:
            remote(
                pbuf.at[k], out_ref.at[z], z_send.at[k], z_recv.at[z], (e, sz)
            ).start()
        else:
            pltpu.make_async_copy(pbuf.at[k], out_ref.at[z], z_own).start()
    for k in order:
        sz = near(z, k, n_z)
        if k:
            remote(
                pbuf.at[k], out_ref.at[sz], z_send.at[k], z_recv.at[sz], (e, sz)
            ).wait()
        else:
            pltpu.make_async_copy(pbuf.at[k], out_ref.at[z], z_own).wait()


def give_back(n_e, n_z, cap, y, picks, number):
    columns = y.shape[-1]
    count = picks.shape[1]
    return pl.pallas_call(
        partial(give_back_kernel, n_e, n_z, cap),
        out_shape=jax.ShapeDtypeStruct((n_z, count, columns), BF),
        in_specs=[ANY, VM],
        out_specs=ANY,
        scratch_shapes=[
            pltpu.VMEM((n_z, n_e, cap, columns), BF),
            pltpu.VMEM((n_z, count, columns), BF),
            DMA((n_z,)),
            DMA((n_z, n_e)),
            DMA((n_z, n_e)),
            DMA,
            DMA((n_z,)),
            DMA((n_z,)),
        ],
        compiler_params=pltpu.CompilerParams(
            collective_id=number, has_side_effects=True, vmem_limit_bytes=BIG
        ),
        name="give_back",
    )(y, picks)


def finish_kernel(
    n_e,
    n_z,
    part_ref,
    gw_ref,
    go_ref,
    gm_ref,
    total_ref,
    gws_ref,
    gos_ref,
    gms_ref,
    own_g,
    a_send,
    a_recv,
    z_send,
    z_recv,
    *scratch,
):
    e, z = place()
    n, me = n_e * n_z, e * n_z + z
    greet_all(n_e, n_z)

    def other_of(k):
        other = lax.rem(me + k, n)
        return other, (other // n_z, lax.rem(other, n_z))

    @pl.loop(1, n)
    def _(k):
        other, where = other_of(k)
        remote(
            gw_ref.at[other], gws_ref.at[me], a_send.at[0, k], a_recv.at[0, me], where
        ).start()
        remote(
            gm_ref.at[other], gms_ref.at[me], a_send.at[1, k], a_recv.at[1, me], where
        ).start()

    for k in range(1, n_z):
        oz = near(z, k, n_z)
        remote(
            go_ref.at[oz], gos_ref.at[z], z_send.at[k], z_recv.at[z], (e, oz)
        ).start()
    mine = (
        (gw_ref.at[me], gws_ref.at[me]),
        (gm_ref.at[me], gms_ref.at[me]),
        (go_ref.at[z], gos_ref.at[z]),
    )
    for i, (src, dst) in enumerate(mine):
        pltpu.make_async_copy(src, dst, own_g.at[i]).start()

    plane_sum_body(n_e, part_ref, total_ref, *scratch)

    @pl.loop(1, n)
    def _(k):
        other, where = other_of(k)
        remote(
            gw_ref.at[other],
            gws_ref.at[other],
            a_send.at[0, k],
            a_recv.at[0, other],
            where,
        ).wait()
        remote(
            gm_ref.at[other],
            gms_ref.at[other],
            a_send.at[1, k],
            a_recv.at[1, other],
            where,
        ).wait()

    for k in range(1, n_z):
        oz = near(z, k, n_z)
        remote(
            go_ref.at[oz], gos_ref.at[oz], z_send.at[k], z_recv.at[oz], (e, oz)
        ).wait()
    for i, (src, dst) in enumerate(mine):
        pltpu.make_async_copy(src, dst, own_g.at[i]).wait()


def finish(n_e, n_z, part, gw, go, gm):
    n = n_e * n_z
    return pl.pallas_call(
        partial(finish_kernel, n_e, n_z),
        out_shape=(
            jax.ShapeDtypeStruct(part.shape[1:], F32),
            jax.ShapeDtypeStruct(gw.shape, gw.dtype),
            jax.ShapeDtypeStruct(go.shape, go.dtype),
            jax.ShapeDtypeStruct(gm.shape, gm.dtype),
        ),
        in_specs=[ANY] * 4,
        out_specs=(VM, ANY, ANY, ANY),
        scratch_shapes=[
            DMA((3,)),
            DMA((2, n)),
            DMA((2, n)),
            DMA((n_z,)),
            DMA((n_z,)),
        ]
        + plane_sum_scratch(n_e, part),
        compiler_params=pltpu.CompilerParams(
            collective_id=8, has_side_effects=True, vmem_limit_bytes=BIG
        ),
        name="finish",
    )(part, gw, go, gm)


def head_norm(u, gain):
    r = lax.rsqrt(jnp.mean(u * u, axis=-1, keepdims=True) + EPSILON)
    return u * r * gain


def turn(u, cos, sin):
    return u * cos + pltpu.roll(u, HEAD // 2, 1) * sin


def turn_back(u, cos, sin):
    return u * cos - pltpu.roll(u, HEAD // 2, 1) * sin


def turns(table):
    other = pltpu.roll(table, HEAD // 2, 1)
    first = lax.broadcasted_iota(jnp.int32, table.shape, 1) < HEAD // 2
    return jnp.where(first, table, other), jnp.where(first, -other, table)


def may_see(seg_row):
    count = seg_row.shape[1]
    i = lax.broadcasted_iota(jnp.int32, (count, count), 0)
    j = lax.broadcasted_iota(jnp.int32, (count, count), 1)
    seg_col = jnp.sum(jnp.where(i == j, seg_row, 0.0), axis=1, keepdims=True)
    return ((seg_col == seg_row) & (seg_col >= 0) & (j <= i)) | (i == j)


def probabilities(q, k, allowed):
    scores = jnp.where(allowed, dot_last(q, k) * (HEAD**-0.5), -1e30)
    peak = jnp.max(scores, axis=-1, keepdims=True)
    weight = jnp.exp(scores - peak)
    return weight / jnp.sum(weight, axis=-1, keepdims=True)


def attend_block(
    heads, x, cos, sin, allowed, w_ref, wo_ref, g1_ref, gh_ref, n1_ref, raw_ref, v_ref, mix_ref
):
    x = x.astype(F32)
    r = lax.rsqrt(jnp.mean(x * x, axis=-1, keepdims=True) + EPSILON)
    n1 = (x * r * g1_ref[...]).astype(BF)
    n1_ref[...] = n1
    raw = dot(n1, w_ref[...])
    qk = (heads + 1) * HEAD
    raw_ref[...] = raw[:, :qk]
    value = raw[:, qk:].astype(BF)
    v_ref[...] = value
    gq, gk = gh_ref[0:1, :], gh_ref[1:2, :]
    key = turn(head_norm(raw[:, heads * HEAD : qk], gk), cos, sin).astype(BF)
    for h in range(heads):
        at = slice(h * HEAD, (h + 1) * HEAD)
        query = turn(head_norm(raw[:, at], gq), cos, sin).astype(BF)
        weight = probabilities(query, key, allowed).astype(BF)
        mix_ref[:, at] = dot(weight, value).astype(BF)
    return dot(mix_ref[...], wo_ref[...]).astype(BF)


def attend_kernel(
    heads,
    x_ref,
    turn_ref,
    seg_ref,
    w_ref,
    wo_ref,
    g1_ref,
    gh_ref,
    n1_ref,
    raw_ref,
    v_ref,
    mix_ref,
    part_ref,
):
    part_ref[0] = attend_block(
        heads,
        x_ref[0],
        *turns(turn_ref[0]),
        may_see(seg_ref[0]),
        w_ref,
        wo_ref,
        g1_ref,
        gh_ref,
        n1_ref.at[0],
        raw_ref.at[0],
        v_ref.at[0],
        mix_ref.at[0],
    )


def attend(n_e, heads, xs, turn_table, seg, w, wo, g1, gh):
    _, count, width = xs.shape

    def block(*shape):
        return pl.BlockSpec((1,) + shape, lambda b: (b, 0, 0))

    def whole(*shape):
        return pl.BlockSpec(shape, lambda b: (0, 0))

    outs = ((width, BF), ((heads + 1) * HEAD, F32), (HEAD, BF), (heads * HEAD, BF), (width, BF))
    return pl.pallas_call(
        partial(attend_kernel, heads),
        grid=(n_e,),
        out_shape=tuple(jax.ShapeDtypeStruct((n_e, count, c), t) for c, t in outs),
        in_specs=[
            block(count, width),
            block(count, HEAD),
            block(1, count),
            whole(*w.shape),
            whole(*wo.shape),
            whole(*g1.shape),
            whole(*gh.shape),
        ],
        out_specs=tuple(block(count, c) for c, _ in outs),
        compiler_params=pltpu.CompilerParams(vmem_limit_bytes=BIG),
        name="attend",
    )(xs, turn_table, seg, w, wo, g1, gh)


def front_kernel(
    n_e,
    n_z,
    cap,
    heads,
    xs_ref,
    ct_ref,
    pick_ref,
    turn_ref,
    seg_ref,
    w_ref,
    wo_ref,
    g1_ref,
    gh_ref,
    n1_ref,
    raw_ref,
    v_ref,
    mix_ref,
    total_ref,
    dy_ref,
    xbuf,
    n1buf,
    rawbuf,
    vbuf,
    mixbuf,
    away,
    mine,
    sib,
    far,
    via,
    zbuf,
    rows,
    x_sem,
    o_sem,
    sib_send,
    sib_recv,
    send,
    recv,
    via_send,
    via_recv,
    z_send,
    z_recv,
    r_send,
    r_recv,
    r_own,
):
    e, z = place()
    nc, chip, core = n_e // 2, e // 2, lax.rem(e, 2)
    sibling = (2 * chip + 1 - core, z)
    count = total_ref.shape[0]
    step = 32
    greet(n_e, n_z, True)
    chain = (lambda s: zbuf.at[s], z_send, z_recv)
    chain_start(n_z, ct_ref, *chain)

    def blocks(k):
        j = partner_chip(chip, nc - 1 - k)
        return j, (2 * j + 1 - core, 2 * j + core)

    half = count // 2

    def via_copy(p):
        rows = pl.ds(pl.multiple_of(p * half, half), half)
        there = (2 * partner_chip(chip, p + 1) + core, z)
        return remote(
            mine.at[partner_chip(chip, nc - 1), rows, :],
            via.at[p],
            via_send.at[p],
            via_recv.at[p],
            there,
        )

    def far_copy(p):
        j = partner_chip(chip, 2 - p)
        return remote(mine.at[j], far.at[p], send.at[p], recv.at[p], (2 * j + core, z))

    def load(b, slot):
        return pltpu.make_async_copy(xs_ref.at[b], xbuf.at[slot], x_sem.at[slot])

    def stores(b, slot):
        pairs = ((n1buf, n1_ref), (rawbuf, raw_ref), (vbuf, v_ref), (mixbuf, mix_ref))
        return [
            pltpu.make_async_copy(src.at[slot], dst.at[b], o_sem.at[i, slot])
            for i, (src, dst) in enumerate(pairs)
        ]

    for slot in range(2):
        load(blocks(0)[1][slot], slot).start()

    @pl.loop(0, nc)
    def _(k):
        j, pair = blocks(k)
        for slot, b in enumerate(pair):
            load(b, slot).wait()

            @pl.when(k > 0)
            def _(b=b, slot=slot):
                for copy in stores(b, slot):
                    copy.wait()

            part = attend_block(
                heads,
                xbuf[slot],
                *turns(turn_ref[b]),
                may_see(seg_ref[b]),
                w_ref,
                wo_ref,
                g1_ref,
                gh_ref,
                n1buf.at[slot],
                rawbuf.at[slot],
                vbuf.at[slot],
                mixbuf.at[slot],
            )
            for copy in stores(b, slot):
                copy.start()

            @pl.when(k < nc - 1)
            def _(slot=slot):
                load(blocks(k + 1)[1][slot], slot).start()

            if slot == 0:
                away[j] = part
                remote(
                    away.at[j], sib.at[j], sib_send.at[j], sib_recv.at[j], sibling
                ).start()
            else:
                mine[j] = part
        remote(away.at[j], sib.at[j], sib_send.at[j], sib_recv.at[j], sibling).wait()

        @pl.when(k < nc - 1)
        def _():
            @pl.loop(0, count, step=step)
            def _(r):
                at = pl.ds(pl.multiple_of(r, step), step)
                mine[j, at, :] = (
                    mine[j, at, :].astype(F32) + sib[j, at, :].astype(F32)
                ).astype(BF)

        @pl.when(k == 0)
        def _():
            for p in range(2):
                via_copy(p).start()

        @pl.when((k > 0) & (k < nc - 1))
        def _():
            via_copy(k - 1).wait_recv()

            @pl.loop(0, half, step=step)
            def _(r):
                at = pl.ds(pl.multiple_of((k - 1) * half + r, step), step)
                came = via[k - 1, pl.ds(pl.multiple_of(r, step), step), :]
                mine[j, at, :] = (mine[j, at, :].astype(F32) + came.astype(F32)).astype(BF)

            far_copy(k - 1).start()

        @pl.when((k > 0) & (k < n_z))
        def _():
            sz = chain_take(n_z, k, *chain)
            rows_out(
                n_e,
                cap,
                k - 1,
                sz,
                zbuf.at[sz],
                pick_ref,
                rows,
                dy_ref,
                r_own,
                r_send,
                r_recv,
            )

    @pl.loop(0, count, step=step)
    def _(r):
        at = pl.ds(pl.multiple_of(r, step), step)
        total_ref[at, :] = mine[chip, at, :].astype(F32) + sib[chip, at, :].astype(F32)

    for p in range(2):
        far_copy(p).wait()

        @pl.loop(0, count, step=step)
        def _(r, p=p):
            at = pl.ds(pl.multiple_of(r, step), step)
            total_ref[at, :] += far[p, at, :].astype(F32)

        via_copy(p).wait_send()

    for slot, b in enumerate(blocks(nc - 1)[1]):
        for copy in stores(b, slot):
            copy.wait()
    for k in range(1, n_z):
        rows_out_wait(
            n_e, cap, k - 1, ranked(z, k, n_z), rows, dy_ref, r_own, r_send, r_recv
        )
    chain_end(n_z, ct_ref, *chain)


def front(n_e, n_z, cap, heads, xs, ct, picks, turn_table, seg, w, wo, g1, gh):
    _, count, width = xs.shape
    nc = n_e // 2
    outs = ((width, BF), ((heads + 1) * HEAD, F32), (HEAD, BF), (heads * HEAD, BF))
    bufs = [pltpu.VMEM((2, count, width), BF)]
    bufs += [pltpu.VMEM((2, count, c), t) for c, t in outs]
    bufs += [pltpu.VMEM((nc, count, width), BF)] * 3
    bufs += [pltpu.VMEM((2, count, width), BF), pltpu.VMEM((2, count // 2, width), BF)]
    bufs += [
        pltpu.VMEM((n_z, count, width), BF),
        pltpu.VMEM((n_z - 1, n_e * cap, width), BF),
    ]
    return pl.pallas_call(
        partial(front_kernel, n_e, n_z, cap, heads),
        out_shape=tuple(jax.ShapeDtypeStruct((n_e, count, c), t) for c, t in outs)
        + (
            jax.ShapeDtypeStruct((count, width), F32),
            jax.ShapeDtypeStruct((n_z, n_e, cap, width), BF),
        ),
        in_specs=[ANY] + [VM] * 8,
        out_specs=(ANY,) * 4 + (VM, ANY),
        scratch_shapes=bufs
        + [
            DMA((2,)),
            DMA((4, 2)),
            DMA((nc,)),
            DMA((nc,)),
            DMA((2,)),
            DMA((2,)),
            DMA((2,)),
            DMA((2,)),
            DMA((n_z + 1,)),
            DMA((n_z,)),
            DMA((n_z, n_e)),
            DMA((n_z, n_e)),
            DMA((n_z,)),
        ],
        compiler_params=pltpu.CompilerParams(
            collective_id=12, has_side_effects=True, vmem_limit_bytes=BIG
        ),
        name="front",
    )(xs, ct, picks, turn_table, seg, w, wo, g1, gh)


def norm_back(u, gain, dv):
    r = lax.rsqrt(jnp.mean(u * u, axis=-1, keepdims=True) + EPSILON)
    nu = u * r
    dgain = jnp.sum(dv * nu, axis=0, keepdims=True)
    scaled = dv * gain
    du = r * (scaled - nu * jnp.mean(scaled * nu, axis=-1, keepdims=True))
    return du, dgain


def attend_back_block(
    heads,
    da,
    n1,
    raw_ref,
    value,
    cos,
    sin,
    allowed,
    w_ref,
    wo_ref,
    gh_ref,
    dmix,
    dcat,
    g1_ref,
    ghg_ref,
):
    dmix[...] = dot_last(da, wo_ref[...]).astype(BF)
    gq, gk = gh_ref[0:1, :], gh_ref[1:2, :]
    qk = (heads + 1) * HEAD
    key_raw = raw_ref[:, heads * HEAD : qk]
    key = turn(head_norm(key_raw, gk), cos, sin).astype(BF)
    count = key.shape[0]
    dkey = jnp.zeros((count, HEAD), F32)
    dvalue = jnp.zeros((count, HEAD), F32)
    dgq = jnp.zeros((1, HEAD), F32)
    scale = HEAD**-0.5
    for h in range(heads):
        at = slice(h * HEAD, (h + 1) * HEAD)
        query_raw = raw_ref[:, at]
        query = turn(head_norm(query_raw, gq), cos, sin).astype(BF)
        weight = probabilities(query, key, allowed)
        dm = dmix[:, at]
        dweight = dot_last(dm, value)
        delta = jnp.sum(weight * dweight, axis=-1, keepdims=True)
        dscore = (weight * (dweight - delta)).astype(BF)
        dquery = dot(dscore, key) * scale
        dkey += dot_first(dscore, query) * scale
        dvalue += dot_first(weight.astype(BF), dm)
        du, dg = norm_back(query_raw, gq, turn_back(dquery, cos, sin))
        dcat[:, at] = du.astype(BF)
        dgq += dg
    du, dgk = norm_back(key_raw, gk, turn_back(dkey, cos, sin))
    dcat[:, heads * HEAD : qk] = du.astype(BF)
    dcat[:, qk:] = dvalue.astype(BF)
    ghg_ref[0:1, :] += dgq
    ghg_ref[1:2, :] += dgk
    dn = dot_last(dcat[...], w_ref[...])
    g1_ref[...] += jnp.sum(dn * n1.astype(F32), axis=0, keepdims=True)
    return dn.astype(BF)


def attend_back_kernel(
    heads,
    steps,
    da_ref,
    n1_ref,
    raw_ref,
    v_ref,
    mix_ref,
    turn_ref,
    seg_ref,
    w_ref,
    wo_ref,
    gh_ref,
    dn_ref,
    gw_ref,
    go_ref,
    g1_ref,
    ghg_ref,
    acc_w,
    acc_o,
    dcat,
    dmix,
):
    step = pl.program_id(0)

    @pl.when(step == 0)
    def _():
        acc_w[...] = jnp.zeros_like(acc_w)
        acc_o[...] = jnp.zeros_like(acc_o)
        g1_ref[...] = jnp.zeros_like(g1_ref)
        ghg_ref[...] = jnp.zeros_like(ghg_ref)

    da, n1 = da_ref[0], n1_ref[0]
    dn_ref[0] = attend_back_block(
        heads,
        da,
        n1,
        raw_ref.at[0],
        v_ref[0],
        *turns(turn_ref[0]),
        may_see(seg_ref[0]),
        w_ref,
        wo_ref,
        gh_ref,
        dmix,
        dcat,
        g1_ref,
        ghg_ref,
    )
    acc_w[...] += dot_first(n1, dcat[...])
    acc_o[...] += dot_first(mix_ref[0], da)

    @pl.when(step == steps - 1)
    def _():
        gw_ref[...] = acc_w[...].astype(BF)
        go_ref[...] = acc_o[...].astype(BF)


def attend_back(n_e, heads, da, n1, raw, v, mix, turn_table, seg, w, wo, gh):
    _, count, width = da.shape

    def block(*shape):
        return pl.BlockSpec((1,) + shape, lambda b: (b, 0, 0))

    def whole(*shape):
        return pl.BlockSpec(shape, lambda b: (0, 0))

    return pl.pallas_call(
        partial(attend_back_kernel, heads, n_e),
        grid=(n_e,),
        out_shape=(
            jax.ShapeDtypeStruct((n_e, count, width), BF),
            jax.ShapeDtypeStruct(w.shape, BF),
            jax.ShapeDtypeStruct(wo.shape, BF),
            jax.ShapeDtypeStruct((1, width), F32),
            jax.ShapeDtypeStruct((8, HEAD), F32),
        ),
        in_specs=[
            block(count, width),
            block(count, width),
            block(*raw.shape[1:]),
            block(count, HEAD),
            block(*mix.shape[1:]),
            block(count, HEAD),
            block(1, count),
            whole(*w.shape),
            whole(*wo.shape),
            whole(*gh.shape),
        ],
        out_specs=(
            block(count, width),
            whole(*w.shape),
            whole(*wo.shape),
            whole(1, width),
            whole(8, HEAD),
        ),
        scratch_shapes=[
            pltpu.VMEM(w.shape, F32),
            pltpu.VMEM(wo.shape, F32),
            pltpu.VMEM((count, (heads + 2) * HEAD), BF),
            pltpu.VMEM((count, heads * HEAD), BF),
        ],
        compiler_params=pltpu.CompilerParams(vmem_limit_bytes=BIG),
        name="attend_back",
    )(da, n1, raw, v, mix, turn_table, seg, w, wo, gh)


def back_kernel(
    n_e,
    n_z,
    cap,
    heads,
    da_ref,
    r_ref,
    rfar_ref,
    gr_ref,
    n1_ref,
    raw_ref,
    v_ref,
    mix_ref,
    unpick_ref,
    g2_ref,
    turn_ref,
    seg_ref,
    w_ref,
    wo_ref,
    g1_ref,
    gh_ref,
    total_ref,
    part_ref,
    gws_ref,
    goo_ref,
    gor_ref,
    gol_ref,
    grs_ref,
    gvs_ref,
    ret_ref,
    gwr_ref,
    gwl_ref,
    rsum,
    gplane,
    das,
    n1s,
    raws,
    vs,
    mixs,
    dcats,
    dmix,
    gsum,
    ghsum,
    gvec,
    gtotal,
    away,
    mine,
    sib,
    far,
    rbuf,
    gob,
    own,
    in_sem,
    raw_sem,
    d_send,
    d_recv,
    ds_send,
    ds_recv,
    a_send,
    a_recv,
    b_send,
    b_recv,
    b_own,
    p_send,
    p_recv,
    o_send,
    or_recv,
    ol_recv,
    w_send,
    wr_recv,
    wl_recv,
    s_send,
    s_recv,
    t_sem,
    v_send,
    v_recv,
    vz_send,
    vz_recv,
    sib_send,
    sib_recv,
    send,
    recv,
):
    e, z = place()
    n, me = n_e * n_z, e * n_z + z
    nc, chip, core = n_e // 2, e // 2, lax.rem(e, 2)
    sibling = (2 * chip + 1 - core, z)
    count, width = total_ref.shape
    shard = width // n
    head_rows = mixs.shape[-1] // n_z
    step = 32
    greet_all(n_e, n_z)

    def other_of(k):
        other = lax.rem(me + k, n)
        return other, (other // n_z, lax.rem(other, n_z))

    def far_chip(k):
        return (2 * partner_chip(chip, k) + core, z)

    def give_da(k):
        return remote(
            da_ref, das.at[e], d_send.at[k], d_recv.at[chip], far_chip(k)
        )

    remote(da_ref, das.at[e], ds_send.at[0], ds_recv.at[chip], sibling).start()
    for k in range(1, nc - 1):
        give_da(k).start()
    own_da = pltpu.make_async_copy(da_ref, das.at[e], own.at[0])
    own_da.start()

    @pl.loop(1, n)
    def _(k):
        other, where = other_of(k)
        remote(
            gr_ref.at[other], grs_ref.at[me], a_send.at[k], a_recv.at[me], where
        ).start()

    own_gr = pltpu.make_async_copy(gr_ref.at[me], grs_ref.at[me], own.at[1])
    own_gr.start()
    for i, (src, dst) in enumerate(((n1_ref, n1s), (v_ref, vs), (mix_ref, mixs))):
        pltpu.make_async_copy(src, dst, in_sem.at[i]).start()

    def load_raw(b, slot):
        return pltpu.make_async_copy(raw_ref.at[b], raws.at[slot], raw_sem.at[slot])

    def blocks(k):
        j = partner_chip(chip, k)
        return j, (2 * j + 1 - core, 2 * j + core)

    def source(k):
        return jnp.where(k == 0, z, ranked(z, k, n_z))

    def give_rows(k):
        sz = source(k)
        for i in range(1, n_e):
            oe = lax.rem(e + i, n_e)
            remote(
                r_ref.at[sz, oe],
                ret_ref.at[sz, e],
                b_send.at[k, i],
                b_recv.at[sz, e],
                (oe, z),
            ).start()
        pltpu.make_async_copy(r_ref.at[sz, e], ret_ref.at[sz, e], b_own.at[k]).start()

    for slot in range(2):
        load_raw(blocks(0)[1][slot], slot).start()
    gsum[...] = jnp.zeros_like(gsum)
    ghsum[...] = jnp.zeros_like(ghsum)
    for i, (src, dst) in enumerate(((n1_ref, n1s), (v_ref, vs), (mix_ref, mixs))):
        pltpu.make_async_copy(src, dst, in_sem.at[i]).wait()

    tokens = n_e * count

    def out_weights():
        da_all = das[...].reshape(tokens, width)
        for oz in range(n_z):
            at = slice(oz * head_rows, (oz + 1) * head_rows)
            gob[oz] = dot_first(mixs[:, :, at].reshape(tokens, head_rows), da_all).astype(BF)
        pass_all(out_pass, 0)

    def pass_sum(d, step, stage, block, inbox, recv, send, add):
        distance = z if step > 0 else n_z - 1 - z
        going = (d > z) if step > 0 else (d < z)

        @pl.when(going & (distance == stage))
        def _():
            if stage:
                remote(block, inbox.at[d], send.at[d], recv.at[d], (e, z - step)).wait_recv()
                add(d, inbox)
            remote(block, inbox.at[d], send.at[d], recv.at[d], (e, z + step)).start()

    def pass_all(one_pass, stage, steps=range(n_z - 1)):
        for d in steps:
            one_pass(n_z - 1 - d, 1, stage)
            one_pass(d, -1, stage)

    def out_add(d, inbox):
        fetch = pltpu.make_async_copy(inbox.at[d], away.at[0:head_rows], t_sem.at[0])
        fetch.start()
        fetch.wait()

        @pl.loop(0, head_rows, step=step)
        def _(r):
            at = pl.ds(pl.multiple_of(r, step), step)
            gob[d, at, :] = (gob[d, at, :].astype(F32) + away[at, :].astype(F32)).astype(BF)

    def out_pass(d, step, stage):
        inbox, recv = (gor_ref, or_recv) if step > 0 else (gol_ref, ol_recv)
        pass_sum(d, step, stage, gob.at[d], inbox, recv, o_send, out_add)

    parts = dcats.shape[-1] // (n_z * shard)

    def shard_at(d):
        return pl.ds(pl.multiple_of(d * shard, shard), shard)

    def weight_add(d, inbox):
        for p in range(parts):
            there = away.at[p * shard : (p + 1) * shard]
            pltpu.make_async_copy(inbox.at[d, p], there, t_sem.at[p]).start()
        for p in range(parts):
            there = away.at[p * shard : (p + 1) * shard]
            pltpu.make_async_copy(inbox.at[d, p], there, t_sem.at[p]).wait()

            @pl.loop(0, shard, step=step)
            def _(r, p=p):
                at = pl.ds(pl.multiple_of(d * shard + r, step), step)
                came = away[pl.ds(pl.multiple_of(p * shard + r, step), step), :]
                n1s[p, at, :] = (n1s[p, at, :].astype(F32) + came.astype(F32)).astype(BF)

    def weight_pass(d, step, stage):
        inbox, recv = (gwr_ref, wr_recv) if step > 0 else (gwl_ref, wl_recv)
        block = n1s.at[0:parts, shard_at(d), :]
        pass_sum(d, step, stage, block, inbox, recv, w_send, weight_add)

    def sum_rows(src, dst, k):
        sz = source(k)
        unpick = unpick_ref[sz]
        cuts = pieces(width)

        def fetch(p):
            start, size = cuts[p]
            return pltpu.make_async_copy(
                src.at[:, :, start : start + size], rbuf.at[p % 2], in_sem.at[p % 2]
            )

        fetch(0).start()
        for p, (start, size) in enumerate(cuts):
            if p + 1 < len(cuts):
                fetch(p + 1).start()
            fetch(p).wait()
            block = rbuf[p % 2].reshape(n_e * cap, size)
            dst[:, start : start + size] = dot(unpick, block).astype(BF)

    def sum_of(k):
        return rsum if k == n_z - 1 else das.at[k]

    def send_sum(k):
        sz = source(k)
        return remote(sum_of(k), part_ref.at[z], p_send.at[k], p_recv.at[z], (e, sz))

    def take_rows(k):
        sz = source(k)
        for i in range(1, n_e):
            oe = lax.rem(e + i, n_e)
            remote(
                r_ref.at[sz, oe],
                ret_ref.at[sz, oe],
                b_send.at[k, i],
                b_recv.at[sz, oe],
                (oe, z),
            ).wait()
        pltpu.make_async_copy(r_ref.at[sz, e], ret_ref.at[sz, e], b_own.at[k]).wait()
        sum_rows(ret_ref.at[sz], sum_of(k), k)

    sum_rows(rfar_ref, rsum, n_z - 1)
    send_sum(n_z - 1).start()

    pltpu.make_async_copy(da_ref, das.at[e], own.at[0]).wait()

    @pl.loop(0, nc)
    def _(k):
        j, pair = blocks(k)
        remote(da_ref, das.at[pair[0]], ds_send.at[k], ds_recv.at[j], sibling).wait_recv()
        pl.when(k == nc - 1)(out_weights)
        to_sibling = remote(
            away, sib.at[lax.rem(k, 2)], sib_send, sib_recv.at[lax.rem(k, 2)], sibling
        )
        for slot, b in enumerate(pair):
            load_raw(b, slot).wait()
            part = attend_back_block(
                heads,
                das[b],
                n1s[b],
                raws.at[slot],
                vs[b],
                *turns(turn_ref[b]),
                may_see(seg_ref[b]),
                w_ref,
                wo_ref,
                gh_ref,
                dmix,
                dcats.at[b],
                gsum,
                ghsum,
            )

            @pl.when(k < nc - 1)
            def _(slot=slot):
                load_raw(blocks(k + 1)[1][slot], slot).start()

            if slot == 1:
                mine[j] = part
                continue
            away[...] = part
            to_sibling.start()

            @pl.when(k == 0)
            def _():
                give_da(nc - 1).start()

            @pl.when(k < nc - 1)
            def _():
                nj = blocks(k + 1)[0]
                block = das.at[2 * nj + core]
                remote(
                    da_ref, block, d_send.at[k + 1], d_recv.at[nj], far_chip(k + 1)
                ).wait_recv()
                remote(block, block, ds_send.at[k + 1], ds_recv.at[nj], sibling).start()

        @pl.when((k > 0) & (k < n_z - 1))
        def _():
            give_rows(n_z - 1 - k)

        to_sibling.wait()

        @pl.when(k > 0)
        def _():
            @pl.loop(0, count, step=step)
            def _(r):
                at = pl.ds(pl.multiple_of(r, step), step)
                mine[j, at, :] = (
                    mine[j, at, :].astype(F32) + sib[lax.rem(k, 2), at, :].astype(F32)
                ).astype(BF)

            remote(
                mine.at[j], far.at[k - 1], send.at[k - 1], recv.at[k - 1], far_chip(k)
            ).start()

        @pl.when(k == 0)
        def _():
            @pl.loop(0, count, step=step)
            def _(r):
                at = pl.ds(pl.multiple_of(r, step), step)
                total_ref[at, :] = mine[j, at, :].astype(F32) + sib[0, at, :].astype(F32)

    remote(da_ref, das.at[e], ds_send.at[0], ds_recv.at[chip], sibling).wait_send()
    for k in range(1, nc):
        give_da(k).wait_send()
        block = das.at[2 * partner_chip(chip, k) + core]
        remote(block, block, ds_send.at[k], ds_recv.at[chip], sibling).wait_send()

    give_rows(0)

    dcat = dcats[...].reshape(tokens, -1)

    @pl.loop(0, n_e)
    def _(t):
        at = pl.ds(pl.multiple_of(t * n_z * shard, n_z * shard), n_z * shard)
        rows = dot_first(n1s[:, :, at].reshape(tokens, n_z * shard), dcat).astype(BF)
        for p in range(parts):
            n1s[p, :, at] = rows[:, p * n_z * shard : (p + 1) * n_z * shard]

    pass_all(weight_pass, 0)
    pltpu.make_async_copy(gob.at[z], goo_ref, own.at[3]).start()
    lanes = 128
    g1 = gsum[...] / g1_ref[...]
    per = width // lanes
    for i in range(per):
        gvec[i : i + 1, :] = g1[:, i * lanes : (i + 1) * lanes]
        gvec[per + i : per + i + 1, :] = g2_ref[:, i * lanes : (i + 1) * lanes]
    gvec[2 * per : 2 * per + 8, :] = ghsum[...]

    for i in range(1, n_e):
        oe = lax.rem(e + i, n_e)
        remote(gvec, gplane.at[e], v_send.at[i], v_recv.at[e], (oe, z)).start()
    gplane[e] = gvec[...]
    pass_all(out_pass, 1)
    take_rows(n_z - 2)
    pass_all(weight_pass, 1, range(1))
    send_sum(n_z - 2).start()
    pass_all(out_pass, 2)
    pass_all(weight_pass, 1, range(1, n_z - 1))
    for k in range(n_z - 3, 0, -1):
        take_rows(k)
        send_sum(k).start()
    pass_all(weight_pass, 2)

    for came, inbox, recv_w, there in (
        (z > 0, gwr_ref, wr_recv, z - 1),
        (z < n_z - 1, gwl_ref, wl_recv, z + 1),
    ):

        @pl.when(came)
        def _(inbox=inbox, recv_w=recv_w, there=there):
            block = n1s.at[0:parts, shard_at(z), :]
            remote(block, inbox.at[z], w_send.at[z], recv_w.at[z], (e, there)).wait_recv()
            weight_add(z, inbox)

    def weight_block(t):
        at = pl.ds(pl.multiple_of(t * n_z * shard, n_z * shard), n_z * shard)
        return n1s.at[0:parts, shard_at(z), at]

    for i in range(1, n_e):
        oe = lax.rem(e + i, n_e)
        remote(weight_block(oe), gws_ref.at[e], s_send.at[i], s_recv.at[e], (oe, z)).start()
    pltpu.make_async_copy(weight_block(e), gws_ref.at[e], own.at[2]).start()
    for k in range(1, nc):
        j = partner_chip(chip, k)
        remote(
            mine.at[j], far.at[k - 1], send.at[k - 1], recv.at[k - 1], far_chip(k)
        ).wait()

        @pl.loop(0, count, step=step)
        def _(r, k=k):
            at = pl.ds(pl.multiple_of(r, step), step)
            total_ref[at, :] += far[k - 1, at, :].astype(F32)

    for i in range(1, n_e):
        oe = lax.rem(e + i, n_e)
        remote(gvec, gplane.at[oe], v_send.at[i], v_recv.at[oe], (oe, z)).wait()
    gtotal[...] = jnp.sum(gplane[...], axis=0)
    for k in range(1, n_z):
        oz = near(z, k, n_z)
        remote(gtotal, gvs_ref.at[z], vz_send.at[k], vz_recv.at[z], (e, oz)).start()
    own_gv = pltpu.make_async_copy(gtotal, gvs_ref.at[z], own.at[4])
    own_gv.start()
    take_rows(0)
    pltpu.make_async_copy(das.at[0], part_ref.at[z], own.at[6]).start()

    @pl.loop(1, n)
    def _(k):
        other, where = other_of(k)
        remote(
            gr_ref.at[other],
            grs_ref.at[other],
            a_send.at[k],
            a_recv.at[other],
            where,
        ).wait()

    for i in range(1, n_e):
        oe = lax.rem(e + i, n_e)
        remote(weight_block(oe), gws_ref.at[oe], s_send.at[i], s_recv.at[oe], (oe, z)).wait()
    for d in range(n_z):

        @pl.when(d != z)
        def _(d=d):
            remote(gob.at[d], gor_ref.at[d], o_send.at[d], or_recv.at[d], (e, d)).wait_send()
            block = n1s.at[0:parts, shard_at(d), :]
            remote(block, gwr_ref.at[d], w_send.at[d], wr_recv.at[d], (e, d)).wait_send()

    for came, inbox, recv_o, there in (
        (z > 0, gor_ref, or_recv, z - 1),
        (z < n_z - 1, gol_ref, ol_recv, z + 1),
    ):

        @pl.when(came)
        def _(inbox=inbox, recv_o=recv_o, there=there):
            remote(
                gob.at[z], inbox.at[z], o_send.at[z], recv_o.at[z], (e, there)
            ).wait_recv()

    for k in range(1, n_z):
        oz = near(z, k, n_z)
        remote(
            gtotal, gvs_ref.at[oz], vz_send.at[k], vz_recv.at[oz], (e, oz)
        ).wait()
        sz = ranked(z, k, n_z)
        remote(
            sum_of(k), part_ref.at[sz], p_send.at[k], p_recv.at[sz], (e, sz)
        ).wait()
    own_gr.wait()
    pltpu.make_async_copy(weight_block(e), gws_ref.at[e], own.at[2]).wait()
    pltpu.make_async_copy(gob.at[z], goo_ref, own.at[3]).wait()
    own_gv.wait()
    pltpu.make_async_copy(das.at[0], part_ref.at[z], own.at[6]).wait()


def back(
    n_e, n_z, cap, heads, da, r_rows, r_far, gr, n1, raw, v, mix, unpicks, g2, turn_table, seg, w, wo, g1, gh
):
    n, nc = n_e * n_z, n_e // 2
    count, width = da.shape
    shard = width // n
    columns = w.shape[1]
    parts = columns // (n_z * shard)
    out_block = (wo.shape[0] // n_z, width)
    vec_rows = 2 * width // 128 + 8
    block = (count, width)

    def sems(*shape):
        return DMA(shape)

    return pl.pallas_call(
        partial(back_kernel, n_e, n_z, cap, heads),
        out_shape=(
            jax.ShapeDtypeStruct(block, F32),
            jax.ShapeDtypeStruct((n_z,) + block, BF),
            jax.ShapeDtypeStruct((n_e, parts, shard, n_z * shard), BF),
            jax.ShapeDtypeStruct(out_block, BF),
            jax.ShapeDtypeStruct((n_z,) + out_block, BF),
            jax.ShapeDtypeStruct((n_z,) + out_block, BF),
            jax.ShapeDtypeStruct(gr.shape, F32),
            jax.ShapeDtypeStruct((n_z, vec_rows, 128), F32),
            jax.ShapeDtypeStruct(r_rows.shape, BF),
            jax.ShapeDtypeStruct((n_z, parts, shard, width), BF),
            jax.ShapeDtypeStruct((n_z, parts, shard, width), BF),
        ),
        in_specs=[ANY] * 8 + [VM] * 8,
        out_specs=(VM,) + (ANY,) * 10,
        scratch_shapes=[
            pltpu.VMEM(block, BF),
            pltpu.VMEM((n_e, vec_rows, 128), F32),
            pltpu.VMEM((n_e,) + block, BF),
            pltpu.VMEM(n1.shape, BF),
            pltpu.VMEM((2,) + raw.shape[1:], F32),
            pltpu.VMEM(v.shape, BF),
            pltpu.VMEM(mix.shape, BF),
            pltpu.VMEM((n_e, count, columns), BF),
            pltpu.VMEM((count, heads * HEAD), BF),
            pltpu.VMEM((1, width), F32),
            pltpu.VMEM((8, HEAD), F32),
            pltpu.VMEM((vec_rows, 128), F32),
            pltpu.VMEM((vec_rows, 128), F32),
            pltpu.VMEM(block, BF),
            pltpu.VMEM((nc,) + block, BF),
            pltpu.VMEM((2,) + block, BF),
            pltpu.VMEM((nc - 1,) + block, BF),
            pltpu.VMEM((2, n_e, cap, pieces(width)[0][1]), BF),
            pltpu.VMEM((n_z, wo.shape[0] // n_z, width), BF),
            sems(7),
            sems(3),
            sems(2),
            sems(nc),
            sems(nc),
            sems(nc),
            sems(nc),
            sems(n),
            sems(n),
            sems(n_z, n_e),
            sems(n_z, n_e),
            sems(n_z),
            sems(n_z),
            sems(n_z),
            sems(n_z),
            sems(n_z),
            sems(n_z),
            sems(n_z),
            sems(n_z),
            sems(n_z),
            sems(n_e),
            sems(n_e),
            sems(parts),
            sems(n_e),
            sems(n_e),
            sems(n_z),
            sems(n_z),
            DMA,
            sems(2),
            sems(nc),
            sems(nc),
        ],
        compiler_params=pltpu.CompilerParams(
            collective_id=14, has_side_effects=True, vmem_limit_bytes=63 * 1024 * 1024
        ),
        name="back",
    )(da, r_rows, r_far, gr, n1, raw, v, mix, unpicks, g2, turn_table, seg, w, wo, g1, gh)


def expert_kernel(
    n_z,
    experts,
    width,
    x_ref,
    dy_ref,
    wg_ref,
    wu_ref,
    wd_ref,
    r_ref,
    dx_ref,
    gg_ref,
    gu_ref,
    gd_ref,
):
    step = pl.program_id(0)

    @pl.when(step == 0)
    def _():
        gg_ref[...] = jnp.zeros_like(gg_ref)
        gu_ref[...] = jnp.zeros_like(gu_ref)
        gd_ref[...] = jnp.zeros_like(gd_ref)

    e, z = place()
    me = e * n_z + z
    x = x_ref[:, :width]
    extra = x_ref[:, width:].astype(F32)
    lane = lax.broadcasted_iota(jnp.int32, extra.shape, 1)
    gate = jnp.sum(
        jnp.where((lane == me) | (lane == experts + me), extra, 0.0), axis=1, keepdims=True
    )
    gate_part = dot(x, wg_ref[...])
    up_part = dot(x, wu_ref[...])
    sig = 1.0 / (1.0 + jnp.exp(-gate_part))
    act = gate_part * sig
    inner = (act * up_part).astype(BF)
    r_ref[...] = (dot(inner, wd_ref[...]) * gate).astype(BF)
    dy = dy_ref[...]
    dinner = dot_last(dy, wd_ref[...])
    inner_f = inner.astype(F32)
    dgate = jnp.sum(dinner * inner_f, axis=1, keepdims=True)
    gd_ref[...] += dot_first((inner_f * gate).astype(BF), dy)
    dinner = dinner * gate
    dgp = (dinner * up_part * sig * (1.0 + gate_part * (1.0 - sig))).astype(BF)
    dup = (dinner * act).astype(BF)
    dx_ref[:, :width] = (dot_last(dgp, wg_ref[...]) + dot_last(dup, wu_ref[...])).astype(BF)
    high = dgate.astype(BF).astype(F32)
    dx_ref[:, width:] = jnp.where(
        lane == me, high, jnp.where(lane == experts + me, dgate - high, 0.0)
    ).astype(BF)
    gg_ref[...] += dot_first(x, dgp)
    gu_ref[...] += dot_first(x, dup)


def expert_run(n_z, experts, x, dy, wg, wu, wd):
    rows, columns = x.shape
    width, hidden = wg.shape
    tile = 512

    def block(c):
        return pl.BlockSpec((tile, c), lambda b: (b, 0))

    def whole(shape):
        return pl.BlockSpec(shape, lambda b: (0, 0), pipeline_mode=pl.Buffered(1))

    return pl.pallas_call(
        partial(expert_kernel, n_z, experts, width),
        grid=(rows // tile,),
        out_shape=(
            jax.ShapeDtypeStruct((rows, width), BF),
            jax.ShapeDtypeStruct((rows, columns), BF),
            jax.ShapeDtypeStruct((width, hidden), F32),
            jax.ShapeDtypeStruct((width, hidden), F32),
            jax.ShapeDtypeStruct((hidden, width), F32),
        ),
        in_specs=[
            block(columns),
            block(width),
            whole(wg.shape),
            whole(wu.shape),
            whole(wd.shape),
        ],
        out_specs=(
            block(width),
            block(columns),
            whole(wg.shape),
            whole(wu.shape),
            whole(wd.shape),
        ),
        compiler_params=pltpu.CompilerParams(vmem_limit_bytes=BIG),
        name="experts",
    )(x, dy, wg, wu, wd)


def expert_tile(width, experts, me, x_ext, dy, wg_ref, wu_ref, wd_ref):
    x = x_ext[:, :width]
    extra = x_ext[:, width:].astype(F32)
    lane = lax.broadcasted_iota(jnp.int32, extra.shape, 1)
    gate = jnp.sum(
        jnp.where((lane == me) | (lane == experts + me), extra, 0.0), axis=1, keepdims=True
    )
    gate_part = dot(x, wg_ref[...])
    up_part = dot(x, wu_ref[...])
    sig = 1.0 / (1.0 + jnp.exp(-gate_part))
    act = gate_part * sig
    inner = (act * up_part).astype(BF)
    result = (dot(inner, wd_ref[...]) * gate).astype(BF)
    dinner = dot_last(dy, wd_ref[...])
    inner_f = inner.astype(F32)
    dgate = jnp.sum(dinner * inner_f, axis=1, keepdims=True)
    gated = (inner_f * gate).astype(BF)
    dinner = dinner * gate
    dgp = (dinner * up_part * sig * (1.0 + gate_part * (1.0 - sig))).astype(BF)
    dup = (dinner * act).astype(BF)
    dx = (dot_last(dgp, wg_ref[...]) + dot_last(dup, wu_ref[...])).astype(BF)
    high = dgate.astype(BF).astype(F32)
    back = jnp.where(
        lane == me, high, jnp.where(lane == experts + me, dgate - high, 0.0)
    ).astype(BF)
    return result, dx, back, gated, dgp, dup


def moe_kernel(
    n_e,
    n_z,
    cap,
    tok_ref,
    pick_ref,
    unpick_ref,
    near_ref,
    far_ref,
    wg_ref,
    wu_ref,
    wd_ref,
    xs_ref,
    r_ref,
    dx_ref,
    ret_ref,
    part_ref,
    gi_ref,
    dg_ref,
    du_ref,
    gg_ref,
    gu_ref,
    gd_ref,
    rret_ref,
    zbuf,
    z_send,
    z_recv,
    r_send,
    r_recv,
    r_own,
    in_sem,
    out_sem,
    b_send,
    b_recv,
    b_own,
    p_send,
    p_recv,
    p_own,
    e_send,
    e_recv,
    g_sem,
    t_sem,
    w_sem,
):
    e, z = place()
    me = e * n_z + z
    width = far_ref.shape[-1]
    hidden = wd_ref.shape[0]
    experts = n_e * n_z
    columns = tok_ref.shape[-1]
    last = n_z - 1
    inner = (z > 0) & (z < last)
    greet(n_e, n_z, True)
    chain = (lambda s: zbuf.at[s], z_send, z_recv)
    chain_start(n_z, tok_ref, *chain)

    def source(k):
        return jnp.where(k == 0, z, ranked(z, k, n_z))

    def give_one(k, i):
        sz, oe = source(k), lax.rem(e + i, n_e)
        return remote(
            dx_ref.at[sz, oe],
            ret_ref.at[sz, e],
            b_send.at[k, i],
            b_recv.at[sz, e],
            (oe, z),
        )

    def give_own(k):
        sz = source(k)
        return pltpu.make_async_copy(dx_ref.at[sz, e], ret_ref.at[sz, e], b_own.at[k])

    def give(k):
        for i in range(1, n_e):
            give_one(k, i).start()
        give_own(k).start()

    def store(k, tiles, i):
        src, dst = tiles[i]
        return pltpu.make_async_copy(src, dst.at[source(k)], out_sem.at[i])

    def first_phase(rows, xt, yt, rt, dxt, git, dgt, dut):
        out_args = (xs_ref, r_own, r_send, r_recv)
        rows_out(n_e, cap, 0, z, tok_ref, pick_ref, rows, *out_args)
        tiles = ((dxt, dx_ref), (rt, r_ref), (git, gi_ref), (dgt, dg_ref), (dut, du_ref))

        def load_y(src):
            return pltpu.make_async_copy(src, yt, in_sem.at[1])

        @pl.loop(0, n_z)
        def _(k):
            sz = source(k)

            @pl.when(k == 0)
            def _():
                load_y(near_ref).start()

            @pl.when(k > 0)
            def _():
                load_y(far_ref.at[sz]).start()

            @pl.when(jnp.where(inner, k == 0, k < last))
            def _():
                chain_take(n_z, k + 1, *chain)

            @pl.when(inner & (k + 2 < n_z))
            def _():
                chain_take(n_z, k + 2, *chain)

            @pl.when(k < last)
            def _():
                nz = source(k + 1)
                rows_out(n_e, cap, k + 1, nz, zbuf.at[nz], pick_ref, rows, *out_args)

            rows_out_wait(n_e, cap, k, sz, rows, *out_args)
            fetch = pltpu.make_async_copy(xs_ref.at[sz], xt, in_sem.at[0])
            fetch.start()
            fetch.wait()
            load_y(far_ref.at[sz]).wait()

            @pl.when((k > 0) & (k < last))
            def _():
                store(k, tiles, 0).wait()

            @pl.when(k > 0)
            def _():
                for i in range(1, 5):
                    store(k, tiles, i).wait()

            result, dx, back, gated, dgp, dup = expert_tile(
                width,
                experts,
                me,
                xt[...].reshape(n_e * cap, -1),
                yt[...].reshape(n_e * cap, -1),
                wg_ref,
                wu_ref,
                wd_ref,
            )
            rt[...] = result.reshape(n_e, cap, -1)
            dxt[:, :, :width] = dx.reshape(n_e, cap, -1)
            dxt[:, :, width:] = back.reshape(n_e, cap, -1)
            git[...] = gated.reshape(n_e, cap, -1)
            dgt[...] = dgp.reshape(n_e, cap, -1)
            dut[...] = dup.reshape(n_e, cap, -1)
            for i in range(5):
                store(k, tiles, i).start()

            @pl.when(k >= last - 1)
            def _():
                store(k, tiles, 0).wait()
                give(k)

        for i in range(1, 5):
            store(last, tiles, i).wait()

    def row_buffer(c):
        return pltpu.VMEM((n_e, cap, c), BF)

    pl.run_scoped(
        first_phase,
        pltpu.VMEM((n_z, n_e * cap, columns), BF),
        row_buffer(columns),
        row_buffer(width),
        row_buffer(width),
        row_buffer(columns),
        row_buffer(hidden),
        row_buffer(hidden),
        row_buffer(hidden),
    )
    chain_end(n_z, tok_ref, *chain)

    give(1)
    far_z = source(last)

    def give_result(i):
        oe = lax.rem(e + i, n_e)
        return remote(
            r_ref.at[far_z, oe], rret_ref.at[e], e_send.at[i], e_recv.at[e], (oe, z)
        )

    give(0)
    for i in range(1, n_e):
        give_result(i).start()
    own_result = pltpu.make_async_copy(r_ref.at[far_z, e], rret_ref.at[e], in_sem.at[0])
    own_result.start()
    size = 256
    count = width // size

    def second_phase(gis, dgs, dus, xc, yc, ggt, gut, gdt, rbuf):
        whole = ((gi_ref, gis), (dg_ref, dgs), (du_ref, dus))
        for i, (src, dst) in enumerate(whole):
            pltpu.make_async_copy(src, dst, g_sem.at[i]).start()

        def pairs(t):
            at = pl.ds(pl.multiple_of(t * size, size), size)
            slot = lax.rem(t, 2)
            copies = [
                pltpu.make_async_copy(xs_ref.at[:, :, :, at], xc.at[slot], t_sem.at[0, slot])
            ]
            for k in range(n_z):
                src = far_ref.at[source(k), :, :, at] if k else near_ref.at[:, :, at]
                copies.append(
                    pltpu.make_async_copy(
                        src, yc.at[slot, source(k)], t_sem.at[1 + k, slot]
                    )
                )
            return copies

        def results(t):
            at = pl.ds(pl.multiple_of(t * size, size), size)
            slot = lax.rem(t, 2)
            return [
                pltpu.make_async_copy(ggt.at[slot], gg_ref.at[at], w_sem.at[0, slot]),
                pltpu.make_async_copy(gut.at[slot], gu_ref.at[at], w_sem.at[1, slot]),
                pltpu.make_async_copy(gdt.at[slot], gd_ref.at[:, at], w_sem.at[2, slot]),
            ]

        def weight_tile(t):
            slot = lax.rem(t, 2)

            @pl.when(t + 1 < count)
            def _():
                for copy in pairs(t + 1):
                    copy.start()

            for copy in pairs(t):
                copy.wait()

            @pl.when(t >= 2)
            def _():
                for copy in results(t):
                    copy.wait()

            total = n_z * n_e * cap
            x = xc[slot].reshape(total, size)
            ggt[slot] = dot_first(x, dgs[...].reshape(total, hidden)).astype(BF)
            gut[slot] = dot_first(x, dus[...].reshape(total, hidden)).astype(BF)
            gdt[slot] = dot_first(
                gis[...].reshape(total, hidden), yc[slot].reshape(total, size)
            ).astype(BF)
            for copy in results(t):
                copy.start()

        def combine(k):
            sz = source(k)
            for i in range(1, n_e):
                oe = lax.rem(e + i, n_e)
                remote(
                    dx_ref.at[sz, oe],
                    ret_ref.at[sz, oe],
                    b_send.at[k, i],
                    b_recv.at[sz, oe],
                    (oe, z),
                ).wait()
            give_own(k).wait()
            unpick = unpick_ref[sz]
            cuts = pieces(columns)

            def fetch(p):
                start, wide = cuts[p]
                return pltpu.make_async_copy(
                    ret_ref.at[sz, :, :, start : start + wide],
                    rbuf.at[p % 2, :, :, 0:wide],
                    in_sem.at[1 + p % 2],
                )

            fetch(0).start()
            for p, (start, wide) in enumerate(cuts):
                if p + 1 < len(cuts):
                    fetch(p + 1).start()
                fetch(p).wait()
                block = rbuf[p % 2, :, :, 0:wide].reshape(n_e * cap, wide)
                zbuf[k, :, start : start + wide] = dot(unpick, block).astype(BF)

            @pl.when(k > 0)
            def _():
                remote(
                    zbuf.at[k], part_ref.at[z], p_send.at[k], p_recv.at[z], (e, sz)
                ).start()

            @pl.when(k == 0)
            def _():
                pltpu.make_async_copy(zbuf.at[k], part_ref.at[z], p_own).start()

        for copy in pairs(0):
            copy.start()
        for i, (src, dst) in enumerate(whole):
            pltpu.make_async_copy(src, dst, g_sem.at[i]).wait()
        share_of = count // n_z

        @pl.loop(0, n_z)
        def _(i):
            @pl.loop(0, share_of)
            def _(t):
                weight_tile(i * share_of + t)

            k = jnp.where(i == 0, last - 1, jnp.where(i == 1, last, last - i))
            combine(k)

        for t in (count - 2, count - 1):
            for copy in results(t):
                copy.wait()

    total_shape = (n_z, n_e, cap)
    pl.run_scoped(
        second_phase,
        pltpu.VMEM(total_shape + (hidden,), BF),
        pltpu.VMEM(total_shape + (hidden,), BF),
        pltpu.VMEM(total_shape + (hidden,), BF),
        pltpu.VMEM((2,) + total_shape + (size,), BF),
        pltpu.VMEM((2,) + total_shape + (size,), BF),
        pltpu.VMEM((2, size, hidden), BF),
        pltpu.VMEM((2, size, hidden), BF),
        pltpu.VMEM((2, hidden, size), BF),
        pltpu.VMEM((2, n_e, cap, pieces(columns)[0][1]), BF),
    )
    for i in range(1, n_e):
        oe = lax.rem(e + i, n_e)
        remote(
            r_ref.at[far_z, oe], rret_ref.at[oe], e_send.at[i], e_recv.at[oe], (oe, z)
        ).wait()
    own_result.wait()
    pltpu.make_async_copy(zbuf.at[0], part_ref.at[z], p_own).wait()
    for k in range(1, n_z):
        sz = ranked(z, k, n_z)
        remote(
            zbuf.at[k], part_ref.at[sz], p_send.at[k], p_recv.at[sz], (e, sz)
        ).wait()


def moe(n_e, n_z, cap, tok, picks, unpicks, dy_near, dy_far, wg, wu, wd):
    count, columns = tok.shape
    width, hidden = wg.shape

    def rows_of(c):
        return jax.ShapeDtypeStruct((n_z, n_e, cap, c), BF)

    return pl.pallas_call(
        partial(moe_kernel, n_e, n_z, cap),
        out_shape=(
            rows_of(columns),
            rows_of(width),
            rows_of(columns),
            rows_of(columns),
            jax.ShapeDtypeStruct((n_z, count, columns), BF),
            rows_of(hidden),
            rows_of(hidden),
            rows_of(hidden),
            jax.ShapeDtypeStruct((width, hidden), BF),
            jax.ShapeDtypeStruct((width, hidden), BF),
            jax.ShapeDtypeStruct((hidden, width), BF),
            jax.ShapeDtypeStruct((n_e, cap, width), BF),
        ),
        in_specs=[VM, VM, VM, ANY, ANY, VM, VM, VM],
        out_specs=(ANY,) * 12,
        scratch_shapes=[
            pltpu.VMEM((n_z, count, columns), BF),
            DMA((n_z + 1,)),
            DMA((n_z,)),
            DMA((n_z, n_e)),
            DMA((n_z, n_e)),
            DMA((n_z,)),
            DMA((3,)),
            DMA((5,)),
            DMA((n_z, n_e)),
            DMA((n_z, n_e)),
            DMA((n_z,)),
            DMA((n_z,)),
            DMA((n_z,)),
            DMA,
            DMA((n_e,)),
            DMA((n_e,)),
            DMA((3,)),
            DMA((1 + n_z, 2)),
            DMA((3, 2)),
        ],
        compiler_params=pltpu.CompilerParams(
            collective_id=13, has_side_effects=True, vmem_limit_bytes=63 * 1024 * 1024
        ),
        name="moe",
    )(tok, picks, unpicks, dy_near, dy_far, wg, wu, wd)


def layout(lengths, owners, device, row_count):
    seq_order = jnp.arange(lengths.shape[0], dtype=jnp.int32)
    owned = (owners == device).astype(jnp.int32)
    earlier = (seq_order[None, :] < seq_order[:, None]).astype(jnp.int32)
    starts = jnp.sum(earlier * (owned * lengths)[None, :], axis=1)
    row_index = jnp.arange(row_count, dtype=jnp.int32)
    inside = (
        owned[None, :]
        * (row_index[:, None] >= starts[None, :]).astype(jnp.int32)
        * (row_index[:, None] < (starts + lengths)[None, :]).astype(jnp.int32)
    )
    live_rows = jnp.sum(inside, axis=1)
    segment = jnp.sum(inside * (seq_order[None, :] + 1), axis=1) - 1
    token_position = jnp.sum(inside * (row_index[:, None] - starts[None, :]), axis=1)
    return (live_rows, segment, token_position)


def named_experts(routes, experts):
    return jnp.any(routes[..., None] == jnp.arange(experts, dtype=jnp.int32), axis=-2)


def slot_picks(n_e, n_z, z, cap, named, live):
    sources, count, experts = named.shape
    used = named & (live[:, :, None] > 0)
    order = jnp.arange(count)
    lower = (order[None, :] < order[:, None]).astype(BF)
    slots = jnp.einsum("ts,zse->zte", lower, used.astype(BF), preferred_element_type=F32)
    slots = jnp.where(used, slots, -1.0)
    column = jnp.arange(n_e * cap, dtype=jnp.int32)
    spread = (
        jnp.arange(experts, dtype=jnp.int32)[:, None] == (column // cap * n_z + z)[None, :]
    ).astype(BF)
    slots = slots.astype(BF)
    slot_ids = lax.rem(column, cap).astype(F32)
    picks = jnp.einsum("ec,ste->sct", spread, slots, preferred_element_type=F32)
    unpicks = jnp.einsum("ste,ec->stc", slots, spread, preferred_element_type=F32)
    return (
        (picks == slot_ids[None, :, None]).astype(BF),
        (unpicks == slot_ids).astype(BF),
    )


def split_float(values):
    high = values.astype(BF)
    return high, (values - high.astype(F32)).astype(BF)


def pad_lanes(values, lanes):
    return jnp.pad(values, ((0, 0), (0, lanes - values.shape[1])))


def local(
    n_e,
    n_z,
    tokens,
    cotangent,
    lengths,
    owners,
    routes,
    w_query,
    key_weight,
    value_weight,
    w_out,
    w_router,
    norm_gains,
    w_gate,
    w_up,
    w_down,
):
    n = n_e * n_z
    count, width = tokens.shape
    shard = w_query.shape[0]
    experts, top = w_router.shape[1], routes.shape[1]
    q_heads, kv_heads = w_query.shape[1] // HEAD, key_weight.shape[1] // HEAD
    heads = q_heads // n_e
    cap = count * top * 5 // (4 * experts)
    cap = -(-cap // 16) * 16
    e, z = place()

    wq_blocks = w_query.reshape(shard, n_e, heads * HEAD)
    sharing = n_e // kv_heads
    wk_blocks = jnp.repeat(key_weight.reshape(shard, kv_heads, HEAD), sharing, axis=1)
    wv_blocks = jnp.repeat(value_weight.reshape(shard, kv_heads, HEAD), sharing, axis=1)
    w_blocks = jnp.concatenate([wq_blocks, wk_blocks, wv_blocks], axis=2).transpose(1, 0, 2)
    router_rows = shard * experts // 128
    gain_rows = -(-norm_gains.shape[0] // 128)
    misc_rows = -(-(router_rows + gain_rows) // 16) * 16
    misc = jnp.concatenate(
        [
            w_router.reshape(-1),
            norm_gains,
            jnp.zeros((misc_rows - router_rows) * 128 - norm_gains.shape[0], BF),
        ]
    ).reshape(misc_rows, 128)
    routes_flat = routes.reshape(-1, 128)

    device = e * n_z + z
    plane_ids = jnp.arange(n_e, dtype=jnp.int32) * n_z + z
    column_ids = e * n_z + jnp.arange(n_z, dtype=jnp.int32)
    live_both, segment, position = jax.vmap(lambda d: layout(lengths, owners, d, count))(
        jnp.concatenate([plane_ids, column_ids])
    )
    live_all = live_both[n_e:]
    live_own = lax.dynamic_index_in_dim(live_all, z, keepdims=False)
    named_own = named_experts(routes, experts)
    small = n_e == 8 and n_z == 4
    if small:
        pick_own = slot_picks(n_e, n_z, z, cap, named_own[None], live_own[None])[0][0]
        xs, rts, w_all, wo_all, misc_all, dy_near = open_layer(
            n_e, n_z, cap, tokens, cotangent, routes_flat, w_blocks, w_out, misc, pick_own
        )
    else:
        xs, cts, rts, w_all, wo_all, misc_all = share(
            n_e, n_z, tokens, cotangent, routes_flat, w_blocks, w_out, misc
        )
    w_all = w_all.reshape(n * shard, -1)
    wo_all = wo_all.reshape(-1, width)
    router_w = misc_all[:, :router_rows].reshape(n * shard, experts)
    gains = (
        misc_all[:, router_rows:]
        .reshape(n, -1)[:, : norm_gains.shape[0]]
        .reshape(-1)
        .astype(F32)
    )
    gain_one = gains[None, :width]
    gain_two = gains[None, width : 2 * width]
    gain_heads = jnp.pad(gains[2 * width :].reshape(2, HEAD), ((0, 6), (0, 0)))

    half = HEAD // 2
    frequency = jnp.power(1000000.0, -2.0 * jnp.arange(half, dtype=F32) / HEAD)
    angles = position[:n_e].astype(F32)[:, :, None] * frequency
    turn_table = jnp.concatenate([jnp.cos(angles), jnp.sin(angles)], axis=-1)
    seg = segment[:n_e].astype(F32)[:, None, :]

    named_all = named_experts(rts.reshape(n_z, count, top), experts)
    picks, unpicks = slot_picks(n_e, n_z, z, cap, named_all, live_all)
    live = live_own.astype(F32)[:, None]
    named = named_own.astype(F32)

    shape = (turn_table, seg, w_all, wo_all, gain_one, gain_heads)
    if small:
        n1, raw, value, mix, attn_rows, dy_far = front(
            n_e, n_z, cap, heads, xs, cotangent, picks, *shape
        )
    else:
        dy_rows = send_rows(n_e, n_z, cap, cts, picks)
        n1, raw, value, mix, part = attend(n_e, heads, xs, *shape)
        attn_rows = plane_sum(n_e, n_z, part)

    inputs = tokens.astype(F32)
    hidden = inputs + live * attn_rows
    r_two = lax.rsqrt(jnp.mean(hidden * hidden, axis=-1, keepdims=True) + EPSILON)
    nu_two = hidden * r_two
    n2 = (nu_two * gain_two).astype(BF)
    logits = dot(n2, router_w)
    probs = jax.nn.softmax(logits, axis=-1)
    chosen = probs * named
    chosen_sum = jnp.sum(chosen, axis=1, keepdims=True)
    gates = chosen / chosen_sum
    lanes = -(-2 * experts // 128) * 128
    extra = pad_lanes(jnp.concatenate(split_float(gates), axis=1), lanes)
    tok = jnp.concatenate([n2, extra], axis=1)
    experts_w = (w_gate[0], w_up[0], w_down[0])
    if small:
        moved = moe(n_e, n_z, cap, tok, picks, unpicks, dy_near, dy_far, *experts_w)
        r_rows, dx_back = moved[1], moved[4]
        grad_gate, grad_up, grad_down = (a.astype(F32) for a in moved[8:11])
        r_far = moved[11]
    else:
        x_rows = dispatch(n_e, n_z, cap, tok, picks)
        r_rows, dx_rows, grad_gate, grad_up, grad_down = expert_run(
            n_z,
            experts,
            x_rows.reshape(-1, width + lanes),
            dy_rows.reshape(-1, width),
            *experts_w,
        )
        r_rows = r_rows.reshape(dy_rows.shape)
        dx_back = give_back(n_e, n_z, cap, dx_rows.reshape(x_rows.shape), unpicks, 6)

    dx_sum = jnp.sum(dx_back.astype(F32), axis=0)
    dgates = dx_sum[:, width : width + experts] + dx_sum[:, width + experts : width + 2 * experts]
    dchosen = (
        named * (dgates - jnp.sum(dgates * gates, axis=1, keepdims=True)) / chosen_sum
    )
    dlogits = (probs * (dchosen - jnp.sum(probs * dchosen, axis=1, keepdims=True))).astype(BF)
    grad_router = dot_first(n2, dlogits)
    dn2 = dx_sum[:, :width] + dot_last(dlogits, router_w)
    upstream = cotangent.astype(F32)
    grad_gain_two = jnp.sum(dn2 * nu_two, axis=0)
    scaled = dn2 * gain_two
    dhidden = upstream + r_two * (
        scaled - nu_two * jnp.mean(scaled * nu_two, axis=-1, keepdims=True)
    )
    da = (live * dhidden).astype(BF)
    gain_size = norm_gains.shape[0]
    grad_router = grad_router.reshape(n, router_rows, 128)
    if small:
        dn1, r_back, gws, goo, gor, gol, grs, gvs, *_ = back(
            n_e,
            n_z,
            cap,
            heads,
            da,
            r_rows,
            r_far,
            grad_router,
            n1,
            raw,
            value,
            mix,
            unpicks,
            grad_gain_two[None],
            *shape,
        )
        gw_sum = gws.astype(F32).transpose(0, 2, 1, 3).reshape(n_e, shard, -1)
        lower_sum, upper_sum = (
            jnp.where(came, lax.dynamic_index_in_dim(inbox, z, keepdims=False).astype(F32), 0.0)
            for came, inbox in ((z > 0, gor), (z < n_z - 1, gol))
        )
        grad_out = goo.astype(F32) + lower_sum + upper_sum
        grad_router = jnp.sum(grs, axis=0)
        grad_gains = lax.dynamic_slice_in_dim(
            jnp.sum(gvs, axis=0).reshape(-1), device * gain_size, gain_size
        )
    else:
        r_back = give_back(n_e, n_z, cap, r_rows, unpicks, 7)
        da_all = plane_gather(n_e, n_z, da)
        dn_part, gw, go, g1_part, gh_part = attend_back(
            n_e,
            heads,
            da_all,
            n1,
            raw,
            value,
            mix,
            turn_table,
            seg,
            w_all,
            wo_all,
            gain_heads,
        )
        gain_all = jnp.concatenate(
            [(g1_part / gain_one)[0], grad_gain_two, gh_part[0], gh_part[1]]
        ).reshape(n, -1)
        grad_rows = -(-(router_rows + gain_rows) // 8) * 8
        gain_all = pad_lanes(gain_all, (grad_rows - router_rows) * 128)
        gm = jnp.concatenate([grad_router, gain_all.reshape(n, -1, 128)], axis=1)
        dn1, gws, gos, gms = finish(
            n_e,
            n_z,
            dn_part,
            gw.reshape(n, shard, -1),
            go.reshape(n_z, -1, width),
            gm,
        )
        gw_sum = jnp.sum(gws.reshape(n_e, n_z, shard, -1).astype(F32), axis=1)
        grad_out = jnp.sum(gos.astype(F32), axis=0)
        gm_sum = jnp.sum(gms, axis=0)
        grad_router = gm_sum[:router_rows]
        grad_gains = gm_sum[router_rows:].reshape(-1)[:gain_size]
    block_out = (hidden + jnp.sum(r_back.astype(F32), axis=0)).astype(BF)
    r_one = lax.rsqrt(jnp.mean(inputs * inputs, axis=-1, keepdims=True) + EPSILON)
    nu_one = inputs * r_one
    scaled = dn1 * gain_one
    grad_tokens = dhidden + r_one * (
        scaled - nu_one * jnp.mean(scaled * nu_one, axis=-1, keepdims=True)
    )
    q_size = heads * HEAD
    grad_query = gw_sum[:, :, :q_size].transpose(1, 0, 2).reshape(shard, -1)
    kv_sum = gw_sum[:, :, q_size:].reshape(kv_heads, -1, shard, 2 * HEAD).sum(axis=1)
    grad_key = kv_sum[:, :, :HEAD].transpose(1, 0, 2).reshape(shard, -1)
    grad_value = kv_sum[:, :, HEAD:].transpose(1, 0, 2).reshape(shard, -1)
    return (
        block_out,
        grad_tokens,
        grad_query,
        grad_key,
        grad_value,
        grad_out,
        grad_router.reshape(shard, experts),
        grad_gains,
        grad_gate[None],
        grad_up[None],
        grad_down[None],
    )


def solution(mesh):
    both = ("expert", "fsdp")
    two, three = P(both, None), P(both, None, None)
    return jax.shard_map(
        partial(local, mesh.shape["expert"], mesh.shape["fsdp"]),
        mesh=mesh,
        in_specs=(two, two, P(), P(), two) + (two,) * 5 + (P(both),) + (three,) * 3,
        out_specs=(two,) * 7 + (P(both),) + (three,) * 3,
        check_vma=False,
    )
```

```python
from functools import partial

import jax
import jax.numpy as jnp
from jax import lax
from jax.experimental import pallas as pl
from jax.experimental.pallas import tpu as pltpu
from jax.sharding import PartitionSpec as P

EPSILON = 1e-06
MESH = pl.DeviceIdType.MESH
BF = jnp.bfloat16
F32 = jnp.float32
HEAD = 128
ANY = pl.BlockSpec(memory_space=pl.ANY)
VM = pl.BlockSpec(memory_space=pltpu.VMEM)
DMA = pltpu.SemaphoreType.DMA
BIG = 60 * 1024 * 1024


def dot(a, b):
    return lax.dot_general(a, b, (((1,), (0,)), ((), ())), preferred_element_type=F32)


def dot_last(a, b):
    return lax.dot_general(a, b, (((1,), (1,)), ((), ())), preferred_element_type=F32)


def dot_first(a, b):
    return lax.dot_general(a, b, (((0,), (0,)), ((), ())), preferred_element_type=F32)


def place():
    return lax.axis_index("expert"), lax.axis_index("fsdp")


def remote(src, dst, send, recv, where):
    return pltpu.make_async_remote_copy(
        src_ref=src,
        dst_ref=dst,
        send_sem=send,
        recv_sem=recv,
        device_id=where,
        device_id_type=MESH,
    )


def near(z, k, n_z):
    sign = 1 - 2 * (z // (n_z // 2))
    return lax.rem(z + sign * k + n_z, n_z)


def greet_all(n_e, n_z):
    e, z = place()
    me, n = e * n_z + z, n_e * n_z
    barrier = pltpu.get_barrier_semaphore()

    @pl.loop(1, n)
    def _(k):
        other = lax.rem(me + k, n)
        pl.semaphore_signal(
            barrier,
            inc=1,
            device_id=(other // n_z, lax.rem(other, n_z)),
            device_id_type=MESH,
        )

    pl.semaphore_wait(barrier, n - 1)


def greet(n_e, n_z, along_z):
    e, z = place()
    barrier = pltpu.get_barrier_semaphore()
    for k in range(1, n_e):
        pl.semaphore_signal(
            barrier, inc=1, device_id=(lax.rem(e + k, n_e), z), device_id_type=MESH
        )
    count = n_e - 1
    if along_z:
        for k in range(1, n_z):
            pl.semaphore_signal(
                barrier, inc=1, device_id=(e, lax.rem(z + k, n_z)), device_id_type=MESH
            )
        count += n_z - 1
    pl.semaphore_wait(barrier, count)


def ranked(z, k, n_z):
    half = n_z // 2
    top = z // half
    low = z + top * (n_z - 1 - 2 * z)
    at = k - low * jnp.where(k == 1, 1, 0)
    return at + top * (n_z - 1 - 2 * at)


def partner_chip(chip, k):
    low = lax.rem(lax.rem(chip, 2) + lax.rem(k, 2), 2)
    high = lax.rem(chip // 2 + k // 2, 2)
    return 2 * high + low


def chain_start(n_z, src, dst_at, send, recv):
    e, z = place()

    @pl.when(z + 1 < n_z)
    def _():
        remote(src, dst_at(z), send.at[0], recv.at[z], (e, z + 1)).start()

    @pl.when(z > 0)
    def _():
        remote(src, dst_at(z), send.at[1], recv.at[z], (e, z - 1)).start()


def chain_take(n_z, k, dst_at, send, recv):
    e, z = place()
    sz = ranked(z, k, n_z)
    block = dst_at(sz)
    step = jnp.where(sz < z, 1, -1)
    remote(block, block, send.at[1 + k], recv.at[sz], (e, sz)).wait_recv()

    @pl.when((z + step >= 0) & (z + step < n_z))
    def _():
        remote(block, block, send.at[1 + k], recv.at[sz], (e, z + step)).start()

    return sz


def chain_end(n_z, src, dst_at, send, recv):
    e, z = place()

    @pl.when(z + 1 < n_z)
    def _():
        remote(src, dst_at(z), send.at[0], recv.at[z], (e, z + 1)).wait_send()

    @pl.when(z > 0)
    def _():
        remote(src, dst_at(z), send.at[1], recv.at[z], (e, z - 1)).wait_send()

    for k in range(1, n_z):
        sz = ranked(z, k, n_z)
        step = jnp.where(sz < z, 1, -1)

        @pl.when((z + step >= 0) & (z + step < n_z))
        def _(k=k, sz=sz, step=step):
            block = dst_at(sz)
            remote(block, block, send.at[1 + k], recv.at[sz], (e, z + step)).wait_send()


def plane_gather_start(n_e, x_ref, out_ref, own, send, recv, sib_send, sib_recv):
    e, z = place()
    nc, chip, core = n_e // 2, e // 2, lax.rem(e, 2)
    pltpu.make_async_copy(x_ref, out_ref.at[e], own).start()
    for k in range(1, nc):
        j = lax.rem(chip + k, nc)
        remote(
            x_ref, out_ref.at[e], send.at[k], recv.at[chip], (2 * j + core, z)
        ).start()
    remote(
        x_ref, out_ref.at[e], sib_send.at[0], sib_recv.at[chip], (2 * chip + 1 - core, z)
    ).start()


def plane_gather_end(n_e, x_ref, out_ref, own, send, recv, sib_send, sib_recv):
    e, z = place()
    nc, chip, core = n_e // 2, e // 2, lax.rem(e, 2)
    sib = (2 * chip + 1 - core, z)
    for k in range(1, nc):
        j = lax.rem(chip + nc - k, nc)
        block = out_ref.at[2 * j + core]
        remote(x_ref, block, send.at[k], recv.at[j], (2 * j + core, z)).wait()
        remote(block, block, sib_send.at[k], sib_recv.at[j], sib).start()
    for k in range(nc):
        j = lax.rem(chip + nc - k, nc)
        block = out_ref.at[2 * j + 1 - core]
        remote(x_ref, block, sib_send.at[k], sib_recv.at[j], sib).wait()
    pltpu.make_async_copy(x_ref, out_ref.at[e], own).wait()


def share_kernel(
    n_e,
    n_z,
    x_ref,
    ct_ref,
    rt_ref,
    wq_ref,
    wo_ref,
    mi_ref,
    xs_ref,
    cts_ref,
    rts_ref,
    wqs_ref,
    wos_ref,
    mis_ref,
    own,
    x_send,
    x_recv,
    sib_send,
    sib_recv,
    z_send,
    z_recv,
    a_send,
    a_recv,
):
    e, z = place()
    n, me = n_e * n_z, e * n_z + z
    greet_all(n_e, n_z)
    gather = (n_e, x_ref, xs_ref, own.at[0], x_send, x_recv, sib_send, sib_recv)
    plane_gather_start(*gather)

    def other_of(k):
        other = lax.rem(me + k, n)
        return other, other // n_z, lax.rem(other, n_z)

    @pl.loop(1, n)
    def _(k):
        other, oe, oz = other_of(k)
        remote(
            wq_ref.at[oe], wqs_ref.at[me], a_send.at[0, k], a_recv.at[0, me], (oe, oz)
        ).start()
        remote(
            mi_ref, mis_ref.at[me], a_send.at[1, k], a_recv.at[1, me], (oe, oz)
        ).start()

    along = ((rt_ref, rts_ref), (wo_ref, wos_ref), (ct_ref, cts_ref))
    for i, (src, dst) in enumerate(along):
        for k in range(1, n_z):
            oz = near(z, k, n_z)
            remote(src, dst.at[z], z_send.at[i, k], z_recv.at[i, z], (e, oz)).start()
        pltpu.make_async_copy(src, dst.at[z], own.at[1 + i]).start()
    pltpu.make_async_copy(wq_ref.at[e], wqs_ref.at[me], own.at[4]).start()
    pltpu.make_async_copy(mi_ref, mis_ref.at[me], own.at[5]).start()

    plane_gather_end(*gather)

    @pl.loop(1, n)
    def _(k):
        other, oe, oz = other_of(k)
        remote(
            wq_ref.at[oe],
            wqs_ref.at[other],
            a_send.at[0, k],
            a_recv.at[0, other],
            (oe, oz),
        ).wait()
        remote(
            mi_ref, mis_ref.at[other], a_send.at[1, k], a_recv.at[1, other], (oe, oz)
        ).wait()

    for i, (src, dst) in enumerate(along):
        for k in range(1, n_z):
            oz = near(z, k, n_z)
            remote(src, dst.at[oz], z_send.at[i, k], z_recv.at[i, oz], (e, oz)).wait()
        pltpu.make_async_copy(src, dst.at[z], own.at[1 + i]).wait()
    pltpu.make_async_copy(wq_ref.at[e], wqs_ref.at[me], own.at[4]).wait()
    pltpu.make_async_copy(mi_ref, mis_ref.at[me], own.at[5]).wait()


def share(n_e, n_z, tokens, cotangent, routes, wq, wo, misc):
    n, nc = n_e * n_z, n_e // 2

    def like(lead, a):
        return jax.ShapeDtypeStruct((lead,) + a.shape, a.dtype)

    return pl.pallas_call(
        partial(share_kernel, n_e, n_z),
        out_shape=(
            like(n_e, tokens),
            like(n_z, cotangent),
            like(n_z, routes),
            like(n, wq[0]),
            like(n_z, wo),
            like(n, misc),
        ),
        in_specs=[ANY] * 6,
        out_specs=(ANY,) * 6,
        scratch_shapes=[
            DMA((6,)),
            DMA((nc,)),
            DMA((nc,)),
            DMA((nc,)),
            DMA((nc,)),
            DMA((3, n_z)),
            DMA((3, n_z)),
            DMA((2, n)),
            DMA((2, n)),
        ],
        compiler_params=pltpu.CompilerParams(collective_id=1, has_side_effects=True),
        name="share",
    )(tokens, cotangent, routes, wq, wo, misc)


def plane_sum_body(
    n_e, part_ref, total_ref, mine, sib, far, own, send, recv, sib_send, sib_recv
):
    e, z = place()
    nc, chip, core = n_e // 2, e // 2, lax.rem(e, 2)
    rows = total_ref.shape[0]
    step = 32
    other = (2 * chip + 1 - core, z)
    for k in range(nc):
        j = lax.rem(chip + 1 + k, nc)
        remote(
            part_ref.at[2 * j + 1 - core],
            sib.at[j],
            sib_send.at[j],
            sib_recv.at[j],
            other,
        ).start()
        pltpu.make_async_copy(part_ref.at[2 * j + core], mine.at[j], own.at[j]).start()
    for k in range(nc):
        j = lax.rem(chip + 1 + k, nc)
        remote(
            part_ref.at[2 * j + 1 - core],
            sib.at[j],
            sib_send.at[j],
            sib_recv.at[j],
            other,
        ).wait()
        pltpu.make_async_copy(part_ref.at[2 * j + core], mine.at[j], own.at[j]).wait()
        if k < nc - 1:

            @pl.loop(0, rows, step=step)
            def _(r, j=j):
                at = pl.ds(pl.multiple_of(r, step), step)
                mine[j, at, :] = (
                    mine[j, at, :].astype(F32) + sib[j, at, :].astype(F32)
                ).astype(BF)

            remote(
                mine.at[j], far.at[chip], send.at[j], recv.at[chip], (2 * j + core, z)
            ).start()
        else:

            @pl.loop(0, rows, step=step)
            def _(r, j=j):
                at = pl.ds(pl.multiple_of(r, step), step)
                total_ref[at, :] = mine[j, at, :].astype(F32) + sib[j, at, :].astype(F32)

    for k in range(1, nc):
        j = lax.rem(chip + nc - k, nc)
        remote(
            mine.at[j], far.at[j], send.at[j], recv.at[j], (2 * j + core, z)
        ).wait()

        @pl.loop(0, rows, step=step)
        def _(r, j=j):
            at = pl.ds(pl.multiple_of(r, step), step)
            total_ref[at, :] += far[j, at, :].astype(F32)


def plane_sum_scratch(n_e, part):
    nc = n_e // 2
    block = (nc,) + part.shape[1:]
    return [pltpu.VMEM(block, BF)] * 3 + [DMA((nc,))] * 5


def plane_sum_kernel(n_e, n_z, part_ref, total_ref, *scratch):
    greet(n_e, n_z, False)
    plane_sum_body(n_e, part_ref, total_ref, *scratch)


def plane_sum(n_e, n_z, part):
    return pl.pallas_call(
        partial(plane_sum_kernel, n_e, n_z),
        out_shape=jax.ShapeDtypeStruct(part.shape[1:], F32),
        in_specs=[ANY],
        out_specs=VM,
        scratch_shapes=plane_sum_scratch(n_e, part),
        compiler_params=pltpu.CompilerParams(
            collective_id=2, has_side_effects=True, vmem_limit_bytes=BIG
        ),
        name="plane_sum",
    )(part)


def plane_gather_kernel(n_e, n_z, x_ref, out_ref, *sems):
    greet(n_e, n_z, False)
    plane_gather_start(n_e, x_ref, out_ref, *sems)
    plane_gather_end(n_e, x_ref, out_ref, *sems)


def plane_gather(n_e, n_z, x):
    nc = n_e // 2
    return pl.pallas_call(
        partial(plane_gather_kernel, n_e, n_z),
        out_shape=jax.ShapeDtypeStruct((n_e,) + x.shape, x.dtype),
        in_specs=[ANY],
        out_specs=ANY,
        scratch_shapes=[DMA] + [DMA((nc,))] * 4,
        compiler_params=pltpu.CompilerParams(collective_id=3, has_side_effects=True),
        name="plane_gather",
    )(x)


def pieces(columns, wide=512):
    cuts = list(range(0, columns - columns % wide, wide)) + [columns - columns % wide]
    spans = [(a, b - a) for a, b in zip(cuts, cuts[1:])]
    if columns % wide:
        spans.append((cuts[-1], columns % wide))
    return spans


def rows_out(n_e, cap, k, sz, src, d_ref, rows, out_ref, own, send, recv):
    e, z = place()
    pick = d_ref[sz]
    for start, size in pieces(src.shape[-1]):
        rows[k, :, start : start + size] = dot(pick, src[:, start : start + size]).astype(BF)
    for i in range(1, n_e + 1):
        oe = lax.rem(e + i, n_e)
        block = rows.at[k, pl.ds(pl.multiple_of(oe * cap, 16), cap), :]
        if i < n_e:
            remote(block, out_ref.at[sz, e], send.at[k, i], recv.at[sz, e], (oe, z)).start()
        else:
            pltpu.make_async_copy(block, out_ref.at[sz, e], own.at[k]).start()


def rows_out_wait(n_e, cap, k, sz, rows, out_ref, own, send, recv):
    e, z = place()
    for i in range(1, n_e + 1):
        oe = lax.rem(e + i, n_e)
        at = pl.ds(pl.multiple_of(oe * cap, 16), cap)
        block = rows.at[k, at, :]
        if i < n_e:
            remote(
                block, out_ref.at[sz, oe], send.at[k, i], recv.at[sz, oe], (oe, z)
            ).wait()
        else:
            pltpu.make_async_copy(block, out_ref.at[sz, e], own.at[k]).wait()


def open_kernel(
    n_e,
    n_z,
    cap,
    x_ref,
    ct_ref,
    rt_ref,
    wq_ref,
    wo_ref,
    mi_ref,
    pick_ref,
    xs_ref,
    rts_ref,
    wqs_ref,
    wos_ref,
    mis_ref,
    dy_ref,
    rows,
    own,
    x_send,
    x_recv,
    sib_send,
    sib_recv,
    w_send,
    w_recv,
    zw_send,
    zw_recv,
    zo_send,
    zo_recv,
    zr_send,
    zr_recv,
    m_send,
    m_recv,
    r_send,
    r_recv,
):
    e, z = place()
    n, me = n_e * n_z, e * n_z + z
    greet_all(n_e, n_z)

    def plane_peer(i):
        return lax.rem(e + i, n_e)

    for i in range(1, n_e):
        oe = plane_peer(i)
        remote(
            wq_ref.at[oe], wqs_ref.at[e, z], w_send.at[i], w_recv.at[e], (oe, z)
        ).start()
    kept = (
        (wq_ref.at[e], wqs_ref.at[e, z]),
        (wo_ref, wos_ref.at[z]),
        (rt_ref, rts_ref.at[z]),
        (mi_ref, mis_ref.at[me]),
    )
    for i, (src, dst) in enumerate(kept):
        pltpu.make_async_copy(src, dst, own.at[i]).start()
    out_chain = (lambda s: wos_ref.at[s], zo_send, zo_recv)
    chain_start(n_z, wo_ref, *out_chain)
    for k in range(1, n_z):
        oz = near(z, k, n_z)
        remote(rt_ref, rts_ref.at[z], zr_send.at[k], zr_recv.at[z], (e, oz)).start()

    def other_of(k):
        other = lax.rem(me + k, n)
        return other, (other // n_z, lax.rem(other, n_z))

    @pl.loop(1, n)
    def _(k):
        other, where = other_of(k)
        remote(mi_ref, mis_ref.at[me], m_send.at[k], m_recv.at[me], where).start()

    gather = (n_e, x_ref, xs_ref, own.at[4], x_send, x_recv, sib_send, sib_recv)
    plane_gather_start(*gather)
    pick = pick_ref[...]
    for start, size in pieces(ct_ref.shape[-1]):
        rows[:, start : start + size] = dot(pick, ct_ref[:, start : start + size]).astype(BF)
    for i in range(1, n_e + 1):
        oe = plane_peer(i)
        block = rows.at[pl.ds(pl.multiple_of(oe * cap, 16), cap), :]
        if i < n_e:
            remote(block, dy_ref.at[e], r_send.at[i], r_recv.at[e], (oe, z)).start()
        else:
            pltpu.make_async_copy(block, dy_ref.at[e], own.at[5]).start()

    for i in range(1, n_e):
        oe = plane_peer(i)
        remote(
            wq_ref.at[oe], wqs_ref.at[oe, z], w_send.at[i], w_recv.at[oe], (oe, z)
        ).wait()
    pltpu.make_async_copy(*kept[0], own.at[0]).wait()
    in_chain = (lambda s: wqs_ref.at[:, s], zw_send, zw_recv)
    chain_start(n_z, wqs_ref.at[:, z], *in_chain)
    for k in range(1, n_z):
        chain_take(n_z, k, *out_chain)
        chain_take(n_z, k, *in_chain)
        if k == n_z - 2:
            plane_gather_end(*gather)
    chain_end(n_z, wo_ref, *out_chain)
    chain_end(n_z, wqs_ref.at[:, z], *in_chain)
    for k in range(1, n_z):
        oz = near(z, k, n_z)
        remote(rt_ref, rts_ref.at[oz], zr_send.at[k], zr_recv.at[oz], (e, oz)).wait()

    @pl.loop(1, n)
    def _(k):
        other, where = other_of(k)
        remote(mi_ref, mis_ref.at[other], m_send.at[k], m_recv.at[other], where).wait()

    for i in range(1, n_e + 1):
        oe = plane_peer(i)
        block = rows.at[pl.ds(pl.multiple_of(oe * cap, 16), cap), :]
        if i < n_e:
            remote(block, dy_ref.at[oe], r_send.at[i], r_recv.at[oe], (oe, z)).wait()
        else:
            pltpu.make_async_copy(block, dy_ref.at[e], own.at[5]).wait()
    for i, (src, dst) in enumerate(kept):
        if i:
            pltpu.make_async_copy(src, dst, own.at[i]).wait()


def open_layer(n_e, n_z, cap, tokens, cotangent, routes, wq, wo, misc, pick):
    n, nc = n_e * n_z, n_e // 2
    _, shard, columns = wq.shape
    width = tokens.shape[1]

    def like(lead, a):
        return jax.ShapeDtypeStruct((lead,) + a.shape, a.dtype)

    return pl.pallas_call(
        partial(open_kernel, n_e, n_z, cap),
        out_shape=(
            like(n_e, tokens),
            like(n_z, routes),
            jax.ShapeDtypeStruct((n_e, n_z, shard, columns), BF),
            like(n_z, wo),
            like(n, misc),
            jax.ShapeDtypeStruct((n_e, cap, width), BF),
        ),
        in_specs=[ANY, VM] + [ANY] * 4 + [VM],
        out_specs=(ANY,) * 6,
        scratch_shapes=[
            pltpu.VMEM((n_e * cap, width), BF),
            DMA((6,)),
            DMA((nc,)),
            DMA((nc,)),
            DMA((nc,)),
            DMA((nc,)),
            DMA((n_e,)),
            DMA((n_e,)),
            DMA((n_z + 1,)),
            DMA((n_z,)),
            DMA((n_z + 1,)),
            DMA((n_z,)),
            DMA((n_z,)),
            DMA((n_z,)),
            DMA((n,)),
            DMA((n,)),
            DMA((n_e,)),
            DMA((n_e,)),
        ],
        compiler_params=pltpu.CompilerParams(
            collective_id=11, has_side_effects=True, vmem_limit_bytes=BIG
        ),
        name="open_layer",
    )(tokens, cotangent, routes, wq, wo, misc, pick)


def dispatch_kernel(
    n_e,
    n_z,
    cap,
    tok_ref,
    d_ref,
    out_ref,
    zbuf,
    rows,
    own,
    z_send,
    z_recv,
    send,
    recv,
):
    e, z = place()
    greet(n_e, n_z, True)
    chain = (lambda s: zbuf.at[s], z_send, z_recv)
    chain_start(n_z, tok_ref, *chain)
    for k in range(n_z):
        sz = chain_take(n_z, k, *chain) if k else z
        src = zbuf.at[sz] if k else tok_ref
        rows_out(n_e, cap, k, sz, src, d_ref, rows, out_ref, own, send, recv)
    for k in range(n_z):
        sz = ranked(z, k, n_z) if k else z
        rows_out_wait(n_e, cap, k, sz, rows, out_ref, own, send, recv)
    chain_end(n_z, tok_ref, *chain)


def dispatch(n_e, n_z, cap, tok, picks):
    count, columns = tok.shape
    return pl.pallas_call(
        partial(dispatch_kernel, n_e, n_z, cap),
        out_shape=jax.ShapeDtypeStruct((n_z, n_e, cap, columns), BF),
        in_specs=[VM, VM],
        out_specs=ANY,
        scratch_shapes=[
            pltpu.VMEM((n_z, count, columns), BF),
            pltpu.VMEM((n_z, n_e * cap, columns), BF),
            DMA((n_z,)),
            DMA((n_z + 1,)),
            DMA((n_z,)),
            DMA((n_z, n_e)),
            DMA((n_z, n_e)),
        ],
        compiler_params=pltpu.CompilerParams(
            collective_id=4, has_side_effects=True, vmem_limit_bytes=BIG
        ),
        name="dispatch",
    )(tok, picks)


def send_kernel(n_e, n_z, cap, src_ref, d_ref, out_ref, rows, own, send, recv):
    e, z = place()
    greet(n_e, n_z, False)
    for k in range(n_z):
        sz = near(z, k, n_z)
        rows_out(n_e, cap, k, sz, src_ref.at[sz], d_ref, rows, out_ref, own, send, recv)
    for k in range(n_z):
        rows_out_wait(n_e, cap, k, near(z, k, n_z), rows, out_ref, own, send, recv)


def send_rows(n_e, n_z, cap, src, picks):
    columns = src.shape[-1]
    return pl.pallas_call(
        partial(send_kernel, n_e, n_z, cap),
        out_shape=jax.ShapeDtypeStruct((n_z, n_e, cap, columns), BF),
        in_specs=[VM, VM],
        out_specs=ANY,
        scratch_shapes=[
            pltpu.VMEM((n_z, n_e * cap, columns), BF),
            DMA((n_z,)),
            DMA((n_z, n_e)),
            DMA((n_z, n_e)),
        ],
        compiler_params=pltpu.CompilerParams(
            collective_id=5, has_side_effects=True, vmem_limit_bytes=BIG
        ),
        name="send_rows",
    )(src, picks)


def give_back_kernel(
    n_e,
    n_z,
    cap,
    y_ref,
    d_ref,
    out_ref,
    rbuf,
    pbuf,
    own,
    send,
    recv,
    z_own,
    z_send,
    z_recv,
):
    e, z = place()
    greet(n_e, n_z, True)
    order = list(range(n_z - 1, -1, -1))
    for k in order:
        sz = near(z, k, n_z)
        for i in range(1, n_e + 1):
            oe = lax.rem(e + i, n_e)
            if i < n_e:
                remote(
                    y_ref.at[sz, oe],
                    rbuf.at[sz, e],
                    send.at[k, i],
                    recv.at[sz, e],
                    (oe, z),
                ).start()
            else:
                pltpu.make_async_copy(y_ref.at[sz, e], rbuf.at[sz, e], own.at[k]).start()
    for k in order:
        sz = near(z, k, n_z)
        for i in range(1, n_e + 1):
            oe = lax.rem(e + i, n_e)
            if i < n_e:
                remote(
                    y_ref.at[sz, oe],
                    rbuf.at[sz, oe],
                    send.at[k, i],
                    recv.at[sz, oe],
                    (oe, z),
                ).wait()
            else:
                pltpu.make_async_copy(y_ref.at[sz, e], rbuf.at[sz, e], own.at[k]).wait()
        pick = d_ref[sz]
        for start, size in pieces(pbuf.shape[-1]):
            block = rbuf[sz, :, :, start : start + size].reshape(n_e * cap, size)
            pbuf[k, :, start : start + size] = dot(pick, block).astype(BF)
        if k:
            remote(
                pbuf.at[k], out_ref.at[z], z_send.at[k], z_recv.at[z], (e, sz)
            ).start()
        else:
            pltpu.make_async_copy(pbuf.at[k], out_ref.at[z], z_own).start()
    for k in order:
        sz = near(z, k, n_z)
        if k:
            remote(
                pbuf.at[k], out_ref.at[sz], z_send.at[k], z_recv.at[sz], (e, sz)
            ).wait()
        else:
            pltpu.make_async_copy(pbuf.at[k], out_ref.at[z], z_own).wait()


def give_back(n_e, n_z, cap, y, picks, number):
    columns = y.shape[-1]
    count = picks.shape[1]
    return pl.pallas_call(
        partial(give_back_kernel, n_e, n_z, cap),
        out_shape=jax.ShapeDtypeStruct((n_z, count, columns), BF),
        in_specs=[ANY, VM],
        out_specs=ANY,
        scratch_shapes=[
            pltpu.VMEM((n_z, n_e, cap, columns), BF),
            pltpu.VMEM((n_z, count, columns), BF),
            DMA((n_z,)),
            DMA((n_z, n_e)),
            DMA((n_z, n_e)),
            DMA,
            DMA((n_z,)),
            DMA((n_z,)),
        ],
        compiler_params=pltpu.CompilerParams(
            collective_id=number, has_side_effects=True, vmem_limit_bytes=BIG
        ),
        name="give_back",
    )(y, picks)


def finish_kernel(
    n_e,
    n_z,
    part_ref,
    gw_ref,
    go_ref,
    gm_ref,
    total_ref,
    gws_ref,
    gos_ref,
    gms_ref,
    own_g,
    a_send,
    a_recv,
    z_send,
    z_recv,
    *scratch,
):
    e, z = place()
    n, me = n_e * n_z, e * n_z + z
    greet_all(n_e, n_z)

    def other_of(k):
        other = lax.rem(me + k, n)
        return other, (other // n_z, lax.rem(other, n_z))

    @pl.loop(1, n)
    def _(k):
        other, where = other_of(k)
        remote(
            gw_ref.at[other], gws_ref.at[me], a_send.at[0, k], a_recv.at[0, me], where
        ).start()
        remote(
            gm_ref.at[other], gms_ref.at[me], a_send.at[1, k], a_recv.at[1, me], where
        ).start()

    for k in range(1, n_z):
        oz = near(z, k, n_z)
        remote(
            go_ref.at[oz], gos_ref.at[z], z_send.at[k], z_recv.at[z], (e, oz)
        ).start()
    mine = (
        (gw_ref.at[me], gws_ref.at[me]),
        (gm_ref.at[me], gms_ref.at[me]),
        (go_ref.at[z], gos_ref.at[z]),
    )
    for i, (src, dst) in enumerate(mine):
        pltpu.make_async_copy(src, dst, own_g.at[i]).start()

    plane_sum_body(n_e, part_ref, total_ref, *scratch)

    @pl.loop(1, n)
    def _(k):
        other, where = other_of(k)
        remote(
            gw_ref.at[other],
            gws_ref.at[other],
            a_send.at[0, k],
            a_recv.at[0, other],
            where,
        ).wait()
        remote(
            gm_ref.at[other],
            gms_ref.at[other],
            a_send.at[1, k],
            a_recv.at[1, other],
            where,
        ).wait()

    for k in range(1, n_z):
        oz = near(z, k, n_z)
        remote(
            go_ref.at[oz], gos_ref.at[oz], z_send.at[k], z_recv.at[oz], (e, oz)
        ).wait()
    for i, (src, dst) in enumerate(mine):
        pltpu.make_async_copy(src, dst, own_g.at[i]).wait()


def finish(n_e, n_z, part, gw, go, gm):
    n = n_e * n_z
    return pl.pallas_call(
        partial(finish_kernel, n_e, n_z),
        out_shape=(
            jax.ShapeDtypeStruct(part.shape[1:], F32),
            jax.ShapeDtypeStruct(gw.shape, gw.dtype),
            jax.ShapeDtypeStruct(go.shape, go.dtype),
            jax.ShapeDtypeStruct(gm.shape, gm.dtype),
        ),
        in_specs=[ANY] * 4,
        out_specs=(VM, ANY, ANY, ANY),
        scratch_shapes=[
            DMA((3,)),
            DMA((2, n)),
            DMA((2, n)),
            DMA((n_z,)),
            DMA((n_z,)),
        ]
        + plane_sum_scratch(n_e, part),
        compiler_params=pltpu.CompilerParams(
            collective_id=8, has_side_effects=True, vmem_limit_bytes=BIG
        ),
        name="finish",
    )(part, gw, go, gm)


def head_norm(u, gain):
    r = lax.rsqrt(jnp.mean(u * u, axis=-1, keepdims=True) + EPSILON)
    return u * r * gain


def turn(u, cos, sin):
    return u * cos + pltpu.roll(u, HEAD // 2, 1) * sin


def turn_back(u, cos, sin):
    return u * cos - pltpu.roll(u, HEAD // 2, 1) * sin


def turns(table):
    other = pltpu.roll(table, HEAD // 2, 1)
    first = lax.broadcasted_iota(jnp.int32, table.shape, 1) < HEAD // 2
    return jnp.where(first, table, other), jnp.where(first, -other, table)


def may_see(seg_row):
    count = seg_row.shape[1]
    i = lax.broadcasted_iota(jnp.int32, (count, count), 0)
    j = lax.broadcasted_iota(jnp.int32, (count, count), 1)
    seg_col = jnp.sum(jnp.where(i == j, seg_row, 0.0), axis=1, keepdims=True)
    return ((seg_col == seg_row) & (seg_col >= 0) & (j <= i)) | (i == j)


def probabilities(q, k, allowed):
    scores = jnp.where(allowed, dot_last(q, k) * (HEAD**-0.5), -1e30)
    peak = jnp.max(scores, axis=-1, keepdims=True)
    weight = jnp.exp(scores - peak)
    return weight / jnp.sum(weight, axis=-1, keepdims=True)


def attend_block(
    heads, x, cos, sin, allowed, w_ref, wo_ref, g1_ref, gh_ref, n1_ref, raw_ref, v_ref, mix_ref
):
    x = x.astype(F32)
    r = lax.rsqrt(jnp.mean(x * x, axis=-1, keepdims=True) + EPSILON)
    n1 = (x * r * g1_ref[...]).astype(BF)
    n1_ref[...] = n1
    raw = dot(n1, w_ref[...])
    qk = (heads + 1) * HEAD
    raw_ref[...] = raw[:, :qk]
    value = raw[:, qk:].astype(BF)
    v_ref[...] = value
    gq, gk = gh_ref[0:1, :], gh_ref[1:2, :]
    key = turn(head_norm(raw[:, heads * HEAD : qk], gk), cos, sin).astype(BF)
    for h in range(heads):
        at = slice(h * HEAD, (h + 1) * HEAD)
        query = turn(head_norm(raw[:, at], gq), cos, sin).astype(BF)
        weight = probabilities(query, key, allowed).astype(BF)
        mix_ref[:, at] = dot(weight, value).astype(BF)
    return dot(mix_ref[...], wo_ref[...]).astype(BF)


def attend_kernel(
    heads,
    x_ref,
    turn_ref,
    seg_ref,
    w_ref,
    wo_ref,
    g1_ref,
    gh_ref,
    n1_ref,
    raw_ref,
    v_ref,
    mix_ref,
    part_ref,
):
    part_ref[0] = attend_block(
        heads,
        x_ref[0],
        *turns(turn_ref[0]),
        may_see(seg_ref[0]),
        w_ref,
        wo_ref,
        g1_ref,
        gh_ref,
        n1_ref.at[0],
        raw_ref.at[0],
        v_ref.at[0],
        mix_ref.at[0],
    )


def attend(n_e, heads, xs, turn_table, seg, w, wo, g1, gh):
    _, count, width = xs.shape

    def block(*shape):
        return pl.BlockSpec((1,) + shape, lambda b: (b, 0, 0))

    def whole(*shape):
        return pl.BlockSpec(shape, lambda b: (0, 0))

    outs = ((width, BF), ((heads + 1) * HEAD, F32), (HEAD, BF), (heads * HEAD, BF), (width, BF))
    return pl.pallas_call(
        partial(attend_kernel, heads),
        grid=(n_e,),
        out_shape=tuple(jax.ShapeDtypeStruct((n_e, count, c), t) for c, t in outs),
        in_specs=[
            block(count, width),
            block(count, HEAD),
            block(1, count),
            whole(*w.shape),
            whole(*wo.shape),
            whole(*g1.shape),
            whole(*gh.shape),
        ],
        out_specs=tuple(block(count, c) for c, _ in outs),
        compiler_params=pltpu.CompilerParams(vmem_limit_bytes=BIG),
        name="attend",
    )(xs, turn_table, seg, w, wo, g1, gh)


def front_kernel(
    n_e,
    n_z,
    cap,
    heads,
    xs_ref,
    ct_ref,
    pick_ref,
    turn_ref,
    seg_ref,
    w_ref,
    wo_ref,
    g1_ref,
    gh_ref,
    n1_ref,
    raw_ref,
    v_ref,
    mix_ref,
    total_ref,
    dy_ref,
    xbuf,
    n1buf,
    rawbuf,
    vbuf,
    mixbuf,
    away,
    mine,
    sib,
    far,
    via,
    zbuf,
    rows,
    x_sem,
    o_sem,
    sib_send,
    sib_recv,
    send,
    recv,
    via_send,
    via_recv,
    z_send,
    z_recv,
    r_send,
    r_recv,
    r_own,
):
    e, z = place()
    nc, chip, core = n_e // 2, e // 2, lax.rem(e, 2)
    sibling = (2 * chip + 1 - core, z)
    count = total_ref.shape[0]
    step = 32
    greet(n_e, n_z, True)
    chain = (lambda s: zbuf.at[s], z_send, z_recv)
    chain_start(n_z, ct_ref, *chain)

    def blocks(k):
        j = partner_chip(chip, nc - 1 - k)
        return j, (2 * j + 1 - core, 2 * j + core)

    half = count // 2

    def via_copy(p):
        rows = pl.ds(pl.multiple_of(p * half, half), half)
        there = (2 * partner_chip(chip, p + 1) + core, z)
        return remote(
            mine.at[partner_chip(chip, nc - 1), rows, :],
            via.at[p],
            via_send.at[p],
            via_recv.at[p],
            there,
        )

    def far_copy(p):
        j = partner_chip(chip, 2 - p)
        return remote(mine.at[j], far.at[p], send.at[p], recv.at[p], (2 * j + core, z))

    def load(b, slot):
        return pltpu.make_async_copy(xs_ref.at[b], xbuf.at[slot], x_sem.at[slot])

    def stores(b, slot):
        pairs = ((n1buf, n1_ref), (rawbuf, raw_ref), (vbuf, v_ref), (mixbuf, mix_ref))
        return [
            pltpu.make_async_copy(src.at[slot], dst.at[b], o_sem.at[i, slot])
            for i, (src, dst) in enumerate(pairs)
        ]

    for slot in range(2):
        load(blocks(0)[1][slot], slot).start()

    @pl.loop(0, nc)
    def _(k):
        j, pair = blocks(k)
        for slot, b in enumerate(pair):
            load(b, slot).wait()

            @pl.when(k > 0)
            def _(b=b, slot=slot):
                for copy in stores(b, slot):
                    copy.wait()

            part = attend_block(
                heads,
                xbuf[slot],
                *turns(turn_ref[b]),
                may_see(seg_ref[b]),
                w_ref,
                wo_ref,
                g1_ref,
                gh_ref,
                n1buf.at[slot],
                rawbuf.at[slot],
                vbuf.at[slot],
                mixbuf.at[slot],
            )
            for copy in stores(b, slot):
                copy.start()

            @pl.when(k < nc - 1)
            def _(slot=slot):
                load(blocks(k + 1)[1][slot], slot).start()

            if slot == 0:
                away[j] = part
                remote(
                    away.at[j], sib.at[j], sib_send.at[j], sib_recv.at[j], sibling
                ).start()
            else:
                mine[j] = part
        remote(away.at[j], sib.at[j], sib_send.at[j], sib_recv.at[j], sibling).wait()

        @pl.when(k < nc - 1)
        def _():
            @pl.loop(0, count, step=step)
            def _(r):
                at = pl.ds(pl.multiple_of(r, step), step)
                mine[j, at, :] = (
                    mine[j, at, :].astype(F32) + sib[j, at, :].astype(F32)
                ).astype(BF)

        @pl.when(k == 0)
        def _():
            for p in range(2):
                via_copy(p).start()

        @pl.when((k > 0) & (k < nc - 1))
        def _():
            via_copy(k - 1).wait_recv()

            @pl.loop(0, half, step=step)
            def _(r):
                at = pl.ds(pl.multiple_of((k - 1) * half + r, step), step)
                came = via[k - 1, pl.ds(pl.multiple_of(r, step), step), :]
                mine[j, at, :] = (mine[j, at, :].astype(F32) + came.astype(F32)).astype(BF)

            far_copy(k - 1).start()

        @pl.when((k > 0) & (k < n_z))
        def _():
            sz = chain_take(n_z, k, *chain)
            rows_out(
                n_e,
                cap,
                k - 1,
                sz,
                zbuf.at[sz],
                pick_ref,
                rows,
                dy_ref,
                r_own,
                r_send,
                r_recv,
            )

    @pl.loop(0, count, step=step)
    def _(r):
        at = pl.ds(pl.multiple_of(r, step), step)
        total_ref[at, :] = mine[chip, at, :].astype(F32) + sib[chip, at, :].astype(F32)

    for p in range(2):
        far_copy(p).wait()

        @pl.loop(0, count, step=step)
        def _(r, p=p):
            at = pl.ds(pl.multiple_of(r, step), step)
            total_ref[at, :] += far[p, at, :].astype(F32)

        via_copy(p).wait_send()

    for slot, b in enumerate(blocks(nc - 1)[1]):
        for copy in stores(b, slot):
            copy.wait()
    for k in range(1, n_z):
        rows_out_wait(
            n_e, cap, k - 1, ranked(z, k, n_z), rows, dy_ref, r_own, r_send, r_recv
        )
    chain_end(n_z, ct_ref, *chain)


def front(n_e, n_z, cap, heads, xs, ct, picks, turn_table, seg, w, wo, g1, gh):
    _, count, width = xs.shape
    nc = n_e // 2
    outs = ((width, BF), ((heads + 1) * HEAD, F32), (HEAD, BF), (heads * HEAD, BF))
    bufs = [pltpu.VMEM((2, count, width), BF)]
    bufs += [pltpu.VMEM((2, count, c), t) for c, t in outs]
    bufs += [pltpu.VMEM((nc, count, width), BF)] * 3
    bufs += [pltpu.VMEM((2, count, width), BF), pltpu.VMEM((2, count // 2, width), BF)]
    bufs += [
        pltpu.VMEM((n_z, count, width), BF),
        pltpu.VMEM((n_z - 1, n_e * cap, width), BF),
    ]
    return pl.pallas_call(
        partial(front_kernel, n_e, n_z, cap, heads),
        out_shape=tuple(jax.ShapeDtypeStruct((n_e, count, c), t) for c, t in outs)
        + (
            jax.ShapeDtypeStruct((count, width), F32),
            jax.ShapeDtypeStruct((n_z, n_e, cap, width), BF),
        ),
        in_specs=[ANY] + [VM] * 8,
        out_specs=(ANY,) * 4 + (VM, ANY),
        scratch_shapes=bufs
        + [
            DMA((2,)),
            DMA((4, 2)),
            DMA((nc,)),
            DMA((nc,)),
            DMA((2,)),
            DMA((2,)),
            DMA((2,)),
            DMA((2,)),
            DMA((n_z + 1,)),
            DMA((n_z,)),
            DMA((n_z, n_e)),
            DMA((n_z, n_e)),
            DMA((n_z,)),
        ],
        compiler_params=pltpu.CompilerParams(
            collective_id=12, has_side_effects=True, vmem_limit_bytes=BIG
        ),
        name="front",
    )(xs, ct, picks, turn_table, seg, w, wo, g1, gh)


def norm_back(u, gain, dv):
    r = lax.rsqrt(jnp.mean(u * u, axis=-1, keepdims=True) + EPSILON)
    nu = u * r
    dgain = jnp.sum(dv * nu, axis=0, keepdims=True)
    scaled = dv * gain
    du = r * (scaled - nu * jnp.mean(scaled * nu, axis=-1, keepdims=True))
    return du, dgain


def attend_back_block(
    heads,
    da,
    n1,
    raw_ref,
    value,
    cos,
    sin,
    allowed,
    w_ref,
    wo_ref,
    gh_ref,
    dmix,
    dcat,
    g1_ref,
    ghg_ref,
):
    dmix[...] = dot_last(da, wo_ref[...]).astype(BF)
    gq, gk = gh_ref[0:1, :], gh_ref[1:2, :]
    qk = (heads + 1) * HEAD
    key_raw = raw_ref[:, heads * HEAD : qk]
    key = turn(head_norm(key_raw, gk), cos, sin).astype(BF)
    count = key.shape[0]
    dkey = jnp.zeros((count, HEAD), F32)
    dvalue = jnp.zeros((count, HEAD), F32)
    dgq = jnp.zeros((1, HEAD), F32)
    scale = HEAD**-0.5
    for h in range(heads):
        at = slice(h * HEAD, (h + 1) * HEAD)
        query_raw = raw_ref[:, at]
        query = turn(head_norm(query_raw, gq), cos, sin).astype(BF)
        weight = probabilities(query, key, allowed)
        dm = dmix[:, at]
        dweight = dot_last(dm, value)
        delta = jnp.sum(weight * dweight, axis=-1, keepdims=True)
        dscore = (weight * (dweight - delta)).astype(BF)
        dquery = dot(dscore, key) * scale
        dkey += dot_first(dscore, query) * scale
        dvalue += dot_first(weight.astype(BF), dm)
        du, dg = norm_back(query_raw, gq, turn_back(dquery, cos, sin))
        dcat[:, at] = du.astype(BF)
        dgq += dg
    du, dgk = norm_back(key_raw, gk, turn_back(dkey, cos, sin))
    dcat[:, heads * HEAD : qk] = du.astype(BF)
    dcat[:, qk:] = dvalue.astype(BF)
    ghg_ref[0:1, :] += dgq
    ghg_ref[1:2, :] += dgk
    dn = dot_last(dcat[...], w_ref[...])
    g1_ref[...] += jnp.sum(dn * n1.astype(F32), axis=0, keepdims=True)
    return dn.astype(BF)


def attend_back_kernel(
    heads,
    steps,
    da_ref,
    n1_ref,
    raw_ref,
    v_ref,
    mix_ref,
    turn_ref,
    seg_ref,
    w_ref,
    wo_ref,
    gh_ref,
    dn_ref,
    gw_ref,
    go_ref,
    g1_ref,
    ghg_ref,
    acc_w,
    acc_o,
    dcat,
    dmix,
):
    step = pl.program_id(0)

    @pl.when(step == 0)
    def _():
        acc_w[...] = jnp.zeros_like(acc_w)
        acc_o[...] = jnp.zeros_like(acc_o)
        g1_ref[...] = jnp.zeros_like(g1_ref)
        ghg_ref[...] = jnp.zeros_like(ghg_ref)

    da, n1 = da_ref[0], n1_ref[0]
    dn_ref[0] = attend_back_block(
        heads,
        da,
        n1,
        raw_ref.at[0],
        v_ref[0],
        *turns(turn_ref[0]),
        may_see(seg_ref[0]),
        w_ref,
        wo_ref,
        gh_ref,
        dmix,
        dcat,
        g1_ref,
        ghg_ref,
    )
    acc_w[...] += dot_first(n1, dcat[...])
    acc_o[...] += dot_first(mix_ref[0], da)

    @pl.when(step == steps - 1)
    def _():
        gw_ref[...] = acc_w[...].astype(BF)
        go_ref[...] = acc_o[...].astype(BF)


def attend_back(n_e, heads, da, n1, raw, v, mix, turn_table, seg, w, wo, gh):
    _, count, width = da.shape

    def block(*shape):
        return pl.BlockSpec((1,) + shape, lambda b: (b, 0, 0))

    def whole(*shape):
        return pl.BlockSpec(shape, lambda b: (0, 0))

    return pl.pallas_call(
        partial(attend_back_kernel, heads, n_e),
        grid=(n_e,),
        out_shape=(
            jax.ShapeDtypeStruct((n_e, count, width), BF),
            jax.ShapeDtypeStruct(w.shape, BF),
            jax.ShapeDtypeStruct(wo.shape, BF),
            jax.ShapeDtypeStruct((1, width), F32),
            jax.ShapeDtypeStruct((8, HEAD), F32),
        ),
        in_specs=[
            block(count, width),
            block(count, width),
            block(*raw.shape[1:]),
            block(count, HEAD),
            block(*mix.shape[1:]),
            block(count, HEAD),
            block(1, count),
            whole(*w.shape),
            whole(*wo.shape),
            whole(*gh.shape),
        ],
        out_specs=(
            block(count, width),
            whole(*w.shape),
            whole(*wo.shape),
            whole(1, width),
            whole(8, HEAD),
        ),
        scratch_shapes=[
            pltpu.VMEM(w.shape, F32),
            pltpu.VMEM(wo.shape, F32),
            pltpu.VMEM((count, (heads + 2) * HEAD), BF),
            pltpu.VMEM((count, heads * HEAD), BF),
        ],
        compiler_params=pltpu.CompilerParams(vmem_limit_bytes=BIG),
        name="attend_back",
    )(da, n1, raw, v, mix, turn_table, seg, w, wo, gh)


def back_kernel(
    n_e,
    n_z,
    cap,
    heads,
    da_ref,
    r_ref,
    rfar_ref,
    gr_ref,
    n1_ref,
    raw_ref,
    v_ref,
    mix_ref,
    unpick_ref,
    g2_ref,
    turn_ref,
    seg_ref,
    w_ref,
    wo_ref,
    g1_ref,
    gh_ref,
    total_ref,
    part_ref,
    gws_ref,
    goo_ref,
    gor_ref,
    gol_ref,
    grs_ref,
    gvs_ref,
    ret_ref,
    gwr_ref,
    gwl_ref,
    rsum,
    gplane,
    das,
    n1s,
    raws,
    vs,
    mixs,
    dcats,
    dmix,
    gsum,
    ghsum,
    gvec,
    gtotal,
    away,
    mine,
    sib,
    far,
    rbuf,
    gob,
    own,
    in_sem,
    raw_sem,
    d_send,
    d_recv,
    via_send,
    via_recv,
    ds_send,
    ds_recv,
    a_send,
    a_recv,
    b_send,
    b_recv,
    b_own,
    p_send,
    p_recv,
    o_send,
    or_recv,
    ol_recv,
    w_send,
    wr_recv,
    wl_recv,
    s_send,
    s_recv,
    t_sem,
    v_send,
    v_recv,
    vz_send,
    vz_recv,
    sib_send,
    sib_recv,
    send,
    recv,
):
    e, z = place()
    n, me = n_e * n_z, e * n_z + z
    nc, chip, core = n_e // 2, e // 2, lax.rem(e, 2)
    sibling = (2 * chip + 1 - core, z)
    count, width = total_ref.shape
    shard = width // n
    head_rows = mixs.shape[-1] // n_z
    step = 32
    greet_all(n_e, n_z)

    def other_of(k):
        other = lax.rem(me + k, n)
        return other, (other // n_z, lax.rem(other, n_z))

    def far_chip(k):
        return (2 * partner_chip(chip, k) + core, z)

    def give_da(k):
        return remote(
            da_ref, das.at[e], d_send.at[k], d_recv.at[chip], far_chip(k)
        )

    def via_da(b, p):
        half = count // 2
        block = das.at[b, pl.ds(pl.multiple_of(p * half, half), half), :]
        return remote(block, block, via_send.at[p], via_recv.at[p], far_chip(2 - p))

    remote(da_ref, das.at[e], ds_send.at[0], ds_recv.at[chip], sibling).start()
    for k in range(1, nc - 1):
        give_da(k).start()
    own_da = pltpu.make_async_copy(da_ref, das.at[e], own.at[0])
    own_da.start()

    @pl.loop(1, n)
    def _(k):
        other, where = other_of(k)
        remote(
            gr_ref.at[other], grs_ref.at[me], a_send.at[k], a_recv.at[me], where
        ).start()

    own_gr = pltpu.make_async_copy(gr_ref.at[me], grs_ref.at[me], own.at[1])
    own_gr.start()
    for i, (src, dst) in enumerate(((n1_ref, n1s), (v_ref, vs), (mix_ref, mixs))):
        pltpu.make_async_copy(src, dst, in_sem.at[i]).start()

    def load_raw(b, slot):
        return pltpu.make_async_copy(raw_ref.at[b], raws.at[slot], raw_sem.at[slot])

    def blocks(k):
        j = partner_chip(chip, k)
        return j, (2 * j + 1 - core, 2 * j + core)

    def source(k):
        return jnp.where(k == 0, z, ranked(z, k, n_z))

    def give_rows(k):
        sz = source(k)
        for i in range(1, n_e):
            oe = lax.rem(e + i, n_e)
            remote(
                r_ref.at[sz, oe],
                ret_ref.at[sz, e],
                b_send.at[k, i],
                b_recv.at[sz, e],
                (oe, z),
            ).start()
        pltpu.make_async_copy(r_ref.at[sz, e], ret_ref.at[sz, e], b_own.at[k]).start()

    for slot in range(2):
        load_raw(blocks(0)[1][slot], slot).start()
    gsum[...] = jnp.zeros_like(gsum)
    ghsum[...] = jnp.zeros_like(ghsum)
    for i, (src, dst) in enumerate(((n1_ref, n1s), (v_ref, vs), (mix_ref, mixs))):
        pltpu.make_async_copy(src, dst, in_sem.at[i]).wait()

    tokens = n_e * count

    def out_weights():
        da_all = das[...].reshape(tokens, width)
        for oz in range(n_z):
            at = slice(oz * head_rows, (oz + 1) * head_rows)
            gob[oz] = dot_first(mixs[:, :, at].reshape(tokens, head_rows), da_all).astype(BF)
        pass_all(out_pass, 0)

    def pass_sum(d, step, stage, block, inbox, recv, send, add):
        distance = z if step > 0 else n_z - 1 - z
        going = (d > z) if step > 0 else (d < z)

        @pl.when(going & (distance == stage))
        def _():
            if stage:
                remote(block, inbox.at[d], send.at[d], recv.at[d], (e, z - step)).wait_recv()
                add(d, inbox)
            remote(block, inbox.at[d], send.at[d], recv.at[d], (e, z + step)).start()

    def pass_all(one_pass, stage, steps=range(n_z - 1)):
        for d in steps:
            one_pass(n_z - 1 - d, 1, stage)
            one_pass(d, -1, stage)

    def out_add(d, inbox):
        fetch = pltpu.make_async_copy(inbox.at[d], away.at[0:head_rows], t_sem.at[0])
        fetch.start()
        fetch.wait()

        @pl.loop(0, head_rows, step=step)
        def _(r):
            at = pl.ds(pl.multiple_of(r, step), step)
            gob[d, at, :] = (gob[d, at, :].astype(F32) + away[at, :].astype(F32)).astype(BF)

    def out_pass(d, step, stage):
        inbox, recv = (gor_ref, or_recv) if step > 0 else (gol_ref, ol_recv)
        pass_sum(d, step, stage, gob.at[d], inbox, recv, o_send, out_add)

    parts = dcats.shape[-1] // (n_z * shard)

    def shard_at(d):
        return pl.ds(pl.multiple_of(d * shard, shard), shard)

    def weight_add(d, inbox):
        for p in range(parts):
            there = away.at[p * shard : (p + 1) * shard]
            pltpu.make_async_copy(inbox.at[d, p], there, t_sem.at[p]).start()
        for p in range(parts):
            there = away.at[p * shard : (p + 1) * shard]
            pltpu.make_async_copy(inbox.at[d, p], there, t_sem.at[p]).wait()

            @pl.loop(0, shard, step=step)
            def _(r, p=p):
                at = pl.ds(pl.multiple_of(d * shard + r, step), step)
                came = away[pl.ds(pl.multiple_of(p * shard + r, step), step), :]
                n1s[p, at, :] = (n1s[p, at, :].astype(F32) + came.astype(F32)).astype(BF)

    def weight_pass(d, step, stage):
        inbox, recv = (gwr_ref, wr_recv) if step > 0 else (gwl_ref, wl_recv)
        block = n1s.at[0:parts, shard_at(d), :]
        pass_sum(d, step, stage, block, inbox, recv, w_send, weight_add)

    def sum_rows(src, dst, k):
        sz = source(k)
        unpick = unpick_ref[sz]
        cuts = pieces(width)

        def fetch(p):
            start, size = cuts[p]
            return pltpu.make_async_copy(
                src.at[:, :, start : start + size], rbuf.at[p % 2], in_sem.at[p % 2]
            )

        fetch(0).start()
        for p, (start, size) in enumerate(cuts):
            if p + 1 < len(cuts):
                fetch(p + 1).start()
            fetch(p).wait()
            block = rbuf[p % 2].reshape(n_e * cap, size)
            dst[:, start : start + size] = dot(unpick, block).astype(BF)

    def sum_of(k):
        return rsum if k == n_z - 1 else das.at[k]

    def send_sum(k):
        sz = source(k)
        return remote(sum_of(k), part_ref.at[z], p_send.at[k], p_recv.at[z], (e, sz))

    def take_rows(k):
        sz = source(k)
        for i in range(1, n_e):
            oe = lax.rem(e + i, n_e)
            remote(
                r_ref.at[sz, oe],
                ret_ref.at[sz, oe],
                b_send.at[k, i],
                b_recv.at[sz, oe],
                (oe, z),
            ).wait()
        pltpu.make_async_copy(r_ref.at[sz, e], ret_ref.at[sz, e], b_own.at[k]).wait()
        sum_rows(ret_ref.at[sz], sum_of(k), k)

    sum_rows(rfar_ref, rsum, n_z - 1)
    send_sum(n_z - 1).start()

    pltpu.make_async_copy(da_ref, das.at[e], own.at[0]).wait()

    @pl.loop(0, nc)
    def _(k):
        j, pair = blocks(k)
        remote(da_ref, das.at[pair[0]], ds_send.at[k], ds_recv.at[j], sibling).wait_recv()
        pl.when(k == nc - 1)(out_weights)
        to_sibling = remote(
            away, sib.at[lax.rem(k, 2)], sib_send, sib_recv.at[lax.rem(k, 2)], sibling
        )
        for slot, b in enumerate(pair):
            load_raw(b, slot).wait()
            part = attend_back_block(
                heads,
                das[b],
                n1s[b],
                raws.at[slot],
                vs[b],
                *turns(turn_ref[b]),
                may_see(seg_ref[b]),
                w_ref,
                wo_ref,
                gh_ref,
                dmix,
                dcats.at[b],
                gsum,
                ghsum,
            )

            @pl.when(k < nc - 1)
            def _(slot=slot):
                load_raw(blocks(k + 1)[1][slot], slot).start()

            if slot == 1:
                mine[j] = part
                continue
            away[...] = part
            to_sibling.start()

            nb = 2 * blocks(k + 1)[0] + core

            def to_core():
                block = das.at[nb]
                nj = nb // 2
                remote(block, block, ds_send.at[k + 1], ds_recv.at[nj], sibling).start()

            @pl.when(k < nc - 2)
            def _():
                remote(
                    da_ref, das.at[nb], d_send.at[k + 1], d_recv.at[nb // 2], far_chip(k + 1)
                ).wait_recv()
                via_da(nb, k).start()
                to_core()

            @pl.when(k == nc - 2)
            def _():
                for p in range(2):
                    via_da(nb, p).wait_recv()
                to_core()

        @pl.when((k > 0) & (k < n_z - 1))
        def _():
            give_rows(n_z - 1 - k)

        to_sibling.wait()

        @pl.when(k > 0)
        def _():
            @pl.loop(0, count, step=step)
            def _(r):
                at = pl.ds(pl.multiple_of(r, step), step)
                mine[j, at, :] = (
                    mine[j, at, :].astype(F32) + sib[lax.rem(k, 2), at, :].astype(F32)
                ).astype(BF)

            remote(
                mine.at[j], far.at[k - 1], send.at[k - 1], recv.at[k - 1], far_chip(k)
            ).start()

        @pl.when(k == 0)
        def _():
            @pl.loop(0, count, step=step)
            def _(r):
                at = pl.ds(pl.multiple_of(r, step), step)
                total_ref[at, :] = mine[j, at, :].astype(F32) + sib[0, at, :].astype(F32)

    remote(da_ref, das.at[e], ds_send.at[0], ds_recv.at[chip], sibling).wait_send()
    for p in range(2):
        give_da(p + 1).wait_send()
        via_da(e, p).wait_send()
    for k in range(1, nc):
        block = das.at[2 * partner_chip(chip, k) + core]
        remote(block, block, ds_send.at[k], ds_recv.at[chip], sibling).wait_send()

    give_rows(0)

    dcat = dcats[...].reshape(tokens, -1)

    @pl.loop(0, n_e)
    def _(t):
        at = pl.ds(pl.multiple_of(t * n_z * shard, n_z * shard), n_z * shard)
        rows = dot_first(n1s[:, :, at].reshape(tokens, n_z * shard), dcat).astype(BF)
        for p in range(parts):
            n1s[p, :, at] = rows[:, p * n_z * shard : (p + 1) * n_z * shard]

    pass_all(weight_pass, 0)
    pltpu.make_async_copy(gob.at[z], goo_ref, own.at[3]).start()
    lanes = 128
    g1 = gsum[...] / g1_ref[...]
    per = width // lanes
    for i in range(per):
        gvec[i : i + 1, :] = g1[:, i * lanes : (i + 1) * lanes]
        gvec[per + i : per + i + 1, :] = g2_ref[:, i * lanes : (i + 1) * lanes]
    gvec[2 * per : 2 * per + 8, :] = ghsum[...]

    for i in range(1, n_e):
        oe = lax.rem(e + i, n_e)
        remote(gvec, gplane.at[e], v_send.at[i], v_recv.at[e], (oe, z)).start()
    gplane[e] = gvec[...]
    pass_all(out_pass, 1)
    take_rows(n_z - 2)
    pass_all(weight_pass, 1, range(1))
    send_sum(n_z - 2).start()
    pass_all(out_pass, 2)
    pass_all(weight_pass, 1, range(1, n_z - 1))
    for k in range(n_z - 3, 0, -1):
        take_rows(k)
        send_sum(k).start()
    pass_all(weight_pass, 2)

    for came, inbox, recv_w, there in (
        (z > 0, gwr_ref, wr_recv, z - 1),
        (z < n_z - 1, gwl_ref, wl_recv, z + 1),
    ):

        @pl.when(came)
        def _(inbox=inbox, recv_w=recv_w, there=there):
            block = n1s.at[0:parts, shard_at(z), :]
            remote(block, inbox.at[z], w_send.at[z], recv_w.at[z], (e, there)).wait_recv()
            weight_add(z, inbox)

    def weight_block(t):
        at = pl.ds(pl.multiple_of(t * n_z * shard, n_z * shard), n_z * shard)
        return n1s.at[0:parts, shard_at(z), at]

    for i in range(1, n_e):
        oe = lax.rem(e + i, n_e)
        remote(weight_block(oe), gws_ref.at[e], s_send.at[i], s_recv.at[e], (oe, z)).start()
    pltpu.make_async_copy(weight_block(e), gws_ref.at[e], own.at[2]).start()
    for k in range(1, nc):
        j = partner_chip(chip, k)
        remote(
            mine.at[j], far.at[k - 1], send.at[k - 1], recv.at[k - 1], far_chip(k)
        ).wait()

        @pl.loop(0, count, step=step)
        def _(r, k=k):
            at = pl.ds(pl.multiple_of(r, step), step)
            total_ref[at, :] += far[k - 1, at, :].astype(F32)

    for i in range(1, n_e):
        oe = lax.rem(e + i, n_e)
        remote(gvec, gplane.at[oe], v_send.at[i], v_recv.at[oe], (oe, z)).wait()
    gtotal[...] = jnp.sum(gplane[...], axis=0)
    for k in range(1, n_z):
        oz = near(z, k, n_z)
        remote(gtotal, gvs_ref.at[z], vz_send.at[k], vz_recv.at[z], (e, oz)).start()
    own_gv = pltpu.make_async_copy(gtotal, gvs_ref.at[z], own.at[4])
    own_gv.start()
    take_rows(0)
    pltpu.make_async_copy(das.at[0], part_ref.at[z], own.at[6]).start()

    @pl.loop(1, n)
    def _(k):
        other, where = other_of(k)
        remote(
            gr_ref.at[other],
            grs_ref.at[other],
            a_send.at[k],
            a_recv.at[other],
            where,
        ).wait()

    for i in range(1, n_e):
        oe = lax.rem(e + i, n_e)
        remote(weight_block(oe), gws_ref.at[oe], s_send.at[i], s_recv.at[oe], (oe, z)).wait()
    for d in range(n_z):

        @pl.when(d != z)
        def _(d=d):
            remote(gob.at[d], gor_ref.at[d], o_send.at[d], or_recv.at[d], (e, d)).wait_send()
            block = n1s.at[0:parts, shard_at(d), :]
            remote(block, gwr_ref.at[d], w_send.at[d], wr_recv.at[d], (e, d)).wait_send()

    for came, inbox, recv_o, there in (
        (z > 0, gor_ref, or_recv, z - 1),
        (z < n_z - 1, gol_ref, ol_recv, z + 1),
    ):

        @pl.when(came)
        def _(inbox=inbox, recv_o=recv_o, there=there):
            remote(
                gob.at[z], inbox.at[z], o_send.at[z], recv_o.at[z], (e, there)
            ).wait_recv()

    for k in range(1, n_z):
        oz = near(z, k, n_z)
        remote(
            gtotal, gvs_ref.at[oz], vz_send.at[k], vz_recv.at[oz], (e, oz)
        ).wait()
        sz = ranked(z, k, n_z)
        remote(
            sum_of(k), part_ref.at[sz], p_send.at[k], p_recv.at[sz], (e, sz)
        ).wait()
    own_gr.wait()
    pltpu.make_async_copy(weight_block(e), gws_ref.at[e], own.at[2]).wait()
    pltpu.make_async_copy(gob.at[z], goo_ref, own.at[3]).wait()
    own_gv.wait()
    pltpu.make_async_copy(das.at[0], part_ref.at[z], own.at[6]).wait()


def back(
    n_e, n_z, cap, heads, da, r_rows, r_far, gr, n1, raw, v, mix, unpicks, g2, turn_table, seg, w, wo, g1, gh
):
    n, nc = n_e * n_z, n_e // 2
    count, width = da.shape
    shard = width // n
    columns = w.shape[1]
    parts = columns // (n_z * shard)
    out_block = (wo.shape[0] // n_z, width)
    vec_rows = 2 * width // 128 + 8
    block = (count, width)

    def sems(*shape):
        return DMA(shape)

    return pl.pallas_call(
        partial(back_kernel, n_e, n_z, cap, heads),
        out_shape=(
            jax.ShapeDtypeStruct(block, F32),
            jax.ShapeDtypeStruct((n_z,) + block, BF),
            jax.ShapeDtypeStruct((n_e, parts, shard, n_z * shard), BF),
            jax.ShapeDtypeStruct(out_block, BF),
            jax.ShapeDtypeStruct((n_z,) + out_block, BF),
            jax.ShapeDtypeStruct((n_z,) + out_block, BF),
            jax.ShapeDtypeStruct(gr.shape, F32),
            jax.ShapeDtypeStruct((n_z, vec_rows, 128), F32),
            jax.ShapeDtypeStruct(r_rows.shape, BF),
            jax.ShapeDtypeStruct((n_z, parts, shard, width), BF),
            jax.ShapeDtypeStruct((n_z, parts, shard, width), BF),
        ),
        in_specs=[ANY] * 8 + [VM] * 8,
        out_specs=(VM,) + (ANY,) * 10,
        scratch_shapes=[
            pltpu.VMEM(block, BF),
            pltpu.VMEM((n_e, vec_rows, 128), F32),
            pltpu.VMEM((n_e,) + block, BF),
            pltpu.VMEM(n1.shape, BF),
            pltpu.VMEM((2,) + raw.shape[1:], F32),
            pltpu.VMEM(v.shape, BF),
            pltpu.VMEM(mix.shape, BF),
            pltpu.VMEM((n_e, count, columns), BF),
            pltpu.VMEM((count, heads * HEAD), BF),
            pltpu.VMEM((1, width), F32),
            pltpu.VMEM((8, HEAD), F32),
            pltpu.VMEM((vec_rows, 128), F32),
            pltpu.VMEM((vec_rows, 128), F32),
            pltpu.VMEM(block, BF),
            pltpu.VMEM((nc,) + block, BF),
            pltpu.VMEM((2,) + block, BF),
            pltpu.VMEM((nc - 1,) + block, BF),
            pltpu.VMEM((2, n_e, cap, pieces(width)[0][1]), BF),
            pltpu.VMEM((n_z, wo.shape[0] // n_z, width), BF),
            sems(7),
            sems(3),
            sems(2),
            sems(nc),
            sems(nc),
            sems(2),
            sems(2),
            sems(nc),
            sems(nc),
            sems(n),
            sems(n),
            sems(n_z, n_e),
            sems(n_z, n_e),
            sems(n_z),
            sems(n_z),
            sems(n_z),
            sems(n_z),
            sems(n_z),
            sems(n_z),
            sems(n_z),
            sems(n_z),
            sems(n_z),
            sems(n_e),
            sems(n_e),
            sems(parts),
            sems(n_e),
            sems(n_e),
            sems(n_z),
            sems(n_z),
            DMA,
            sems(2),
            sems(nc),
            sems(nc),
        ],
        compiler_params=pltpu.CompilerParams(
            collective_id=14, has_side_effects=True, vmem_limit_bytes=63 * 1024 * 1024
        ),
        name="back",
    )(da, r_rows, r_far, gr, n1, raw, v, mix, unpicks, g2, turn_table, seg, w, wo, g1, gh)


def expert_kernel(
    n_z,
    experts,
    width,
    x_ref,
    dy_ref,
    wg_ref,
    wu_ref,
    wd_ref,
    r_ref,
    dx_ref,
    gg_ref,
    gu_ref,
    gd_ref,
):
    step = pl.program_id(0)

    @pl.when(step == 0)
    def _():
        gg_ref[...] = jnp.zeros_like(gg_ref)
        gu_ref[...] = jnp.zeros_like(gu_ref)
        gd_ref[...] = jnp.zeros_like(gd_ref)

    e, z = place()
    me = e * n_z + z
    x = x_ref[:, :width]
    extra = x_ref[:, width:].astype(F32)
    lane = lax.broadcasted_iota(jnp.int32, extra.shape, 1)
    gate = jnp.sum(
        jnp.where((lane == me) | (lane == experts + me), extra, 0.0), axis=1, keepdims=True
    )
    gate_part = dot(x, wg_ref[...])
    up_part = dot(x, wu_ref[...])
    sig = 1.0 / (1.0 + jnp.exp(-gate_part))
    act = gate_part * sig
    inner = (act * up_part).astype(BF)
    r_ref[...] = (dot(inner, wd_ref[...]) * gate).astype(BF)
    dy = dy_ref[...]
    dinner = dot_last(dy, wd_ref[...])
    inner_f = inner.astype(F32)
    dgate = jnp.sum(dinner * inner_f, axis=1, keepdims=True)
    gd_ref[...] += dot_first((inner_f * gate).astype(BF), dy)
    dinner = dinner * gate
    dgp = (dinner * up_part * sig * (1.0 + gate_part * (1.0 - sig))).astype(BF)
    dup = (dinner * act).astype(BF)
    dx_ref[:, :width] = (dot_last(dgp, wg_ref[...]) + dot_last(dup, wu_ref[...])).astype(BF)
    high = dgate.astype(BF).astype(F32)
    dx_ref[:, width:] = jnp.where(
        lane == me, high, jnp.where(lane == experts + me, dgate - high, 0.0)
    ).astype(BF)
    gg_ref[...] += dot_first(x, dgp)
    gu_ref[...] += dot_first(x, dup)


def expert_run(n_z, experts, x, dy, wg, wu, wd):
    rows, columns = x.shape
    width, hidden = wg.shape
    tile = 512

    def block(c):
        return pl.BlockSpec((tile, c), lambda b: (b, 0))

    def whole(shape):
        return pl.BlockSpec(shape, lambda b: (0, 0), pipeline_mode=pl.Buffered(1))

    return pl.pallas_call(
        partial(expert_kernel, n_z, experts, width),
        grid=(rows // tile,),
        out_shape=(
            jax.ShapeDtypeStruct((rows, width), BF),
            jax.ShapeDtypeStruct((rows, columns), BF),
            jax.ShapeDtypeStruct((width, hidden), F32),
            jax.ShapeDtypeStruct((width, hidden), F32),
            jax.ShapeDtypeStruct((hidden, width), F32),
        ),
        in_specs=[
            block(columns),
            block(width),
            whole(wg.shape),
            whole(wu.shape),
            whole(wd.shape),
        ],
        out_specs=(
            block(width),
            block(columns),
            whole(wg.shape),
            whole(wu.shape),
            whole(wd.shape),
        ),
        compiler_params=pltpu.CompilerParams(vmem_limit_bytes=BIG),
        name="experts",
    )(x, dy, wg, wu, wd)


def expert_tile(width, experts, me, x_ext, dy, wg_ref, wu_ref, wd_ref):
    x = x_ext[:, :width]
    extra = x_ext[:, width:].astype(F32)
    lane = lax.broadcasted_iota(jnp.int32, extra.shape, 1)
    gate = jnp.sum(
        jnp.where((lane == me) | (lane == experts + me), extra, 0.0), axis=1, keepdims=True
    )
    gate_part = dot(x, wg_ref[...])
    up_part = dot(x, wu_ref[...])
    sig = 1.0 / (1.0 + jnp.exp(-gate_part))
    act = gate_part * sig
    inner = (act * up_part).astype(BF)
    result = (dot(inner, wd_ref[...]) * gate).astype(BF)
    dinner = dot_last(dy, wd_ref[...])
    inner_f = inner.astype(F32)
    dgate = jnp.sum(dinner * inner_f, axis=1, keepdims=True)
    gated = (inner_f * gate).astype(BF)
    dinner = dinner * gate
    dgp = (dinner * up_part * sig * (1.0 + gate_part * (1.0 - sig))).astype(BF)
    dup = (dinner * act).astype(BF)
    dx = (dot_last(dgp, wg_ref[...]) + dot_last(dup, wu_ref[...])).astype(BF)
    high = dgate.astype(BF).astype(F32)
    back = jnp.where(
        lane == me, high, jnp.where(lane == experts + me, dgate - high, 0.0)
    ).astype(BF)
    return result, dx, back, gated, dgp, dup


def moe_kernel(
    n_e,
    n_z,
    cap,
    tok_ref,
    pick_ref,
    unpick_ref,
    near_ref,
    far_ref,
    wg_ref,
    wu_ref,
    wd_ref,
    xs_ref,
    r_ref,
    dx_ref,
    ret_ref,
    part_ref,
    gi_ref,
    dg_ref,
    du_ref,
    gg_ref,
    gu_ref,
    gd_ref,
    rret_ref,
    zbuf,
    z_send,
    z_recv,
    r_send,
    r_recv,
    r_own,
    in_sem,
    out_sem,
    b_send,
    b_recv,
    b_own,
    p_send,
    p_recv,
    p_own,
    e_send,
    e_recv,
    g_sem,
    t_sem,
    w_sem,
):
    e, z = place()
    me = e * n_z + z
    width = far_ref.shape[-1]
    hidden = wd_ref.shape[0]
    experts = n_e * n_z
    columns = tok_ref.shape[-1]
    last = n_z - 1
    inner = (z > 0) & (z < last)
    greet(n_e, n_z, True)
    chain = (lambda s: zbuf.at[s], z_send, z_recv)
    chain_start(n_z, tok_ref, *chain)

    def source(k):
        return jnp.where(k == 0, z, ranked(z, k, n_z))

    def give_one(k, i):
        sz, oe = source(k), lax.rem(e + i, n_e)
        return remote(
            dx_ref.at[sz, oe],
            ret_ref.at[sz, e],
            b_send.at[k, i],
            b_recv.at[sz, e],
            (oe, z),
        )

    def give_own(k):
        sz = source(k)
        return pltpu.make_async_copy(dx_ref.at[sz, e], ret_ref.at[sz, e], b_own.at[k])

    def give(k):
        for i in range(1, n_e):
            give_one(k, i).start()
        give_own(k).start()

    def store(k, tiles, i):
        src, dst = tiles[i]
        return pltpu.make_async_copy(src, dst.at[source(k)], out_sem.at[i])

    def first_phase(rows, xt, yt, rt, dxt, git, dgt, dut):
        out_args = (xs_ref, r_own, r_send, r_recv)
        rows_out(n_e, cap, 0, z, tok_ref, pick_ref, rows, *out_args)
        tiles = ((dxt, dx_ref), (rt, r_ref), (git, gi_ref), (dgt, dg_ref), (dut, du_ref))

        def load_y(src):
            return pltpu.make_async_copy(src, yt, in_sem.at[1])

        @pl.loop(0, n_z)
        def _(k):
            sz = source(k)

            @pl.when(k == 0)
            def _():
                load_y(near_ref).start()

            @pl.when(k > 0)
            def _():
                load_y(far_ref.at[sz]).start()

            @pl.when(jnp.where(inner, k == 0, k < last))
            def _():
                chain_take(n_z, k + 1, *chain)

            @pl.when(inner & (k + 2 < n_z))
            def _():
                chain_take(n_z, k + 2, *chain)

            @pl.when(k < last)
            def _():
                nz = source(k + 1)
                rows_out(n_e, cap, k + 1, nz, zbuf.at[nz], pick_ref, rows, *out_args)

            rows_out_wait(n_e, cap, k, sz, rows, *out_args)
            fetch = pltpu.make_async_copy(xs_ref.at[sz], xt, in_sem.at[0])
            fetch.start()
            fetch.wait()
            load_y(far_ref.at[sz]).wait()

            @pl.when((k > 0) & (k < last))
            def _():
                store(k, tiles, 0).wait()

            @pl.when(k > 0)
            def _():
                for i in range(1, 5):
                    store(k, tiles, i).wait()

            result, dx, back, gated, dgp, dup = expert_tile(
                width,
                experts,
                me,
                xt[...].reshape(n_e * cap, -1),
                yt[...].reshape(n_e * cap, -1),
                wg_ref,
                wu_ref,
                wd_ref,
            )
            rt[...] = result.reshape(n_e, cap, -1)
            dxt[:, :, :width] = dx.reshape(n_e, cap, -1)
            dxt[:, :, width:] = back.reshape(n_e, cap, -1)
            git[...] = gated.reshape(n_e, cap, -1)
            dgt[...] = dgp.reshape(n_e, cap, -1)
            dut[...] = dup.reshape(n_e, cap, -1)
            for i in range(5):
                store(k, tiles, i).start()

            @pl.when(k >= last - 1)
            def _():
                store(k, tiles, 0).wait()
                give(k)

        for i in range(1, 5):
            store(last, tiles, i).wait()

    def row_buffer(c):
        return pltpu.VMEM((n_e, cap, c), BF)

    pl.run_scoped(
        first_phase,
        pltpu.VMEM((n_z, n_e * cap, columns), BF),
        row_buffer(columns),
        row_buffer(width),
        row_buffer(width),
        row_buffer(columns),
        row_buffer(hidden),
        row_buffer(hidden),
        row_buffer(hidden),
    )
    chain_end(n_z, tok_ref, *chain)

    give(1)
    far_z = source(last)

    def give_result(i):
        oe = lax.rem(e + i, n_e)
        return remote(
            r_ref.at[far_z, oe], rret_ref.at[e], e_send.at[i], e_recv.at[e], (oe, z)
        )

    give(0)
    for i in range(1, n_e):
        give_result(i).start()
    own_result = pltpu.make_async_copy(r_ref.at[far_z, e], rret_ref.at[e], in_sem.at[0])
    own_result.start()
    size = 256
    count = width // size

    def second_phase(gis, dgs, dus, xc, yc, ggt, gut, gdt, rbuf):
        whole = ((gi_ref, gis), (dg_ref, dgs), (du_ref, dus))
        for i, (src, dst) in enumerate(whole):
            pltpu.make_async_copy(src, dst, g_sem.at[i]).start()

        def pairs(t):
            at = pl.ds(pl.multiple_of(t * size, size), size)
            slot = lax.rem(t, 2)
            copies = [
                pltpu.make_async_copy(xs_ref.at[:, :, :, at], xc.at[slot], t_sem.at[0, slot])
            ]
            for k in range(n_z):
                src = far_ref.at[source(k), :, :, at] if k else near_ref.at[:, :, at]
                copies.append(
                    pltpu.make_async_copy(
                        src, yc.at[slot, source(k)], t_sem.at[1 + k, slot]
                    )
                )
            return copies

        def results(t):
            at = pl.ds(pl.multiple_of(t * size, size), size)
            slot = lax.rem(t, 2)
            return [
                pltpu.make_async_copy(ggt.at[slot], gg_ref.at[at], w_sem.at[0, slot]),
                pltpu.make_async_copy(gut.at[slot], gu_ref.at[at], w_sem.at[1, slot]),
                pltpu.make_async_copy(gdt.at[slot], gd_ref.at[:, at], w_sem.at[2, slot]),
            ]

        def weight_tile(t):
            slot = lax.rem(t, 2)

            @pl.when(t + 1 < count)
            def _():
                for copy in pairs(t + 1):
                    copy.start()

            for copy in pairs(t):
                copy.wait()

            @pl.when(t >= 2)
            def _():
                for copy in results(t):
                    copy.wait()

            total = n_z * n_e * cap
            x = xc[slot].reshape(total, size)
            ggt[slot] = dot_first(x, dgs[...].reshape(total, hidden)).astype(BF)
            gut[slot] = dot_first(x, dus[...].reshape(total, hidden)).astype(BF)
            gdt[slot] = dot_first(
                gis[...].reshape(total, hidden), yc[slot].reshape(total, size)
            ).astype(BF)
            for copy in results(t):
                copy.start()

        def combine(k):
            sz = source(k)
            for i in range(1, n_e):
                oe = lax.rem(e + i, n_e)
                remote(
                    dx_ref.at[sz, oe],
                    ret_ref.at[sz, oe],
                    b_send.at[k, i],
                    b_recv.at[sz, oe],
                    (oe, z),
                ).wait()
            give_own(k).wait()
            unpick = unpick_ref[sz]
            cuts = pieces(columns)

            def fetch(p):
                start, wide = cuts[p]
                return pltpu.make_async_copy(
                    ret_ref.at[sz, :, :, start : start + wide],
                    rbuf.at[p % 2, :, :, 0:wide],
                    in_sem.at[1 + p % 2],
                )

            fetch(0).start()
            for p, (start, wide) in enumerate(cuts):
                if p + 1 < len(cuts):
                    fetch(p + 1).start()
                fetch(p).wait()
                block = rbuf[p % 2, :, :, 0:wide].reshape(n_e * cap, wide)
                zbuf[k, :, start : start + wide] = dot(unpick, block).astype(BF)

            @pl.when(k > 0)
            def _():
                remote(
                    zbuf.at[k], part_ref.at[z], p_send.at[k], p_recv.at[z], (e, sz)
                ).start()

            @pl.when(k == 0)
            def _():
                pltpu.make_async_copy(zbuf.at[k], part_ref.at[z], p_own).start()

        for copy in pairs(0):
            copy.start()
        for i, (src, dst) in enumerate(whole):
            pltpu.make_async_copy(src, dst, g_sem.at[i]).wait()
        share_of = count // n_z

        @pl.loop(0, n_z)
        def _(i):
            @pl.loop(0, share_of)
            def _(t):
                weight_tile(i * share_of + t)

            k = jnp.where(i == 0, last - 1, jnp.where(i == 1, last, last - i))
            combine(k)

        for t in (count - 2, count - 1):
            for copy in results(t):
                copy.wait()

    total_shape = (n_z, n_e, cap)
    pl.run_scoped(
        second_phase,
        pltpu.VMEM(total_shape + (hidden,), BF),
        pltpu.VMEM(total_shape + (hidden,), BF),
        pltpu.VMEM(total_shape + (hidden,), BF),
        pltpu.VMEM((2,) + total_shape + (size,), BF),
        pltpu.VMEM((2,) + total_shape + (size,), BF),
        pltpu.VMEM((2, size, hidden), BF),
        pltpu.VMEM((2, size, hidden), BF),
        pltpu.VMEM((2, hidden, size), BF),
        pltpu.VMEM((2, n_e, cap, pieces(columns)[0][1]), BF),
    )
    for i in range(1, n_e):
        oe = lax.rem(e + i, n_e)
        remote(
            r_ref.at[far_z, oe], rret_ref.at[oe], e_send.at[i], e_recv.at[oe], (oe, z)
        ).wait()
    own_result.wait()
    pltpu.make_async_copy(zbuf.at[0], part_ref.at[z], p_own).wait()
    for k in range(1, n_z):
        sz = ranked(z, k, n_z)
        remote(
            zbuf.at[k], part_ref.at[sz], p_send.at[k], p_recv.at[sz], (e, sz)
        ).wait()


def moe(n_e, n_z, cap, tok, picks, unpicks, dy_near, dy_far, wg, wu, wd):
    count, columns = tok.shape
    width, hidden = wg.shape

    def rows_of(c):
        return jax.ShapeDtypeStruct((n_z, n_e, cap, c), BF)

    return pl.pallas_call(
        partial(moe_kernel, n_e, n_z, cap),
        out_shape=(
            rows_of(columns),
            rows_of(width),
            rows_of(columns),
            rows_of(columns),
            jax.ShapeDtypeStruct((n_z, count, columns), BF),
            rows_of(hidden),
            rows_of(hidden),
            rows_of(hidden),
            jax.ShapeDtypeStruct((width, hidden), BF),
            jax.ShapeDtypeStruct((width, hidden), BF),
            jax.ShapeDtypeStruct((hidden, width), BF),
            jax.ShapeDtypeStruct((n_e, cap, width), BF),
        ),
        in_specs=[VM, VM, VM, ANY, ANY, VM, VM, VM],
        out_specs=(ANY,) * 12,
        scratch_shapes=[
            pltpu.VMEM((n_z, count, columns), BF),
            DMA((n_z + 1,)),
            DMA((n_z,)),
            DMA((n_z, n_e)),
            DMA((n_z, n_e)),
            DMA((n_z,)),
            DMA((3,)),
            DMA((5,)),
            DMA((n_z, n_e)),
            DMA((n_z, n_e)),
            DMA((n_z,)),
            DMA((n_z,)),
            DMA((n_z,)),
            DMA,
            DMA((n_e,)),
            DMA((n_e,)),
            DMA((3,)),
            DMA((1 + n_z, 2)),
            DMA((3, 2)),
        ],
        compiler_params=pltpu.CompilerParams(
            collective_id=13, has_side_effects=True, vmem_limit_bytes=63 * 1024 * 1024
        ),
        name="moe",
    )(tok, picks, unpicks, dy_near, dy_far, wg, wu, wd)


def layout(lengths, owners, device, row_count):
    seq_order = jnp.arange(lengths.shape[0], dtype=jnp.int32)
    owned = (owners == device).astype(jnp.int32)
    earlier = (seq_order[None, :] < seq_order[:, None]).astype(jnp.int32)
    starts = jnp.sum(earlier * (owned * lengths)[None, :], axis=1)
    row_index = jnp.arange(row_count, dtype=jnp.int32)
    inside = (
        owned[None, :]
        * (row_index[:, None] >= starts[None, :]).astype(jnp.int32)
        * (row_index[:, None] < (starts + lengths)[None, :]).astype(jnp.int32)
    )
    live_rows = jnp.sum(inside, axis=1)
    segment = jnp.sum(inside * (seq_order[None, :] + 1), axis=1) - 1
    token_position = jnp.sum(inside * (row_index[:, None] - starts[None, :]), axis=1)
    return (live_rows, segment, token_position)


def named_experts(routes, experts):
    return jnp.any(routes[..., None] == jnp.arange(experts, dtype=jnp.int32), axis=-2)


def slot_picks(n_e, n_z, z, cap, named, live):
    sources, count, experts = named.shape
    used = named & (live[:, :, None] > 0)
    order = jnp.arange(count)
    lower = (order[None, :] < order[:, None]).astype(BF)
    slots = jnp.einsum("ts,zse->zte", lower, used.astype(BF), preferred_element_type=F32)
    slots = jnp.where(used, slots, -1.0)
    column = jnp.arange(n_e * cap, dtype=jnp.int32)
    spread = (
        jnp.arange(experts, dtype=jnp.int32)[:, None] == (column // cap * n_z + z)[None, :]
    ).astype(BF)
    slots = slots.astype(BF)
    slot_ids = lax.rem(column, cap).astype(F32)
    picks = jnp.einsum("ec,ste->sct", spread, slots, preferred_element_type=F32)
    unpicks = jnp.einsum("ste,ec->stc", slots, spread, preferred_element_type=F32)
    return (
        (picks == slot_ids[None, :, None]).astype(BF),
        (unpicks == slot_ids).astype(BF),
    )


def split_float(values):
    high = values.astype(BF)
    return high, (values - high.astype(F32)).astype(BF)


def pad_lanes(values, lanes):
    return jnp.pad(values, ((0, 0), (0, lanes - values.shape[1])))


def local(
    n_e,
    n_z,
    tokens,
    cotangent,
    lengths,
    owners,
    routes,
    w_query,
    key_weight,
    value_weight,
    w_out,
    w_router,
    norm_gains,
    w_gate,
    w_up,
    w_down,
):
    n = n_e * n_z
    count, width = tokens.shape
    shard = w_query.shape[0]
    experts, top = w_router.shape[1], routes.shape[1]
    q_heads, kv_heads = w_query.shape[1] // HEAD, key_weight.shape[1] // HEAD
    heads = q_heads // n_e
    cap = count * top * 5 // (4 * experts)
    cap = -(-cap // 16) * 16
    e, z = place()

    wq_blocks = w_query.reshape(shard, n_e, heads * HEAD)
    sharing = n_e // kv_heads
    wk_blocks = jnp.repeat(key_weight.reshape(shard, kv_heads, HEAD), sharing, axis=1)
    wv_blocks = jnp.repeat(value_weight.reshape(shard, kv_heads, HEAD), sharing, axis=1)
    w_blocks = jnp.concatenate([wq_blocks, wk_blocks, wv_blocks], axis=2).transpose(1, 0, 2)
    router_rows = shard * experts // 128
    gain_rows = -(-norm_gains.shape[0] // 128)
    misc_rows = -(-(router_rows + gain_rows) // 16) * 16
    misc = jnp.concatenate(
        [
            w_router.reshape(-1),
            norm_gains,
            jnp.zeros((misc_rows - router_rows) * 128 - norm_gains.shape[0], BF),
        ]
    ).reshape(misc_rows, 128)
    routes_flat = routes.reshape(-1, 128)

    device = e * n_z + z
    plane_ids = jnp.arange(n_e, dtype=jnp.int32) * n_z + z
    column_ids = e * n_z + jnp.arange(n_z, dtype=jnp.int32)
    live_both, segment, position = jax.vmap(lambda d: layout(lengths, owners, d, count))(
        jnp.concatenate([plane_ids, column_ids])
    )
    live_all = live_both[n_e:]
    live_own = lax.dynamic_index_in_dim(live_all, z, keepdims=False)
    named_own = named_experts(routes, experts)
    small = n_e == 8 and n_z == 4
    if small:
        pick_own = slot_picks(n_e, n_z, z, cap, named_own[None], live_own[None])[0][0]
        xs, rts, w_all, wo_all, misc_all, dy_near = open_layer(
            n_e, n_z, cap, tokens, cotangent, routes_flat, w_blocks, w_out, misc, pick_own
        )
    else:
        xs, cts, rts, w_all, wo_all, misc_all = share(
            n_e, n_z, tokens, cotangent, routes_flat, w_blocks, w_out, misc
        )
    w_all = w_all.reshape(n * shard, -1)
    wo_all = wo_all.reshape(-1, width)
    router_w = misc_all[:, :router_rows].reshape(n * shard, experts)
    gains = (
        misc_all[:, router_rows:]
        .reshape(n, -1)[:, : norm_gains.shape[0]]
        .reshape(-1)
        .astype(F32)
    )
    gain_one = gains[None, :width]
    gain_two = gains[None, width : 2 * width]
    gain_heads = jnp.pad(gains[2 * width :].reshape(2, HEAD), ((0, 6), (0, 0)))

    half = HEAD // 2
    frequency = jnp.power(1000000.0, -2.0 * jnp.arange(half, dtype=F32) / HEAD)
    angles = position[:n_e].astype(F32)[:, :, None] * frequency
    turn_table = jnp.concatenate([jnp.cos(angles), jnp.sin(angles)], axis=-1)
    seg = segment[:n_e].astype(F32)[:, None, :]

    named_all = named_experts(rts.reshape(n_z, count, top), experts)
    picks, unpicks = slot_picks(n_e, n_z, z, cap, named_all, live_all)
    live = live_own.astype(F32)[:, None]
    named = named_own.astype(F32)

    shape = (turn_table, seg, w_all, wo_all, gain_one, gain_heads)
    if small:
        n1, raw, value, mix, attn_rows, dy_far = front(
            n_e, n_z, cap, heads, xs, cotangent, picks, *shape
        )
    else:
        dy_rows = send_rows(n_e, n_z, cap, cts, picks)
        n1, raw, value, mix, part = attend(n_e, heads, xs, *shape)
        attn_rows = plane_sum(n_e, n_z, part)

    inputs = tokens.astype(F32)
    hidden = inputs + live * attn_rows
    r_two = lax.rsqrt(jnp.mean(hidden * hidden, axis=-1, keepdims=True) + EPSILON)
    nu_two = hidden * r_two
    n2 = (nu_two * gain_two).astype(BF)
    logits = dot(n2, router_w)
    probs = jax.nn.softmax(logits, axis=-1)
    chosen = probs * named
    chosen_sum = jnp.sum(chosen, axis=1, keepdims=True)
    gates = chosen / chosen_sum
    lanes = -(-2 * experts // 128) * 128
    extra = pad_lanes(jnp.concatenate(split_float(gates), axis=1), lanes)
    tok = jnp.concatenate([n2, extra], axis=1)
    experts_w = (w_gate[0], w_up[0], w_down[0])
    if small:
        moved = moe(n_e, n_z, cap, tok, picks, unpicks, dy_near, dy_far, *experts_w)
        r_rows, dx_back = moved[1], moved[4]
        grad_gate, grad_up, grad_down = (a.astype(F32) for a in moved[8:11])
        r_far = moved[11]
    else:
        x_rows = dispatch(n_e, n_z, cap, tok, picks)
        r_rows, dx_rows, grad_gate, grad_up, grad_down = expert_run(
            n_z,
            experts,
            x_rows.reshape(-1, width + lanes),
            dy_rows.reshape(-1, width),
            *experts_w,
        )
        r_rows = r_rows.reshape(dy_rows.shape)
        dx_back = give_back(n_e, n_z, cap, dx_rows.reshape(x_rows.shape), unpicks, 6)

    dx_sum = jnp.sum(dx_back.astype(F32), axis=0)
    dgates = dx_sum[:, width : width + experts] + dx_sum[:, width + experts : width + 2 * experts]
    dchosen = (
        named * (dgates - jnp.sum(dgates * gates, axis=1, keepdims=True)) / chosen_sum
    )
    dlogits = (probs * (dchosen - jnp.sum(probs * dchosen, axis=1, keepdims=True))).astype(BF)
    grad_router = dot_first(n2, dlogits)
    dn2 = dx_sum[:, :width] + dot_last(dlogits, router_w)
    upstream = cotangent.astype(F32)
    grad_gain_two = jnp.sum(dn2 * nu_two, axis=0)
    scaled = dn2 * gain_two
    dhidden = upstream + r_two * (
        scaled - nu_two * jnp.mean(scaled * nu_two, axis=-1, keepdims=True)
    )
    da = (live * dhidden).astype(BF)
    gain_size = norm_gains.shape[0]
    grad_router = grad_router.reshape(n, router_rows, 128)
    if small:
        dn1, r_back, gws, goo, gor, gol, grs, gvs, *_ = back(
            n_e,
            n_z,
            cap,
            heads,
            da,
            r_rows,
            r_far,
            grad_router,
            n1,
            raw,
            value,
            mix,
            unpicks,
            grad_gain_two[None],
            *shape,
        )
        gw_sum = gws.astype(F32).transpose(0, 2, 1, 3).reshape(n_e, shard, -1)
        lower_sum, upper_sum = (
            jnp.where(came, lax.dynamic_index_in_dim(inbox, z, keepdims=False).astype(F32), 0.0)
            for came, inbox in ((z > 0, gor), (z < n_z - 1, gol))
        )
        grad_out = goo.astype(F32) + lower_sum + upper_sum
        grad_router = jnp.sum(grs, axis=0)
        grad_gains = lax.dynamic_slice_in_dim(
            jnp.sum(gvs, axis=0).reshape(-1), device * gain_size, gain_size
        )
    else:
        r_back = give_back(n_e, n_z, cap, r_rows, unpicks, 7)
        da_all = plane_gather(n_e, n_z, da)
        dn_part, gw, go, g1_part, gh_part = attend_back(
            n_e,
            heads,
            da_all,
            n1,
            raw,
            value,
            mix,
            turn_table,
            seg,
            w_all,
            wo_all,
            gain_heads,
        )
        gain_all = jnp.concatenate(
            [(g1_part / gain_one)[0], grad_gain_two, gh_part[0], gh_part[1]]
        ).reshape(n, -1)
        grad_rows = -(-(router_rows + gain_rows) // 8) * 8
        gain_all = pad_lanes(gain_all, (grad_rows - router_rows) * 128)
        gm = jnp.concatenate([grad_router, gain_all.reshape(n, -1, 128)], axis=1)
        dn1, gws, gos, gms = finish(
            n_e,
            n_z,
            dn_part,
            gw.reshape(n, shard, -1),
            go.reshape(n_z, -1, width),
            gm,
        )
        gw_sum = jnp.sum(gws.reshape(n_e, n_z, shard, -1).astype(F32), axis=1)
        grad_out = jnp.sum(gos.astype(F32), axis=0)
        gm_sum = jnp.sum(gms, axis=0)
        grad_router = gm_sum[:router_rows]
        grad_gains = gm_sum[router_rows:].reshape(-1)[:gain_size]
    block_out = (hidden + jnp.sum(r_back.astype(F32), axis=0)).astype(BF)
    r_one = lax.rsqrt(jnp.mean(inputs * inputs, axis=-1, keepdims=True) + EPSILON)
    nu_one = inputs * r_one
    scaled = dn1 * gain_one
    grad_tokens = dhidden + r_one * (
        scaled - nu_one * jnp.mean(scaled * nu_one, axis=-1, keepdims=True)
    )
    q_size = heads * HEAD
    grad_query = gw_sum[:, :, :q_size].transpose(1, 0, 2).reshape(shard, -1)
    kv_sum = gw_sum[:, :, q_size:].reshape(kv_heads, -1, shard, 2 * HEAD).sum(axis=1)
    grad_key = kv_sum[:, :, :HEAD].transpose(1, 0, 2).reshape(shard, -1)
    grad_value = kv_sum[:, :, HEAD:].transpose(1, 0, 2).reshape(shard, -1)
    return (
        block_out,
        grad_tokens,
        grad_query,
        grad_key,
        grad_value,
        grad_out,
        grad_router.reshape(shard, experts),
        grad_gains,
        grad_gate[None],
        grad_up[None],
        grad_down[None],
    )


def solution(mesh):
    both = ("expert", "fsdp")
    two, three = P(both, None), P(both, None, None)
    return jax.shard_map(
        partial(local, mesh.shape["expert"], mesh.shape["fsdp"]),
        mesh=mesh,
        in_specs=(two, two, P(), P(), two) + (two,) * 5 + (P(both),) + (three,) * 3,
        out_specs=(two,) * 7 + (P(both),) + (three,) * 3,
        check_vma=False,
    )
```
